32 devices in a mesh: tm: 32 (over z, y, x, core), chan: 1.
Axes of the slice: x: 2, y: 2, z: 4, core: 2. Of those that a mesh axis runs over, the one named last changes fastest.
Arguments:
- signal: bfloat16 [384, 4096], P('chan', 'tm'), may hold values from -6 to 6
- codes_init: float32 [128, 4096], P(None, 'tm'), may hold values from -2 to 2
- dictionary_init: float32 [128, 36864], P(None, 'chan'), may hold values from -6 to 6
- threshold: float32 [128], replicated, may hold values from 0.05 to 0.5
- plan: int32 [8], replicated, may hold values from 0 to 7, each once
Outputs:
- sparse_codes: float32 [128, 4096], P(None, 'tm')
- dictionary: float32 [128, 36864], P(None, 'chan')
- residual: float32 [384, 4096], P('chan', 'tm')
The draws below stay inside these ranges and needn't reach their ends.
Inputs may be any that keep to these rules, and one draw needn't show every extreme that they name: `plan`: every atom block from 0 to 7 appears exactly once.
All inputs are finite; a program needn't handle non-finite values.
Results may differ from the reference program's by a relative error of at most 0.013.
Values may be sent and summed in bfloat16 or wider, within the bound.
No kernel may reach another device: no remote copies, remote signals or barrier semaphores. Data moves between devices by JAX's collectives and lax.ppermute only.
A program may use at most 128 MiB of HBM per device.

```python
import math
import jax
import jax.numpy as jnp
from jax import lax

C = 384
K = 128
L = 96
BLOCKS = 8
BLOCK_ATOMS = 16
INNER = 2
OUTER = 2
TIME = 4096


def steps_of(key, extent, cuts, low, high):
    def one(dim, blocks):
        draws = jax.random.uniform(jax.random.fold_in(jax.random.fold_in(key, 6), dim), (blocks,), jnp.float32, low / len(cuts), high / len(cuts))
        return jnp.repeat(jnp.exp(draws), extent[dim] // blocks).reshape((-1,) + (1,) * (len(extent) - dim - 1))

    gain = one(*cuts[0])
    for cut in cuts[1:]:
        gain = gain * one(*cut)
    return gain


def centred(stream_key, extent, deviation, bound, pieces=(), kind=jnp.bfloat16):
    drawn = deviation * jax.random.normal(stream_key, extent, jnp.float32)
    if pieces:
        drawn = drawn * steps_of(stream_key, extent, pieces, -0.22, 0.18)
    return jnp.clip(drawn, -bound, bound).astype(kind)


def setup_inputs(seed: int = 0) -> dict:
    arg_keys = jax.random.split(jax.random.key(seed), 6)
    signal = centred(arg_keys[0], (C, TIME), 1.0, 6.0, ((1, 32),))
    codes_init = centred(arg_keys[1], (K, TIME), 0.3, 2.0, ((1, 32),), jnp.float32)
    dictionary_init = centred(arg_keys[2], (K, C * L), 1.0, 6.0, (), jnp.float32)
    threshold = jnp.clip(jnp.exp(jax.random.uniform(arg_keys[3], (K,), jnp.float32, math.log(0.05), math.log(0.5))), 0.05, 0.5)
    plan = jax.random.permutation(arg_keys[4], BLOCKS).astype(jnp.int32)
    return {"signal": signal, "codes_init": codes_init, "dictionary_init": dictionary_init, "threshold": threshold, "plan": plan}


code_rate = 0.3
move_rate = 0.5
tiny_eps = 1e-06

def convolve(dict_low, code_low):
    samples = code_low.shape[1]
    atom_cube = dict_low.astype(jnp.float32).reshape(K, C, L)
    padded = jnp.concatenate([jnp.zeros((K, L - 1), jnp.float32), code_low.astype(jnp.float32)], axis=1)

    def accumulate(offset, running):
        column = lax.dynamic_index_in_dim(atom_cube, offset, 2, keepdims=False)
        shifted = lax.dynamic_slice_in_dim(padded, L - 1 - offset, samples, 1)
        return running + jnp.dot(column.T, shifted, precision=lax.Precision.HIGHEST)
    total_sum = lax.fori_loop(0, L, accumulate, jnp.zeros((C, samples), jnp.float32))
    return total_sum * (C * L) ** (-0.5)

def pad_right(resid_low):
    return jnp.concatenate([resid_low.astype(jnp.float32), jnp.zeros((C, L - 1), jnp.float32)], axis=1)

def correlate(dict_low, resid_low):
    samples = resid_low.shape[1]
    atom_cube = dict_low.astype(jnp.float32).reshape(K, C, L)
    padded = pad_right(resid_low)

    def accumulate(offset, running):
        column = lax.dynamic_index_in_dim(atom_cube, offset, 2, keepdims=False)
        shifted = lax.dynamic_slice_in_dim(padded, offset, samples, 1)
        return running + jnp.dot(column, shifted, precision=lax.Precision.HIGHEST)
    total_sum = lax.fori_loop(0, L, accumulate, jnp.zeros((K, samples), jnp.float32))
    return total_sum * (C * L) ** (-0.5)

def block_gradient(code_block, resid_low):
    samples = resid_low.shape[1]
    padded = pad_right(resid_low)
    block_f = code_block.astype(jnp.float32)

    def per_offset(offset):
        shifted = lax.dynamic_slice_in_dim(padded, offset, samples, 1)
        return jnp.dot(block_f, shifted.T, precision=lax.Precision.HIGHEST)
    stacked = lax.map(per_offset, jnp.arange(L))
    return jnp.transpose(stacked, (1, 2, 0)).reshape(BLOCK_ATOMS, C * L)

def reference(signal, codes_init, dictionary_init, threshold, plan):
    code_state = codes_init
    dictionary = dictionary_init
    limit = threshold[:, None]
    entries = C * L
    residual = signal.astype(jnp.float32)
    for outer_step in range(OUTER):
        dict_low = dictionary.astype(jnp.bfloat16)
        for inner_step in range(INNER):
            code_low = code_state.astype(jnp.bfloat16)
            residual = signal.astype(jnp.float32) - convolve(dict_low, code_low)
            scores = correlate(dict_low, residual.astype(jnp.bfloat16))
            stepped = code_state + code_rate * scores
            code_state = stepped - jnp.clip(stepped, -limit, limit)
        code_low = code_state.astype(jnp.bfloat16)
        residual = signal.astype(jnp.float32) - convolve(dict_low, code_low)
        resid_low = residual.astype(jnp.bfloat16)
        first_row = (plan[outer_step] * BLOCK_ATOMS).astype(jnp.int32)
        code_block = lax.dynamic_slice_in_dim(code_low, first_row, BLOCK_ATOMS, 0)
        gradient = block_gradient(code_block, resid_low)
        old_atoms = lax.dynamic_slice_in_dim(dictionary, first_row, BLOCK_ATOMS, 0)
        mean_sq = lax.optimization_barrier(jnp.sum(old_atoms * old_atoms, axis=1)) / entries + tiny_eps
        along_coef = lax.optimization_barrier(jnp.sum(gradient * old_atoms, axis=1)) / entries / mean_sq
        across = gradient - along_coef[:, None] * old_atoms
        spread = lax.optimization_barrier(jnp.sum(across * across, axis=1)) / entries + tiny_eps
        renewed = (old_atoms + move_rate * across / jnp.sqrt(spread)[:, None]) / jnp.sqrt(mean_sq + 0.25)[:, None]
        dictionary = lax.dynamic_update_slice_in_dim(dictionary, renewed, first_row, 0)
    return (code_state, dictionary, residual)
```

```python
import functools

import jax
import jax.numpy as jnp
from jax import lax
from jax.experimental import pallas as pl
from jax.experimental.pallas import tpu as pltpu
from jax.sharding import PartitionSpec as P

C = 384
K = 128
L = 96
BLOCK_ATOMS = 16
INNER = 2
OUTER = 2

code_rate = 0.3
move_rate = 0.5
tiny_eps = 1e-06

ROWS = 16
COARSE = L // ROWS
FINE = 4
LANES = 128
VMEM_BYTES = 56 * 1024 * 1024

NN = (((1,), (0,)), ((), ()))
NT = (((1,), (1,)), ((), ()))


def shifted(shard, axis, by):
    peers = lax.axis_size(axis)
    pairs = [(i, i + by) for i in range(peers) if 0 <= i + by < peers]
    return lax.ppermute(shard, axis, pairs)


def by_tap(columns_ref, turned_ref):
    width = columns_ref.shape[1]
    for start in range(0, width, 384):
        turned_ref[start : start + 384, :] = columns_ref[:, start : start + 384].T


def layout_kernel(dict_ref, taps_ref, turned_ref):
    by_tap(dict_ref, turned_ref)
    for tap in range(L):
        taps_ref[tap] = turned_ref[pl.ds(tap, ROWS, stride=L), :].astype(jnp.bfloat16)


def layout(dictionary, channels):
    steps = channels // ROWS
    return pl.pallas_call(
        layout_kernel,
        grid=(steps,),
        in_specs=[pl.BlockSpec((K, ROWS * L), lambda i: (0, i))],
        out_specs=pl.BlockSpec((L, ROWS, K), lambda i: (0, i, 0)),
        out_shape=jax.ShapeDtypeStruct((L, channels, K), jnp.bfloat16),
        scratch_shapes=[pltpu.VMEM((ROWS * L, K), jnp.float32)],
        compiler_params=pltpu.CompilerParams(vmem_limit_bytes=VMEM_BYTES),
        name="layout",
    )(dictionary)


def patch_kernel(row_ref, atoms_ref, taps_ref, out_ref, columns_ref, turned_ref):
    first_row = pl.multiple_of(row_ref[0], BLOCK_ATOMS)

    @pl.when(pl.program_id(0) == 0)
    def _():
        columns_ref[...] = jnp.zeros_like(columns_ref)

    columns_ref[pl.ds(first_row, BLOCK_ATOMS), :] = atoms_ref[...]
    by_tap(columns_ref, turned_ref)
    lane = lax.broadcasted_iota(jnp.int32, (ROWS, K), 1)
    renewed = (lane >= first_row) & (lane < first_row + BLOCK_ATOMS)
    for tap in range(L):
        fresh = turned_ref[pl.ds(tap, ROWS, stride=L), :]
        kept = taps_ref[tap].astype(jnp.float32)
        out_ref[tap] = jnp.where(renewed, fresh, kept).astype(jnp.bfloat16)


def patch(first_row, atoms, taps):
    channels = taps.shape[1]
    steps = channels // ROWS
    return pl.pallas_call(
        patch_kernel,
        grid_spec=pltpu.PrefetchScalarGridSpec(
            num_scalar_prefetch=1,
            grid=(steps,),
            in_specs=[
                pl.BlockSpec((BLOCK_ATOMS, ROWS * L), lambda i, r: (0, i)),
                pl.BlockSpec((L, ROWS, K), lambda i, r: (0, i, 0)),
            ],
            out_specs=pl.BlockSpec((L, ROWS, K), lambda i, r: (0, i, 0)),
            scratch_shapes=[
                pltpu.VMEM((K, ROWS * L), jnp.float32),
                pltpu.VMEM((ROWS * L, K), jnp.float32),
            ],
        ),
        out_shape=jax.ShapeDtypeStruct(taps.shape, jnp.bfloat16),
        input_output_aliases={2: 0},
        compiler_params=pltpu.CompilerParams(vmem_limit_bytes=VMEM_BYTES),
        name="patch",
    )(first_row, atoms, taps)


def extents():
    reach = [(L, 0)]
    for _ in range(INNER):
        reach.insert(0, (reach[0][0] + L, reach[0][1] + L))
    return reach


def hops_of(reach, segment):
    return -(-reach // segment)


def codes_kernel(
    segment,
    peers,
    code_hops,
    signal_hops,
    place_ref,
    limit_ref,
    *refs,
):
    code_refs = refs[: len(code_hops)]
    signal_refs = refs[len(code_hops) : len(code_hops) + len(signal_hops)]
    taps_hbm, codes_out, resid_out, payload_out = refs[len(code_hops) + len(signal_hops) :][:4]
    taps, zf, zb, sf, rb, zz, rr, fine, acc, tall, sems = refs[len(code_hops) + len(signal_hops) + 4 :]
    channels = taps.shape[2]
    tiles = channels // LANES
    scale = (C * L) ** (-0.5)
    base = place_ref[0]
    first_row = pl.multiple_of(place_ref[1], BLOCK_ATOMS)
    total_time = peers * segment
    reach = extents()
    z_left, z_right = reach[0]
    s_left, s_right = z_left - L, z_right
    passes = ROWS // FINE

    def tap_copy(step):
        return pltpu.make_async_copy(
            taps_hbm.at[:, pl.ds(step * FINE, FINE)],
            taps.at[:, pl.ds(step * FINE, FINE)],
            sems.at[step],
        )

    for step in range(passes):
        tap_copy(step).start()

    for hop, ref in zip(code_hops, code_refs):
        low = max(-z_left, hop * segment)
        high = min(segment + z_right, (hop + 1) * segment)
        piece = ref[...].T
        zf[low + z_left : high + z_left, :] = piece[low - hop * segment : high - hop * segment]
    for hop, ref in zip(signal_hops, signal_refs):
        low = max(-s_left, hop * segment)
        high = min(segment + s_right, (hop + 1) * segment)
        piece = ref[...].astype(jnp.float32).T
        sf[low + s_left : high + s_left, :] = piece[low - hop * segment : high - hop * segment]
    zb[...] = zf[...].astype(jnp.bfloat16)

    def moment(start, count, width):
        return base + start + lax.broadcasted_iota(jnp.int32, (count, width), 0)

    def convolve(start, count, wait):
        rows = count + ROWS
        for coarse in range(COARSE):
            begin = start - ROWS - ROWS * coarse + z_left
            zz[:rows, coarse * K : (coarse + 1) * K] = zb[begin : begin + rows, :]
        acc[:, :count, :] = jnp.zeros((tiles, count, LANES), jnp.float32)

        def one_pass(step, carry):
            if wait:
                tap_copy(step).wait()
            for pair in range(FINE // 2):
                fine_lag = step * FINE + 2 * pair
                weights = jnp.concatenate(
                    [
                        jnp.concatenate([taps[m, fine_lag + j] for m in range(COARSE)], axis=1)
                        for j in range(2)
                    ],
                    axis=0,
                )
                product = lax.dot_general(
                    zz[:rows, :], weights, NT, preferred_element_type=jnp.float32
                )
                for j in range(2):
                    for tile in range(tiles):
                        column = j * channels + tile * LANES
                        fine[2 * pair + j, tile, :rows, :] = product[:, column : column + LANES]
            for tile in range(tiles):
                total = acc[tile, :count, :]
                for j in range(FINE):
                    total += fine[j, tile, pl.ds(ROWS - step * FINE - j, count), :]
                acc[tile, :count, :] = total
            return carry

        lax.fori_loop(0, passes, one_pass, 0)

    def correlate(start, count):
        rows = count + ROWS
        for coarse in range(COARSE):
            begin = start + ROWS * coarse + s_left
            rr[:rows, coarse * channels : (coarse + 1) * channels] = rb[begin : begin + rows, :]
        acc[0, :count, :] = jnp.zeros((count, LANES), jnp.float32)

        def one_pass(step, carry):
            for pair in range(FINE // 2):
                fine_lag = step * FINE + 2 * pair
                weights = jnp.concatenate(
                    [
                        jnp.concatenate([taps[m, fine_lag + j] for m in range(COARSE)], axis=0)
                        for j in range(2)
                    ],
                    axis=1,
                )
                product = lax.dot_general(
                    rr[:rows, :], weights, NN, preferred_element_type=jnp.float32
                )
                for j in range(2):
                    fine[2 * pair + j, 0, :rows, :] = product[:, j * K : (j + 1) * K]
            total = acc[0, :count, :]
            for j in range(FINE):
                total += fine[j, 0, pl.ds(step * FINE + j, count), :]
            acc[0, :count, :] = total
            return carry

        lax.fori_loop(0, passes, one_pass, 0)

    limit = limit_ref[...]
    for step in range(INNER):
        left, right = reach[step + 1]
        start, count = -left, left + segment + right + L
        convolve(start, count, step == 0)
        inside = moment(start, count, LANES) < total_time
        for tile in range(tiles):
            column = slice(tile * LANES, (tile + 1) * LANES)
            value = sf[start + s_left : start + s_left + count, column] - scale * acc[tile, :count, :]
            rb[start + s_left : start + s_left + count, column] = jnp.where(
                inside, value, 0.0
            ).astype(jnp.bfloat16)
        count = left + segment + right
        correlate(start, count)
        window = slice(start + z_left, start + z_left + count)
        stepped = zf[window, :] + code_rate * (scale * acc[0, :count, :])
        state = stepped - jnp.clip(stepped, -limit, limit)
        state = jnp.where(moment(start, count, K) >= 0, state, 0.0)
        zf[window, :] = state
        zb[window, :] = state.astype(jnp.bfloat16)

    convolve(0, segment, False)
    for tile in range(tiles):
        column = slice(tile * LANES, (tile + 1) * LANES)
        value = sf[s_left : s_left + segment, column] - scale * acc[tile, :segment, :]
        value = value.T
        resid_out[column, :] = value
        tall[column, :] = value
    codes_out[...] = zf[z_left : z_left + segment, :].T
    block = codes_out[pl.ds(first_row, BLOCK_ATOMS), :].astype(jnp.bfloat16)
    share = channels // peers
    share_rows = payload_out.shape[1] - BLOCK_ATOMS
    for peer in range(peers):
        payload_out[peer, :share_rows, :] = tall[peer * share : peer * share + share_rows, :].astype(
            jnp.bfloat16
        )
        payload_out[peer, share_rows:, :] = block


def run_codes(place, limit, codes, signals, taps, segment, peers):
    code_hops, signal_hops = tuple(codes), tuple(signals)
    channels = taps.shape[1]
    share = channels // peers
    share_rows = -(-share // ROWS) * ROWS
    reach = extents()
    z_rows = reach[0][0] + segment + reach[0][1]
    s_rows = z_rows - L
    longest = s_rows + ROWS
    scored = reach[1][0] + segment + reach[1][1] + ROWS
    whole = lambda: pl.BlockSpec(memory_space=pltpu.VMEM)
    return pl.pallas_call(
        functools.partial(codes_kernel, segment, peers, code_hops, signal_hops),
        in_specs=[pl.BlockSpec(memory_space=pltpu.SMEM), whole()]
        + [whole() for _ in code_hops + signal_hops]
        + [pl.BlockSpec(memory_space=pl.ANY)],
        out_specs=[whole(), whole(), whole()],
        out_shape=[
            jax.ShapeDtypeStruct((K, segment), jnp.float32),
            jax.ShapeDtypeStruct((channels, segment), jnp.float32),
            jax.ShapeDtypeStruct((peers, share_rows + BLOCK_ATOMS, segment), jnp.bfloat16),
        ],
        scratch_shapes=[
            pltpu.VMEM((COARSE, ROWS, channels, K), jnp.bfloat16),
            pltpu.VMEM((z_rows, K), jnp.float32),
            pltpu.VMEM((z_rows, K), jnp.bfloat16),
            pltpu.VMEM((s_rows, channels), jnp.float32),
            pltpu.VMEM((s_rows, channels), jnp.bfloat16),
            pltpu.VMEM((longest, COARSE * K), jnp.bfloat16),
            pltpu.VMEM((scored, COARSE * channels), jnp.bfloat16),
            pltpu.VMEM((FINE, channels // LANES, longest, LANES), jnp.float32),
            pltpu.VMEM((channels // LANES, s_rows, LANES), jnp.float32),
            pltpu.VMEM((channels + ROWS, segment), jnp.float32),
            pltpu.SemaphoreType.DMA((ROWS // FINE,)),
        ],
        compiler_params=pltpu.CompilerParams(vmem_limit_bytes=VMEM_BYTES),
        name="codes",
    )(
        place,
        limit,
        *codes.values(),
        *signals.values(),
        taps.reshape(COARSE, ROWS, channels, K),
    )


def gradient_kernel(share, source_ref, blocks_ref, out_ref, rf, zf, rr, zz):
    peers, rows, segment = blocks_ref.shape
    share_rows = rows - BLOCK_ATOMS
    span = peers * segment
    rf[:, span:] = jnp.zeros((share_rows, LANES), jnp.float32)
    zf[:, :LANES] = jnp.zeros((BLOCK_ATOMS, LANES), jnp.float32)
    for peer in range(peers):
        column = peer * segment
        rf[:, column : column + segment] = blocks_ref[peer, :share_rows, :].astype(jnp.float32)
        zf[:, LANES + column : LANES + column + segment] = blocks_ref[peer, share_rows:, :].astype(
            jnp.float32
        )
    for lag in range(ROWS):
        rr[lag * share_rows : (lag + 1) * share_rows, :] = rf[:, lag : lag + span].astype(jnp.bfloat16)
    for coarse in range(COARSE):
        begin = LANES - ROWS * coarse
        zz[coarse * BLOCK_ATOMS : (coarse + 1) * BLOCK_ATOMS, :] = zf[:, begin : begin + span].astype(
            jnp.bfloat16
        )
    lagged = lax.dot_general(zz[...], rr[...], NT, preferred_element_type=jnp.float32)
    lagged = lagged.astype(jnp.bfloat16)
    wide = ROWS * share_rows
    entries = share * L
    total = jnp.zeros((BLOCK_ATOMS, entries), jnp.float32)
    for coarse in range(COARSE):
        row = lax.broadcasted_iota(jnp.int32, (wide, entries), 0) + coarse * wide
        chosen = (row == source_ref[...]).astype(jnp.float32).astype(jnp.bfloat16)
        total += lax.dot_general(
            lagged[coarse * BLOCK_ATOMS : (coarse + 1) * BLOCK_ATOMS, :],
            chosen,
            NN,
            preferred_element_type=jnp.float32,
        )
    out_ref[...] = total.astype(jnp.bfloat16)


def share_gradient(blocks, share):
    peers, rows, segment = blocks.shape
    share_rows = rows - BLOCK_ATOMS
    span = peers * segment
    entry = jnp.arange(share * L, dtype=jnp.int32)
    channel, tap = entry // L, entry % L
    source = (tap // ROWS) * (ROWS * share_rows) + (tap % ROWS) * share_rows + channel
    return pl.pallas_call(
        functools.partial(gradient_kernel, share),
        out_shape=jax.ShapeDtypeStruct((BLOCK_ATOMS, share * L), jnp.bfloat16),
        scratch_shapes=[
            pltpu.VMEM((share_rows, span + LANES), jnp.float32),
            pltpu.VMEM((BLOCK_ATOMS, LANES + span), jnp.float32),
            pltpu.VMEM((ROWS * share_rows, span), jnp.bfloat16),
            pltpu.VMEM((COARSE * BLOCK_ATOMS, span), jnp.bfloat16),
        ],
        compiler_params=pltpu.CompilerParams(vmem_limit_bytes=VMEM_BYTES),
        name="gradient",
    )(source[None, :], blocks)


def renew_kernel(row_ref, grad_ref, dict_hbm, out_hbm, atoms_ref, old, across, sems):
    first_row = pl.multiple_of(row_ref[0], BLOCK_ATOMS)
    peers, _, width = grad_ref.shape
    entries = C * L
    fetch = pltpu.make_async_copy(dict_hbm.at[pl.ds(first_row, BLOCK_ATOMS)], old, sems.at[0])
    fetch.start()
    fetch.wait()

    def column(peer):
        return pl.ds(pl.multiple_of(peer * width, LANES), width)

    zeros = jnp.zeros((BLOCK_ATOMS, width), jnp.float32)

    def sums(peer, carry):
        square, dot = carry
        before = old[:, column(peer)]
        return square + before * before, dot + grad_ref[peer].astype(jnp.float32) * before

    square, dot = lax.fori_loop(0, peers, sums, (zeros, zeros))
    mean_sq = jnp.sum(square, axis=1, keepdims=True) / entries + tiny_eps
    along = jnp.sum(dot, axis=1, keepdims=True) / entries / mean_sq

    def project(peer, square):
        value = grad_ref[peer].astype(jnp.float32) - along * old[:, column(peer)]
        across[:, column(peer)] = value
        return square + value * value

    square = lax.fori_loop(0, peers, project, zeros)
    spread = jnp.sum(square, axis=1, keepdims=True) / entries + tiny_eps
    step = move_rate / jnp.sqrt(spread)
    norm = 1.0 / jnp.sqrt(mean_sq + 0.25)

    def renew(peer, carry):
        atoms_ref[:, column(peer)] = (old[:, column(peer)] + step * across[:, column(peer)]) * norm
        return carry

    lax.fori_loop(0, peers, renew, 0)
    store = pltpu.make_async_copy(atoms_ref, out_hbm.at[pl.ds(first_row, BLOCK_ATOMS)], sems.at[1])
    store.start()
    store.wait()


def renew(first_row, gradient, dictionary):
    width = dictionary.shape[1]
    return pl.pallas_call(
        renew_kernel,
        in_specs=[
            pl.BlockSpec(memory_space=pltpu.SMEM),
            pl.BlockSpec(memory_space=pltpu.VMEM),
            pl.BlockSpec(memory_space=pl.ANY),
        ],
        out_specs=[pl.BlockSpec(memory_space=pl.ANY), pl.BlockSpec(memory_space=pltpu.VMEM)],
        out_shape=[
            jax.ShapeDtypeStruct(dictionary.shape, jnp.float32),
            jax.ShapeDtypeStruct((BLOCK_ATOMS, width), jnp.float32),
        ],
        scratch_shapes=[
            pltpu.VMEM((BLOCK_ATOMS, width), jnp.float32),
            pltpu.VMEM((BLOCK_ATOMS, width), jnp.float32),
            pltpu.SemaphoreType.DMA((2,)),
        ],
        input_output_aliases={2: 0},
        compiler_params=pltpu.CompilerParams(vmem_limit_bytes=VMEM_BYTES),
        name="renew",
    )(first_row, gradient, dictionary)


def whole_channels(signal, codes_init, dictionary_init, threshold, plan):
    channels, segment = signal.shape
    peers = lax.axis_size("tm")
    share = channels // peers
    limit = threshold[None, :]
    reach = extents()
    z_left, z_right = reach[0]
    s_left, s_right = z_left - L, z_right

    def window(shard, left, right):
        hops = range(-hops_of(left, segment), hops_of(right, segment) + 1)
        return {hop: shard if hop == 0 else shifted(shard, "tm", -hop) for hop in hops}

    base = lax.axis_index("tm") * segment
    signals = window(signal, s_left, s_right)
    code_state = codes_init
    dictionary = dictionary_init
    taps = layout(dictionary, channels)
    for outer_step in range(OUTER):
        first_row = plan[outer_step] * BLOCK_ATOMS
        place = jnp.stack([base, first_row]).astype(jnp.int32)
        codes = window(code_state, z_left, z_right)
        code_state, residual, payload = run_codes(
            place, limit, codes, signals, taps, segment, peers
        )
        blocks = lax.all_to_all(payload, "tm", 0, 0, tiled=True)
        piece = share_gradient(blocks, share)
        gradient = lax.all_gather(piece, "tm")
        dictionary, atoms = renew(first_row[None].astype(jnp.int32), gradient, dictionary)
        if outer_step + 1 < OUTER:
            taps = patch(first_row[None].astype(jnp.int32), atoms, taps)
    return code_state, dictionary, residual


def renew_atoms(old_atoms, across, mean_sq, spread):
    return (old_atoms + move_rate * across / jnp.sqrt(spread)[:, None]) / jnp.sqrt(mean_sq + 0.25)[
        :, None
    ]


def split_channels(signal, codes_init, dictionary_init, threshold, plan):
    segment = signal.shape[1]
    local_chan = signal.shape[0]
    unit_scale = (C * L) ** (-0.5)
    entries = C * L
    limit = threshold[:, None]

    def convolve(atom_cube, code_low):
        code_edge = shifted(code_low[:, segment - (L - 1) :], "tm", 1)
        extended = jnp.concatenate([code_edge, code_low], axis=1)
        lagged = jnp.stack(
            [extended[:, L - 1 - offset : L - 1 - offset + segment] for offset in range(L)], axis=1
        )
        return unit_scale * jnp.einsum(
            "kcl,klt->ct", atom_cube, lagged, preferred_element_type=jnp.float32
        )

    def resid_columns(resid_low):
        resid_edge = shifted(resid_low[:, : L - 1], "tm", -1)
        extended = jnp.concatenate([resid_low, resid_edge], axis=1)
        lagged = jnp.stack([extended[:, offset : offset + segment] for offset in range(L)], axis=1)
        return lagged.reshape(local_chan * L, segment)

    code_state = codes_init
    dictionary = dictionary_init
    residual = signal.astype(jnp.float32)
    for outer_step in range(OUTER):
        dict_low = dictionary.astype(jnp.bfloat16)
        atom_cube = dict_low.reshape(K, local_chan, L)
        for inner_step in range(INNER):
            code_low = code_state.astype(jnp.bfloat16)
            residual = signal.astype(jnp.float32) - convolve(atom_cube, code_low)
            lagged = resid_columns(residual.astype(jnp.bfloat16))
            partial_value = unit_scale * jnp.dot(
                dict_low, lagged, preferred_element_type=jnp.float32
            )
            scores = lax.psum(partial_value.astype(jnp.bfloat16), "chan").astype(jnp.float32)
            stepped = code_state + code_rate * scores
            code_state = stepped - jnp.clip(stepped, -limit, limit)
        code_low = code_state.astype(jnp.bfloat16)
        residual = signal.astype(jnp.float32) - convolve(atom_cube, code_low)
        lagged = resid_columns(residual.astype(jnp.bfloat16))
        first_row = plan[outer_step] * BLOCK_ATOMS
        code_block = lax.dynamic_slice_in_dim(code_low, first_row, BLOCK_ATOMS, 0)
        local_grad = lax.dot_general(
            code_block, lagged, (((1,), (1,)), ((), ())), preferred_element_type=jnp.float32
        )
        old_atoms = lax.dynamic_slice_in_dim(dictionary, first_row, BLOCK_ATOMS, 0)
        gradient = lax.psum(local_grad, "tm")
        dot_sum, square_sum = lax.psum(
            (jnp.sum(gradient * old_atoms, axis=1), jnp.sum(old_atoms * old_atoms, axis=1)), "chan"
        )
        mean_sq = square_sum / entries + tiny_eps
        along_coef = dot_sum / entries / mean_sq
        across = gradient - along_coef[:, None] * old_atoms
        spread = lax.psum(jnp.sum(across * across, axis=1), "chan") / entries + tiny_eps
        renewed = renew_atoms(old_atoms, across, mean_sq, spread)
        dictionary = lax.dynamic_update_slice_in_dim(dictionary, renewed, first_row, 0)
    return (code_state, dictionary, residual)


def shards(signal, codes_init, dictionary_init, threshold, plan):
    channels, segment = signal.shape
    peers = lax.axis_size("tm")
    fits = (
        lax.axis_size("chan") == 1
        and segment % LANES == 0
        and channels % LANES == 0
        and channels % peers == 0
        and (channels // peers * L) % LANES == 0
    )
    body = whole_channels if fits else split_channels
    return body(signal, codes_init, dictionary_init, threshold, plan)


def solution(mesh):
    placed = (P("chan", "tm"), P(None, "tm"), P(None, "chan"), P(), P())
    return jax.shard_map(
        shards,
        mesh=mesh,
        in_specs=placed,
        out_specs=(P(None, "tm"), P(None, "chan"), P("chan", "tm")),
        check_vma=False,
    )
```

```python
import functools

import jax
import jax.numpy as jnp
from jax import lax
from jax.experimental import pallas as pl
from jax.experimental.pallas import tpu as pltpu
from jax.sharding import PartitionSpec as P

C = 384
K = 128
L = 96
BLOCK_ATOMS = 16
INNER = 2
OUTER = 2

code_rate = 0.3
move_rate = 0.5
tiny_eps = 1e-06

ROWS = 16
COARSE = L // ROWS
STRIDE = L + 1
FINE = 4
LANES = 128
VMEM_BYTES = 56 * 1024 * 1024

NN = (((1,), (0,)), ((), ()))
NT = (((1,), (1,)), ((), ()))


def shifted(shard, axis, by):
    peers = lax.axis_size(axis)
    pairs = [(i, i + by) for i in range(peers) if 0 <= i + by < peers]
    return lax.ppermute(shard, axis, pairs)


def by_tap(columns_ref, turned_ref):
    width = columns_ref.shape[1]
    for start in range(0, width, 4 * L):
        turned = columns_ref[:, start : start + 4 * L].T
        for q in range(4):
            row = (start // L + q) * STRIDE
            turned_ref[row : row + L, :] = turned[q * L : (q + 1) * L]


def layout_kernel(dict_ref, taps_ref, turned_ref):
    by_tap(dict_ref, turned_ref)
    for tap in range(L):
        taps_ref[tap] = turned_ref[pl.ds(tap, ROWS, stride=STRIDE), :].astype(jnp.bfloat16)


def layout(dictionary, channels):
    steps = channels // ROWS
    return pl.pallas_call(
        layout_kernel,
        grid=(steps,),
        in_specs=[pl.BlockSpec((K, ROWS * L), lambda i: (0, i))],
        out_specs=pl.BlockSpec((L, ROWS, K), lambda i: (0, i, 0)),
        out_shape=jax.ShapeDtypeStruct((L, channels, K), jnp.bfloat16),
        scratch_shapes=[pltpu.VMEM((ROWS * STRIDE, K), jnp.float32)],
        compiler_params=pltpu.CompilerParams(vmem_limit_bytes=VMEM_BYTES),
        name="layout",
    )(dictionary)


def extents():
    reach = [(L, 0)]
    for _ in range(INNER):
        reach.insert(0, (reach[0][0] + L, reach[0][1] + L))
    return reach


def hops_of(reach, segment):
    return -(-reach // segment)


def codes_kernel(segment, peers, code_hops, signal_hops, packed, atoms_count, copies, *refs):
    refs = list(refs)

    def take(count):
        taken = refs[:count]
        del refs[:count]
        return taken

    place_ref, limit_ref = take(2)
    code_refs = take(len(code_hops))
    signal_refs = take(len(signal_hops))
    atoms_refs = take(atoms_count)
    (taps_hbm,) = take(1)
    dict_hbm = take(1) if copies else None
    codes_out, resid_out, payload_out = take(3)
    dict_out = take(1) if copies else None
    taps, zf, zb, sf, rb, zz, rr, fine, acc, tall, sems = take(11)
    copy_sems = take(1) if copies else None
    columns, turned = take(2) if atoms_count else (None, None)
    channels = taps.shape[2]
    tiles = channels // LANES
    scale = (C * L) ** (-0.5)
    base = place_ref[0]
    first_row = pl.multiple_of(place_ref[1], BLOCK_ATOMS)
    total_time = peers * segment
    reach = extents()
    z_left, z_right = reach[0]
    s_left, s_right = z_left - L, z_right
    passes = ROWS // FINE

    def tap_copy(step):
        return pltpu.make_async_copy(
            taps_hbm.at[:, pl.ds(step * FINE, FINE)],
            taps.at[:, pl.ds(step * FINE, FINE)],
            sems.at[step],
        )

    for step in range(passes):
        tap_copy(step).start()

    def dict_copy(step):
        rows = pl.ds(step * BLOCK_ATOMS, BLOCK_ATOMS)
        return pltpu.make_async_copy(dict_hbm[0].at[rows], dict_out[0].at[rows], copy_sems[0].at[step])

    if copies:
        for step in range(K // BLOCK_ATOMS):
            dict_copy(step).start()

    for hop, ref in zip(code_hops, code_refs):
        low = max(-z_left, hop * segment)
        high = min(segment + z_right, (hop + 1) * segment)
        if hop in packed:
            piece = ref[channels : channels + K, :].astype(jnp.float32)
            piece = (piece + ref[channels + K :, :].astype(jnp.float32)).T
        else:
            piece = ref[...].T
        zf[low + z_left : high + z_left, :] = piece[low - hop * segment : high - hop * segment]
    for hop, ref in zip(signal_hops, signal_refs):
        low = max(-s_left, hop * segment)
        high = min(segment + s_right, (hop + 1) * segment)
        piece = ref[:channels, :].astype(jnp.float32).T
        sf[low + s_left : high + s_left, :] = piece[low - hop * segment : high - hop * segment]
    zb[...] = zf[...].astype(jnp.bfloat16)

    def moment(start, count, width):
        return base + start + lax.broadcasted_iota(jnp.int32, (count, width), 0)

    def convolve(start, count, wait):
        rows = count + ROWS
        for coarse in range(COARSE):
            begin = start - ROWS - ROWS * coarse + z_left
            zz[:rows, coarse * K : (coarse + 1) * K] = zb[begin : begin + rows, :]
        acc[:, :count, :] = jnp.zeros((tiles, count, LANES), jnp.float32)

        def one_pass(step, carry):
            if wait:
                tap_copy(step).wait()
            for pair in range(FINE // 2):
                fine_lag = step * FINE + 2 * pair
                weights = jnp.concatenate(
                    [
                        jnp.concatenate([taps[m, fine_lag + j] for m in range(COARSE)], axis=1)
                        for j in range(2)
                    ],
                    axis=0,
                )
                product = lax.dot_general(
                    zz[:rows, :], weights, NT, preferred_element_type=jnp.float32
                )
                for j in range(2):
                    for tile in range(tiles):
                        column = j * channels + tile * LANES
                        fine[2 * pair + j, tile, :rows, :] = product[:, column : column + LANES]
            for tile in range(tiles):
                total = acc[tile, :count, :]
                for j in range(FINE):
                    total += fine[j, tile, pl.ds(ROWS - step * FINE - j, count), :]
                acc[tile, :count, :] = total
            return carry

        lax.fori_loop(0, passes, one_pass, 0)

    def correlate(start, count):
        rows = count + ROWS
        for coarse in range(COARSE):
            begin = start + ROWS * coarse + s_left
            rr[:rows, coarse * channels : (coarse + 1) * channels] = rb[begin : begin + rows, :]
        acc[0, :count, :] = jnp.zeros((count, LANES), jnp.float32)

        def one_pass(step, carry):
            for pair in range(FINE // 2):
                fine_lag = step * FINE + 2 * pair
                weights = jnp.concatenate(
                    [
                        jnp.concatenate([taps[m, fine_lag + j] for m in range(COARSE)], axis=0)
                        for j in range(2)
                    ],
                    axis=1,
                )
                product = lax.dot_general(
                    rr[:rows, :], weights, NN, preferred_element_type=jnp.float32
                )
                for j in range(2):
                    fine[2 * pair + j, 0, :rows, :] = product[:, j * K : (j + 1) * K]
            total = acc[0, :count, :]
            for j in range(FINE):
                total += fine[j, 0, pl.ds(step * FINE + j, count), :]
            acc[0, :count, :] = total
            return carry

        lax.fori_loop(0, passes, one_pass, 0)

    if atoms_count:
        for step in range(passes):
            tap_copy(step).wait()
    for index in range(atoms_count):
        row = pl.multiple_of(place_ref[2 + index], BLOCK_ATOMS)
        lane = lax.broadcasted_iota(jnp.int32, (ROWS, K), 1)
        renewed = (lane >= row) & (lane < row + BLOCK_ATOMS)
        columns[...] = jnp.zeros_like(columns)

        def patch(group, carry):
            part = pl.ds(pl.multiple_of(group * (ROWS * L), LANES), ROWS * L)
            columns[pl.ds(row, BLOCK_ATOMS), :] = atoms_refs[index][:, part]
            by_tap(columns, turned)
            own = pl.ds(pl.multiple_of(group * ROWS, ROWS), ROWS)
            for tap in range(L):
                fresh = turned[pl.ds(tap, ROWS, stride=STRIDE), :]
                kept = taps[tap // ROWS, tap % ROWS, own, :].astype(jnp.float32)
                taps[tap // ROWS, tap % ROWS, own, :] = jnp.where(renewed, fresh, kept).astype(
                    jnp.bfloat16
                )
            return carry

        lax.fori_loop(0, channels // ROWS, patch, 0)

    limit = limit_ref[...]
    for step in range(INNER):
        left, right = reach[step + 1]
        start, count = -left, left + segment + right + L
        convolve(start, count, step == 0 and not atoms_count)
        inside = moment(start, count, LANES) < total_time
        for tile in range(tiles):
            column = slice(tile * LANES, (tile + 1) * LANES)
            value = sf[start + s_left : start + s_left + count, column] - scale * acc[tile, :count, :]
            rb[start + s_left : start + s_left + count, column] = jnp.where(
                inside, value, 0.0
            ).astype(jnp.bfloat16)
        count = left + segment + right
        correlate(start, count)
        window = slice(start + z_left, start + z_left + count)
        stepped = zf[window, :] + code_rate * (scale * acc[0, :count, :])
        state = stepped - jnp.clip(stepped, -limit, limit)
        state = jnp.where(moment(start, count, K) >= 0, state, 0.0)
        zf[window, :] = state
        zb[window, :] = state.astype(jnp.bfloat16)

    convolve(0, segment, False)
    for tile in range(tiles):
        column = slice(tile * LANES, (tile + 1) * LANES)
        value = sf[s_left : s_left + segment, column] - scale * acc[tile, :segment, :]
        value = value.T
        resid_out[column, :] = value
        tall[column, :] = value
    codes_out[...] = zf[z_left : z_left + segment, :].T
    block = codes_out[pl.ds(first_row, BLOCK_ATOMS), :].astype(jnp.bfloat16)
    share = channels // peers
    share_rows = payload_out.shape[1] - BLOCK_ATOMS
    for peer in range(peers):
        payload_out[peer, :share_rows, :] = tall[peer * share : peer * share + share_rows, :].astype(
            jnp.bfloat16
        )
        payload_out[peer, share_rows:, :] = block
    if copies:
        for step in range(K // BLOCK_ATOMS):
            dict_copy(step).wait()


def run_codes(place, limit, codes, signals, packed, atoms, taps, dictionary, segment, peers):
    code_hops, signal_hops = tuple(codes), tuple(signals)
    channels = taps.shape[1]
    share = channels // peers
    share_rows = -(-share // ROWS) * ROWS
    reach = extents()
    z_rows = reach[0][0] + segment + reach[0][1]
    s_rows = z_rows - L
    longest = s_rows + ROWS
    scored = reach[1][0] + segment + reach[1][1] + ROWS
    copies = dictionary is not None
    whole = lambda: pl.BlockSpec(memory_space=pltpu.VMEM)
    remote = lambda: pl.BlockSpec(memory_space=pl.ANY)
    patching = [
        pltpu.VMEM((K, ROWS * L), jnp.float32),
        pltpu.VMEM((ROWS * STRIDE, K), jnp.float32),
    ]
    return pl.pallas_call(
        functools.partial(
            codes_kernel, segment, peers, code_hops, signal_hops, packed, len(atoms), copies
        ),
        in_specs=[pl.BlockSpec(memory_space=pltpu.SMEM), whole()]
        + [whole() for _ in code_hops + signal_hops]
        + [whole() for _ in atoms]
        + [remote()] * (1 + copies),
        out_specs=[whole(), whole(), whole()] + [remote()] * copies,
        out_shape=[
            jax.ShapeDtypeStruct((K, segment), jnp.float32),
            jax.ShapeDtypeStruct((channels, segment), jnp.float32),
            jax.ShapeDtypeStruct((peers, share_rows + BLOCK_ATOMS, segment), jnp.bfloat16),
        ]
        + ([jax.ShapeDtypeStruct(dictionary.shape, jnp.float32)] if copies else []),
        scratch_shapes=[
            pltpu.VMEM((COARSE, ROWS, channels, K), jnp.bfloat16),
            pltpu.VMEM((z_rows, K), jnp.float32),
            pltpu.VMEM((z_rows, K), jnp.bfloat16),
            pltpu.VMEM((s_rows, channels), jnp.float32),
            pltpu.VMEM((s_rows, channels), jnp.bfloat16),
            pltpu.VMEM((longest, COARSE * K), jnp.bfloat16),
            pltpu.VMEM((scored, COARSE * channels), jnp.bfloat16),
            pltpu.VMEM((FINE, channels // LANES, longest, LANES), jnp.float32),
            pltpu.VMEM((channels // LANES, s_rows, LANES), jnp.float32),
            pltpu.VMEM((channels + ROWS, segment), jnp.float32),
            pltpu.SemaphoreType.DMA((ROWS // FINE,)),
        ]
        + ([pltpu.SemaphoreType.DMA((K // BLOCK_ATOMS,))] if copies else [])
        + (patching if atoms else []),
        compiler_params=pltpu.CompilerParams(vmem_limit_bytes=VMEM_BYTES),
        name="codes",
    )(
        place,
        limit,
        *codes.values(),
        *signals.values(),
        *atoms,
        taps.reshape(COARSE, ROWS, channels, K),
        *([dictionary] if copies else []),
    )


def gradient_kernel(share, source_ref, blocks_ref, out_ref, rf, zf, rr, zz):
    peers, rows, segment = blocks_ref.shape
    share_rows = rows - BLOCK_ATOMS
    span = peers * segment
    rf[:, span:] = jnp.zeros((share_rows, LANES), jnp.float32)
    zf[:, :LANES] = jnp.zeros((BLOCK_ATOMS, LANES), jnp.float32)
    for peer in range(peers):
        column = peer * segment
        rf[:, column : column + segment] = blocks_ref[peer, :share_rows, :].astype(jnp.float32)
        zf[:, LANES + column : LANES + column + segment] = blocks_ref[peer, share_rows:, :].astype(
            jnp.float32
        )
    for lag in range(ROWS):
        rr[lag * share_rows : (lag + 1) * share_rows, :] = rf[:, lag : lag + span].astype(jnp.bfloat16)
    for coarse in range(COARSE):
        begin = LANES - ROWS * coarse
        zz[coarse * BLOCK_ATOMS : (coarse + 1) * BLOCK_ATOMS, :] = zf[:, begin : begin + span].astype(
            jnp.bfloat16
        )
    lagged = lax.dot_general(zz[...], rr[...], NT, preferred_element_type=jnp.float32)
    lagged = lagged.astype(jnp.bfloat16)
    wide = ROWS * share_rows
    entries = share * L
    total = jnp.zeros((BLOCK_ATOMS, entries), jnp.float32)
    for coarse in range(COARSE):
        row = lax.broadcasted_iota(jnp.int32, (wide, entries), 0) + coarse * wide
        chosen = (row == source_ref[...]).astype(jnp.float32).astype(jnp.bfloat16)
        total += lax.dot_general(
            lagged[coarse * BLOCK_ATOMS : (coarse + 1) * BLOCK_ATOMS, :],
            chosen,
            NN,
            preferred_element_type=jnp.float32,
        )
    out_ref[...] = total.astype(jnp.bfloat16)


def share_gradient(blocks, share):
    peers, rows, segment = blocks.shape
    share_rows = rows - BLOCK_ATOMS
    span = peers * segment
    entry = jnp.arange(share * L, dtype=jnp.int32)
    channel, tap = entry // L, entry % L
    source = (tap // ROWS) * (ROWS * share_rows) + (tap % ROWS) * share_rows + channel
    return pl.pallas_call(
        functools.partial(gradient_kernel, share),
        out_shape=jax.ShapeDtypeStruct((BLOCK_ATOMS, share * L), jnp.bfloat16),
        scratch_shapes=[
            pltpu.VMEM((share_rows, span + LANES), jnp.float32),
            pltpu.VMEM((BLOCK_ATOMS, LANES + span), jnp.float32),
            pltpu.VMEM((ROWS * share_rows, span), jnp.bfloat16),
            pltpu.VMEM((COARSE * BLOCK_ATOMS, span), jnp.bfloat16),
        ],
        compiler_params=pltpu.CompilerParams(vmem_limit_bytes=VMEM_BYTES),
        name="gradient",
    )(source[None, :], blocks)


def gather_pieces(piece):
    peers = lax.axis_size("tm")
    held = piece[None]
    bit = peers // 2
    while bit > 1:
        came = lax.ppermute(held, "tm", [(i, i ^ bit) for i in range(peers)])
        held = jnp.concatenate([held, came], axis=0)
        bit //= 2
    return held, lax.ppermute(held, "tm", [(i, i ^ 1) for i in range(peers)])


def renew_kernel(place_ref, held_hbm, came_hbm, dict_hbm, out_hbm, atoms_ref, grad, old, across, sems):
    me = place_ref[0]
    first_row = pl.multiple_of(place_ref[1], BLOCK_ATOMS)
    peers, _, width = grad.shape
    half = peers // 2
    entries = C * L
    fetch = pltpu.make_async_copy(dict_hbm.at[pl.ds(first_row, BLOCK_ATOMS)], old, sems.at[peers])
    fetch.start()
    pieces = []
    for slot in range(half):
        flips = sum(((slot >> i) & 1) * (half >> i) for i in range(half.bit_length() - 1))
        for source, extra in ((held_hbm, 0), (came_hbm, 1)):
            owner = me ^ (flips + extra)
            pieces.append(
                pltpu.make_async_copy(source.at[slot], grad.at[owner], sems.at[2 * slot + extra])
            )
            pieces[-1].start()
    for piece in pieces:
        piece.wait()
    fetch.wait()

    def column(peer):
        return pl.ds(pl.multiple_of(peer * width, LANES), width)

    zeros = jnp.zeros((BLOCK_ATOMS, width), jnp.float32)

    def sums(peer, carry):
        square, dot = carry
        before = old[:, column(peer)]
        return square + before * before, dot + grad[peer].astype(jnp.float32) * before

    square, dot = lax.fori_loop(0, peers, sums, (zeros, zeros))
    mean_sq = jnp.sum(square, axis=1, keepdims=True) / entries + tiny_eps
    along = jnp.sum(dot, axis=1, keepdims=True) / entries / mean_sq

    def project(peer, square):
        value = grad[peer].astype(jnp.float32) - along * old[:, column(peer)]
        across[:, column(peer)] = value
        return square + value * value

    square = lax.fori_loop(0, peers, project, zeros)
    spread = jnp.sum(square, axis=1, keepdims=True) / entries + tiny_eps
    step = move_rate / jnp.sqrt(spread)
    norm = 1.0 / jnp.sqrt(mean_sq + 0.25)

    def renew(peer, carry):
        atoms_ref[:, column(peer)] = (old[:, column(peer)] + step * across[:, column(peer)]) * norm
        return carry

    lax.fori_loop(0, peers, renew, 0)
    store = pltpu.make_async_copy(atoms_ref, out_hbm.at[pl.ds(first_row, BLOCK_ATOMS)], sems.at[peers])
    store.start()
    store.wait()


def renew(place, held, came, dictionary):
    channels_taps = dictionary.shape[1]
    peers = 2 * held.shape[0]
    width = held.shape[2]
    remote = pl.BlockSpec(memory_space=pl.ANY)
    return pl.pallas_call(
        renew_kernel,
        in_specs=[pl.BlockSpec(memory_space=pltpu.SMEM), remote, remote, remote],
        out_specs=[remote, pl.BlockSpec(memory_space=pltpu.VMEM)],
        out_shape=[
            jax.ShapeDtypeStruct(dictionary.shape, jnp.float32),
            jax.ShapeDtypeStruct((BLOCK_ATOMS, channels_taps), jnp.float32),
        ],
        scratch_shapes=[
            pltpu.VMEM((peers, BLOCK_ATOMS, width), jnp.bfloat16),
            pltpu.VMEM((BLOCK_ATOMS, channels_taps), jnp.float32),
            pltpu.VMEM((BLOCK_ATOMS, channels_taps), jnp.float32),
            pltpu.SemaphoreType.DMA((peers + 1,)),
        ],
        input_output_aliases={3: 0},
        compiler_params=pltpu.CompilerParams(vmem_limit_bytes=VMEM_BYTES),
        name="renew",
    )(place, held, came, dictionary)


def whole_channels(signal, codes_init, dictionary_init, threshold, plan):
    channels, segment = signal.shape
    peers = lax.axis_size("tm")
    share = channels // peers
    limit = threshold[None, :]
    reach = extents()
    z_left, z_right = reach[0]
    s_left, s_right = z_left - L, z_right

    def hops(left, right):
        return [h for h in range(-hops_of(left, segment), hops_of(right, segment) + 1) if h]

    index = lax.axis_index("tm").astype(jnp.int32)
    code_hops, signal_hops = hops(z_left, z_right), hops(s_left, s_right)
    high = lax.reduce_precision(codes_init, exponent_bits=8, mantissa_bits=7)
    bundle = jnp.concatenate(
        [signal, high.astype(jnp.bfloat16), (codes_init - high).astype(jnp.bfloat16)], axis=0
    )
    bundles = {hop: shifted(bundle, "tm", -hop) for hop in signal_hops}
    signals = {0: signal, **bundles}
    code_state = codes_init
    dictionary = dictionary_init
    taps = layout(dictionary, channels)
    first_rows = [plan[step].astype(jnp.int32) * BLOCK_ATOMS for step in range(OUTER)]
    renewed = []
    for step in range(OUTER):
        packed = tuple(bundles) if step == 0 else ()
        codes = {0: code_state}
        for hop in code_hops:
            codes[hop] = bundles[hop] if hop in packed else shifted(code_state, "tm", -hop)
        place = jnp.stack([index * segment, first_rows[step], *first_rows[:step]])
        results = run_codes(
            place,
            limit,
            codes,
            signals,
            packed,
            renewed,
            taps,
            dictionary if step == 0 else None,
            segment,
            peers,
        )
        code_state, residual, payload = results[:3]
        if step == 0:
            dictionary = results[3]
        blocks = lax.all_to_all(payload, "tm", 0, 0, tiled=True)
        held, came = gather_pieces(share_gradient(blocks, share))
        dictionary, atoms = renew(jnp.stack([index, first_rows[step]]), held, came, dictionary)
        renewed = renewed + [atoms]
    return code_state, dictionary, residual


def renew_atoms(old_atoms, across, mean_sq, spread):
    return (old_atoms + move_rate * across / jnp.sqrt(spread)[:, None]) / jnp.sqrt(mean_sq + 0.25)[
        :, None
    ]


def split_channels(signal, codes_init, dictionary_init, threshold, plan):
    segment = signal.shape[1]
    local_chan = signal.shape[0]
    unit_scale = (C * L) ** (-0.5)
    entries = C * L
    limit = threshold[:, None]

    def convolve(atom_cube, code_low):
        code_edge = shifted(code_low[:, segment - (L - 1) :], "tm", 1)
        extended = jnp.concatenate([code_edge, code_low], axis=1)
        lagged = jnp.stack(
            [extended[:, L - 1 - offset : L - 1 - offset + segment] for offset in range(L)], axis=1
        )
        return unit_scale * jnp.einsum(
            "kcl,klt->ct", atom_cube, lagged, preferred_element_type=jnp.float32
        )

    def resid_columns(resid_low):
        resid_edge = shifted(resid_low[:, : L - 1], "tm", -1)
        extended = jnp.concatenate([resid_low, resid_edge], axis=1)
        lagged = jnp.stack([extended[:, offset : offset + segment] for offset in range(L)], axis=1)
        return lagged.reshape(local_chan * L, segment)

    code_state = codes_init
    dictionary = dictionary_init
    residual = signal.astype(jnp.float32)
    for outer_step in range(OUTER):
        dict_low = dictionary.astype(jnp.bfloat16)
        atom_cube = dict_low.reshape(K, local_chan, L)
        for inner_step in range(INNER):
            code_low = code_state.astype(jnp.bfloat16)
            residual = signal.astype(jnp.float32) - convolve(atom_cube, code_low)
            lagged = resid_columns(residual.astype(jnp.bfloat16))
            partial_value = unit_scale * jnp.dot(
                dict_low, lagged, preferred_element_type=jnp.float32
            )
            scores = lax.psum(partial_value.astype(jnp.bfloat16), "chan").astype(jnp.float32)
            stepped = code_state + code_rate * scores
            code_state = stepped - jnp.clip(stepped, -limit, limit)
        code_low = code_state.astype(jnp.bfloat16)
        residual = signal.astype(jnp.float32) - convolve(atom_cube, code_low)
        lagged = resid_columns(residual.astype(jnp.bfloat16))
        first_row = plan[outer_step] * BLOCK_ATOMS
        code_block = lax.dynamic_slice_in_dim(code_low, first_row, BLOCK_ATOMS, 0)
        local_grad = lax.dot_general(
            code_block, lagged, (((1,), (1,)), ((), ())), preferred_element_type=jnp.float32
        )
        old_atoms = lax.dynamic_slice_in_dim(dictionary, first_row, BLOCK_ATOMS, 0)
        gradient = lax.psum(local_grad, "tm")
        dot_sum, square_sum = lax.psum(
            (jnp.sum(gradient * old_atoms, axis=1), jnp.sum(old_atoms * old_atoms, axis=1)), "chan"
        )
        mean_sq = square_sum / entries + tiny_eps
        along_coef = dot_sum / entries / mean_sq
        across = gradient - along_coef[:, None] * old_atoms
        spread = lax.psum(jnp.sum(across * across, axis=1), "chan") / entries + tiny_eps
        renewed = renew_atoms(old_atoms, across, mean_sq, spread)
        dictionary = lax.dynamic_update_slice_in_dim(dictionary, renewed, first_row, 0)
    return (code_state, dictionary, residual)


def shards(signal, codes_init, dictionary_init, threshold, plan):
    channels, segment = signal.shape
    peers = lax.axis_size("tm")
    fits = (
        lax.axis_size("chan") == 1
        and segment % LANES == 0
        and channels % LANES == 0
        and channels % peers == 0
        and (channels // peers * L) % LANES == 0
        and peers > 1
        and peers & (peers - 1) == 0
    )
    body = whole_channels if fits else split_channels
    return body(signal, codes_init, dictionary_init, threshold, plan)


def solution(mesh):
    placed = (P("chan", "tm"), P(None, "tm"), P(None, "chan"), P(), P())
    return jax.shard_map(
        shards,
        mesh=mesh,
        in_specs=placed,
        out_specs=(P(None, "tm"), P(None, "chan"), P("chan", "tm")),
        check_vma=False,
    )
```

```python
import functools

import jax
import jax.numpy as jnp
from jax import lax
from jax.experimental import pallas as pl
from jax.experimental.pallas import tpu as pltpu
from jax.sharding import PartitionSpec as P

C = 384
K = 128
L = 96
BLOCK_ATOMS = 16
INNER = 2
OUTER = 2

code_rate = 0.3
move_rate = 0.5
tiny_eps = 1e-06

ROWS = 16
COARSE = L // ROWS
STRIDE = L + 1
FINE = 4
LANES = 128
VMEM_BYTES = 56 * 1024 * 1024

NN = (((1,), (0,)), ((), ()))
NT = (((1,), (1,)), ((), ()))


def shifted(shard, axis, by):
    peers = lax.axis_size(axis)
    pairs = [(i, i + by) for i in range(peers) if 0 <= i + by < peers]
    return lax.ppermute(shard, axis, pairs)


def turn(columns_ref, start, turned_ref):
    for quad in range(ROWS // 4):
        part = pl.ds(start + quad * 4 * L, 4 * L)
        turned = columns_ref[:, part].T
        for q in range(4):
            row = (quad * 4 + q) * STRIDE
            turned_ref[row : row + L, :] = turned[q * L : (q + 1) * L]


def layout_kernel(dict_ref, taps_ref, copy_hbm, even, odd, sem):
    width = dict_ref.shape[1]
    column = pl.multiple_of(pl.program_id(0) * width, LANES)
    copy = pltpu.make_async_copy(dict_ref, copy_hbm.at[:, pl.ds(column, width)], sem)
    copy.start()
    groups = width // (ROWS * L)
    turn(dict_ref, 0, even)
    for group in range(groups):
        now, later = (even, odd) if group % 2 == 0 else (odd, even)
        if group + 1 < groups:
            turn(dict_ref, (group + 1) * ROWS * L, later)
        for tap in range(L):
            taps_ref[tap, group * ROWS : (group + 1) * ROWS, :] = now[
                pl.ds(tap, ROWS, stride=STRIDE), :
            ].astype(jnp.bfloat16)
    copy.wait()


def layout(dictionary, channels):
    block = 4 * ROWS
    return pl.pallas_call(
        layout_kernel,
        grid=(channels // block,),
        in_specs=[pl.BlockSpec((K, block * L), lambda i: (0, i))],
        out_specs=[
            pl.BlockSpec((L, block, K), lambda i: (0, i, 0)),
            pl.BlockSpec(memory_space=pl.ANY),
        ],
        out_shape=[
            jax.ShapeDtypeStruct((L, channels, K), jnp.bfloat16),
            jax.ShapeDtypeStruct(dictionary.shape, jnp.float32),
        ],
        scratch_shapes=[
            pltpu.VMEM((ROWS * STRIDE, K), jnp.float32),
            pltpu.VMEM((ROWS * STRIDE, K), jnp.float32),
            pltpu.SemaphoreType.DMA,
        ],
        compiler_params=pltpu.CompilerParams(vmem_limit_bytes=VMEM_BYTES),
        name="layout",
    )(dictionary)


def fetch_taps(taps_hbm, taps, sems):
    copies = [
        pltpu.make_async_copy(
            taps_hbm.at[:, pl.ds(lag, FINE)], taps.at[:, pl.ds(lag, FINE)], sems.at[lag // FINE]
        )
        for lag in range(0, ROWS, FINE)
    ]
    for copy in copies:
        copy.start()
    return [copy.wait for copy in copies]


def convolve(zb, begin, count, taps, zz, fine, acc, waits):
    channels = taps.shape[2]
    tiles = channels // LANES
    rows = count + ROWS
    for coarse in range(COARSE):
        first = begin - ROWS - ROWS * coarse
        zz[:rows, coarse * K : (coarse + 1) * K] = zb[first : first + rows, :]
    for lag in range(0, ROWS, FINE):
        if waits:
            waits[lag // FINE]()
        slot = lag // FINE % 2 * FINE
        for pair in range(0, FINE, 2):
            weights = jnp.concatenate(
                [
                    jnp.concatenate([taps[m, lag + pair + j] for m in range(COARSE)], axis=1)
                    for j in range(2)
                ],
                axis=0,
            )
            product = lax.dot_general(zz[:rows, :], weights, NT, preferred_element_type=jnp.float32)
            for j in range(2):
                for tile in range(tiles):
                    column = j * channels + tile * LANES
                    fine[slot + pair + j, tile, :rows, :] = product[:, column : column + LANES]
        for tile in range(tiles):
            total = None if lag == 0 else acc[tile, :count, :]
            for j in range(FINE):
                first = ROWS - lag - j
                part = fine[slot + j, tile, first : first + count, :]
                total = part if total is None else total + part
            acc[tile, :count, :] = total


def correlate(rb, count, taps, rr, fine, acc):
    channels = taps.shape[2]
    rows = count + ROWS
    for coarse in range(COARSE):
        first = ROWS * coarse
        rr[:rows, coarse * channels : (coarse + 1) * channels] = rb[first : first + rows, :]
    for lag in range(0, ROWS, FINE):
        slot = lag // FINE % 2 * FINE
        for pair in range(0, FINE, 2):
            weights = jnp.concatenate(
                [
                    jnp.concatenate([taps[m, lag + pair + j] for m in range(COARSE)], axis=0)
                    for j in range(2)
                ],
                axis=1,
            )
            product = lax.dot_general(rr[:rows, :], weights, NN, preferred_element_type=jnp.float32)
            for j in range(2):
                fine[slot + pair + j, 0, :rows, :] = product[:, j * K : (j + 1) * K]
        total = None if lag == 0 else acc[0, :count, :]
        for j in range(FINE):
            part = fine[slot + j, 0, lag + j : lag + j + count, :]
            total = part if total is None else total + part
        acc[0, :count, :] = total


def patch_taps(row, atoms_ref, taps, columns, even, odd):
    channels = taps.shape[2]
    lane = lax.broadcasted_iota(jnp.int32, (ROWS, K), 1)
    renewed = (lane >= row) & (lane < row + BLOCK_ATOMS)
    columns[...] = jnp.zeros_like(columns)

    def patch(step, carry):
        width = 2 * ROWS * L
        part = pl.ds(pl.multiple_of(step * width, LANES), width)
        columns[pl.ds(row, BLOCK_ATOMS), :] = atoms_ref[:, part]
        turn(columns, 0, even)
        turn(columns, ROWS * L, odd)
        for half, turned in ((0, even), (1, odd)):
            own = pl.ds(pl.multiple_of((2 * step + half) * ROWS, ROWS), ROWS)
            for tap in range(L):
                fresh = turned[pl.ds(tap, ROWS, stride=STRIDE), :]
                kept = taps[tap // ROWS, tap % ROWS, own, :].astype(jnp.float32)
                taps[tap // ROWS, tap % ROWS, own, :] = jnp.where(renewed, fresh, kept).astype(
                    jnp.bfloat16
                )
        return carry

    lax.fori_loop(0, channels // (2 * ROWS), patch, 0)


def put_codes(zb, own, left, right):
    segment = own.shape[1]
    zb[:L, :] = left[...].astype(jnp.float32).T[segment - L :].astype(jnp.bfloat16)
    zb[L : L + segment, :] = own[...].T.astype(jnp.bfloat16)
    if right is not None:
        zb[L + segment :, :] = right[:K, :].astype(jnp.float32).T[:L].astype(jnp.bfloat16)


def iterate_kernel(total_time, patching, place_ref, limit_ref, *refs):
    code_ref, left_ref, right_ref, signal_ref, next_ref = refs[:5]
    refs = refs[5:]
    if patching:
        atoms_ref, refs = refs[0], refs[1:]
    taps_hbm, state_out, low_out = refs[:3]
    refs = refs[3:]
    if patching:
        taps_out, refs = refs[0], refs[1:]
    taps, zb, rb, zz, rr, fine, acc, sems = refs[:8]
    channels, segment = signal_ref.shape
    tiles = channels // LANES
    scale = (C * L) ** (-0.5)
    waits = fetch_taps(taps_hbm, taps, sems)
    put_codes(zb, code_ref, left_ref, right_ref)
    if patching:
        columns, even, odd, out_sem = refs[8:]
        for wait in waits:
            wait()
        waits = None
        patch_taps(pl.multiple_of(place_ref[1], BLOCK_ATOMS), atoms_ref, taps, columns, even, odd)
        store = pltpu.make_async_copy(taps, taps_out, out_sem)
        store.start()
    reach = segment + L
    convolve(zb, L, reach, taps, zz, fine, acc, waits)
    moment = place_ref[0] + lax.broadcasted_iota(jnp.int32, (reach, LANES), 0)
    inside = moment < total_time
    for tile in range(tiles):
        column = slice(tile * LANES, (tile + 1) * LANES)
        first = signal_ref[column, :].astype(jnp.float32).T
        second = next_ref[K + tile * LANES : K + (tile + 1) * LANES, :].astype(jnp.float32).T[:L]
        value = jnp.concatenate([first, second], axis=0) - scale * acc[tile, :reach, :]
        rb[:, column] = jnp.where(inside, value, 0.0).astype(jnp.bfloat16)
    correlate(rb, segment, taps, rr, fine, acc)
    limit = limit_ref[...]
    stepped = code_ref[...].T + code_rate * (scale * acc[0, :segment, :])
    state = (stepped - jnp.clip(stepped, -limit, limit)).T
    state_out[...] = state
    low_out[...] = state.astype(jnp.bfloat16)
    if patching:
        store.wait()


def iterate(place, limit, code, left, right, signal, following, taps, atoms, peers):
    channels, segment = signal.shape
    patching = atoms is not None
    reach = segment + L
    whole = pl.BlockSpec(memory_space=pltpu.VMEM)
    remote = pl.BlockSpec(memory_space=pl.ANY)
    cube = (COARSE, ROWS, channels, K)
    return pl.pallas_call(
        functools.partial(iterate_kernel, peers * segment, patching),
        in_specs=[pl.BlockSpec(memory_space=pltpu.SMEM)] + [whole] * (6 + patching) + [remote],
        out_specs=[whole, whole] + [remote] * patching,
        out_shape=[
            jax.ShapeDtypeStruct((K, segment), jnp.float32),
            jax.ShapeDtypeStruct((K, segment), jnp.bfloat16),
        ]
        + [jax.ShapeDtypeStruct(cube, jnp.bfloat16)] * patching,
        scratch_shapes=[
            pltpu.VMEM(cube, jnp.bfloat16),
            pltpu.VMEM((L + reach, K), jnp.bfloat16),
            pltpu.VMEM((reach, channels), jnp.bfloat16),
            pltpu.VMEM((reach + ROWS, COARSE * K), jnp.bfloat16),
            pltpu.VMEM((segment + ROWS, COARSE * channels), jnp.bfloat16),
            pltpu.VMEM((2 * FINE, channels // LANES, reach + ROWS, LANES), jnp.float32),
            pltpu.VMEM((channels // LANES, reach, LANES), jnp.float32),
            pltpu.SemaphoreType.DMA((ROWS // FINE,)),
        ]
        + [
            pltpu.VMEM((K, 2 * ROWS * L), jnp.float32),
            pltpu.VMEM((ROWS * STRIDE, K), jnp.float32),
            pltpu.VMEM((ROWS * STRIDE, K), jnp.float32),
            pltpu.SemaphoreType.DMA,
        ]
        * patching,
        compiler_params=pltpu.CompilerParams(vmem_limit_bytes=VMEM_BYTES),
        name="iterate",
    )(place, limit, code, left, right, signal, following, *([atoms] * patching), taps)


def finish_kernel(
    peers, place_ref, code_ref, left_ref, signal_ref, taps_hbm, resid_out, payload_out, taps, zb, zz, fine, acc, tall, sems
):
    channels, segment = signal_ref.shape
    scale = (C * L) ** (-0.5)
    waits = fetch_taps(taps_hbm, taps, sems)
    put_codes(zb, code_ref, left_ref, None)
    convolve(zb, L, segment, taps, zz, fine, acc, waits)
    for tile in range(channels // LANES):
        column = slice(tile * LANES, (tile + 1) * LANES)
        value = signal_ref[column, :].astype(jnp.float32) - scale * acc[tile, :segment, :].T
        resid_out[column, :] = value
        tall[column, :] = value
    row = pl.multiple_of(place_ref[0], BLOCK_ATOMS)
    block = code_ref[pl.ds(row, BLOCK_ATOMS), :].astype(jnp.bfloat16)
    share = channels // peers
    share_rows = payload_out.shape[1] - BLOCK_ATOMS
    tall[channels:, :] = jnp.zeros((tall.shape[0] - channels, segment), jnp.float32)
    for peer in range(peers):
        part = tall[peer * share : peer * share + share_rows, :]
        payload_out[peer, :share_rows, :] = part.astype(jnp.bfloat16)
        payload_out[peer, share_rows:, :] = block


def finish(place, code, left, signal, taps, peers):
    channels, segment = signal.shape
    share = channels // peers
    share_rows = -(-share // ROWS) * ROWS
    whole = pl.BlockSpec(memory_space=pltpu.VMEM)
    return pl.pallas_call(
        functools.partial(finish_kernel, peers),
        in_specs=[pl.BlockSpec(memory_space=pltpu.SMEM), whole, whole, whole]
        + [pl.BlockSpec(memory_space=pl.ANY)],
        out_specs=[whole, whole],
        out_shape=[
            jax.ShapeDtypeStruct((channels, segment), jnp.float32),
            jax.ShapeDtypeStruct((peers, share_rows + BLOCK_ATOMS, segment), jnp.bfloat16),
        ],
        scratch_shapes=[
            pltpu.VMEM((COARSE, ROWS, channels, K), jnp.bfloat16),
            pltpu.VMEM((L + segment, K), jnp.bfloat16),
            pltpu.VMEM((segment + ROWS, COARSE * K), jnp.bfloat16),
            pltpu.VMEM((2 * FINE, channels // LANES, segment + ROWS, LANES), jnp.float32),
            pltpu.VMEM((channels // LANES, segment, LANES), jnp.float32),
            pltpu.VMEM((channels + ROWS, segment), jnp.float32),
            pltpu.SemaphoreType.DMA((ROWS // FINE,)),
        ],
        compiler_params=pltpu.CompilerParams(vmem_limit_bytes=VMEM_BYTES),
        name="finish",
    )(place, code, left, signal, taps)


def gradient_kernel(share, source_ref, blocks_ref, out_ref, rf, zf, rr, zz):
    peers, rows, segment = blocks_ref.shape
    share_rows = rows - BLOCK_ATOMS
    span = peers * segment
    rf[:, span:] = jnp.zeros((share_rows, LANES), jnp.float32)
    zf[:, :LANES] = jnp.zeros((BLOCK_ATOMS, LANES), jnp.float32)
    for peer in range(peers):
        column = peer * segment
        rf[:, column : column + segment] = blocks_ref[peer, :share_rows, :].astype(jnp.float32)
        zf[:, LANES + column : LANES + column + segment] = blocks_ref[peer, share_rows:, :].astype(
            jnp.float32
        )
    for lag in range(ROWS):
        rr[lag * share_rows : (lag + 1) * share_rows, :] = rf[:, lag : lag + span].astype(jnp.bfloat16)
    for coarse in range(COARSE):
        begin = LANES - ROWS * coarse
        zz[coarse * BLOCK_ATOMS : (coarse + 1) * BLOCK_ATOMS, :] = zf[:, begin : begin + span].astype(
            jnp.bfloat16
        )
    lagged = lax.dot_general(zz[...], rr[...], NT, preferred_element_type=jnp.float32)
    lagged = lagged.astype(jnp.bfloat16)
    wide = ROWS * share_rows
    entries = share * L
    total = jnp.zeros((BLOCK_ATOMS, entries), jnp.float32)
    for coarse in range(COARSE):
        row = lax.broadcasted_iota(jnp.int32, (wide, entries), 0) + coarse * wide
        chosen = (row == source_ref[...]).astype(jnp.float32).astype(jnp.bfloat16)
        total += lax.dot_general(
            lagged[coarse * BLOCK_ATOMS : (coarse + 1) * BLOCK_ATOMS, :],
            chosen,
            NN,
            preferred_element_type=jnp.float32,
        )
    out_ref[...] = total.astype(jnp.bfloat16)


def share_gradient(blocks, share):
    peers, rows, segment = blocks.shape
    share_rows = rows - BLOCK_ATOMS
    span = peers * segment
    entry = jnp.arange(share * L, dtype=jnp.int32)
    channel, tap = entry // L, entry % L
    source = (tap // ROWS) * (ROWS * share_rows) + (tap % ROWS) * share_rows + channel
    return pl.pallas_call(
        functools.partial(gradient_kernel, share),
        out_shape=jax.ShapeDtypeStruct((BLOCK_ATOMS, share * L), jnp.bfloat16),
        scratch_shapes=[
            pltpu.VMEM((share_rows, span + LANES), jnp.float32),
            pltpu.VMEM((BLOCK_ATOMS, LANES + span), jnp.float32),
            pltpu.VMEM((ROWS * share_rows, span), jnp.bfloat16),
            pltpu.VMEM((COARSE * BLOCK_ATOMS, span), jnp.bfloat16),
        ],
        compiler_params=pltpu.CompilerParams(vmem_limit_bytes=VMEM_BYTES),
        name="gradient",
    )(source[None, :], blocks)


def gather_steps(peers):
    bits = [1 << i for i in range(peers.bit_length() - 2, 0, -1)]
    steps = []
    for first in range(0, len(bits), 2):
        pair = bits[first : first + 2]
        steps.append(pair + [sum(pair)] if len(pair) == 2 else pair)
    return steps


def gather_slots(peers):
    flips = [0]
    for masks in gather_steps(peers):
        flips = [f ^ m for m in [0] + masks for f in flips]
    return flips


def gather_pieces(piece):
    peers = lax.axis_size("tm")

    def exchanged(shard, mask):
        return lax.ppermute(shard, "tm", [(i, i ^ mask) for i in range(peers)])

    held = piece[None]
    for masks in gather_steps(peers):
        held = jnp.concatenate([held] + [exchanged(held, mask) for mask in masks], axis=0)
    return held, exchanged(held, 1)


def renew_kernel(place_ref, held_hbm, came_hbm, dict_hbm, out_hbm, atoms_ref, grad, old, across, sems):
    me = place_ref[0]
    first_row = pl.multiple_of(place_ref[1], BLOCK_ATOMS)
    peers, _, width = grad.shape
    entries = C * L
    fetch = pltpu.make_async_copy(dict_hbm.at[pl.ds(first_row, BLOCK_ATOMS)], old, sems.at[peers])
    fetch.start()
    pieces = []
    for slot, flips in enumerate(gather_slots(peers)):
        for source, extra in ((held_hbm, 0), (came_hbm, 1)):
            owner = me ^ (flips + extra)
            pieces.append(
                pltpu.make_async_copy(source.at[slot], grad.at[owner], sems.at[2 * slot + extra])
            )
            pieces[-1].start()
    for piece in pieces:
        piece.wait()
    fetch.wait()

    def column(peer):
        return pl.ds(pl.multiple_of(peer * width, LANES), width)

    zeros = jnp.zeros((BLOCK_ATOMS, width), jnp.float32)

    def sums(peer, carry):
        square, dot = carry
        before = old[:, column(peer)]
        return square + before * before, dot + grad[peer].astype(jnp.float32) * before

    square, dot = lax.fori_loop(0, peers, sums, (zeros, zeros))
    mean_sq = jnp.sum(square, axis=1, keepdims=True) / entries + tiny_eps
    along = jnp.sum(dot, axis=1, keepdims=True) / entries / mean_sq

    def project(peer, square):
        value = grad[peer].astype(jnp.float32) - along * old[:, column(peer)]
        across[:, column(peer)] = value
        return square + value * value

    square = lax.fori_loop(0, peers, project, zeros)
    spread = jnp.sum(square, axis=1, keepdims=True) / entries + tiny_eps
    step = move_rate / jnp.sqrt(spread)
    norm = 1.0 / jnp.sqrt(mean_sq + 0.25)

    def renew(peer, carry):
        atoms_ref[:, column(peer)] = (old[:, column(peer)] + step * across[:, column(peer)]) * norm
        return carry

    lax.fori_loop(0, peers, renew, 0)
    store = pltpu.make_async_copy(atoms_ref, out_hbm.at[pl.ds(first_row, BLOCK_ATOMS)], sems.at[peers])
    store.start()
    store.wait()


def renew(place, held, came, dictionary):
    channels_taps = dictionary.shape[1]
    peers = 2 * held.shape[0]
    width = held.shape[2]
    remote = pl.BlockSpec(memory_space=pl.ANY)
    return pl.pallas_call(
        renew_kernel,
        in_specs=[pl.BlockSpec(memory_space=pltpu.SMEM), remote, remote, remote],
        out_specs=[remote, pl.BlockSpec(memory_space=pltpu.VMEM)],
        out_shape=[
            jax.ShapeDtypeStruct(dictionary.shape, jnp.float32),
            jax.ShapeDtypeStruct((BLOCK_ATOMS, channels_taps), jnp.float32),
        ],
        scratch_shapes=[
            pltpu.VMEM((peers, BLOCK_ATOMS, width), jnp.bfloat16),
            pltpu.VMEM((BLOCK_ATOMS, channels_taps), jnp.float32),
            pltpu.VMEM((BLOCK_ATOMS, channels_taps), jnp.float32),
            pltpu.SemaphoreType.DMA((peers + 1,)),
        ],
        input_output_aliases={3: 0},
        compiler_params=pltpu.CompilerParams(vmem_limit_bytes=VMEM_BYTES),
        name="renew",
    )(place, held, came, dictionary)


def whole_channels(signal, codes_init, dictionary_init, threshold, plan):
    channels, segment = signal.shape
    peers = lax.axis_size("tm")
    limit = threshold[None, :]
    index = lax.axis_index("tm").astype(jnp.int32)
    first_rows = [plan[step].astype(jnp.int32) * BLOCK_ATOMS for step in range(OUTER)]
    low = codes_init.astype(jnp.bfloat16)
    following = shifted(jnp.concatenate([low, signal], axis=0), "tm", -1)
    left, right = shifted(low, "tm", 1), following
    taps, dictionary = layout(dictionary_init, channels)
    taps = taps.reshape(COARSE, ROWS, channels, K)
    code_state, atoms = codes_init, None
    for step in range(OUTER):
        place = jnp.stack([index * segment, first_rows[step - 1] if step else first_rows[0]])
        for inner in range(INNER):
            fresh = atoms if inner == 0 else None
            results = iterate(
                place, limit, code_state, left, right, signal, following, taps, fresh, peers
            )
            code_state, low = results[:2]
            if fresh is not None:
                taps = results[2]
            left = shifted(low, "tm", 1)
            if step + 1 < OUTER or inner + 1 < INNER:
                right = shifted(low, "tm", -1)
        residual, payload = finish(first_rows[step][None], code_state, left, signal, taps, peers)
        blocks = lax.all_to_all(payload, "tm", 0, 0, tiled=True)
        held, came = gather_pieces(share_gradient(blocks, channels // peers))
        dictionary, atoms = renew(jnp.stack([index, first_rows[step]]), held, came, dictionary)
    return code_state, dictionary, residual


def renew_atoms(old_atoms, across, mean_sq, spread):
    return (old_atoms + move_rate * across / jnp.sqrt(spread)[:, None]) / jnp.sqrt(mean_sq + 0.25)[
        :, None
    ]


def split_channels(signal, codes_init, dictionary_init, threshold, plan):
    segment = signal.shape[1]
    local_chan = signal.shape[0]
    unit_scale = (C * L) ** (-0.5)
    entries = C * L
    limit = threshold[:, None]

    def convolve(atom_cube, code_low):
        code_edge = shifted(code_low[:, segment - (L - 1) :], "tm", 1)
        extended = jnp.concatenate([code_edge, code_low], axis=1)
        lagged = jnp.stack(
            [extended[:, L - 1 - offset : L - 1 - offset + segment] for offset in range(L)], axis=1
        )
        return unit_scale * jnp.einsum(
            "kcl,klt->ct", atom_cube, lagged, preferred_element_type=jnp.float32
        )

    def resid_columns(resid_low):
        resid_edge = shifted(resid_low[:, : L - 1], "tm", -1)
        extended = jnp.concatenate([resid_low, resid_edge], axis=1)
        lagged = jnp.stack([extended[:, offset : offset + segment] for offset in range(L)], axis=1)
        return lagged.reshape(local_chan * L, segment)

    code_state = codes_init
    dictionary = dictionary_init
    residual = signal.astype(jnp.float32)
    for outer_step in range(OUTER):
        dict_low = dictionary.astype(jnp.bfloat16)
        atom_cube = dict_low.reshape(K, local_chan, L)
        for inner_step in range(INNER):
            code_low = code_state.astype(jnp.bfloat16)
            residual = signal.astype(jnp.float32) - convolve(atom_cube, code_low)
            lagged = resid_columns(residual.astype(jnp.bfloat16))
            partial_value = unit_scale * jnp.dot(
                dict_low, lagged, preferred_element_type=jnp.float32
            )
            scores = lax.psum(partial_value.astype(jnp.bfloat16), "chan").astype(jnp.float32)
            stepped = code_state + code_rate * scores
            code_state = stepped - jnp.clip(stepped, -limit, limit)
        code_low = code_state.astype(jnp.bfloat16)
        residual = signal.astype(jnp.float32) - convolve(atom_cube, code_low)
        lagged = resid_columns(residual.astype(jnp.bfloat16))
        first_row = plan[outer_step] * BLOCK_ATOMS
        code_block = lax.dynamic_slice_in_dim(code_low, first_row, BLOCK_ATOMS, 0)
        local_grad = lax.dot_general(
            code_block, lagged, (((1,), (1,)), ((), ())), preferred_element_type=jnp.float32
        )
        old_atoms = lax.dynamic_slice_in_dim(dictionary, first_row, BLOCK_ATOMS, 0)
        gradient = lax.psum(local_grad, "tm")
        dot_sum, square_sum = lax.psum(
            (jnp.sum(gradient * old_atoms, axis=1), jnp.sum(old_atoms * old_atoms, axis=1)), "chan"
        )
        mean_sq = square_sum / entries + tiny_eps
        along_coef = dot_sum / entries / mean_sq
        across = gradient - along_coef[:, None] * old_atoms
        spread = lax.psum(jnp.sum(across * across, axis=1), "chan") / entries + tiny_eps
        renewed = renew_atoms(old_atoms, across, mean_sq, spread)
        dictionary = lax.dynamic_update_slice_in_dim(dictionary, renewed, first_row, 0)
    return (code_state, dictionary, residual)


def shards(signal, codes_init, dictionary_init, threshold, plan):
    channels, segment = signal.shape
    peers = lax.axis_size("tm")
    fits = (
        lax.axis_size("chan") == 1
        and segment % LANES == 0
        and channels % (4 * ROWS) == 0
        and channels % LANES == 0
        and channels % peers == 0
        and (channels // peers * L) % LANES == 0
        and peers > 1
        and peers & (peers - 1) == 0
    )
    body = whole_channels if fits else split_channels
    return body(signal, codes_init, dictionary_init, threshold, plan)


def solution(mesh):
    placed = (P("chan", "tm"), P(None, "tm"), P(None, "chan"), P(), P())
    return jax.shard_map(
        shards,
        mesh=mesh,
        in_specs=placed,
        out_specs=(P(None, "tm"), P(None, "chan"), P("chan", "tm")),
        check_vma=False,
    )
```

```python
import functools

import jax
import jax.numpy as jnp
from jax import lax
from jax.experimental import pallas as pl
from jax.experimental.pallas import tpu as pltpu
from jax.sharding import PartitionSpec as P

C = 384
K = 128
L = 96
BLOCK_ATOMS = 16
INNER = 2
OUTER = 2

code_rate = 0.3
move_rate = 0.5
tiny_eps = 1e-06

ROWS = 16
COARSE = L // ROWS
STRIDE = L + 1
FINE = 4
LANES = 128
VMEM_BYTES = 24 * 1024 * 1024

NN = (((1,), (0,)), ((), ()))
NT = (((1,), (1,)), ((), ()))


def shifted(shard, axis, by):
    peers = lax.axis_size(axis)
    pairs = [(i, i + by) for i in range(peers) if 0 <= i + by < peers]
    return lax.ppermute(shard, axis, pairs)


def resident(value):
    return pltpu.with_memory_space_constraint(value, pltpu.VMEM)


def vmem():
    return pl.BlockSpec(memory_space=pltpu.VMEM)


def turn(columns_ref, start, turned_ref):
    side = 2 * LANES
    row = lax.broadcasted_iota(jnp.int32, (side, side), 0)
    column = lax.broadcasted_iota(jnp.int32, (side, side), 1)
    identity = (row == column).astype(jnp.float32).astype(jnp.bfloat16)
    for first in range(0, ROWS * L, 2 * side):
        pair = jnp.concatenate(
            [columns_ref[:, pl.ds(start + first + half * side, side)] for half in range(2)], axis=0
        ).astype(jnp.bfloat16)
        turned = lax.dot_general(identity, pair, NT, preferred_element_type=jnp.float32)
        for half in range(2):
            entry = first + half * side
            end = entry + side
            begin = entry
            while begin < end:
                channel, tap = begin // L, begin % L
                count = min(end - begin, L - tap)
                target = channel * STRIDE + tap
                turned_ref[target : target + count, :] = turned[
                    begin - entry : begin - entry + count, half * K : (half + 1) * K
                ]
                begin += count


def layout_kernel(dict_ref, taps_ref, copy_hbm, even, odd, sem):
    width = dict_ref.shape[1]
    column = pl.multiple_of(pl.program_id(0) * width, LANES)
    copy = pltpu.make_async_copy(dict_ref, copy_hbm.at[:, pl.ds(column, width)], sem)
    copy.start()
    groups = width // (ROWS * L)
    turn(dict_ref, 0, even)
    for group in range(groups):
        now, later = (even, odd) if group % 2 == 0 else (odd, even)
        if group + 1 < groups:
            turn(dict_ref, (group + 1) * ROWS * L, later)
        own = pl.ds(pl.multiple_of((pl.program_id(0) * groups + group) * ROWS, ROWS), ROWS)
        for tap in range(L):
            taps_ref[tap // ROWS, tap % ROWS, own, :] = now[
                pl.ds(tap, ROWS, stride=STRIDE), :
            ].astype(jnp.bfloat16)
    copy.wait()


def layout(dictionary, channels):
    block = 4 * ROWS
    return pl.pallas_call(
        layout_kernel,
        grid=(channels // block,),
        in_specs=[pl.BlockSpec((K, block * L), lambda i: (0, i))],
        out_specs=[vmem(), pl.BlockSpec(memory_space=pl.ANY)],
        out_shape=[
            pltpu.VMEM((COARSE, ROWS, channels, K), jnp.bfloat16),
            jax.ShapeDtypeStruct(dictionary.shape, jnp.float32),
        ],
        scratch_shapes=[
            pltpu.VMEM((ROWS * STRIDE, K), jnp.float32),
            pltpu.VMEM((ROWS * STRIDE, K), jnp.float32),
            pltpu.SemaphoreType.DMA,
        ],
        compiler_params=pltpu.CompilerParams(vmem_limit_bytes=VMEM_BYTES),
        name="layout",
    )(dictionary)


def convolve(zb, begin, count, taps, zz, fine, acc):
    channels = taps.shape[2]
    tiles = channels // LANES
    rows = count + ROWS
    for coarse in range(COARSE):
        first = begin - ROWS - ROWS * coarse
        zz[:rows, coarse * K : (coarse + 1) * K] = zb[first : first + rows, :]
    for lag in range(0, ROWS, FINE):
        slot = lag // FINE % 2 * FINE
        for pair in range(0, FINE, 2):
            weights = jnp.concatenate(
                [
                    jnp.concatenate([taps[m, lag + pair + j] for m in range(COARSE)], axis=1)
                    for j in range(2)
                ],
                axis=0,
            )
            product = lax.dot_general(zz[:rows, :], weights, NT, preferred_element_type=jnp.float32)
            for j in range(2):
                for tile in range(tiles):
                    column = j * channels + tile * LANES
                    fine[slot + pair + j, tile, :rows, :] = product[:, column : column + LANES]
        for tile in range(tiles):
            total = None if lag == 0 else acc[tile, :count, :]
            for j in range(FINE):
                first = ROWS - lag - j
                part = fine[slot + j, tile, first : first + count, :]
                total = part if total is None else total + part
            acc[tile, :count, :] = total


def correlate(rb, count, taps, rr, fine, acc):
    channels = taps.shape[2]
    rows = count + ROWS
    for coarse in range(COARSE):
        first = ROWS * coarse
        rr[:rows, coarse * channels : (coarse + 1) * channels] = rb[first : first + rows, :]
    for lag in range(0, ROWS, FINE):
        slot = lag // FINE % 2 * FINE
        for pair in range(0, FINE, 2):
            weights = jnp.concatenate(
                [
                    jnp.concatenate([taps[m, lag + pair + j] for m in range(COARSE)], axis=0)
                    for j in range(2)
                ],
                axis=1,
            )
            product = lax.dot_general(rr[:rows, :], weights, NN, preferred_element_type=jnp.float32)
            for j in range(2):
                fine[slot + pair + j, 0, :rows, :] = product[:, j * K : (j + 1) * K]
        total = None if lag == 0 else acc[0, :count, :]
        for j in range(FINE):
            part = fine[slot + j, 0, lag + j : lag + j + count, :]
            total = part if total is None else total + part
        acc[0, :count, :] = total


def patch_taps(row, atoms_ref, taps, columns, even, odd):
    channels = taps.shape[2]
    lane = lax.broadcasted_iota(jnp.int32, (ROWS, K), 1)
    renewed = (lane >= row) & (lane < row + BLOCK_ATOMS)
    columns[...] = jnp.zeros_like(columns)

    def patch(step, carry):
        width = 2 * ROWS * L
        part = pl.ds(pl.multiple_of(step * width, LANES), width)
        columns[pl.ds(row, BLOCK_ATOMS), :] = atoms_ref[:, part]
        turn(columns, 0, even)
        turn(columns, ROWS * L, odd)
        for half, turned in ((0, even), (1, odd)):
            own = pl.ds(pl.multiple_of((2 * step + half) * ROWS, ROWS), ROWS)
            for tap in range(L):
                fresh = turned[pl.ds(tap, ROWS, stride=STRIDE), :]
                kept = taps[tap // ROWS, tap % ROWS, own, :].astype(jnp.float32)
                taps[tap // ROWS, tap % ROWS, own, :] = jnp.where(renewed, fresh, kept).astype(
                    jnp.bfloat16
                )
        return carry

    lax.fori_loop(0, channels // (2 * ROWS), patch, 0)


def put_codes(zb, own, first_ref, second_ref, even):
    segment = own.shape[1]
    zb[L : L + segment, :] = own[...].T.astype(jnp.bfloat16)

    def put(left, right):
        zb[:L, :] = left[:K, :].astype(jnp.float32).T[segment - L :].astype(jnp.bfloat16)
        if zb.shape[0] > L + segment:
            zb[L + segment :, :] = right[:K, :].astype(jnp.float32).T[:L].astype(jnp.bfloat16)

    pl.when(even)(lambda: put(second_ref, first_ref))
    pl.when(jnp.logical_not(even))(lambda: put(first_ref, second_ref))


def iterate_kernel(total_time, patching, place_ref, limit_ref, *refs):
    code_ref, first_ref, second_ref, signal_ref, next_first, next_second = refs[:6]
    refs = refs[6:]
    if patching:
        atoms_ref, refs = refs[0], refs[1:]
    taps, state_out, low_out = refs[:3]
    refs = refs[3:]
    if patching:
        taps, refs = refs[0], refs[1:]
    zb, rb, zz, rr, fine, acc, beyond = refs[:7]
    channels, segment = signal_ref.shape
    tiles = channels // LANES
    scale = (C * L) ** (-0.5)
    even = place_ref[2] == 0
    put_codes(zb, code_ref, first_ref, second_ref, even)

    def put(following):
        for tile in range(tiles):
            own = slice(K + tile * LANES, K + (tile + 1) * LANES)
            turned = following[own, :].astype(jnp.float32).T
            beyond[:, tile * LANES : (tile + 1) * LANES] = turned[:L]

    pl.when(even)(lambda: put(next_first))
    pl.when(jnp.logical_not(even))(lambda: put(next_second))
    if patching:
        columns, even_ref, odd_ref = refs[7:]
        patch_taps(pl.multiple_of(place_ref[1], BLOCK_ATOMS), atoms_ref, taps, columns, even_ref, odd_ref)
    reach = segment + L
    convolve(zb, L, reach, taps, zz, fine, acc)
    moment = place_ref[0] + lax.broadcasted_iota(jnp.int32, (reach, LANES), 0)
    inside = moment < total_time
    for tile in range(tiles):
        column = slice(tile * LANES, (tile + 1) * LANES)
        own = signal_ref[column, :].astype(jnp.float32).T
        value = jnp.concatenate([own, beyond[:, column]], axis=0) - scale * acc[tile, :reach, :]
        rb[:, column] = jnp.where(inside, value, 0.0).astype(jnp.bfloat16)
    correlate(rb, segment, taps, rr, fine, acc)
    limit = limit_ref[...]
    stepped = code_ref[...].T + code_rate * (scale * acc[0, :segment, :])
    state = (stepped - jnp.clip(stepped, -limit, limit)).T
    state_out[...] = state
    low_out[...] = state.astype(jnp.bfloat16)


def iterate(place, limit, code, swapped, signal, following, taps, atoms, peers):
    channels, segment = signal.shape
    patching = atoms is not None
    reach = segment + L
    return pl.pallas_call(
        functools.partial(iterate_kernel, peers * segment, patching),
        in_specs=[pl.BlockSpec(memory_space=pltpu.SMEM)] + [vmem()] * (8 + patching),
        out_specs=[vmem()] * (2 + patching),
        out_shape=[
            jax.ShapeDtypeStruct((K, segment), jnp.float32),
            jax.ShapeDtypeStruct((K, segment), jnp.bfloat16),
        ]
        + [pltpu.VMEM(taps.shape, jnp.bfloat16)] * patching,
        scratch_shapes=[
            pltpu.VMEM((L + reach, K), jnp.bfloat16),
            pltpu.VMEM((reach, channels), jnp.bfloat16),
            pltpu.VMEM((reach + ROWS, COARSE * K), jnp.bfloat16),
            pltpu.VMEM((segment + ROWS, COARSE * channels), jnp.bfloat16),
            pltpu.VMEM((2 * FINE, channels // LANES, reach + ROWS, LANES), jnp.float32),
            pltpu.VMEM((channels // LANES, reach, LANES), jnp.float32),
            pltpu.VMEM((L, channels), jnp.float32),
        ]
        + [
            pltpu.VMEM((K, 2 * ROWS * L), jnp.float32),
            pltpu.VMEM((ROWS * STRIDE, K), jnp.float32),
            pltpu.VMEM((ROWS * STRIDE, K), jnp.float32),
        ]
        * patching,
        input_output_aliases={9: 2} if patching else {},
        compiler_params=pltpu.CompilerParams(vmem_limit_bytes=VMEM_BYTES),
        name="iterate",
    )(place, limit, code, *swapped, signal, *following, *([resident(atoms)] if patching else []), resident(taps))


def finish_kernel(
    peers, place_ref, code_ref, first_ref, second_ref, signal_ref, taps, resid_out, payload_out, zb, zz, fine, acc, tall
):
    channels, segment = signal_ref.shape
    scale = (C * L) ** (-0.5)
    put_codes(zb, code_ref, first_ref, second_ref, place_ref[1] == 0)
    convolve(zb, L, segment, taps, zz, fine, acc)
    for tile in range(channels // LANES):
        column = slice(tile * LANES, (tile + 1) * LANES)
        value = signal_ref[column, :].astype(jnp.float32) - scale * acc[tile, :segment, :].T
        resid_out[column, :] = value
        tall[column, :] = value
    row = pl.multiple_of(place_ref[0], BLOCK_ATOMS)
    block = code_ref[pl.ds(row, BLOCK_ATOMS), :].astype(jnp.bfloat16)
    share = channels // peers
    share_rows = payload_out.shape[1] - BLOCK_ATOMS
    tall[channels:, :] = jnp.zeros((tall.shape[0] - channels, segment), jnp.float32)
    for peer in range(peers):
        part = tall[peer * share : peer * share + share_rows, :]
        payload_out[peer, :share_rows, :] = part.astype(jnp.bfloat16)
        payload_out[peer, share_rows:, :] = block


def finish(place, code, swapped, signal, taps, peers):
    channels, segment = signal.shape
    share = channels // peers
    share_rows = -(-share // ROWS) * ROWS
    return pl.pallas_call(
        functools.partial(finish_kernel, peers),
        in_specs=[pl.BlockSpec(memory_space=pltpu.SMEM)] + [vmem()] * 5,
        out_specs=[vmem(), vmem()],
        out_shape=[
            jax.ShapeDtypeStruct((channels, segment), jnp.float32),
            jax.ShapeDtypeStruct((peers, share_rows + BLOCK_ATOMS, segment), jnp.bfloat16),
        ],
        scratch_shapes=[
            pltpu.VMEM((L + segment, K), jnp.bfloat16),
            pltpu.VMEM((segment + ROWS, COARSE * K), jnp.bfloat16),
            pltpu.VMEM((2 * FINE, channels // LANES, segment + ROWS, LANES), jnp.float32),
            pltpu.VMEM((channels // LANES, segment, LANES), jnp.float32),
            pltpu.VMEM((channels + ROWS, segment), jnp.float32),
        ],
        compiler_params=pltpu.CompilerParams(vmem_limit_bytes=VMEM_BYTES),
        name="finish",
    )(place, code, *swapped, signal, resident(taps))


def gradient_kernel(share, place_ref, source_ref, blocks_ref, dict_hbm, out_ref, rf, zf, rr, zz, old, sem):
    peers, rows, segment = blocks_ref.shape
    share_rows = rows - BLOCK_ATOMS
    span = peers * segment
    entries = share * L
    rows_of = pl.ds(pl.multiple_of(place_ref[1], BLOCK_ATOMS), BLOCK_ATOMS)
    columns_of = pl.ds(pl.multiple_of(place_ref[0] * entries, LANES), entries)
    fetch = pltpu.make_async_copy(dict_hbm.at[rows_of, columns_of], old, sem)
    fetch.start()
    rf[:, span:] = jnp.zeros((share_rows, LANES), jnp.float32)
    zf[:, :LANES] = jnp.zeros((BLOCK_ATOMS, LANES), jnp.float32)
    for peer in range(peers):
        column = peer * segment
        rf[:, column : column + segment] = blocks_ref[peer, :share_rows, :].astype(jnp.float32)
        zf[:, LANES + column : LANES + column + segment] = blocks_ref[peer, share_rows:, :].astype(
            jnp.float32
        )
    for lag in range(ROWS):
        rr[lag * share_rows : (lag + 1) * share_rows, :] = rf[:, lag : lag + span].astype(jnp.bfloat16)
    for coarse in range(COARSE):
        begin = LANES - ROWS * coarse
        zz[coarse * BLOCK_ATOMS : (coarse + 1) * BLOCK_ATOMS, :] = zf[:, begin : begin + span].astype(
            jnp.bfloat16
        )
    lagged = lax.dot_general(zz[...], rr[...], NT, preferred_element_type=jnp.float32)
    wide = ROWS * share_rows
    parts = []
    left = lagged
    for _ in range(3):
        parts.append(left.astype(jnp.bfloat16))
        left = left - parts[-1].astype(jnp.float32)
    total = jnp.zeros((3 * BLOCK_ATOMS, entries), jnp.float32)
    for coarse in range(COARSE):
        row = lax.broadcasted_iota(jnp.int32, (wide, entries), 0) + coarse * wide
        chosen = (row == source_ref[...]).astype(jnp.float32).astype(jnp.bfloat16)
        total += lax.dot_general(
            jnp.concatenate(
                [part[coarse * BLOCK_ATOMS : (coarse + 1) * BLOCK_ATOMS, :] for part in parts], axis=0
            ),
            chosen,
            NN,
            preferred_element_type=jnp.float32,
        )
    gradient = total[:BLOCK_ATOMS] + total[BLOCK_ATOMS : 2 * BLOCK_ATOMS] + total[2 * BLOCK_ATOMS :]
    fetch.wait()
    before = old[...]
    square = jnp.sum(before * before, axis=1, keepdims=True)
    along = jnp.sum(gradient * before, axis=1, keepdims=True) / (square + tiny_eps)
    out_ref[:, :entries] = (gradient - along * before).astype(jnp.bfloat16)
    lane = lax.broadcasted_iota(jnp.int32, (BLOCK_ATOMS, LANES), 1)
    terms = jnp.zeros((BLOCK_ATOMS, LANES), jnp.float32)
    for i in range(3):
        term = along.astype(jnp.bfloat16).astype(jnp.float32)
        along = along - term
        terms = jnp.where(lane == i, term, terms)
    out_ref[:, entries:] = terms.astype(jnp.bfloat16)


def share_gradient(place, blocks, dictionary, share):
    peers, rows, segment = blocks.shape
    share_rows = rows - BLOCK_ATOMS
    span = peers * segment
    entry = jnp.arange(share * L, dtype=jnp.int32)
    channel, tap = entry // L, entry % L
    source = (tap // ROWS) * (ROWS * share_rows) + (tap % ROWS) * share_rows + channel
    return pl.pallas_call(
        functools.partial(gradient_kernel, share),
        in_specs=[pl.BlockSpec(memory_space=pltpu.SMEM), vmem(), vmem(), pl.BlockSpec(memory_space=pl.ANY)],
        out_shape=jax.ShapeDtypeStruct((BLOCK_ATOMS, share * L + LANES), jnp.bfloat16),
        scratch_shapes=[
            pltpu.VMEM((share_rows, span + LANES), jnp.float32),
            pltpu.VMEM((BLOCK_ATOMS, LANES + span), jnp.float32),
            pltpu.VMEM((ROWS * share_rows, span), jnp.bfloat16),
            pltpu.VMEM((COARSE * BLOCK_ATOMS, span), jnp.bfloat16),
            pltpu.VMEM((BLOCK_ATOMS, share * L), jnp.float32),
            pltpu.SemaphoreType.DMA,
        ],
        compiler_params=pltpu.CompilerParams(vmem_limit_bytes=VMEM_BYTES),
        name="gradient",
    )(place, source[None, :], blocks, dictionary)


def gather_steps(peers):
    bits = [1 << i for i in range(peers.bit_length() - 2, 0, -1)]
    steps = []
    for first in range(0, len(bits), 2):
        pair = bits[first : first + 2]
        steps.append(pair + [sum(pair)] if len(pair) == 2 else pair)
    return steps


def gather_slots(peers):
    flips = [0]
    for masks in gather_steps(peers):
        flips = [f ^ m for m in [0] + masks for f in flips]
    return flips


def gather_pieces(piece):
    peers = lax.axis_size("tm")

    def exchanged(shard, mask):
        return lax.ppermute(shard, "tm", [(i, i ^ mask) for i in range(peers)])

    held = piece[None]
    for masks in gather_steps(peers):
        held = jnp.concatenate([held] + [exchanged(held, mask) for mask in masks], axis=0)
    return held, exchanged(held, 1)


def recall_kernel(place_ref, dict_hbm, piece_ref, old_ref, mean_ref, sem):
    del piece_ref
    first_row = pl.multiple_of(place_ref[1], BLOCK_ATOMS)
    fetch = pltpu.make_async_copy(dict_hbm.at[pl.ds(first_row, BLOCK_ATOMS)], old_ref, sem)
    fetch.start()
    fetch.wait()
    width = 9 * LANES if old_ref.shape[1] % (9 * LANES) == 0 else LANES

    def add(step, square):
        before = old_ref[:, pl.ds(pl.multiple_of(step * width, LANES), width)]
        return square + before * before

    square = lax.fori_loop(
        0, old_ref.shape[1] // width, add, jnp.zeros((BLOCK_ATOMS, width), jnp.float32)
    )
    mean_sq = jnp.sum(square, axis=1, keepdims=True) / (C * L) + tiny_eps
    mean_ref[...] = jnp.broadcast_to(mean_sq, mean_ref.shape)


def recall(place, dictionary, piece):
    remote = pl.BlockSpec(memory_space=pl.ANY)
    return pl.pallas_call(
        recall_kernel,
        in_specs=[pl.BlockSpec(memory_space=pltpu.SMEM), remote, remote],
        out_specs=[vmem(), vmem()],
        out_shape=[
            pltpu.VMEM((BLOCK_ATOMS, dictionary.shape[1]), jnp.float32),
            jax.ShapeDtypeStruct((BLOCK_ATOMS, LANES), jnp.float32),
        ],
        scratch_shapes=[pltpu.SemaphoreType.DMA],
        compiler_params=pltpu.CompilerParams(vmem_limit_bytes=VMEM_BYTES),
        name="recall",
    )(place, dictionary, piece)


def renew_kernel(place_ref, held_ref, came_ref, old, mean_ref, dict_hbm, out_hbm, atoms_ref, grad, sems):
    del dict_hbm
    me = place_ref[0]
    first_row = pl.multiple_of(place_ref[1], BLOCK_ATOMS)
    half, _, wide = held_ref.shape
    width = wide - LANES
    entries = C * L
    shares = []
    for slot, flips in enumerate(gather_slots(2 * half)):
        for source, extra in ((held_ref, 0), (came_ref, 1)):
            owner = me ^ (flips + extra)
            shares.append((source.at[slot], pl.ds(pl.multiple_of(owner * width, LANES), width)))
    zeros = jnp.zeros((BLOCK_ATOMS, width), jnp.float32)
    dot = zeros
    for source, column in shares:
        before = old[:, column]
        along = jnp.sum(source[:, width:].astype(jnp.float32), axis=1, keepdims=True)
        value = source[:, :width].astype(jnp.float32) + along * before
        grad[:, column] = value
        dot += value * before
    mean_sq = mean_ref[:, :1]
    along = jnp.sum(dot, axis=1, keepdims=True) / entries / mean_sq
    square = zeros
    for _, column in shares:
        value = grad[:, column] - along * old[:, column]
        grad[:, column] = value
        square += value * value
    spread = jnp.sum(square, axis=1, keepdims=True) / entries + tiny_eps
    step = move_rate / jnp.sqrt(spread)
    norm = 1.0 / jnp.sqrt(mean_sq + 0.25)
    stores = []
    for index, (_, column) in enumerate(shares):
        atoms_ref[:, column] = (old[:, column] + step * grad[:, column]) * norm
        stores.append(
            pltpu.make_async_copy(
                atoms_ref.at[:, column],
                out_hbm.at[pl.ds(first_row, BLOCK_ATOMS), column],
                sems.at[index],
            )
        )
        stores[-1].start()
    for store in stores:
        store.wait()


def renew(place, held, came, old, mean_sq, dictionary):
    entries = dictionary.shape[1]
    remote = pl.BlockSpec(memory_space=pl.ANY)
    return pl.pallas_call(
        renew_kernel,
        in_specs=[pl.BlockSpec(memory_space=pltpu.SMEM)] + [vmem()] * 4 + [remote],
        out_specs=[remote, vmem()],
        out_shape=[
            jax.ShapeDtypeStruct(dictionary.shape, jnp.float32),
            pltpu.VMEM((BLOCK_ATOMS, entries), jnp.float32),
        ],
        scratch_shapes=[
            pltpu.VMEM((BLOCK_ATOMS, entries), jnp.float32),
            pltpu.SemaphoreType.DMA((2 * held.shape[0],)),
        ],
        input_output_aliases={5: 0},
        compiler_params=pltpu.CompilerParams(vmem_limit_bytes=VMEM_BYTES),
        name="renew",
    )(place, held, came, resident(old), mean_sq, dictionary)


def whole_channels(signal, codes_init, dictionary_init, threshold, plan):
    channels, segment = signal.shape
    peers = lax.axis_size("tm")
    limit = threshold[None, :]
    index = lax.axis_index("tm").astype(jnp.int32)
    first_rows = [plan[step].astype(jnp.int32) * BLOCK_ATOMS for step in range(OUTER)]
    even = index % 2

    def swaps(shard):
        ends = [range(first, peers - 1, 2) for first in (0, 1)]
        pairs = [[p for i in end for p in ((i, i + 1), (i + 1, i))] for end in ends]
        return [lax.ppermute(shard, "tm", pair) for pair in pairs]

    low = codes_init.astype(jnp.bfloat16)
    following = swaps(jnp.concatenate([low, signal], axis=0))
    swapped = following
    taps, dictionary = layout(dictionary_init, channels)
    code_state, atoms = codes_init, None
    for step in range(OUTER):
        previous = first_rows[step - 1] if step else first_rows[0]
        place = jnp.stack([index * segment, previous, even])
        for inner in range(INNER):
            fresh = atoms if inner == 0 else None
            results = iterate(
                place, limit, code_state, swapped, signal, following, taps, fresh, peers
            )
            code_state, low = results[:2]
            if fresh is not None:
                taps = results[2]
            swapped = swaps(low)
        place = jnp.stack([first_rows[step], even])
        residual, payload = finish(place, code_state, swapped, signal, taps, peers)
        blocks = lax.all_to_all(payload, "tm", 0, 0, tiled=True)
        place = jnp.stack([index, first_rows[step]])
        piece = share_gradient(place, blocks, dictionary, channels // peers)
        held, came = gather_pieces(piece)
        old, mean_sq = recall(place, dictionary, piece)
        dictionary, atoms = renew(place, held, came, old, mean_sq, dictionary)
    return code_state, dictionary, residual


def renew_atoms(old_atoms, across, mean_sq, spread):
    return (old_atoms + move_rate * across / jnp.sqrt(spread)[:, None]) / jnp.sqrt(mean_sq + 0.25)[
        :, None
    ]


def split_channels(signal, codes_init, dictionary_init, threshold, plan):
    segment = signal.shape[1]
    local_chan = signal.shape[0]
    unit_scale = (C * L) ** (-0.5)
    entries = C * L
    limit = threshold[:, None]

    def convolve(atom_cube, code_low):
        code_edge = shifted(code_low[:, segment - (L - 1) :], "tm", 1)
        extended = jnp.concatenate([code_edge, code_low], axis=1)
        lagged = jnp.stack(
            [extended[:, L - 1 - offset : L - 1 - offset + segment] for offset in range(L)], axis=1
        )
        return unit_scale * jnp.einsum(
            "kcl,klt->ct", atom_cube, lagged, preferred_element_type=jnp.float32
        )

    def resid_columns(resid_low):
        resid_edge = shifted(resid_low[:, : L - 1], "tm", -1)
        extended = jnp.concatenate([resid_low, resid_edge], axis=1)
        lagged = jnp.stack([extended[:, offset : offset + segment] for offset in range(L)], axis=1)
        return lagged.reshape(local_chan * L, segment)

    code_state = codes_init
    dictionary = dictionary_init
    residual = signal.astype(jnp.float32)
    for outer_step in range(OUTER):
        dict_low = dictionary.astype(jnp.bfloat16)
        atom_cube = dict_low.reshape(K, local_chan, L)
        for inner_step in range(INNER):
            code_low = code_state.astype(jnp.bfloat16)
            residual = signal.astype(jnp.float32) - convolve(atom_cube, code_low)
            lagged = resid_columns(residual.astype(jnp.bfloat16))
            partial_value = unit_scale * jnp.dot(
                dict_low, lagged, preferred_element_type=jnp.float32
            )
            scores = lax.psum(partial_value.astype(jnp.bfloat16), "chan").astype(jnp.float32)
            stepped = code_state + code_rate * scores
            code_state = stepped - jnp.clip(stepped, -limit, limit)
        code_low = code_state.astype(jnp.bfloat16)
        residual = signal.astype(jnp.float32) - convolve(atom_cube, code_low)
        lagged = resid_columns(residual.astype(jnp.bfloat16))
        first_row = plan[outer_step] * BLOCK_ATOMS
        code_block = lax.dynamic_slice_in_dim(code_low, first_row, BLOCK_ATOMS, 0)
        local_grad = lax.dot_general(
            code_block, lagged, (((1,), (1,)), ((), ())), preferred_element_type=jnp.float32
        )
        old_atoms = lax.dynamic_slice_in_dim(dictionary, first_row, BLOCK_ATOMS, 0)
        gradient = lax.psum(local_grad, "tm")
        dot_sum, square_sum = lax.psum(
            (jnp.sum(gradient * old_atoms, axis=1), jnp.sum(old_atoms * old_atoms, axis=1)), "chan"
        )
        mean_sq = square_sum / entries + tiny_eps
        along_coef = dot_sum / entries / mean_sq
        across = gradient - along_coef[:, None] * old_atoms
        spread = lax.psum(jnp.sum(across * across, axis=1), "chan") / entries + tiny_eps
        renewed = renew_atoms(old_atoms, across, mean_sq, spread)
        dictionary = lax.dynamic_update_slice_in_dim(dictionary, renewed, first_row, 0)
    return (code_state, dictionary, residual)


def shards(signal, codes_init, dictionary_init, threshold, plan):
    channels, segment = signal.shape
    peers = lax.axis_size("tm")
    fits = (
        lax.axis_size("chan") == 1
        and segment % LANES == 0
        and channels % (4 * ROWS) == 0
        and channels % LANES == 0
        and channels % peers == 0
        and (channels // peers * L) % LANES == 0
        and peers > 1
        and peers & (peers - 1) == 0
    )
    body = whole_channels if fits else split_channels
    return body(signal, codes_init, dictionary_init, threshold, plan)


def solution(mesh):
    placed = (P("chan", "tm"), P(None, "tm"), P(None, "chan"), P(), P())
    return jax.shard_map(
        shards,
        mesh=mesh,
        in_specs=placed,
        out_specs=(P(None, "tm"), P(None, "chan"), P("chan", "tm")),
        check_vma=False,
    )
```

```python
import functools

import jax
import jax.numpy as jnp
from jax import lax
from jax.experimental import pallas as pl
from jax.experimental.pallas import tpu as pltpu
from jax.sharding import PartitionSpec as P

C = 384
K = 128
L = 96
BLOCK_ATOMS = 16
INNER = 2
OUTER = 2

code_rate = 0.3
move_rate = 0.5
tiny_eps = 1e-06

ROWS = 16
COARSE = L // ROWS
STRIDE = L + 1
FINE = 4
LANES = 128
VMEM_BYTES = 24 * 1024 * 1024

NN = (((1,), (0,)), ((), ()))
NT = (((1,), (1,)), ((), ()))


def shifted(shard, axis, by):
    peers = lax.axis_size(axis)
    pairs = [(i, i + by) for i in range(peers) if 0 <= i + by < peers]
    return lax.ppermute(shard, axis, pairs)


def resident(value):
    return pltpu.with_memory_space_constraint(value, pltpu.VMEM)


def far(value):
    return pltpu.with_memory_space_constraint(value, pltpu.HBM)


def hbm():
    return pl.BlockSpec(memory_space=pltpu.HBM)


def scalars():
    return pl.BlockSpec(memory_space=pltpu.SMEM)


def first_row_of(plan_ref, step):
    return pl.multiple_of(plan_ref[step] * BLOCK_ATOMS, BLOCK_ATOMS)


def vmem():
    return pl.BlockSpec(memory_space=pltpu.VMEM)


def turn(columns_ref, start, turned_ref):
    side = 2 * LANES
    row = lax.broadcasted_iota(jnp.int32, (side, side), 0)
    column = lax.broadcasted_iota(jnp.int32, (side, side), 1)
    identity = (row == column).astype(jnp.float32).astype(jnp.bfloat16)
    for first in range(0, ROWS * L, 2 * side):
        pair = jnp.concatenate(
            [columns_ref[:, pl.ds(start + first + half * side, side)] for half in range(2)], axis=0
        ).astype(jnp.bfloat16)
        turned = lax.dot_general(identity, pair, NT, preferred_element_type=jnp.float32)
        for half in range(2):
            entry = first + half * side
            end = entry + side
            begin = entry
            while begin < end:
                channel, tap = begin // L, begin % L
                count = min(end - begin, L - tap)
                target = channel * STRIDE + tap
                turned_ref[target : target + count, :] = turned[
                    begin - entry : begin - entry + count, half * K : (half + 1) * K
                ]
                begin += count


def layout_kernel(dict_ref, taps_ref, copy_hbm, even, odd, sem):
    width = dict_ref.shape[1]
    column = pl.multiple_of(pl.program_id(0) * width, LANES)
    copy = pltpu.make_async_copy(dict_ref, copy_hbm.at[:, pl.ds(column, width)], sem)
    copy.start()
    groups = width // (ROWS * L)
    turn(dict_ref, 0, even)
    for group in range(groups):
        now, later = (even, odd) if group % 2 == 0 else (odd, even)
        if group + 1 < groups:
            turn(dict_ref, (group + 1) * ROWS * L, later)
        own = pl.ds(pl.multiple_of((pl.program_id(0) * groups + group) * ROWS, ROWS), ROWS)
        for tap in range(L):
            taps_ref[tap // ROWS, tap % ROWS, own, :] = now[
                pl.ds(tap, ROWS, stride=STRIDE), :
            ].astype(jnp.bfloat16)
    copy.wait()


def layout(dictionary, channels):
    block = 4 * ROWS
    return pl.pallas_call(
        layout_kernel,
        grid=(channels // block,),
        in_specs=[pl.BlockSpec((K, block * L), lambda i: (0, i))],
        out_specs=[vmem(), hbm()],
        out_shape=[
            pltpu.VMEM((COARSE, ROWS, channels, K), jnp.bfloat16),
            pltpu.HBM(dictionary.shape, jnp.float32),
        ],
        scratch_shapes=[
            pltpu.VMEM((ROWS * STRIDE, K), jnp.float32),
            pltpu.VMEM((ROWS * STRIDE, K), jnp.float32),
            pltpu.SemaphoreType.DMA,
        ],
        compiler_params=pltpu.CompilerParams(vmem_limit_bytes=VMEM_BYTES),
        name="layout",
    )(far(dictionary))


def convolve(zb, begin, count, taps, zz, fine, acc):
    channels = taps.shape[2]
    tiles = channels // LANES
    rows = count + ROWS
    for coarse in range(COARSE):
        first = begin - ROWS - ROWS * coarse
        zz[:rows, coarse * K : (coarse + 1) * K] = zb[first : first + rows, :]
    for lag in range(0, ROWS, FINE):
        slot = lag // FINE % 2 * FINE
        for pair in range(0, FINE, 2):
            weights = jnp.concatenate(
                [
                    jnp.concatenate([taps[m, lag + pair + j] for m in range(COARSE)], axis=1)
                    for j in range(2)
                ],
                axis=0,
            )
            product = lax.dot_general(zz[:rows, :], weights, NT, preferred_element_type=jnp.float32)
            for j in range(2):
                for tile in range(tiles):
                    column = j * channels + tile * LANES
                    fine[slot + pair + j, tile, :rows, :] = product[:, column : column + LANES]
        for tile in range(tiles):
            total = None if lag == 0 else acc[tile, :count, :]
            for j in range(FINE):
                first = ROWS - lag - j
                part = fine[slot + j, tile, first : first + count, :]
                total = part if total is None else total + part
            acc[tile, :count, :] = total


def correlate(rb, count, taps, rr, fine, acc):
    channels = taps.shape[2]
    rows = count + ROWS
    for coarse in range(COARSE):
        first = ROWS * coarse
        rr[:rows, coarse * channels : (coarse + 1) * channels] = rb[first : first + rows, :]
    for lag in range(0, ROWS, FINE):
        slot = lag // FINE % 2 * FINE
        for pair in range(0, FINE, 2):
            weights = jnp.concatenate(
                [
                    jnp.concatenate([taps[m, lag + pair + j] for m in range(COARSE)], axis=0)
                    for j in range(2)
                ],
                axis=1,
            )
            product = lax.dot_general(rr[:rows, :], weights, NN, preferred_element_type=jnp.float32)
            for j in range(2):
                fine[slot + pair + j, 0, :rows, :] = product[:, j * K : (j + 1) * K]
        total = None if lag == 0 else acc[0, :count, :]
        for j in range(FINE):
            part = fine[slot + j, 0, lag + j : lag + j + count, :]
            total = part if total is None else total + part
        acc[0, :count, :] = total


def patch_taps(row, atoms_ref, taps, columns, turned):
    channels = taps.shape[2]
    lane = lax.broadcasted_iota(jnp.int32, (ROWS, K), 1)
    renewed = (lane >= row) & (lane < row + BLOCK_ATOMS)
    groups = K // BLOCK_ATOMS
    width = ROWS * L

    def patch(step, carry):
        for group in range(groups):
            part = pl.ds(pl.multiple_of((step * groups + group) * width, LANES), width)
            columns[group * BLOCK_ATOMS : (group + 1) * BLOCK_ATOMS, :] = atoms_ref[:, part]
        turn(columns, 0, turned)
        for tap in range(L):
            fresh = turned[pl.ds(tap, ROWS, stride=STRIDE), :]
            for group in range(groups):
                placed = pltpu.roll(fresh, (row + K - group * BLOCK_ATOMS) % K, 1)
                own = pl.ds(pl.multiple_of((step * groups + group) * ROWS, ROWS), ROWS)
                kept = taps[tap // ROWS, tap % ROWS, own, :].astype(jnp.float32)
                taps[tap // ROWS, tap % ROWS, own, :] = jnp.where(renewed, placed, kept).astype(
                    jnp.bfloat16
                )
        return carry

    lax.fori_loop(0, channels // (groups * ROWS), patch, 0)


def put_codes(zb, own, first_ref, second_ref, even):
    segment = own.shape[1]
    zb[L : L + segment, :] = own[...].astype(jnp.float32).T.astype(jnp.bfloat16)

    def put(left, right):
        zb[:L, :] = left[:K, :].astype(jnp.float32).T[segment - L :].astype(jnp.bfloat16)
        if zb.shape[0] > L + segment:
            zb[L + segment :, :] = right[:K, :].astype(jnp.float32).T[:L].astype(jnp.bfloat16)

    pl.when(even)(lambda: put(second_ref, first_ref))
    pl.when(jnp.logical_not(even))(lambda: put(first_ref, second_ref))


def iterate_kernel(total_time, patching, plan_ref, limit_ref, *refs):
    code_ref, first_ref, second_ref, signal_ref, next_first, next_second = refs[:6]
    refs = refs[6:]
    if patching:
        atoms_ref, refs = refs[0], refs[1:]
    taps, state_out, low_out = refs[:3]
    refs = refs[3:]
    if patching:
        taps, refs = refs[0], refs[1:]
    zb, rb, zz, rr, fine, acc, beyond = refs[:7]
    channels, segment = signal_ref.shape
    tiles = channels // LANES
    scale = (C * L) ** (-0.5)
    me = lax.axis_index("tm")
    even = me % 2 == 0
    put_codes(zb, code_ref, first_ref, second_ref, even)

    def put(following):
        for tile in range(tiles):
            own = slice(K + tile * LANES, K + (tile + 1) * LANES)
            turned = following[own, :].astype(jnp.float32).T
            beyond[:, tile * LANES : (tile + 1) * LANES] = turned[:L]

    pl.when(even)(lambda: put(next_first))
    pl.when(jnp.logical_not(even))(lambda: put(next_second))
    if patching:
        columns, turned = refs[7:]
        patch_taps(first_row_of(plan_ref, patching - 1), atoms_ref, taps, columns, turned)
    reach = segment + L
    convolve(zb, L, reach, taps, zz, fine, acc)
    moment = me * segment + lax.broadcasted_iota(jnp.int32, (reach, LANES), 0)
    inside = moment < total_time
    for tile in range(tiles):
        column = slice(tile * LANES, (tile + 1) * LANES)
        own = signal_ref[column, :].astype(jnp.float32).T
        value = jnp.concatenate([own, beyond[:, column]], axis=0) - scale * acc[tile, :reach, :]
        rb[:, column] = jnp.where(inside, value, 0.0).astype(jnp.bfloat16)
    correlate(rb, segment, taps, rr, fine, acc)
    limit = limit_ref[...]
    stepped = code_ref[...].T + code_rate * (scale * acc[0, :segment, :])
    state = (stepped - jnp.clip(stepped, -limit, limit)).T
    state_out[...] = state
    low_out[...] = state.astype(jnp.bfloat16)


def iterate(plan, step, limit, code, swapped, signal, following, taps, atoms, peers):
    channels, segment = signal.shape
    patching = atoms is not None
    reach = segment + L
    return pl.pallas_call(
        functools.partial(iterate_kernel, peers * segment, step if patching else 0),
        in_specs=[scalars()] + [vmem()] * (8 + patching),
        out_specs=[vmem()] * (2 + patching),
        out_shape=[
            jax.ShapeDtypeStruct((K, segment), jnp.float32),
            jax.ShapeDtypeStruct((K, segment), jnp.bfloat16),
        ]
        + [pltpu.VMEM(taps.shape, jnp.bfloat16)] * patching,
        scratch_shapes=[
            pltpu.VMEM((L + reach, K), jnp.bfloat16),
            pltpu.VMEM((reach, channels), jnp.bfloat16),
            pltpu.VMEM((reach + ROWS, COARSE * K), jnp.bfloat16),
            pltpu.VMEM((segment + ROWS, COARSE * channels), jnp.bfloat16),
            pltpu.VMEM((2 * FINE, channels // LANES, reach + ROWS, LANES), jnp.float32),
            pltpu.VMEM((channels // LANES, reach, LANES), jnp.float32),
            pltpu.VMEM((L, channels), jnp.float32),
        ]
        + [
            pltpu.VMEM((K, ROWS * L), jnp.float32),
            pltpu.VMEM((ROWS * STRIDE, K), jnp.float32),
        ]
        * patching,
        input_output_aliases={9: 2} if patching else {},
        compiler_params=pltpu.CompilerParams(vmem_limit_bytes=VMEM_BYTES),
        name="iterate",
    )(plan, limit, code, *swapped, signal, *following, *([resident(atoms)] if patching else []), resident(taps))


def finish_kernel(
    peers, step, plan_ref, low_ref, first_ref, second_ref, signal_ref, taps, resid_out, payload_out, zb, zz, fine, acc, tall
):
    channels, segment = signal_ref.shape
    scale = (C * L) ** (-0.5)
    put_codes(zb, low_ref, first_ref, second_ref, lax.axis_index("tm") % 2 == 0)
    convolve(zb, L, segment, taps, zz, fine, acc)
    for tile in range(channels // LANES):
        column = slice(tile * LANES, (tile + 1) * LANES)
        value = signal_ref[column, :].astype(jnp.float32) - scale * acc[tile, :segment, :].T
        resid_out[column, :] = value
        tall[column, :] = value
    block = low_ref[pl.ds(first_row_of(plan_ref, step), BLOCK_ATOMS), :]
    share = channels // peers
    share_rows = payload_out.shape[1] - BLOCK_ATOMS
    tall[channels:, :] = jnp.zeros((tall.shape[0] - channels, segment), jnp.float32)
    for peer in range(peers):
        part = tall[peer * share : peer * share + share_rows, :]
        payload_out[peer, :share_rows, :] = part.astype(jnp.bfloat16)
        payload_out[peer, share_rows:, :] = block


def finish(plan, step, low, swapped, signal, taps, peers):
    channels, segment = signal.shape
    share = channels // peers
    share_rows = -(-share // ROWS) * ROWS
    return pl.pallas_call(
        functools.partial(finish_kernel, peers, step),
        in_specs=[scalars()] + [vmem()] * 5,
        out_specs=[vmem(), vmem()],
        out_shape=[
            jax.ShapeDtypeStruct((channels, segment), jnp.float32),
            jax.ShapeDtypeStruct((peers, share_rows + BLOCK_ATOMS, segment), jnp.bfloat16),
        ],
        scratch_shapes=[
            pltpu.VMEM((L + segment, K), jnp.bfloat16),
            pltpu.VMEM((segment + ROWS, COARSE * K), jnp.bfloat16),
            pltpu.VMEM((2 * FINE, channels // LANES, segment + ROWS, LANES), jnp.float32),
            pltpu.VMEM((channels // LANES, segment, LANES), jnp.float32),
            pltpu.VMEM((channels + ROWS, segment), jnp.float32),
        ],
        compiler_params=pltpu.CompilerParams(vmem_limit_bytes=VMEM_BYTES),
        name="finish",
    )(plan, low, *swapped, signal, resident(taps))


def gradient_kernel(share, step, plan_ref, source_ref, blocks_ref, dict_hbm, out_ref, rf, zf, rr, zz, old, sem):
    peers, rows, segment = blocks_ref.shape
    share_rows = rows - BLOCK_ATOMS
    span = peers * segment
    entries = share * L
    rows_of = pl.ds(first_row_of(plan_ref, step), BLOCK_ATOMS)
    columns_of = pl.ds(pl.multiple_of(lax.axis_index("tm") * entries, LANES), entries)
    fetch = pltpu.make_async_copy(dict_hbm.at[rows_of, columns_of], old, sem)
    fetch.start()
    rf[:, span:] = jnp.zeros((share_rows, LANES), jnp.float32)
    zf[:, :LANES] = jnp.zeros((BLOCK_ATOMS, LANES), jnp.float32)
    for peer in range(peers):
        column = peer * segment
        rf[:, column : column + segment] = blocks_ref[peer, :share_rows, :].astype(jnp.float32)
        zf[:, LANES + column : LANES + column + segment] = blocks_ref[peer, share_rows:, :].astype(
            jnp.float32
        )
    for lag in range(ROWS):
        rr[lag * share_rows : (lag + 1) * share_rows, :] = rf[:, lag : lag + span].astype(jnp.bfloat16)
    for coarse in range(COARSE):
        begin = LANES - ROWS * coarse
        zz[coarse * BLOCK_ATOMS : (coarse + 1) * BLOCK_ATOMS, :] = zf[:, begin : begin + span].astype(
            jnp.bfloat16
        )
    lagged = lax.dot_general(zz[...], rr[...], NT, preferred_element_type=jnp.float32)
    wide = ROWS * share_rows
    parts = []
    left = lagged
    for _ in range(3):
        parts.append(left.astype(jnp.bfloat16))
        left = left - parts[-1].astype(jnp.float32)
    total = jnp.zeros((3 * BLOCK_ATOMS, entries), jnp.float32)
    for coarse in range(COARSE):
        row = lax.broadcasted_iota(jnp.int32, (wide, entries), 0) + coarse * wide
        chosen = (row == source_ref[...]).astype(jnp.float32).astype(jnp.bfloat16)
        total += lax.dot_general(
            jnp.concatenate(
                [part[coarse * BLOCK_ATOMS : (coarse + 1) * BLOCK_ATOMS, :] for part in parts], axis=0
            ),
            chosen,
            NN,
            preferred_element_type=jnp.float32,
        )
    gradient = total[:BLOCK_ATOMS] + total[BLOCK_ATOMS : 2 * BLOCK_ATOMS] + total[2 * BLOCK_ATOMS :]
    fetch.wait()
    before = old[...]
    square = jnp.sum(before * before, axis=1, keepdims=True)
    along = jnp.sum(gradient * before, axis=1, keepdims=True) / (square + tiny_eps)
    out_ref[:, :entries] = (gradient - along * before).astype(jnp.bfloat16)
    lane = lax.broadcasted_iota(jnp.int32, (BLOCK_ATOMS, LANES), 1)
    terms = jnp.zeros((BLOCK_ATOMS, LANES), jnp.float32)
    for i in range(3):
        term = along.astype(jnp.bfloat16).astype(jnp.float32)
        along = along - term
        terms = jnp.where(lane == i, term, terms)
    out_ref[:, entries:] = terms.astype(jnp.bfloat16)


def share_gradient(plan, step, blocks, dictionary, share):
    peers, rows, segment = blocks.shape
    share_rows = rows - BLOCK_ATOMS
    span = peers * segment
    entry = jnp.arange(share * L, dtype=jnp.int32)
    channel, tap = entry // L, entry % L
    source = (tap // ROWS) * (ROWS * share_rows) + (tap % ROWS) * share_rows + channel
    return pl.pallas_call(
        functools.partial(gradient_kernel, share, step),
        in_specs=[scalars(), vmem(), vmem(), hbm()],
        out_shape=jax.ShapeDtypeStruct((BLOCK_ATOMS, share * L + LANES), jnp.bfloat16),
        scratch_shapes=[
            pltpu.VMEM((share_rows, span + LANES), jnp.float32),
            pltpu.VMEM((BLOCK_ATOMS, LANES + span), jnp.float32),
            pltpu.VMEM((ROWS * share_rows, span), jnp.bfloat16),
            pltpu.VMEM((COARSE * BLOCK_ATOMS, span), jnp.bfloat16),
            pltpu.VMEM((BLOCK_ATOMS, share * L), jnp.float32),
            pltpu.SemaphoreType.DMA,
        ],
        compiler_params=pltpu.CompilerParams(vmem_limit_bytes=VMEM_BYTES),
        name="gradient",
    )(plan, source[None, :], blocks, far(dictionary))


def gather_steps(peers):
    bits = [1 << i for i in range(peers.bit_length() - 2, 0, -1)]
    steps = []
    for first in range(0, len(bits), 2):
        pair = bits[first : first + 2]
        steps.append(pair + [sum(pair)] if len(pair) == 2 else pair)
    return steps


def gather_slots(peers):
    flips = [0]
    for masks in gather_steps(peers):
        flips = [f ^ m for m in [0] + masks for f in flips]
    return flips


def gather_pieces(piece):
    peers = lax.axis_size("tm")

    def exchanged(shard, mask):
        return lax.ppermute(shard, "tm", [(i, i ^ mask) for i in range(peers)])

    held = piece[None]
    for masks in gather_steps(peers):
        held = jnp.concatenate([held] + [exchanged(held, mask) for mask in masks], axis=0)
    return held, exchanged(held, 1)


def recall_kernel(step, plan_ref, dict_hbm, piece_ref, old_ref, mean_ref, sem):
    del piece_ref
    first_row = first_row_of(plan_ref, step)
    fetch = pltpu.make_async_copy(dict_hbm.at[pl.ds(first_row, BLOCK_ATOMS)], old_ref, sem)
    fetch.start()
    fetch.wait()
    width = 9 * LANES if old_ref.shape[1] % (9 * LANES) == 0 else LANES

    def add(step, square):
        before = old_ref[:, pl.ds(pl.multiple_of(step * width, LANES), width)]
        return square + before * before

    square = lax.fori_loop(
        0, old_ref.shape[1] // width, add, jnp.zeros((BLOCK_ATOMS, width), jnp.float32)
    )
    mean_sq = jnp.sum(square, axis=1, keepdims=True) / (C * L) + tiny_eps
    mean_ref[...] = jnp.broadcast_to(mean_sq, mean_ref.shape)


def recall(plan, step, dictionary, piece):
    return pl.pallas_call(
        functools.partial(recall_kernel, step),
        in_specs=[scalars(), hbm(), pl.BlockSpec(memory_space=pl.ANY)],
        out_specs=[vmem(), vmem()],
        out_shape=[
            pltpu.VMEM((BLOCK_ATOMS, dictionary.shape[1]), jnp.float32),
            jax.ShapeDtypeStruct((BLOCK_ATOMS, LANES), jnp.float32),
        ],
        scratch_shapes=[pltpu.SemaphoreType.DMA],
        compiler_params=pltpu.CompilerParams(vmem_limit_bytes=VMEM_BYTES),
        name="recall",
    )(plan, far(dictionary), piece)


def renew_kernel(plan_step, plan_ref, held_ref, came_ref, old, mean_ref, dict_hbm, out_hbm, atoms_ref, grad, sems):
    del dict_hbm
    me = lax.axis_index("tm")
    first_row = first_row_of(plan_ref, plan_step)
    half, _, wide = held_ref.shape
    width = wide - LANES
    entries = C * L
    shares = []
    for slot, flips in enumerate(gather_slots(2 * half)):
        for source, extra in ((held_ref, 0), (came_ref, 1)):
            owner = me ^ (flips + extra)
            shares.append((source.at[slot], pl.ds(pl.multiple_of(owner * width, LANES), width)))
    zeros = jnp.zeros((BLOCK_ATOMS, width), jnp.float32)
    dot = zeros
    for source, column in shares:
        before = old[:, column]
        along = jnp.sum(source[:, width:].astype(jnp.float32), axis=1, keepdims=True)
        value = source[:, :width].astype(jnp.float32) + along * before
        grad[:, column] = value
        dot += value * before
    mean_sq = mean_ref[:, :1]
    along = jnp.sum(dot, axis=1, keepdims=True) / entries / mean_sq
    square = zeros
    for _, column in shares:
        value = grad[:, column] - along * old[:, column]
        grad[:, column] = value
        square += value * value
    spread = jnp.sum(square, axis=1, keepdims=True) / entries + tiny_eps
    step = move_rate / jnp.sqrt(spread)
    norm = 1.0 / jnp.sqrt(mean_sq + 0.25)
    stores = []
    for index, (_, column) in enumerate(shares):
        atoms_ref[:, column] = (old[:, column] + step * grad[:, column]) * norm
        stores.append(
            pltpu.make_async_copy(
                atoms_ref.at[:, column],
                out_hbm.at[pl.ds(first_row, BLOCK_ATOMS), column],
                sems.at[index],
            )
        )
        stores[-1].start()
    for store in stores:
        store.wait()


def renew(plan, step, held, came, old, mean_sq, dictionary):
    entries = dictionary.shape[1]
    return pl.pallas_call(
        functools.partial(renew_kernel, step),
        in_specs=[scalars()] + [vmem()] * 4 + [hbm()],
        out_specs=[hbm(), vmem()],
        out_shape=[
            pltpu.HBM(dictionary.shape, jnp.float32),
            pltpu.VMEM((BLOCK_ATOMS, entries), jnp.float32),
        ],
        scratch_shapes=[
            pltpu.VMEM((BLOCK_ATOMS, entries), jnp.float32),
            pltpu.SemaphoreType.DMA((2 * held.shape[0],)),
        ],
        input_output_aliases={5: 0},
        compiler_params=pltpu.CompilerParams(vmem_limit_bytes=VMEM_BYTES),
        name="renew",
    )(plan, held, came, resident(old), mean_sq, far(dictionary))


def whole_channels(signal, codes_init, dictionary_init, threshold, plan):
    channels, segment = signal.shape
    peers = lax.axis_size("tm")
    limit = threshold[None, :]
    def swaps(shard):
        ends = [range(first, peers - 1, 2) for first in (0, 1)]
        pairs = [[p for i in end for p in ((i, i + 1), (i + 1, i))] for end in ends]
        return [lax.ppermute(shard, "tm", pair) for pair in pairs]

    low = codes_init.astype(jnp.bfloat16)
    following = swaps(jnp.concatenate([low, signal], axis=0))
    swapped = following
    taps, dictionary = layout(dictionary_init, channels)
    code_state, atoms = codes_init, None
    for step in range(OUTER):
        for inner in range(INNER):
            fresh = atoms if inner == 0 else None
            results = iterate(
                plan, step, limit, code_state, swapped, signal, following, taps, fresh, peers
            )
            code_state, low = results[:2]
            if fresh is not None:
                taps = results[2]
            swapped = swaps(low)
        residual, payload = finish(plan, step, low, swapped, signal, taps, peers)
        blocks = lax.all_to_all(payload, "tm", 0, 0, tiled=True)
        piece = share_gradient(plan, step, blocks, dictionary, channels // peers)
        held, came = gather_pieces(piece)
        old, mean_sq = recall(plan, step, dictionary, piece)
        dictionary, atoms = renew(plan, step, held, came, old, mean_sq, dictionary)
    return code_state, dictionary, residual


def renew_atoms(old_atoms, across, mean_sq, spread):
    return (old_atoms + move_rate * across / jnp.sqrt(spread)[:, None]) / jnp.sqrt(mean_sq + 0.25)[
        :, None
    ]


def split_channels(signal, codes_init, dictionary_init, threshold, plan):
    segment = signal.shape[1]
    local_chan = signal.shape[0]
    unit_scale = (C * L) ** (-0.5)
    entries = C * L
    limit = threshold[:, None]

    def convolve(atom_cube, code_low):
        code_edge = shifted(code_low[:, segment - (L - 1) :], "tm", 1)
        extended = jnp.concatenate([code_edge, code_low], axis=1)
        lagged = jnp.stack(
            [extended[:, L - 1 - offset : L - 1 - offset + segment] for offset in range(L)], axis=1
        )
        return unit_scale * jnp.einsum(
            "kcl,klt->ct", atom_cube, lagged, preferred_element_type=jnp.float32
        )

    def resid_columns(resid_low):
        resid_edge = shifted(resid_low[:, : L - 1], "tm", -1)
        extended = jnp.concatenate([resid_low, resid_edge], axis=1)
        lagged = jnp.stack([extended[:, offset : offset + segment] for offset in range(L)], axis=1)
        return lagged.reshape(local_chan * L, segment)

    code_state = codes_init
    dictionary = dictionary_init
    residual = signal.astype(jnp.float32)
    for outer_step in range(OUTER):
        dict_low = dictionary.astype(jnp.bfloat16)
        atom_cube = dict_low.reshape(K, local_chan, L)
        for inner_step in range(INNER):
            code_low = code_state.astype(jnp.bfloat16)
            residual = signal.astype(jnp.float32) - convolve(atom_cube, code_low)
            lagged = resid_columns(residual.astype(jnp.bfloat16))
            partial_value = unit_scale * jnp.dot(
                dict_low, lagged, preferred_element_type=jnp.float32
            )
            scores = lax.psum(partial_value.astype(jnp.bfloat16), "chan").astype(jnp.float32)
            stepped = code_state + code_rate * scores
            code_state = stepped - jnp.clip(stepped, -limit, limit)
        code_low = code_state.astype(jnp.bfloat16)
        residual = signal.astype(jnp.float32) - convolve(atom_cube, code_low)
        lagged = resid_columns(residual.astype(jnp.bfloat16))
        first_row = plan[outer_step] * BLOCK_ATOMS
        code_block = lax.dynamic_slice_in_dim(code_low, first_row, BLOCK_ATOMS, 0)
        local_grad = lax.dot_general(
            code_block, lagged, (((1,), (1,)), ((), ())), preferred_element_type=jnp.float32
        )
        old_atoms = lax.dynamic_slice_in_dim(dictionary, first_row, BLOCK_ATOMS, 0)
        gradient = lax.psum(local_grad, "tm")
        dot_sum, square_sum = lax.psum(
            (jnp.sum(gradient * old_atoms, axis=1), jnp.sum(old_atoms * old_atoms, axis=1)), "chan"
        )
        mean_sq = square_sum / entries + tiny_eps
        along_coef = dot_sum / entries / mean_sq
        across = gradient - along_coef[:, None] * old_atoms
        spread = lax.psum(jnp.sum(across * across, axis=1), "chan") / entries + tiny_eps
        renewed = renew_atoms(old_atoms, across, mean_sq, spread)
        dictionary = lax.dynamic_update_slice_in_dim(dictionary, renewed, first_row, 0)
    return (code_state, dictionary, residual)


def shards(signal, codes_init, dictionary_init, threshold, plan):
    channels, segment = signal.shape
    peers = lax.axis_size("tm")
    fits = (
        lax.axis_size("chan") == 1
        and segment % LANES == 0
        and channels % (4 * ROWS) == 0
        and channels % LANES == 0
        and channels % peers == 0
        and (channels // peers * L) % LANES == 0
        and peers > 1
        and peers & (peers - 1) == 0
    )
    body = whole_channels if fits else split_channels
    return body(signal, codes_init, dictionary_init, threshold, plan)


def solution(mesh):
    placed = (P("chan", "tm"), P(None, "tm"), P(None, "chan"), P(), P())
    return jax.shard_map(
        shards,
        mesh=mesh,
        in_specs=placed,
        out_specs=(P(None, "tm"), P(None, "chan"), P("chan", "tm")),
        check_vma=False,
    )
```

```python
import functools

import jax
import jax.numpy as jnp
import numpy as np
from jax import lax
from jax.experimental import pallas as pl
from jax.experimental.pallas import tpu as pltpu
from jax.sharding import PartitionSpec as P

C = 384
K = 128
L = 96
BLOCK_ATOMS = 16
INNER = 2
OUTER = 2

code_rate = 0.3
move_rate = 0.5
tiny_eps = 1e-06

ROWS = 16
COARSE = L // ROWS
FINE = 4
LANES = 128
VMEM_BYTES = 24 * 1024 * 1024

NN = (((1,), (0,)), ((), ()))
NT = (((1,), (1,)), ((), ()))


def shifted(shard, axis, by):
    peers = lax.axis_size(axis)
    pairs = [(i, i + by) for i in range(peers) if 0 <= i + by < peers]
    return lax.ppermute(shard, axis, pairs)


def resident(value):
    return pltpu.with_memory_space_constraint(value, pltpu.VMEM)


def far(value):
    return pltpu.with_memory_space_constraint(value, pltpu.HBM)


def hbm():
    return pl.BlockSpec(memory_space=pltpu.HBM)


def scalars():
    return pl.BlockSpec(memory_space=pltpu.SMEM)


def first_row_of(plan_ref, step):
    return pl.multiple_of(plan_ref[step] * BLOCK_ATOMS, BLOCK_ATOMS)


def vmem():
    return pl.BlockSpec(memory_space=pltpu.VMEM)


def reorder_matrix():
    target = np.arange(8 * L)
    source = target % 8 * L + target // 8
    return jnp.asarray(source[:, None] == np.arange(8 * L)[None, :], jnp.bfloat16)


def by_tap(columns, reorder_ref):
    pair = jnp.concatenate([columns[:, : 8 * L], columns[:, 8 * L :]], axis=0)
    return lax.dot_general(reorder_ref[...], pair, NT, preferred_element_type=jnp.float32)


def tap_of(turned, tap):
    rows = turned[tap * 8 : (tap + 1) * 8]
    return jnp.concatenate([rows[:, :K], rows[:, K:]], axis=0).astype(jnp.bfloat16)


def layout_kernel(reorder_ref, dict_ref, taps_ref, copy_hbm, sem):
    width = dict_ref.shape[1]
    column = pl.multiple_of(pl.program_id(0) * width, LANES)
    copy = pltpu.make_async_copy(dict_ref, copy_hbm.at[:, pl.ds(column, width)], sem)
    copy.start()
    groups = width // (ROWS * L)
    for group in range(groups):
        columns = dict_ref[:, group * ROWS * L : (group + 1) * ROWS * L].astype(jnp.bfloat16)
        turned = by_tap(columns, reorder_ref)
        own = pl.ds(pl.multiple_of((pl.program_id(0) * groups + group) * ROWS, ROWS), ROWS)
        for tap in range(L):
            taps_ref[tap // ROWS, tap % ROWS, own, :] = tap_of(turned, tap)
    copy.wait()


def layout(reorder, dictionary, channels):
    block = 2 * ROWS
    return pl.pallas_call(
        layout_kernel,
        grid=(channels // block,),
        in_specs=[vmem(), pl.BlockSpec((K, block * L), lambda i: (0, i))],
        out_specs=[vmem(), hbm()],
        out_shape=[
            pltpu.VMEM((COARSE, ROWS, channels, K), jnp.bfloat16),
            pltpu.HBM(dictionary.shape, jnp.float32),
        ],
        scratch_shapes=[pltpu.SemaphoreType.DMA],
        compiler_params=pltpu.CompilerParams(vmem_limit_bytes=VMEM_BYTES),
        name="layout",
    )(reorder, far(dictionary))


def convolve(zb, begin, count, taps, zz, fine, acc):
    channels = taps.shape[2]
    tiles = channels // LANES
    rows = count + ROWS
    for coarse in range(COARSE):
        first = begin - ROWS - ROWS * coarse
        zz[:rows, coarse * K : (coarse + 1) * K] = zb[first : first + rows, :]
    for lag in range(0, ROWS, FINE):
        slot = lag // FINE % 2 * FINE
        for pair in range(0, FINE, 2):
            weights = jnp.concatenate(
                [
                    jnp.concatenate([taps[m, lag + pair + j] for m in range(COARSE)], axis=1)
                    for j in range(2)
                ],
                axis=0,
            )
            product = lax.dot_general(zz[:rows, :], weights, NT, preferred_element_type=jnp.float32)
            for j in range(2):
                for tile in range(tiles):
                    column = j * channels + tile * LANES
                    fine[slot + pair + j, tile, :rows, :] = product[:, column : column + LANES]
        for tile in range(tiles):
            total = None if lag == 0 else acc[tile, :count, :]
            for j in range(FINE):
                first = ROWS - lag - j
                part = fine[slot + j, tile, first : first + count, :]
                total = part if total is None else total + part
            acc[tile, :count, :] = total


def correlate(rb, count, taps, rr, fine, acc):
    channels = taps.shape[2]
    rows = count + ROWS
    for coarse in range(COARSE):
        first = ROWS * coarse
        rr[:rows, coarse * channels : (coarse + 1) * channels] = rb[first : first + rows, :]
    for lag in range(0, ROWS, FINE):
        slot = lag // FINE % 2 * FINE
        for pair in range(0, FINE, 2):
            weights = jnp.concatenate(
                [
                    jnp.concatenate([taps[m, lag + pair + j] for m in range(COARSE)], axis=0)
                    for j in range(2)
                ],
                axis=1,
            )
            product = lax.dot_general(rr[:rows, :], weights, NN, preferred_element_type=jnp.float32)
            for j in range(2):
                fine[slot + pair + j, 0, :rows, :] = product[:, j * K : (j + 1) * K]
        total = None if lag == 0 else acc[0, :count, :]
        for j in range(FINE):
            part = fine[slot + j, 0, lag + j : lag + j + count, :]
            total = part if total is None else total + part
        acc[0, :count, :] = total


def patch_taps(row, atoms_ref, taps, reorder_ref, columns):
    channels = taps.shape[2]
    lane = lax.broadcasted_iota(jnp.int32, (ROWS, K), 1)
    kept = (lane < row) | (lane >= row + BLOCK_ATOMS)
    keep = kept.astype(jnp.float32).astype(jnp.bfloat16)
    columns[...] = jnp.zeros_like(columns)

    def patch(group, carry):
        part = pl.ds(pl.multiple_of(group * (ROWS * L), LANES), ROWS * L)
        columns[pl.ds(row, BLOCK_ATOMS), :] = atoms_ref[:, part].astype(jnp.bfloat16)
        turned = by_tap(columns[...], reorder_ref)
        own = pl.ds(pl.multiple_of(group * ROWS, ROWS), ROWS)
        for tap in range(L):
            before = taps[tap // ROWS, tap % ROWS, own, :]
            taps[tap // ROWS, tap % ROWS, own, :] = before * keep + tap_of(turned, tap)
        return carry

    lax.fori_loop(0, channels // ROWS, patch, 0)


def put_edges(edge_refs, values):
    even = lax.axis_index("tm") % 2 == 0

    def put(first, second):
        first[...] = values[-L:]
        second[...] = values[:L]

    pl.when(even)(lambda: put(*edge_refs))
    pl.when(jnp.logical_not(even))(lambda: put(*edge_refs[::-1]))


def begin_kernel(code_ref, signal_ref, state_out, signal_out, first_out, second_out):
    state = code_ref[...].T
    signal = signal_ref[...].astype(jnp.float32).T.astype(jnp.bfloat16)
    state_out[...] = state
    signal_out[...] = signal
    put_edges((first_out, second_out), jnp.concatenate([state.astype(jnp.bfloat16), signal], axis=1))


def begin(code, signal):
    channels, segment = signal.shape
    return pl.pallas_call(
        begin_kernel,
        in_specs=[vmem()] * 2,
        out_specs=[vmem()] * 4,
        out_shape=[
            pltpu.VMEM((segment, K), jnp.float32),
            pltpu.VMEM((segment, channels), jnp.bfloat16),
        ]
        + [jax.ShapeDtypeStruct((L, K + channels), jnp.bfloat16)] * 2,
        compiler_params=pltpu.CompilerParams(vmem_limit_bytes=VMEM_BYTES),
        name="begin",
    )(code, signal)


def put_codes(zb, state_ref, first_ref, second_ref):
    segment = state_ref.shape[0]
    even = lax.axis_index("tm") % 2 == 0
    zb[L : L + segment, :] = state_ref[...].astype(jnp.bfloat16)

    def put(left, right):
        zb[:L, :] = left[:, :K]
        if zb.shape[0] > L + segment:
            zb[L + segment :, :] = right[:, :K]

    pl.when(even)(lambda: put(second_ref, first_ref))
    pl.when(jnp.logical_not(even))(lambda: put(first_ref, second_ref))


def iterate_kernel(total_time, patching, plan_ref, limit_ref, *refs):
    state_ref, first_ref, second_ref, signal_ref, next_first, next_second = refs[:6]
    refs = refs[6:]
    if patching:
        (atoms_ref, reorder_ref), refs = refs[:2], refs[2:]
    taps, state_out, *edges = refs[:4]
    refs = refs[4:]
    if patching:
        taps, refs = refs[0], refs[1:]
    zb, rb, zz, rr, fine, acc, beyond = refs[:7]
    segment, channels = signal_ref.shape
    tiles = channels // LANES
    scale = (C * L) ** (-0.5)
    me = lax.axis_index("tm")
    even = me % 2 == 0
    put_codes(zb, state_ref, first_ref, second_ref)

    def put(following):
        beyond[...] = following[:, K:]

    pl.when(even)(lambda: put(next_first))
    pl.when(jnp.logical_not(even))(lambda: put(next_second))
    if patching:
        patch_taps(first_row_of(plan_ref, patching - 1), atoms_ref, taps, reorder_ref, refs[7])
    reach = segment + L
    convolve(zb, L, reach, taps, zz, fine, acc)
    moment = me * segment + lax.broadcasted_iota(jnp.int32, (reach, LANES), 0)
    inside = moment < total_time
    for tile in range(tiles):
        column = slice(tile * LANES, (tile + 1) * LANES)
        signal = jnp.concatenate([signal_ref[:, column], beyond[:, column]], axis=0)
        value = signal.astype(jnp.float32) - scale * acc[tile, :reach, :]
        rb[:, column] = jnp.where(inside, value, 0.0).astype(jnp.bfloat16)
    correlate(rb, segment, taps, rr, fine, acc)
    limit = limit_ref[...]
    stepped = state_ref[...] + code_rate * (scale * acc[0, :segment, :])
    state = stepped - jnp.clip(stepped, -limit, limit)
    state_out[...] = state
    put_edges(edges, state.astype(jnp.bfloat16))


def iterate(plan, step, limit, state, swapped, signal, following, taps, atoms, reorder, peers):
    segment, channels = signal.shape
    patching = atoms is not None
    reach = segment + L
    return pl.pallas_call(
        functools.partial(iterate_kernel, peers * segment, step if patching else 0),
        in_specs=[scalars()] + [vmem()] * (8 + 2 * patching),
        out_specs=[vmem()] * (3 + patching),
        out_shape=[pltpu.VMEM((segment, K), jnp.float32)]
        + [jax.ShapeDtypeStruct((L, K), jnp.bfloat16)] * 2
        + [pltpu.VMEM(taps.shape, jnp.bfloat16)] * patching,
        scratch_shapes=[
            pltpu.VMEM((L + reach, K), jnp.bfloat16),
            pltpu.VMEM((reach, channels), jnp.bfloat16),
            pltpu.VMEM((reach + ROWS, COARSE * K), jnp.bfloat16),
            pltpu.VMEM((segment + ROWS, COARSE * channels), jnp.bfloat16),
            pltpu.VMEM((2 * FINE, channels // LANES, reach + ROWS, LANES), jnp.float32),
            pltpu.VMEM((channels // LANES, reach, LANES), jnp.float32),
            pltpu.VMEM((L, channels), jnp.bfloat16),
        ]
        + [pltpu.VMEM((K, ROWS * L), jnp.bfloat16)] * patching,
        input_output_aliases={10: 3} if patching else {},
        compiler_params=pltpu.CompilerParams(vmem_limit_bytes=VMEM_BYTES),
        name="iterate",
    )(
        plan,
        limit,
        resident(state),
        *swapped,
        resident(signal),
        *following,
        *([resident(atoms), reorder] if patching else []),
        resident(taps),
    )


def finish_kernel(
    peers, step, plan_ref, state_ref, first_ref, second_ref, signal_ref, taps, payload_out, *refs
):
    last = step + 1 == OUTER
    if last:
        resid_out, codes_out, zb, zz, fine, acc, tall = refs
    else:
        zb, zz, fine, acc, tall, codes_out = refs
    segment, channels = signal_ref.shape
    scale = (C * L) ** (-0.5)
    put_codes(zb, state_ref, first_ref, second_ref)
    codes_out[...] = state_ref[...].T
    convolve(zb, L, segment, taps, zz, fine, acc)
    for tile in range(channels // LANES):
        column = slice(tile * LANES, (tile + 1) * LANES)
        value = signal_ref[:, column].astype(jnp.float32) - scale * acc[tile, :segment, :]
        value = value.T
        tall[column, :] = value
        if last:
            resid_out[column, :] = value
    block = codes_out[pl.ds(first_row_of(plan_ref, step), BLOCK_ATOMS), :].astype(jnp.bfloat16)
    share = channels // peers
    share_rows = payload_out.shape[1] - BLOCK_ATOMS
    tall[channels:, :] = jnp.zeros((tall.shape[0] - channels, segment), jnp.float32)
    for peer in range(peers):
        part = tall[peer * share : peer * share + share_rows, :]
        payload_out[peer, :share_rows, :] = part.astype(jnp.bfloat16)
        payload_out[peer, share_rows:, :] = block


def finish(plan, step, state, swapped, signal, taps, peers):
    segment, channels = signal.shape
    share = channels // peers
    share_rows = -(-share // ROWS) * ROWS
    last = step + 1 == OUTER
    return pl.pallas_call(
        functools.partial(finish_kernel, peers, step),
        in_specs=[scalars()] + [vmem()] * 5,
        out_specs=[vmem()] * (3 if last else 1),
        out_shape=[
            jax.ShapeDtypeStruct((peers, share_rows + BLOCK_ATOMS, segment), jnp.bfloat16),
            pltpu.VMEM((channels, segment), jnp.float32),
            pltpu.VMEM((K, segment), jnp.float32),
        ][: 3 if last else 1],
        scratch_shapes=[
            pltpu.VMEM((L + segment, K), jnp.bfloat16),
            pltpu.VMEM((segment + ROWS, COARSE * K), jnp.bfloat16),
            pltpu.VMEM((2 * FINE, channels // LANES, segment + ROWS, LANES), jnp.float32),
            pltpu.VMEM((channels // LANES, segment, LANES), jnp.float32),
            pltpu.VMEM((channels + ROWS, segment), jnp.float32),
        ]
        + ([] if last else [pltpu.VMEM((K, segment), jnp.float32)]),
        compiler_params=pltpu.CompilerParams(vmem_limit_bytes=VMEM_BYTES),
        name="finish",
    )(plan, resident(state), *swapped, resident(signal), resident(taps))


def gradient_kernel(share, step, plan_ref, source_ref, blocks_ref, dict_hbm, out_ref, rf, zf, rr, zz, old, sem):
    peers, rows, segment = blocks_ref.shape
    share_rows = rows - BLOCK_ATOMS
    span = peers * segment
    entries = share * L
    rows_of = pl.ds(first_row_of(plan_ref, step), BLOCK_ATOMS)
    columns_of = pl.ds(pl.multiple_of(lax.axis_index("tm") * entries, LANES), entries)
    fetch = pltpu.make_async_copy(dict_hbm.at[rows_of, columns_of], old, sem)
    fetch.start()
    rf[:, span:] = jnp.zeros((share_rows, LANES), jnp.float32)
    zf[:, :LANES] = jnp.zeros((BLOCK_ATOMS, LANES), jnp.float32)
    for peer in range(peers):
        column = peer * segment
        rf[:, column : column + segment] = blocks_ref[peer, :share_rows, :].astype(jnp.float32)
        zf[:, LANES + column : LANES + column + segment] = blocks_ref[peer, share_rows:, :].astype(
            jnp.float32
        )
    for lag in range(ROWS):
        rr[lag * share_rows : (lag + 1) * share_rows, :] = rf[:, lag : lag + span].astype(jnp.bfloat16)
    for coarse in range(COARSE):
        begin = LANES - ROWS * coarse
        zz[coarse * BLOCK_ATOMS : (coarse + 1) * BLOCK_ATOMS, :] = zf[:, begin : begin + span].astype(
            jnp.bfloat16
        )
    lagged = lax.dot_general(zz[...], rr[...], NT, preferred_element_type=jnp.float32)
    wide = ROWS * share_rows
    parts = []
    left = lagged
    for _ in range(3):
        parts.append(left.astype(jnp.bfloat16))
        left = left - parts[-1].astype(jnp.float32)
    total = jnp.zeros((3 * BLOCK_ATOMS, entries), jnp.float32)
    for coarse in range(COARSE):
        row = lax.broadcasted_iota(jnp.int32, (wide, entries), 0) + coarse * wide
        chosen = (row == source_ref[...]).astype(jnp.float32).astype(jnp.bfloat16)
        total += lax.dot_general(
            jnp.concatenate(
                [part[coarse * BLOCK_ATOMS : (coarse + 1) * BLOCK_ATOMS, :] for part in parts], axis=0
            ),
            chosen,
            NN,
            preferred_element_type=jnp.float32,
        )
    gradient = total[:BLOCK_ATOMS] + total[BLOCK_ATOMS : 2 * BLOCK_ATOMS] + total[2 * BLOCK_ATOMS :]
    fetch.wait()
    before = old[...]
    square = jnp.sum(before * before, axis=1, keepdims=True)
    along = jnp.sum(gradient * before, axis=1, keepdims=True) / (square + tiny_eps)
    out_ref[:, :entries] = (gradient - along * before).astype(jnp.bfloat16)
    lane = lax.broadcasted_iota(jnp.int32, (BLOCK_ATOMS, LANES), 1)
    terms = jnp.zeros((BLOCK_ATOMS, LANES), jnp.float32)
    for i in range(3):
        term = along.astype(jnp.bfloat16).astype(jnp.float32)
        along = along - term
        terms = jnp.where(lane == i, term, terms)
    out_ref[:, entries:] = terms.astype(jnp.bfloat16)


def share_gradient(plan, step, blocks, dictionary, share):
    peers, rows, segment = blocks.shape
    share_rows = rows - BLOCK_ATOMS
    span = peers * segment
    entry = jnp.arange(share * L, dtype=jnp.int32)
    channel, tap = entry // L, entry % L
    source = (tap // ROWS) * (ROWS * share_rows) + (tap % ROWS) * share_rows + channel
    return pl.pallas_call(
        functools.partial(gradient_kernel, share, step),
        in_specs=[scalars(), vmem(), vmem(), hbm()],
        out_shape=jax.ShapeDtypeStruct((BLOCK_ATOMS, share * L + LANES), jnp.bfloat16),
        scratch_shapes=[
            pltpu.VMEM((share_rows, span + LANES), jnp.float32),
            pltpu.VMEM((BLOCK_ATOMS, LANES + span), jnp.float32),
            pltpu.VMEM((ROWS * share_rows, span), jnp.bfloat16),
            pltpu.VMEM((COARSE * BLOCK_ATOMS, span), jnp.bfloat16),
            pltpu.VMEM((BLOCK_ATOMS, share * L), jnp.float32),
            pltpu.SemaphoreType.DMA,
        ],
        compiler_params=pltpu.CompilerParams(vmem_limit_bytes=VMEM_BYTES),
        name="gradient",
    )(plan, source[None, :], blocks, far(dictionary))


def gather_steps(peers):
    bits = [1 << i for i in range(peers.bit_length() - 2, 0, -1)]
    steps = []
    for first in range(0, len(bits), 2):
        pair = bits[first : first + 2]
        steps.append(pair + [sum(pair)] if len(pair) == 2 else pair)
    return steps


def gather_slots(peers):
    flips = [0]
    for masks in gather_steps(peers):
        flips = [f ^ m for m in [0] + masks for f in flips]
    return flips


def gather_pieces(piece):
    peers = lax.axis_size("tm")

    def exchanged(shard, mask):
        return lax.ppermute(shard, "tm", [(i, i ^ mask) for i in range(peers)])

    held = piece[None]
    for masks in gather_steps(peers):
        held = jnp.concatenate([held] + [exchanged(held, mask) for mask in masks], axis=0)
    return held, exchanged(held, 1)


def recall_kernel(step, plan_ref, dict_hbm, piece_ref, old_ref, mean_ref, sem):
    del piece_ref
    first_row = first_row_of(plan_ref, step)
    fetch = pltpu.make_async_copy(dict_hbm.at[pl.ds(first_row, BLOCK_ATOMS)], old_ref, sem)
    fetch.start()
    fetch.wait()
    width = 9 * LANES if old_ref.shape[1] % (9 * LANES) == 0 else LANES

    def add(step, square):
        before = old_ref[:, pl.ds(pl.multiple_of(step * width, LANES), width)]
        return square + before * before

    square = lax.fori_loop(
        0, old_ref.shape[1] // width, add, jnp.zeros((BLOCK_ATOMS, width), jnp.float32)
    )
    mean_sq = jnp.sum(square, axis=1, keepdims=True) / (C * L) + tiny_eps
    mean_ref[...] = jnp.broadcast_to(mean_sq, mean_ref.shape)


def recall(plan, step, dictionary, piece):
    return pl.pallas_call(
        functools.partial(recall_kernel, step),
        in_specs=[scalars(), hbm(), pl.BlockSpec(memory_space=pl.ANY)],
        out_specs=[vmem(), vmem()],
        out_shape=[
            pltpu.VMEM((BLOCK_ATOMS, dictionary.shape[1]), jnp.float32),
            jax.ShapeDtypeStruct((BLOCK_ATOMS, LANES), jnp.float32),
        ],
        scratch_shapes=[pltpu.SemaphoreType.DMA],
        compiler_params=pltpu.CompilerParams(vmem_limit_bytes=VMEM_BYTES),
        name="recall",
    )(plan, far(dictionary), piece)


def renew_kernel(plan_step, plan_ref, held_ref, came_ref, old, mean_ref, dict_hbm, out_hbm, atoms_ref, grad, sems):
    del dict_hbm
    me = lax.axis_index("tm")
    first_row = first_row_of(plan_ref, plan_step)
    half, _, wide = held_ref.shape
    width = wide - LANES
    entries = C * L
    shares = []
    for slot, flips in enumerate(gather_slots(2 * half)):
        for source, extra in ((held_ref, 0), (came_ref, 1)):
            owner = me ^ (flips + extra)
            shares.append((source.at[slot], pl.ds(pl.multiple_of(owner * width, LANES), width)))
    zeros = jnp.zeros((BLOCK_ATOMS, width), jnp.float32)
    dot = zeros
    for source, column in shares:
        before = old[:, column]
        along = jnp.sum(source[:, width:].astype(jnp.float32), axis=1, keepdims=True)
        value = source[:, :width].astype(jnp.float32) + along * before
        grad[:, column] = value
        dot += value * before
    mean_sq = mean_ref[:, :1]
    along = jnp.sum(dot, axis=1, keepdims=True) / entries / mean_sq
    square = zeros
    for _, column in shares:
        value = grad[:, column] - along * old[:, column]
        grad[:, column] = value
        square += value * value
    spread = jnp.sum(square, axis=1, keepdims=True) / entries + tiny_eps
    step = move_rate / jnp.sqrt(spread)
    norm = 1.0 / jnp.sqrt(mean_sq + 0.25)
    stores = []
    for index, (_, column) in enumerate(shares):
        atoms_ref[:, column] = (old[:, column] + step * grad[:, column]) * norm
        stores.append(
            pltpu.make_async_copy(
                atoms_ref.at[:, column],
                out_hbm.at[pl.ds(first_row, BLOCK_ATOMS), column],
                sems.at[index],
            )
        )
        stores[-1].start()
    for store in stores:
        store.wait()


def renew(plan, step, held, came, old, mean_sq, dictionary):
    entries = dictionary.shape[1]
    last = step + 1 == OUTER
    return pl.pallas_call(
        functools.partial(renew_kernel, step),
        in_specs=[scalars()] + [vmem()] * 4 + [hbm()],
        out_specs=[hbm()] + [vmem()] * (1 - last),
        out_shape=[pltpu.HBM(dictionary.shape, jnp.float32)]
        + [pltpu.VMEM((BLOCK_ATOMS, entries), jnp.float32)] * (1 - last),
        scratch_shapes=[pltpu.VMEM((BLOCK_ATOMS, entries), jnp.float32)] * (1 + last)
        + [
            pltpu.SemaphoreType.DMA((2 * held.shape[0],)),
        ],
        input_output_aliases={5: 0},
        compiler_params=pltpu.CompilerParams(vmem_limit_bytes=VMEM_BYTES),
        name="renew",
    )(plan, held, came, resident(old), mean_sq, far(dictionary))


def whole_channels(signal, codes_init, dictionary_init, threshold, plan):
    channels, segment = signal.shape
    peers = lax.axis_size("tm")
    limit = threshold[None, :]
    def swaps(edges):
        ends = [range(first, peers - 1, 2) for first in (0, 1)]
        pairs = [[p for i in end for p in ((i, i + 1), (i + 1, i))] for end in ends]
        return [lax.ppermute(edge, "tm", pair) for edge, pair in zip(edges, pairs)]

    state, signal, *edges = begin(codes_init, signal)
    following = swaps(edges)
    swapped = following
    reorder = reorder_matrix()
    taps, dictionary = layout(reorder, dictionary_init, channels)
    atoms = None
    for step in range(OUTER):
        for inner in range(INNER):
            fresh = atoms if inner == 0 else None
            state, *results = iterate(
                plan, step, limit, state, swapped, signal, following, taps, fresh, reorder, peers
            )
            swapped = swaps(results[:2])
            if fresh is not None:
                taps = results[2]
        payload, *finals = finish(plan, step, state, swapped, signal, taps, peers)
        blocks = lax.all_to_all(payload, "tm", 0, 0, tiled=True)
        piece = share_gradient(plan, step, blocks, dictionary, channels // peers)
        held, came = gather_pieces(piece)
        old, mean_sq = recall(plan, step, dictionary, piece)
        dictionary, *renewed = renew(plan, step, held, came, old, mean_sq, dictionary)
        atoms = renewed[0] if renewed else None
    residual, codes = finals
    return codes, dictionary, residual


def renew_atoms(old_atoms, across, mean_sq, spread):
    return (old_atoms + move_rate * across / jnp.sqrt(spread)[:, None]) / jnp.sqrt(mean_sq + 0.25)[
        :, None
    ]


def split_channels(signal, codes_init, dictionary_init, threshold, plan):
    segment = signal.shape[1]
    local_chan = signal.shape[0]
    unit_scale = (C * L) ** (-0.5)
    entries = C * L
    limit = threshold[:, None]

    def convolve(atom_cube, code_low):
        code_edge = shifted(code_low[:, segment - (L - 1) :], "tm", 1)
        extended = jnp.concatenate([code_edge, code_low], axis=1)
        lagged = jnp.stack(
            [extended[:, L - 1 - offset : L - 1 - offset + segment] for offset in range(L)], axis=1
        )
        return unit_scale * jnp.einsum(
            "kcl,klt->ct", atom_cube, lagged, preferred_element_type=jnp.float32
        )

    def resid_columns(resid_low):
        resid_edge = shifted(resid_low[:, : L - 1], "tm", -1)
        extended = jnp.concatenate([resid_low, resid_edge], axis=1)
        lagged = jnp.stack([extended[:, offset : offset + segment] for offset in range(L)], axis=1)
        return lagged.reshape(local_chan * L, segment)

    code_state = codes_init
    dictionary = dictionary_init
    residual = signal.astype(jnp.float32)
    for outer_step in range(OUTER):
        dict_low = dictionary.astype(jnp.bfloat16)
        atom_cube = dict_low.reshape(K, local_chan, L)
        for inner_step in range(INNER):
            code_low = code_state.astype(jnp.bfloat16)
            residual = signal.astype(jnp.float32) - convolve(atom_cube, code_low)
            lagged = resid_columns(residual.astype(jnp.bfloat16))
            partial_value = unit_scale * jnp.dot(
                dict_low, lagged, preferred_element_type=jnp.float32
            )
            scores = lax.psum(partial_value.astype(jnp.bfloat16), "chan").astype(jnp.float32)
            stepped = code_state + code_rate * scores
            code_state = stepped - jnp.clip(stepped, -limit, limit)
        code_low = code_state.astype(jnp.bfloat16)
        residual = signal.astype(jnp.float32) - convolve(atom_cube, code_low)
        lagged = resid_columns(residual.astype(jnp.bfloat16))
        first_row = plan[outer_step] * BLOCK_ATOMS
        code_block = lax.dynamic_slice_in_dim(code_low, first_row, BLOCK_ATOMS, 0)
        local_grad = lax.dot_general(
            code_block, lagged, (((1,), (1,)), ((), ())), preferred_element_type=jnp.float32
        )
        old_atoms = lax.dynamic_slice_in_dim(dictionary, first_row, BLOCK_ATOMS, 0)
        gradient = lax.psum(local_grad, "tm")
        dot_sum, square_sum = lax.psum(
            (jnp.sum(gradient * old_atoms, axis=1), jnp.sum(old_atoms * old_atoms, axis=1)), "chan"
        )
        mean_sq = square_sum / entries + tiny_eps
        along_coef = dot_sum / entries / mean_sq
        across = gradient - along_coef[:, None] * old_atoms
        spread = lax.psum(jnp.sum(across * across, axis=1), "chan") / entries + tiny_eps
        renewed = renew_atoms(old_atoms, across, mean_sq, spread)
        dictionary = lax.dynamic_update_slice_in_dim(dictionary, renewed, first_row, 0)
    return (code_state, dictionary, residual)


def shards(signal, codes_init, dictionary_init, threshold, plan):
    channels, segment = signal.shape
    peers = lax.axis_size("tm")
    fits = (
        lax.axis_size("chan") == 1
        and segment % LANES == 0
        and channels % (4 * ROWS) == 0
        and channels % LANES == 0
        and channels % peers == 0
        and (channels // peers * L) % LANES == 0
        and peers > 1
        and peers & (peers - 1) == 0
    )
    body = whole_channels if fits else split_channels
    return body(signal, codes_init, dictionary_init, threshold, plan)


def solution(mesh):
    placed = (P("chan", "tm"), P(None, "tm"), P(None, "chan"), P(), P())
    return jax.shard_map(
        shards,
        mesh=mesh,
        in_specs=placed,
        out_specs=(P(None, "tm"), P(None, "chan"), P("chan", "tm")),
        check_vma=False,
    )
```

```python
import functools

import jax
import jax.numpy as jnp
from jax import lax
from jax.experimental import pallas as pl
from jax.experimental.pallas import tpu as pltpu
from jax.sharding import PartitionSpec as P

C = 384
K = 128
L = 96
BLOCK_ATOMS = 16
INNER = 2
OUTER = 2

code_rate = 0.3
move_rate = 0.5
tiny_eps = 1e-06

ROWS = 16
COARSE = L // ROWS
STRIDE = L + 1
GROUPS = 4
SUBLANES = 8
COPIED = (56, 48, 24)
FINE = 4
LANES = 128
VMEM_BYTES = 24 * 1024 * 1024

NN = (((1,), (0,)), ((), ()))
NT = (((1,), (1,)), ((), ()))


def shifted(shard, axis, by):
    peers = lax.axis_size(axis)
    pairs = [(i, i + by) for i in range(peers) if 0 <= i + by < peers]
    return lax.ppermute(shard, axis, pairs)


def resident(value):
    return pltpu.with_memory_space_constraint(value, pltpu.VMEM)


def far(value):
    return pltpu.with_memory_space_constraint(value, pltpu.HBM)


def hbm():
    return pl.BlockSpec(memory_space=pltpu.HBM)


def scalars():
    return pl.BlockSpec(memory_space=pltpu.SMEM)


def first_row_of(plan_ref, step):
    return pl.multiple_of(plan_ref[step] * BLOCK_ATOMS, BLOCK_ATOMS)


def vmem():
    return pl.BlockSpec(memory_space=pltpu.VMEM)


def turn(columns, turned_ref):
    side = 2 * LANES
    row = lax.broadcasted_iota(jnp.int32, (side, side), 0)
    column = lax.broadcasted_iota(jnp.int32, (side, side), 1)
    identity = (row == column).astype(jnp.float32).astype(jnp.bfloat16)
    columns = columns.astype(jnp.bfloat16)
    for first in range(0, ROWS * L, 2 * side):
        pair = jnp.concatenate(
            [columns[:, first + half * side : first + (half + 1) * side] for half in range(2)], axis=0
        )
        turned = lax.dot_general(identity, pair, NT, preferred_element_type=jnp.float32)
        for half in range(2):
            entry = first + half * side
            end = entry + side
            begin = entry
            while begin < end:
                channel, tap = begin // L, begin % L
                count = min(end - begin, L - tap)
                target = channel * STRIDE + tap
                turned_ref[target : target + count, :] = turned[
                    begin - entry : begin - entry + count, half * K : (half + 1) * K
                ]
                begin += count


def tap_of(turned_ref, tap):
    return turned_ref[pl.ds(tap, ROWS, stride=STRIDE), :].astype(jnp.bfloat16)


def layout_kernel(dict_ref, taps_ref, *turned):
    def part(group):
        return dict_ref[:, group * ROWS * L : (group + 1) * ROWS * L]

    turn(part(0), turned[0])
    for group in range(GROUPS):
        if group + 1 < GROUPS:
            turn(part(group + 1), turned[group + 1])
        own = pl.ds(pl.multiple_of((pl.program_id(0) * GROUPS + group) * ROWS, ROWS), ROWS)
        for tap in range(L):
            taps_ref[tap // ROWS, tap % ROWS, own, :] = tap_of(turned[group], tap)


def layout(dictionary, channels):
    block = GROUPS * ROWS
    return pl.pallas_call(
        layout_kernel,
        grid=(channels // block,),
        in_specs=[pl.BlockSpec((K, block * L), lambda i: (0, i))],
        out_specs=vmem(),
        out_shape=pltpu.VMEM((COARSE, ROWS, channels, K), jnp.bfloat16),
        scratch_shapes=[pltpu.VMEM((ROWS * STRIDE, K), jnp.float32)] * GROUPS,
        compiler_params=pltpu.CompilerParams(vmem_limit_bytes=VMEM_BYTES),
        name="layout",
    )(far(dictionary))


class Ferry:
    def __init__(self, source, target, first, buffer, sems):
        self.steps = []
        for step in range(buffer.shape[0] // SUBLANES):
            held = buffer.at[pl.ds(step * SUBLANES, SUBLANES)]
            rows = pl.ds(first + step * SUBLANES, SUBLANES)
            fetch = pltpu.make_async_copy(source.at[rows], held, sems.at[0, step])
            store = pltpu.make_async_copy(held, target.at[rows], sems.at[1, step])
            fetch.start()
            self.steps.append((fetch, store))
        self.stored = 0

    def tick(self):
        if self.stored < len(self.steps):
            fetch, store = self.steps[self.stored]
            fetch.wait()
            store.start()
            self.stored += 1

    def close(self):
        while self.stored < len(self.steps):
            self.tick()
        for _, store in self.steps:
            store.wait()


def ferry_scratch(count, entries):
    return [
        pltpu.VMEM((count, entries), jnp.float32),
        pltpu.SemaphoreType.DMA((2, count // SUBLANES)),
    ]


def convolve(zb, begin, count, taps, zz, fine, acc, ferry):
    channels = taps.shape[2]
    tiles = channels // LANES
    rows = count + ROWS
    for coarse in range(COARSE):
        first = begin - ROWS - ROWS * coarse
        zz[:rows, coarse * K : (coarse + 1) * K] = zb[first : first + rows, :]
    for lag in range(0, ROWS, FINE):
        slot = lag // FINE % 2 * FINE
        for pair in range(0, FINE, 2):
            weights = jnp.concatenate(
                [
                    jnp.concatenate([taps[m, lag + pair + j] for m in range(COARSE)], axis=1)
                    for j in range(2)
                ],
                axis=0,
            )
            product = lax.dot_general(zz[:rows, :], weights, NT, preferred_element_type=jnp.float32)
            for j in range(2):
                for tile in range(tiles):
                    column = j * channels + tile * LANES
                    fine[slot + pair + j, tile, :rows, :] = product[:, column : column + LANES]
        if ferry:
            ferry.tick()
        for tile in range(tiles):
            total = None if lag == 0 else acc[tile, :count, :]
            for j in range(FINE):
                first = ROWS - lag - j
                part = fine[slot + j, tile, first : first + count, :]
                total = part if total is None else total + part
            acc[tile, :count, :] = total


def correlate(rb, count, taps, rr, fine, acc, ferry):
    channels = taps.shape[2]
    rows = count + ROWS
    for coarse in range(COARSE):
        first = ROWS * coarse
        rr[:rows, coarse * channels : (coarse + 1) * channels] = rb[first : first + rows, :]
    for lag in range(0, ROWS, FINE):
        slot = lag // FINE % 2 * FINE
        for pair in range(0, FINE, 2):
            weights = jnp.concatenate(
                [
                    jnp.concatenate([taps[m, lag + pair + j] for m in range(COARSE)], axis=0)
                    for j in range(2)
                ],
                axis=1,
            )
            product = lax.dot_general(rr[:rows, :], weights, NN, preferred_element_type=jnp.float32)
            for j in range(2):
                fine[slot + pair + j, 0, :rows, :] = product[:, j * K : (j + 1) * K]
        if ferry:
            ferry.tick()
        total = None if lag == 0 else acc[0, :count, :]
        for j in range(FINE):
            part = fine[slot + j, 0, lag + j : lag + j + count, :]
            total = part if total is None else total + part
        acc[0, :count, :] = total


def patch_taps(row, atoms_ref, taps, columns, turned):
    channels = taps.shape[2]
    lane = lax.broadcasted_iota(jnp.int32, (ROWS, K), 1)
    kept = (lane < row) | (lane >= row + BLOCK_ATOMS)
    keep = kept.astype(jnp.float32).astype(jnp.bfloat16)
    columns[...] = jnp.zeros_like(columns)
    width = ROWS * L

    def patch(step, carry):
        part = pl.ds(pl.multiple_of(step * (GROUPS * width), LANES), GROUPS * width)
        columns[pl.ds(row, BLOCK_ATOMS), :] = atoms_ref[:, part].astype(jnp.bfloat16)
        turn(columns[:, :width], turned[0])
        for group in range(GROUPS):
            if group + 1 < GROUPS:
                turn(columns[:, (group + 1) * width : (group + 2) * width], turned[group + 1])
            own = pl.ds(pl.multiple_of((step * GROUPS + group) * ROWS, ROWS), ROWS)
            for tap in range(L):
                before = taps[tap // ROWS, tap % ROWS, own, :]
                taps[tap // ROWS, tap % ROWS, own, :] = before * keep + tap_of(turned[group], tap)
        return carry

    lax.fori_loop(0, channels // (GROUPS * ROWS), patch, 0)


def put_edges(edge_refs, values):
    even = lax.axis_index("tm") % 2 == 0

    def put(first, second):
        first[...] = values[-L:]
        second[...] = values[:L]

    pl.when(even)(lambda: put(*edge_refs))
    pl.when(jnp.logical_not(even))(lambda: put(*edge_refs[::-1]))


def begin_kernel(code_hbm, signal_hbm, state_out, signal_out, first_out, second_out, code_ref, signal_ref, sems):
    fetches = [
        pltpu.make_async_copy(code_hbm, code_ref, sems.at[0]),
        pltpu.make_async_copy(signal_hbm, signal_ref, sems.at[1]),
    ]
    for fetch in fetches:
        fetch.start()
    for fetch in fetches:
        fetch.wait()
    state = code_ref[...].T
    signal = signal_ref[...].astype(jnp.float32).T.astype(jnp.bfloat16)
    state_out[...] = state
    signal_out[...] = signal
    put_edges((first_out, second_out), jnp.concatenate([state.astype(jnp.bfloat16), signal], axis=1))


def begin(code, signal):
    channels, segment = signal.shape
    return pl.pallas_call(
        begin_kernel,
        in_specs=[hbm()] * 2,
        out_specs=[vmem()] * 4,
        out_shape=[
            pltpu.VMEM((segment, K), jnp.float32),
            pltpu.VMEM((segment, channels), jnp.bfloat16),
        ]
        + [jax.ShapeDtypeStruct((L, K + channels), jnp.bfloat16)] * 2,
        scratch_shapes=[
            pltpu.VMEM(code.shape, code.dtype),
            pltpu.VMEM(signal.shape, signal.dtype),
            pltpu.SemaphoreType.DMA((2,)),
        ],
        compiler_params=pltpu.CompilerParams(vmem_limit_bytes=VMEM_BYTES),
        name="begin",
    )(far(code), far(signal))


def put_codes(zb, state_ref, first_ref, second_ref):
    segment = state_ref.shape[0]
    even = lax.axis_index("tm") % 2 == 0
    zb[L : L + segment, :] = state_ref[...].astype(jnp.bfloat16)

    def put(left, right):
        zb[:L, :] = left[:, :K]
        if zb.shape[0] > L + segment:
            zb[L + segment :, :] = right[:, :K]

    pl.when(even)(lambda: put(second_ref, first_ref))
    pl.when(jnp.logical_not(even))(lambda: put(first_ref, second_ref))


def iterate_kernel(total_time, patching, copied, plan_ref, limit_ref, *refs):
    refs = list(refs)

    def take(count):
        taken = refs[:count]
        del refs[:count]
        return taken

    state_ref, first_ref, second_ref, signal_ref, next_first, next_second = take(6)
    atoms = take(1 if patching else 0)
    (taps,) = take(1)
    source = take(1 if copied else 0)
    take(1 if copied and copied[0] else 0)
    state_out, *edges = take(3)
    taps = (take(1) if patching else [taps])[0]
    target = take(1 if copied else 0)
    zb, rb, zz, rr, fine, acc, beyond = take(7)
    ferry = Ferry(source[0], target[0], copied[0], *take(2)) if copied else None
    segment, channels = signal_ref.shape
    tiles = channels // LANES
    scale = (C * L) ** (-0.5)
    me = lax.axis_index("tm")
    even = me % 2 == 0
    put_codes(zb, state_ref, first_ref, second_ref)

    def put(following):
        beyond[...] = following[:, K:]

    pl.when(even)(lambda: put(next_first))
    pl.when(jnp.logical_not(even))(lambda: put(next_second))
    if patching:
        columns, *turned = refs
        patch_taps(first_row_of(plan_ref, patching - 1), atoms[0], taps, columns, turned)
    reach = segment + L
    convolve(zb, L, reach, taps, zz, fine, acc, ferry)
    moment = me * segment + lax.broadcasted_iota(jnp.int32, (reach, LANES), 0)
    inside = moment < total_time
    for tile in range(tiles):
        column = slice(tile * LANES, (tile + 1) * LANES)
        signal = jnp.concatenate([signal_ref[:, column], beyond[:, column]], axis=0)
        value = signal.astype(jnp.float32) - scale * acc[tile, :reach, :]
        rb[:, column] = jnp.where(inside, value, 0.0).astype(jnp.bfloat16)
    correlate(rb, segment, taps, rr, fine, acc, ferry)
    limit = limit_ref[...]
    stepped = state_ref[...] + code_rate * (scale * acc[0, :segment, :])
    state = stepped - jnp.clip(stepped, -limit, limit)
    state_out[...] = state
    put_edges(edges, state.astype(jnp.bfloat16))
    if ferry:
        ferry.close()


def iterate(plan, step, limit, state, swapped, signal, following, taps, atoms, ferry, peers):
    segment, channels = signal.shape
    patching = atoms is not None
    reach = segment + L
    carried = [far(value) for value in (ferry or ())[:2] if value is not None]
    aliases = {9: 3} if patching else {}
    if len(carried) == 2:
        aliases[10 + patching] = 3 + patching
    return pl.pallas_call(
        functools.partial(
            iterate_kernel, peers * segment, step if patching else 0, ferry[2:] if ferry else None
        ),
        in_specs=[scalars()] + [vmem()] * (8 + patching) + [hbm()] * len(carried),
        out_specs=[vmem()] * (3 + patching) + [hbm()] * (ferry is not None),
        out_shape=[pltpu.VMEM((segment, K), jnp.float32)]
        + [jax.ShapeDtypeStruct((L, K), jnp.bfloat16)] * 2
        + [pltpu.VMEM(taps.shape, jnp.bfloat16)] * patching
        + ([pltpu.HBM(ferry[0].shape, jnp.float32)] if ferry else []),
        scratch_shapes=[
            pltpu.VMEM((L + reach, K), jnp.bfloat16),
            pltpu.VMEM((reach, channels), jnp.bfloat16),
            pltpu.VMEM((reach + ROWS, COARSE * K), jnp.bfloat16),
            pltpu.VMEM((segment + ROWS, COARSE * channels), jnp.bfloat16),
            pltpu.VMEM((2 * FINE, channels // LANES, reach + ROWS, LANES), jnp.float32),
            pltpu.VMEM((channels // LANES, reach, LANES), jnp.float32),
            pltpu.VMEM((L, channels), jnp.bfloat16),
        ]
        + (ferry_scratch(ferry[3], ferry[0].shape[1]) if ferry else [])
        + (
            [pltpu.VMEM((K, GROUPS * ROWS * L), jnp.bfloat16)]
            + [pltpu.VMEM((ROWS * STRIDE, K), jnp.float32)] * GROUPS
        )
        * patching,
        input_output_aliases=aliases,
        compiler_params=pltpu.CompilerParams(vmem_limit_bytes=VMEM_BYTES),
        name="iterate",
    )(
        plan,
        limit,
        resident(state),
        *swapped,
        resident(signal),
        *following,
        *([resident(atoms)] if patching else []),
        resident(taps),
        *carried,
    )


def finish_kernel(
    peers, step, copied, plan_ref, state_ref, first_ref, second_ref, signal_ref, taps, *refs
):
    refs = list(refs)

    def take(count):
        taken = refs[:count]
        del refs[:count]
        return taken

    last = step + 1 == OUTER
    source = take(2 if copied else 0)
    (payload_out,) = take(1)
    outs = take(2 if last else 0)
    target = take(1 if copied else 0)
    zb, zz, fine, acc, tall = take(5)
    ferry = Ferry(source[0], target[0], copied[0], *take(2)) if copied else None
    resid_out, codes_out = outs if last else (None, *refs)
    segment, channels = signal_ref.shape
    scale = (C * L) ** (-0.5)
    put_codes(zb, state_ref, first_ref, second_ref)
    codes_out[...] = state_ref[...].T
    convolve(zb, L, segment, taps, zz, fine, acc, ferry)
    for tile in range(channels // LANES):
        column = slice(tile * LANES, (tile + 1) * LANES)
        value = signal_ref[:, column].astype(jnp.float32) - scale * acc[tile, :segment, :]
        value = value.T
        tall[column, :] = value
        if last:
            resid_out[column, :] = value
    block = codes_out[pl.ds(first_row_of(plan_ref, step), BLOCK_ATOMS), :].astype(jnp.bfloat16)
    share = channels // peers
    share_rows = payload_out.shape[1] - BLOCK_ATOMS
    tall[channels:, :] = jnp.zeros((tall.shape[0] - channels, segment), jnp.float32)
    for peer in range(peers):
        part = tall[peer * share : peer * share + share_rows, :]
        payload_out[peer, :share_rows, :] = part.astype(jnp.bfloat16)
        payload_out[peer, share_rows:, :] = block
    if ferry:
        ferry.close()


def finish(plan, step, state, swapped, signal, taps, ferry, peers):
    segment, channels = signal.shape
    share = channels // peers
    share_rows = -(-share // ROWS) * ROWS
    last = step + 1 == OUTER
    carried = [far(value) for value in (ferry or ())[:2]]
    return pl.pallas_call(
        functools.partial(finish_kernel, peers, step, ferry[2:] if ferry else None),
        in_specs=[scalars()] + [vmem()] * 5 + [hbm()] * len(carried),
        out_specs=[vmem()] * (3 if last else 1) + [hbm()] * (len(carried) // 2),
        out_shape=[
            jax.ShapeDtypeStruct((peers, share_rows + BLOCK_ATOMS, segment), jnp.bfloat16),
            pltpu.VMEM((channels, segment), jnp.float32),
            pltpu.VMEM((K, segment), jnp.float32),
        ][: 3 if last else 1]
        + [pltpu.HBM(value.shape, jnp.float32) for value in carried[1:]],
        scratch_shapes=[
            pltpu.VMEM((L + segment, K), jnp.bfloat16),
            pltpu.VMEM((segment + ROWS, COARSE * K), jnp.bfloat16),
            pltpu.VMEM((2 * FINE, channels // LANES, segment + ROWS, LANES), jnp.float32),
            pltpu.VMEM((channels // LANES, segment, LANES), jnp.float32),
            pltpu.VMEM((channels + ROWS, segment), jnp.float32),
        ]
        + (ferry_scratch(ferry[3], ferry[0].shape[1]) if ferry else [])
        + ([] if last else [pltpu.VMEM((K, segment), jnp.float32)]),
        input_output_aliases={7: 3 if last else 1} if carried else {},
        compiler_params=pltpu.CompilerParams(vmem_limit_bytes=VMEM_BYTES),
        name="finish",
    )(plan, resident(state), *swapped, resident(signal), resident(taps), *carried)


def gradient_kernel(share, step, plan_ref, source_ref, blocks_ref, dict_hbm, out_ref, rf, zf, rr, zz, old, sem):
    peers, rows, segment = blocks_ref.shape
    share_rows = rows - BLOCK_ATOMS
    span = peers * segment
    entries = share * L
    rows_of = pl.ds(first_row_of(plan_ref, step), BLOCK_ATOMS)
    columns_of = pl.ds(pl.multiple_of(lax.axis_index("tm") * entries, LANES), entries)
    fetch = pltpu.make_async_copy(dict_hbm.at[rows_of, columns_of], old, sem)
    fetch.start()
    rf[:, span:] = jnp.zeros((share_rows, LANES), jnp.float32)
    zf[:, :LANES] = jnp.zeros((BLOCK_ATOMS, LANES), jnp.float32)
    for peer in range(peers):
        column = peer * segment
        rf[:, column : column + segment] = blocks_ref[peer, :share_rows, :].astype(jnp.float32)
        zf[:, LANES + column : LANES + column + segment] = blocks_ref[peer, share_rows:, :].astype(
            jnp.float32
        )
    for lag in range(ROWS):
        rr[lag * share_rows : (lag + 1) * share_rows, :] = rf[:, lag : lag + span].astype(jnp.bfloat16)
    for coarse in range(COARSE):
        begin = LANES - ROWS * coarse
        zz[coarse * BLOCK_ATOMS : (coarse + 1) * BLOCK_ATOMS, :] = zf[:, begin : begin + span].astype(
            jnp.bfloat16
        )
    lagged = lax.dot_general(zz[...], rr[...], NT, preferred_element_type=jnp.float32)
    wide = ROWS * share_rows
    parts = []
    left = lagged
    for _ in range(3):
        parts.append(left.astype(jnp.bfloat16))
        left = left - parts[-1].astype(jnp.float32)
    total = jnp.zeros((3 * BLOCK_ATOMS, entries), jnp.float32)
    for coarse in range(COARSE):
        row = lax.broadcasted_iota(jnp.int32, (wide, entries), 0) + coarse * wide
        chosen = (row == source_ref[...]).astype(jnp.float32).astype(jnp.bfloat16)
        total += lax.dot_general(
            jnp.concatenate(
                [part[coarse * BLOCK_ATOMS : (coarse + 1) * BLOCK_ATOMS, :] for part in parts], axis=0
            ),
            chosen,
            NN,
            preferred_element_type=jnp.float32,
        )
    gradient = total[:BLOCK_ATOMS] + total[BLOCK_ATOMS : 2 * BLOCK_ATOMS] + total[2 * BLOCK_ATOMS :]
    fetch.wait()
    before = old[...]
    square = jnp.sum(before * before, axis=1, keepdims=True)
    along = jnp.sum(gradient * before, axis=1, keepdims=True) / (square + tiny_eps)
    out_ref[:, :entries] = (gradient - along * before).astype(jnp.bfloat16)
    lane = lax.broadcasted_iota(jnp.int32, (BLOCK_ATOMS, LANES), 1)
    terms = jnp.zeros((BLOCK_ATOMS, LANES), jnp.float32)
    for i in range(3):
        term = along.astype(jnp.bfloat16).astype(jnp.float32)
        along = along - term
        terms = jnp.where(lane == i, term, terms)
    out_ref[:, entries:] = terms.astype(jnp.bfloat16)


def share_gradient(plan, step, blocks, dictionary, share):
    peers, rows, segment = blocks.shape
    share_rows = rows - BLOCK_ATOMS
    span = peers * segment
    entry = jnp.arange(share * L, dtype=jnp.int32)
    channel, tap = entry // L, entry % L
    source = (tap // ROWS) * (ROWS * share_rows) + (tap % ROWS) * share_rows + channel
    return pl.pallas_call(
        functools.partial(gradient_kernel, share, step),
        in_specs=[scalars(), vmem(), vmem(), hbm()],
        out_shape=jax.ShapeDtypeStruct((BLOCK_ATOMS, share * L + LANES), jnp.bfloat16),
        scratch_shapes=[
            pltpu.VMEM((share_rows, span + LANES), jnp.float32),
            pltpu.VMEM((BLOCK_ATOMS, LANES + span), jnp.float32),
            pltpu.VMEM((ROWS * share_rows, span), jnp.bfloat16),
            pltpu.VMEM((COARSE * BLOCK_ATOMS, span), jnp.bfloat16),
            pltpu.VMEM((BLOCK_ATOMS, share * L), jnp.float32),
            pltpu.SemaphoreType.DMA,
        ],
        compiler_params=pltpu.CompilerParams(vmem_limit_bytes=VMEM_BYTES),
        name="gradient",
    )(plan, source[None, :], blocks, far(dictionary))


def gather_steps(peers):
    bits = [1 << i for i in range(peers.bit_length() - 2, 0, -1)]
    steps = []
    for first in range(0, len(bits), 2):
        pair = bits[first : first + 2]
        steps.append(pair + [sum(pair)] if len(pair) == 2 else pair)
    return steps


def gather_slots(peers):
    flips = [0]
    for masks in gather_steps(peers):
        flips = [f ^ m for m in [0] + masks for f in flips]
    return flips


def gather_pieces(piece, before_last):
    peers = lax.axis_size("tm")

    def exchanged(shard, mask):
        return lax.ppermute(shard, "tm", [(i, i ^ mask) for i in range(peers)])

    held = piece[None]
    for masks in gather_steps(peers):
        held = jnp.concatenate([held] + [exchanged(held, mask) for mask in masks], axis=0)
    ready, _ = lax.optimization_barrier((held, before_last))
    return held, exchanged(ready, 1)


def recall_kernel(step, plan_ref, dict_hbm, piece_ref, old_ref, mean_ref, sem):
    del piece_ref
    first_row = first_row_of(plan_ref, step)
    fetch = pltpu.make_async_copy(dict_hbm.at[pl.ds(first_row, BLOCK_ATOMS)], old_ref, sem)
    fetch.start()
    fetch.wait()
    width = 9 * LANES if old_ref.shape[1] % (9 * LANES) == 0 else LANES

    def add(step, square):
        before = old_ref[:, pl.ds(pl.multiple_of(step * width, LANES), width)]
        return square + before * before

    square = lax.fori_loop(
        0, old_ref.shape[1] // width, add, jnp.zeros((BLOCK_ATOMS, width), jnp.float32)
    )
    mean_sq = jnp.sum(square, axis=1, keepdims=True) / (C * L) + tiny_eps
    mean_ref[...] = jnp.broadcast_to(mean_sq, mean_ref.shape)


def recall(plan, step, dictionary, piece):
    return pl.pallas_call(
        functools.partial(recall_kernel, step),
        in_specs=[scalars(), hbm(), pl.BlockSpec(memory_space=pl.ANY)],
        out_specs=[vmem(), vmem()],
        out_shape=[
            pltpu.VMEM((BLOCK_ATOMS, dictionary.shape[1]), jnp.float32),
            jax.ShapeDtypeStruct((BLOCK_ATOMS, LANES), jnp.float32),
        ],
        scratch_shapes=[pltpu.SemaphoreType.DMA],
        compiler_params=pltpu.CompilerParams(vmem_limit_bytes=VMEM_BYTES),
        name="recall",
    )(plan, far(dictionary), piece)


def renew_kernel(plan_step, plan_ref, held_ref, came_ref, old, mean_ref, dict_hbm, out_hbm, atoms_ref, grad, sems):
    del dict_hbm
    me = lax.axis_index("tm")
    first_row = first_row_of(plan_ref, plan_step)
    half, _, wide = held_ref.shape
    width = wide - LANES
    entries = C * L
    shares = []
    for slot, flips in enumerate(gather_slots(2 * half)):
        for source, extra in ((held_ref, 0), (came_ref, 1)):
            owner = me ^ (flips + extra)
            shares.append((source.at[slot], pl.ds(pl.multiple_of(owner * width, LANES), width)))
    zeros = jnp.zeros((BLOCK_ATOMS, width), jnp.float32)
    dot = zeros
    for source, column in shares:
        before = old[:, column]
        along = jnp.sum(source[:, width:].astype(jnp.float32), axis=1, keepdims=True)
        value = source[:, :width].astype(jnp.float32) + along * before
        grad[:, column] = value
        dot += value * before
    mean_sq = mean_ref[:, :1]
    along = jnp.sum(dot, axis=1, keepdims=True) / entries / mean_sq
    square = zeros
    for _, column in shares:
        value = grad[:, column] - along * old[:, column]
        grad[:, column] = value
        square += value * value
    spread = jnp.sum(square, axis=1, keepdims=True) / entries + tiny_eps
    step = move_rate / jnp.sqrt(spread)
    norm = 1.0 / jnp.sqrt(mean_sq + 0.25)
    stores = []
    for index, (_, column) in enumerate(shares):
        atoms_ref[:, column] = (old[:, column] + step * grad[:, column]) * norm
        stores.append(
            pltpu.make_async_copy(
                atoms_ref.at[:, column],
                out_hbm.at[pl.ds(first_row, BLOCK_ATOMS), column],
                sems.at[index],
            )
        )
        stores[-1].start()
    for store in stores:
        store.wait()


def renew(plan, step, held, came, old, mean_sq, dictionary):
    entries = dictionary.shape[1]
    last = step + 1 == OUTER
    return pl.pallas_call(
        functools.partial(renew_kernel, step),
        in_specs=[scalars()] + [vmem()] * 4 + [hbm()],
        out_specs=[hbm()] + [vmem()] * (1 - last),
        out_shape=[pltpu.HBM(dictionary.shape, jnp.float32)]
        + [pltpu.VMEM((BLOCK_ATOMS, entries), jnp.float32)] * (1 - last),
        scratch_shapes=[pltpu.VMEM((BLOCK_ATOMS, entries), jnp.float32)] * (1 + last)
        + [
            pltpu.SemaphoreType.DMA((2 * held.shape[0],)),
        ],
        input_output_aliases={5: 0},
        compiler_params=pltpu.CompilerParams(vmem_limit_bytes=VMEM_BYTES),
        name="renew",
    )(plan, held, came, resident(old), mean_sq, far(dictionary))


def whole_channels(signal, codes_init, dictionary_init, threshold, plan):
    channels, segment = signal.shape
    peers = lax.axis_size("tm")
    limit = threshold[None, :]
    def swaps(edges):
        ends = [range(first, peers - 1, 2) for first in (0, 1)]
        pairs = [[p for i in end for p in ((i, i + 1), (i + 1, i))] for end in ends]
        return [lax.ppermute(edge, "tm", pair) for edge, pair in zip(edges, pairs)]

    state, signal, *edges = begin(codes_init, signal)
    following = swaps(edges)
    swapped = following
    taps = layout(dictionary_init, channels)
    atoms = dictionary = None
    for step in range(OUTER):
        for inner in range(INNER + 1):
            ferry = None
            if step == 0:
                ferry = (dictionary_init, dictionary, sum(COPIED[:inner]), COPIED[inner])
            if inner == INNER:
                payload, *finals = finish(plan, step, state, swapped, signal, taps, ferry, peers)
                if ferry:
                    *finals, dictionary = finals
                break
            fresh = atoms if inner == 0 else None
            state, *results = iterate(
                plan, step, limit, state, swapped, signal, following, taps, fresh, ferry, peers
            )
            swapped = swaps(results[:2])
            if fresh is not None:
                taps = results[2]
            if ferry:
                dictionary = results[-1]
        blocks = lax.all_to_all(payload, "tm", 0, 0, tiled=True)
        piece = share_gradient(plan, step, blocks, dictionary, channels // peers)
        old, mean_sq = recall(plan, step, dictionary, piece)
        held, came = gather_pieces(piece, old)
        dictionary, *renewed = renew(plan, step, held, came, old, mean_sq, dictionary)
        atoms = renewed[0] if renewed else None
    residual, codes = finals
    return codes, dictionary, residual


def renew_atoms(old_atoms, across, mean_sq, spread):
    return (old_atoms + move_rate * across / jnp.sqrt(spread)[:, None]) / jnp.sqrt(mean_sq + 0.25)[
        :, None
    ]


def split_channels(signal, codes_init, dictionary_init, threshold, plan):
    segment = signal.shape[1]
    local_chan = signal.shape[0]
    unit_scale = (C * L) ** (-0.5)
    entries = C * L
    limit = threshold[:, None]

    def convolve(atom_cube, code_low):
        code_edge = shifted(code_low[:, segment - (L - 1) :], "tm", 1)
        extended = jnp.concatenate([code_edge, code_low], axis=1)
        lagged = jnp.stack(
            [extended[:, L - 1 - offset : L - 1 - offset + segment] for offset in range(L)], axis=1
        )
        return unit_scale * jnp.einsum(
            "kcl,klt->ct", atom_cube, lagged, preferred_element_type=jnp.float32
        )

    def resid_columns(resid_low):
        resid_edge = shifted(resid_low[:, : L - 1], "tm", -1)
        extended = jnp.concatenate([resid_low, resid_edge], axis=1)
        lagged = jnp.stack([extended[:, offset : offset + segment] for offset in range(L)], axis=1)
        return lagged.reshape(local_chan * L, segment)

    code_state = codes_init
    dictionary = dictionary_init
    residual = signal.astype(jnp.float32)
    for outer_step in range(OUTER):
        dict_low = dictionary.astype(jnp.bfloat16)
        atom_cube = dict_low.reshape(K, local_chan, L)
        for inner_step in range(INNER):
            code_low = code_state.astype(jnp.bfloat16)
            residual = signal.astype(jnp.float32) - convolve(atom_cube, code_low)
            lagged = resid_columns(residual.astype(jnp.bfloat16))
            partial_value = unit_scale * jnp.dot(
                dict_low, lagged, preferred_element_type=jnp.float32
            )
            scores = lax.psum(partial_value.astype(jnp.bfloat16), "chan").astype(jnp.float32)
            stepped = code_state + code_rate * scores
            code_state = stepped - jnp.clip(stepped, -limit, limit)
        code_low = code_state.astype(jnp.bfloat16)
        residual = signal.astype(jnp.float32) - convolve(atom_cube, code_low)
        lagged = resid_columns(residual.astype(jnp.bfloat16))
        first_row = plan[outer_step] * BLOCK_ATOMS
        code_block = lax.dynamic_slice_in_dim(code_low, first_row, BLOCK_ATOMS, 0)
        local_grad = lax.dot_general(
            code_block, lagged, (((1,), (1,)), ((), ())), preferred_element_type=jnp.float32
        )
        old_atoms = lax.dynamic_slice_in_dim(dictionary, first_row, BLOCK_ATOMS, 0)
        gradient = lax.psum(local_grad, "tm")
        dot_sum, square_sum = lax.psum(
            (jnp.sum(gradient * old_atoms, axis=1), jnp.sum(old_atoms * old_atoms, axis=1)), "chan"
        )
        mean_sq = square_sum / entries + tiny_eps
        along_coef = dot_sum / entries / mean_sq
        across = gradient - along_coef[:, None] * old_atoms
        spread = lax.psum(jnp.sum(across * across, axis=1), "chan") / entries + tiny_eps
        renewed = renew_atoms(old_atoms, across, mean_sq, spread)
        dictionary = lax.dynamic_update_slice_in_dim(dictionary, renewed, first_row, 0)
    return (code_state, dictionary, residual)


def shards(signal, codes_init, dictionary_init, threshold, plan):
    channels, segment = signal.shape
    peers = lax.axis_size("tm")
    fits = (
        lax.axis_size("chan") == 1
        and segment % LANES == 0
        and channels % (GROUPS * ROWS) == 0
        and channels % LANES == 0
        and channels % peers == 0
        and (channels // peers * L) % LANES == 0
        and peers > 1
        and peers & (peers - 1) == 0
    )
    body = whole_channels if fits else split_channels
    return body(signal, codes_init, dictionary_init, threshold, plan)


def solution(mesh):
    placed = (P("chan", "tm"), P(None, "tm"), P(None, "chan"), P(), P())
    return jax.shard_map(
        shards,
        mesh=mesh,
        in_specs=placed,
        out_specs=(P(None, "tm"), P(None, "chan"), P("chan", "tm")),
        check_vma=False,
    )
```

```python
import functools

import jax
import jax.numpy as jnp
from jax import lax
from jax.experimental import pallas as pl
from jax.experimental.pallas import tpu as pltpu
from jax.sharding import PartitionSpec as P

C = 384
K = 128
L = 96
BLOCK_ATOMS = 16
INNER = 2
OUTER = 2

code_rate = 0.3
move_rate = 0.5
tiny_eps = 1e-06

ROWS = 16
COARSE = L // ROWS
STRIDE = L + 1
GROUPS = 4
SUBLANES = 8
COPIED = (16, 24, 16, 48, 24, 0)
FINE = 4
LANES = 128
VMEM_BYTES = 24 * 1024 * 1024

NN = (((1,), (0,)), ((), ()))
NT = (((1,), (1,)), ((), ()))


def shifted(shard, axis, by):
    peers = lax.axis_size(axis)
    pairs = [(i, i + by) for i in range(peers) if 0 <= i + by < peers]
    return lax.ppermute(shard, axis, pairs)


def resident(value):
    return pltpu.with_memory_space_constraint(value, pltpu.VMEM)


def far(value):
    return pltpu.with_memory_space_constraint(value, pltpu.HBM)


def hbm():
    return pl.BlockSpec(memory_space=pltpu.HBM)


def scalars():
    return pl.BlockSpec(memory_space=pltpu.SMEM)


def first_row_of(plan_ref, step):
    return pl.multiple_of(plan_ref[step] * BLOCK_ATOMS, BLOCK_ATOMS)


def vmem():
    return pl.BlockSpec(memory_space=pltpu.VMEM)


def turn(columns, turned_ref):
    side = 2 * LANES
    row = lax.broadcasted_iota(jnp.int32, (side, side), 0)
    column = lax.broadcasted_iota(jnp.int32, (side, side), 1)
    identity = (row == column).astype(jnp.float32).astype(jnp.bfloat16)

    def put(entry, rows):
        end = entry + rows.shape[0]
        begin = entry
        while begin < end:
            channel, tap = begin // L, begin % L
            count = min(end - begin, L - tap)
            target = channel * STRIDE + tap
            turned_ref[target : target + count, :] = rows[begin - entry : begin - entry + count]
            begin += count

    low = columns.astype(jnp.bfloat16)
    through_matrix = ROWS * L // (6 * side) * 4 * side
    for first in range(0, through_matrix, 2 * side):
        pair = jnp.concatenate(
            [low[:, first + half * side : first + (half + 1) * side] for half in range(2)], axis=0
        )
        turned = lax.dot_general(identity, pair, NT, preferred_element_type=jnp.float32)
        for half in range(2):
            put(first + half * side, turned[:, half * K : (half + 1) * K])
    for first in range(through_matrix, ROWS * L, LANES):
        put(first, columns[:, first : first + LANES].astype(jnp.float32).T)


def tap_of(turned_ref, tap):
    return turned_ref[pl.ds(tap, ROWS, stride=STRIDE), :].astype(jnp.bfloat16)


def layout_kernel(dict_ref, taps_ref, *turned):
    def part(group):
        return dict_ref[:, group * ROWS * L : (group + 1) * ROWS * L]

    turn(part(0), turned[0])
    for group in range(GROUPS):
        if group + 1 < GROUPS:
            turn(part(group + 1), turned[group + 1])
        own = pl.ds(pl.multiple_of((pl.program_id(0) * GROUPS + group) * ROWS, ROWS), ROWS)
        for tap in range(L):
            taps_ref[tap // ROWS, tap % ROWS, own, :] = tap_of(turned[group], tap)


def layout(dictionary, channels):
    block = GROUPS * ROWS
    return pl.pallas_call(
        layout_kernel,
        grid=(channels // block,),
        in_specs=[pl.BlockSpec((K, block * L), lambda i: (0, i))],
        out_specs=vmem(),
        out_shape=pltpu.VMEM((COARSE, ROWS, channels, K), jnp.bfloat16),
        scratch_shapes=[pltpu.VMEM((ROWS * STRIDE, K), jnp.float32)] * GROUPS,
        compiler_params=pltpu.CompilerParams(vmem_limit_bytes=VMEM_BYTES),
        name="layout",
    )(far(dictionary))


class Ferry:
    def __init__(self, source, target, first, buffer, sems):
        self.steps = []
        for step in range(buffer.shape[0] // SUBLANES):
            held = buffer.at[pl.ds(step * SUBLANES, SUBLANES)]
            rows = pl.ds(first + step * SUBLANES, SUBLANES)
            fetch = pltpu.make_async_copy(source.at[rows], held, sems.at[0, step])
            store = pltpu.make_async_copy(held, target.at[rows], sems.at[1, step])
            fetch.start()
            self.steps.append((fetch, store))
        self.stored = 0

    def tick(self):
        if self.stored < len(self.steps):
            fetch, store = self.steps[self.stored]
            fetch.wait()
            store.start()
            self.stored += 1

    def close(self):
        while self.stored < len(self.steps):
            self.tick()
        for _, store in self.steps:
            store.wait()


def ferry_scratch(count, entries):
    return [
        pltpu.VMEM((count, entries), jnp.float32),
        pltpu.SemaphoreType.DMA((2, count // SUBLANES)),
    ]


def convolve(zb, begin, count, taps, zz, fine, acc, ferry):
    channels = taps.shape[2]
    tiles = channels // LANES
    rows = count + ROWS
    for coarse in range(COARSE):
        first = begin - ROWS - ROWS * coarse
        zz[:rows, coarse * K : (coarse + 1) * K] = zb[first : first + rows, :]
    for lag in range(0, ROWS, FINE):
        slot = lag // FINE % 2 * FINE
        for pair in range(0, FINE, 2):
            weights = jnp.concatenate(
                [
                    jnp.concatenate([taps[m, lag + pair + j] for m in range(COARSE)], axis=1)
                    for j in range(2)
                ],
                axis=0,
            )
            product = lax.dot_general(zz[:rows, :], weights, NT, preferred_element_type=jnp.float32)
            for j in range(2):
                for tile in range(tiles):
                    column = j * channels + tile * LANES
                    fine[slot + pair + j, tile, :rows, :] = product[:, column : column + LANES]
        if ferry:
            ferry.tick()
        for tile in range(tiles):
            total = None if lag == 0 else acc[tile, :count, :]
            for j in range(FINE):
                first = ROWS - lag - j
                part = fine[slot + j, tile, first : first + count, :]
                total = part if total is None else total + part
            acc[tile, :count, :] = total


def correlate(rb, count, taps, rr, fine, acc, ferry):
    channels = taps.shape[2]
    rows = count + ROWS
    for coarse in range(COARSE):
        first = ROWS * coarse
        rr[:rows, coarse * channels : (coarse + 1) * channels] = rb[first : first + rows, :]
    for lag in range(0, ROWS, FINE):
        slot = lag // FINE % 2 * FINE
        for pair in range(0, FINE, 2):
            weights = jnp.concatenate(
                [
                    jnp.concatenate([taps[m, lag + pair + j] for m in range(COARSE)], axis=0)
                    for j in range(2)
                ],
                axis=1,
            )
            product = lax.dot_general(rr[:rows, :], weights, NN, preferred_element_type=jnp.float32)
            for j in range(2):
                fine[slot + pair + j, 0, :rows, :] = product[:, j * K : (j + 1) * K]
        if ferry:
            ferry.tick()
        total = None if lag == 0 else acc[0, :count, :]
        for j in range(FINE):
            part = fine[slot + j, 0, lag + j : lag + j + count, :]
            total = part if total is None else total + part
        acc[0, :count, :] = total


def patch_taps(row, atoms_ref, taps, columns, turned):
    channels = taps.shape[2]
    lane = lax.broadcasted_iota(jnp.int32, (ROWS, K), 1)
    kept = (lane < row) | (lane >= row + BLOCK_ATOMS)
    keep = kept.astype(jnp.float32).astype(jnp.bfloat16)
    columns[...] = jnp.zeros_like(columns)
    width = ROWS * L

    def patch(step, carry):
        part = pl.ds(pl.multiple_of(step * (GROUPS * width), LANES), GROUPS * width)
        columns[pl.ds(row, BLOCK_ATOMS), :] = atoms_ref[:, part].astype(jnp.bfloat16)
        turn(columns[:, :width], turned[0])
        for group in range(GROUPS):
            if group + 1 < GROUPS:
                turn(columns[:, (group + 1) * width : (group + 2) * width], turned[group + 1])
            own = pl.ds(pl.multiple_of((step * GROUPS + group) * ROWS, ROWS), ROWS)
            for tap in range(L):
                before = taps[tap // ROWS, tap % ROWS, own, :]
                taps[tap // ROWS, tap % ROWS, own, :] = before * keep + tap_of(turned[group], tap)
        return carry

    lax.fori_loop(0, channels // (GROUPS * ROWS), patch, 0)


def put_edges(edge_refs, values):
    even = lax.axis_index("tm") % 2 == 0

    def put(first, second):
        first[...] = values[-L:]
        second[...] = values[:L]

    pl.when(even)(lambda: put(*edge_refs))
    pl.when(jnp.logical_not(even))(lambda: put(*edge_refs[::-1]))


def begin_kernel(code_hbm, signal_hbm, state_out, signal_out, first_out, second_out, code_ref, signal_ref, sems):
    fetches = [
        pltpu.make_async_copy(code_hbm, code_ref, sems.at[0]),
        pltpu.make_async_copy(signal_hbm, signal_ref, sems.at[1]),
    ]
    for fetch in fetches:
        fetch.start()
    for fetch in fetches:
        fetch.wait()
    state = code_ref[...].T
    signal = signal_ref[...].astype(jnp.float32).T.astype(jnp.bfloat16)
    state_out[...] = state
    signal_out[...] = signal
    put_edges((first_out, second_out), jnp.concatenate([state.astype(jnp.bfloat16), signal], axis=1))


def begin(code, signal):
    channels, segment = signal.shape
    return pl.pallas_call(
        begin_kernel,
        in_specs=[hbm()] * 2,
        out_specs=[vmem()] * 4,
        out_shape=[
            pltpu.VMEM((segment, K), jnp.float32),
            pltpu.VMEM((segment, channels), jnp.bfloat16),
        ]
        + [jax.ShapeDtypeStruct((L, K + channels), jnp.bfloat16)] * 2,
        scratch_shapes=[
            pltpu.VMEM(code.shape, code.dtype),
            pltpu.VMEM(signal.shape, signal.dtype),
            pltpu.SemaphoreType.DMA((2,)),
        ],
        compiler_params=pltpu.CompilerParams(vmem_limit_bytes=VMEM_BYTES),
        name="begin",
    )(far(code), far(signal))


def put_codes(zb, state_ref, first_ref, second_ref):
    segment = state_ref.shape[0]
    even = lax.axis_index("tm") % 2 == 0
    zb[L : L + segment, :] = state_ref[...].astype(jnp.bfloat16)

    def put(left, right):
        zb[:L, :] = left[:, :K]
        if zb.shape[0] > L + segment:
            zb[L + segment :, :] = right[:, :K]

    pl.when(even)(lambda: put(second_ref, first_ref))
    pl.when(jnp.logical_not(even))(lambda: put(first_ref, second_ref))


def iterate_kernel(total_time, patching, copied, plan_ref, limit_ref, *refs):
    refs = list(refs)

    def take(count):
        taken = refs[:count]
        del refs[:count]
        return taken

    state_ref, first_ref, second_ref, signal_ref, next_first, next_second = take(6)
    atoms = take(1 if patching else 0)
    (taps,) = take(1)
    source = take(1 if copied else 0)
    take(1 if copied and copied[0] else 0)
    state_out, *edges = take(3)
    taps = (take(1) if patching else [taps])[0]
    target = take(1 if copied else 0)
    zb, rb, zz, rr, fine, acc, beyond = take(7)
    ferry = Ferry(source[0], target[0], copied[0], *take(2)) if copied else None
    segment, channels = signal_ref.shape
    tiles = channels // LANES
    scale = (C * L) ** (-0.5)
    me = lax.axis_index("tm")
    even = me % 2 == 0
    put_codes(zb, state_ref, first_ref, second_ref)

    def put(following):
        beyond[...] = following[:, K:]

    pl.when(even)(lambda: put(next_first))
    pl.when(jnp.logical_not(even))(lambda: put(next_second))
    if patching:
        columns, *turned = refs
        patch_taps(first_row_of(plan_ref, patching - 1), atoms[0], taps, columns, turned)
    reach = segment + L
    convolve(zb, L, reach, taps, zz, fine, acc, ferry)
    moment = me * segment + lax.broadcasted_iota(jnp.int32, (reach, LANES), 0)
    inside = moment < total_time
    for tile in range(tiles):
        column = slice(tile * LANES, (tile + 1) * LANES)
        signal = jnp.concatenate([signal_ref[:, column], beyond[:, column]], axis=0)
        value = signal.astype(jnp.float32) - scale * acc[tile, :reach, :]
        rb[:, column] = jnp.where(inside, value, 0.0).astype(jnp.bfloat16)
    correlate(rb, segment, taps, rr, fine, acc, ferry)
    limit = limit_ref[...]
    stepped = state_ref[...] + code_rate * (scale * acc[0, :segment, :])
    state = stepped - jnp.clip(stepped, -limit, limit)
    state_out[...] = state
    put_edges(edges, state.astype(jnp.bfloat16))
    if ferry:
        ferry.close()


def iterate(plan, step, limit, state, swapped, signal, following, taps, atoms, ferry, peers):
    segment, channels = signal.shape
    patching = atoms is not None
    reach = segment + L
    carried = [far(value) for value in (ferry or ())[:2] if value is not None]
    aliases = {9: 3} if patching else {}
    if len(carried) == 2:
        aliases[10 + patching] = 3 + patching
    return pl.pallas_call(
        functools.partial(
            iterate_kernel, peers * segment, step if patching else 0, ferry[2:] if ferry else None
        ),
        in_specs=[scalars()] + [vmem()] * (8 + patching) + [hbm()] * len(carried),
        out_specs=[vmem()] * (3 + patching) + [hbm()] * (ferry is not None),
        out_shape=[pltpu.VMEM((segment, K), jnp.float32)]
        + [jax.ShapeDtypeStruct((L, K), jnp.bfloat16)] * 2
        + [pltpu.VMEM(taps.shape, jnp.bfloat16)] * patching
        + ([pltpu.HBM(ferry[0].shape, jnp.float32)] if ferry else []),
        scratch_shapes=[
            pltpu.VMEM((L + reach, K), jnp.bfloat16),
            pltpu.VMEM((reach, channels), jnp.bfloat16),
            pltpu.VMEM((reach + ROWS, COARSE * K), jnp.bfloat16),
            pltpu.VMEM((segment + ROWS, COARSE * channels), jnp.bfloat16),
            pltpu.VMEM((2 * FINE, channels // LANES, reach + ROWS, LANES), jnp.float32),
            pltpu.VMEM((channels // LANES, reach, LANES), jnp.float32),
            pltpu.VMEM((L, channels), jnp.bfloat16),
        ]
        + (ferry_scratch(ferry[3], ferry[0].shape[1]) if ferry else [])
        + (
            [pltpu.VMEM((K, GROUPS * ROWS * L), jnp.bfloat16)]
            + [pltpu.VMEM((ROWS * STRIDE, K), jnp.float32)] * GROUPS
        )
        * patching,
        input_output_aliases=aliases,
        compiler_params=pltpu.CompilerParams(vmem_limit_bytes=VMEM_BYTES),
        name="iterate",
    )(
        plan,
        limit,
        resident(state),
        *swapped,
        resident(signal),
        *following,
        *([resident(atoms)] if patching else []),
        resident(taps),
        *carried,
    )


def finish_kernel(
    peers, step, copied, plan_ref, state_ref, first_ref, second_ref, signal_ref, taps, *refs
):
    refs = list(refs)

    def take(count):
        taken = refs[:count]
        del refs[:count]
        return taken

    last = step + 1 == OUTER
    source = take(2 if copied else 0)
    (payload_out,) = take(1)
    outs = take(2 if last else 0)
    target = take(1 if copied else 0)
    zb, zz, fine, acc, tall = take(5)
    ferry = Ferry(source[0], target[0], copied[0], *take(2)) if copied else None
    resid_out, codes_out = outs if last else (None, *refs)
    segment, channels = signal_ref.shape
    scale = (C * L) ** (-0.5)
    put_codes(zb, state_ref, first_ref, second_ref)
    codes_out[...] = state_ref[...].T
    convolve(zb, L, segment, taps, zz, fine, acc, ferry)
    for tile in range(channels // LANES):
        column = slice(tile * LANES, (tile + 1) * LANES)
        value = signal_ref[:, column].astype(jnp.float32) - scale * acc[tile, :segment, :]
        value = value.T
        tall[column, :] = value
        if last:
            resid_out[column, :] = value
    block = codes_out[pl.ds(first_row_of(plan_ref, step), BLOCK_ATOMS), :].astype(jnp.bfloat16)
    share = channels // peers
    share_rows = payload_out.shape[1] - BLOCK_ATOMS
    tall[channels:, :] = jnp.zeros((tall.shape[0] - channels, segment), jnp.float32)
    for peer in range(peers):
        part = tall[peer * share : peer * share + share_rows, :]
        payload_out[peer, :share_rows, :] = part.astype(jnp.bfloat16)
        payload_out[peer, share_rows:, :] = block
    if ferry:
        ferry.close()


def finish(plan, step, state, swapped, signal, taps, ferry, peers):
    segment, channels = signal.shape
    share = channels // peers
    share_rows = -(-share // ROWS) * ROWS
    last = step + 1 == OUTER
    carried = [far(value) for value in (ferry or ())[:2]]
    return pl.pallas_call(
        functools.partial(finish_kernel, peers, step, ferry[2:] if ferry else None),
        in_specs=[scalars()] + [vmem()] * 5 + [hbm()] * len(carried),
        out_specs=[vmem()] * (3 if last else 1) + [hbm()] * (len(carried) // 2),
        out_shape=[
            jax.ShapeDtypeStruct((peers, share_rows + BLOCK_ATOMS, segment), jnp.bfloat16),
            pltpu.VMEM((channels, segment), jnp.float32),
            pltpu.VMEM((K, segment), jnp.float32),
        ][: 3 if last else 1]
        + [pltpu.HBM(value.shape, jnp.float32) for value in carried[1:]],
        scratch_shapes=[
            pltpu.VMEM((L + segment, K), jnp.bfloat16),
            pltpu.VMEM((segment + ROWS, COARSE * K), jnp.bfloat16),
            pltpu.VMEM((2 * FINE, channels // LANES, segment + ROWS, LANES), jnp.float32),
            pltpu.VMEM((channels // LANES, segment, LANES), jnp.float32),
            pltpu.VMEM((channels + ROWS, segment), jnp.float32),
        ]
        + (ferry_scratch(ferry[3], ferry[0].shape[1]) if ferry else [])
        + ([] if last else [pltpu.VMEM((K, segment), jnp.float32)]),
        input_output_aliases={7: 3 if last else 1} if carried else {},
        compiler_params=pltpu.CompilerParams(vmem_limit_bytes=VMEM_BYTES),
        name="finish",
    )(plan, resident(state), *swapped, resident(signal), resident(taps), *carried)


def gradient_kernel(share, step, plan_ref, blocks_ref, dict_hbm, out_ref, rf, zf, rr, zz, old, sem):
    peers, rows, segment = blocks_ref.shape
    share_rows = rows - BLOCK_ATOMS
    span = peers * segment
    entries = share * L
    rows_of = pl.ds(first_row_of(plan_ref, step), BLOCK_ATOMS)
    columns_of = pl.ds(pl.multiple_of(lax.axis_index("tm") * entries, LANES), entries)
    fetch = pltpu.make_async_copy(dict_hbm.at[rows_of, columns_of], old, sem)
    fetch.start()
    rf[:, span:] = jnp.zeros((share_rows, LANES), jnp.float32)
    zf[:, :LANES] = jnp.zeros((BLOCK_ATOMS, LANES), jnp.float32)
    for peer in range(peers):
        column = peer * segment
        rf[:, column : column + segment] = blocks_ref[peer, :share_rows, :].astype(jnp.float32)
        zf[:, LANES + column : LANES + column + segment] = blocks_ref[peer, share_rows:, :].astype(
            jnp.float32
        )
    for lag in range(ROWS):
        rr[lag * share_rows : (lag + 1) * share_rows, :] = rf[:, lag : lag + span].astype(jnp.bfloat16)
    for coarse in range(COARSE):
        begin = LANES - ROWS * coarse
        zz[coarse * BLOCK_ATOMS : (coarse + 1) * BLOCK_ATOMS, :] = zf[:, begin : begin + span].astype(
            jnp.bfloat16
        )
    lagged = lax.dot_general(zz[...], rr[...], NT, preferred_element_type=jnp.float32)
    wide = ROWS * share_rows
    parts = []
    left = lagged
    for _ in range(3):
        parts.append(left.astype(jnp.bfloat16))
        left = left - parts[-1].astype(jnp.float32)
    row = lax.broadcasted_iota(jnp.int32, (wide, wide), 0)
    column = lax.broadcasted_iota(jnp.int32, (wide, wide), 1)
    chosen = (row // share_rows == column % ROWS) & (row % share_rows == column // ROWS)
    chosen = chosen.astype(jnp.float32).astype(jnp.bfloat16)
    by_channel = lax.dot_general(
        jnp.concatenate(parts, axis=0), chosen, NN, preferred_element_type=jnp.float32
    )
    count = COARSE * BLOCK_ATOMS
    by_channel = by_channel[:count] + by_channel[count : 2 * count] + by_channel[2 * count :]
    lane = lax.broadcasted_iota(jnp.int32, (BLOCK_ATOMS, LANES), 1)
    tiles = []
    for tile in range(entries // LANES):
        total = jnp.zeros((BLOCK_ATOMS, LANES), jnp.float32)
        for place in range(LANES // ROWS):
            channel, coarse = divmod(tile * (LANES // ROWS) + place, COARSE)
            first = channel * ROWS // LANES * LANES
            source = by_channel[coarse * BLOCK_ATOMS : (coarse + 1) * BLOCK_ATOMS, first : first + LANES]
            by = (place * ROWS - channel * ROWS) % LANES
            moved = pltpu.roll(source, by, 1) if by else source
            total = jnp.where(lane // ROWS == place, moved, total)
        tiles.append(total)
    gradient = jnp.concatenate(tiles, axis=1)
    fetch.wait()
    before = old[...]
    square = jnp.sum(before * before, axis=1, keepdims=True)
    along = jnp.sum(gradient * before, axis=1, keepdims=True) / (square + tiny_eps)
    out_ref[:, :entries] = (gradient - along * before).astype(jnp.bfloat16)
    terms = jnp.zeros((BLOCK_ATOMS, LANES), jnp.float32)
    for i in range(3):
        term = along.astype(jnp.bfloat16).astype(jnp.float32)
        along = along - term
        terms = jnp.where(lane == i, term, terms)
    out_ref[:, entries:] = terms.astype(jnp.bfloat16)


def share_gradient(plan, step, blocks, dictionary, share):
    peers, rows, segment = blocks.shape
    share_rows = rows - BLOCK_ATOMS
    span = peers * segment
    return pl.pallas_call(
        functools.partial(gradient_kernel, share, step),
        in_specs=[scalars(), vmem(), hbm()],
        out_shape=jax.ShapeDtypeStruct((BLOCK_ATOMS, share * L + LANES), jnp.bfloat16),
        scratch_shapes=[
            pltpu.VMEM((share_rows, span + LANES), jnp.float32),
            pltpu.VMEM((BLOCK_ATOMS, LANES + span), jnp.float32),
            pltpu.VMEM((ROWS * share_rows, span), jnp.bfloat16),
            pltpu.VMEM((COARSE * BLOCK_ATOMS, span), jnp.bfloat16),
            pltpu.VMEM((BLOCK_ATOMS, share * L), jnp.float32),
            pltpu.SemaphoreType.DMA,
        ],
        compiler_params=pltpu.CompilerParams(vmem_limit_bytes=VMEM_BYTES),
        name="gradient",
    )(plan, blocks, far(dictionary))


def gather_steps(peers):
    bits = [1 << i for i in range(peers.bit_length() - 2, 0, -1)]
    steps = []
    for first in range(0, len(bits), 2):
        pair = bits[first : first + 2]
        steps.append(pair + [sum(pair)] if len(pair) == 2 else pair)
    return steps


def gather_slots(peers):
    flips = [0]
    for masks in gather_steps(peers):
        flips = [f ^ m for m in [0] + masks for f in flips]
    return flips


def gather_pieces(piece, meanwhile):
    peers = lax.axis_size("tm")

    def exchanged(shard, mask):
        return lax.ppermute(shard, "tm", [(i, i ^ mask) for i in range(peers)])

    held = piece[None]
    beside = None
    for masks in gather_steps(peers):
        held = jnp.concatenate([held] + [exchanged(held, mask) for mask in masks], axis=0)
        if beside is None:
            beside = meanwhile(held)
    ready, _ = lax.optimization_barrier((held, beside))
    return held, exchanged(ready, 1)


def recall_kernel(step, plan_ref, dict_hbm, piece_ref, old_ref, mean_ref, sem):
    del piece_ref
    first_row = first_row_of(plan_ref, step)
    fetch = pltpu.make_async_copy(dict_hbm.at[pl.ds(first_row, BLOCK_ATOMS)], old_ref, sem)
    fetch.start()
    fetch.wait()
    width = 9 * LANES if old_ref.shape[1] % (9 * LANES) == 0 else LANES

    def add(step, square):
        before = old_ref[:, pl.ds(pl.multiple_of(step * width, LANES), width)]
        return square + before * before

    square = lax.fori_loop(
        0, old_ref.shape[1] // width, add, jnp.zeros((BLOCK_ATOMS, width), jnp.float32)
    )
    mean_sq = jnp.sum(square, axis=1, keepdims=True) / (C * L) + tiny_eps
    mean_ref[...] = jnp.broadcast_to(mean_sq, mean_ref.shape)


def recall(plan, step, dictionary, piece):
    return pl.pallas_call(
        functools.partial(recall_kernel, step),
        in_specs=[scalars(), hbm(), pl.BlockSpec(memory_space=pl.ANY)],
        out_specs=[vmem(), vmem()],
        out_shape=[
            pltpu.VMEM((BLOCK_ATOMS, dictionary.shape[1]), jnp.float32),
            jax.ShapeDtypeStruct((BLOCK_ATOMS, LANES), jnp.float32),
        ],
        scratch_shapes=[pltpu.SemaphoreType.DMA],
        compiler_params=pltpu.CompilerParams(vmem_limit_bytes=VMEM_BYTES),
        name="recall",
    )(plan, far(dictionary), piece)


def renew_kernel(plan_step, earlier, plan_ref, held_ref, came_ref, old, mean_ref, *refs):
    me = lax.axis_index("tm")
    half, _, wide = held_ref.shape
    width = wide - LANES
    entries = C * L
    before_refs, refs = refs[:earlier], refs[earlier:]
    last = plan_step + 1 == OUTER
    if last:
        _, out_hbm, atoms_ref, grad, sems = refs
    else:
        atoms_ref, grad = refs

    def rows_of(step):
        return pl.ds(first_row_of(plan_ref, step), BLOCK_ATOMS)

    stores = []
    for step in range(earlier):
        stores.append(
            pltpu.make_async_copy(before_refs[step], out_hbm.at[rows_of(step)], sems.at[2 * half + step])
        )
        stores[-1].start()
    shares = []
    for slot, flips in enumerate(gather_slots(2 * half)):
        for source, extra in ((held_ref, 0), (came_ref, 1)):
            owner = me ^ (flips + extra)
            shares.append((source.at[slot], pl.ds(pl.multiple_of(owner * width, LANES), width)))
    zeros = jnp.zeros((BLOCK_ATOMS, width), jnp.float32)
    dot = zeros
    for source, column in shares:
        before = old[:, column]
        along = jnp.sum(source[:, width:].astype(jnp.float32), axis=1, keepdims=True)
        value = source[:, :width].astype(jnp.float32) + along * before
        grad[:, column] = value
        dot += value * before
    mean_sq = mean_ref[:, :1]
    along = jnp.sum(dot, axis=1, keepdims=True) / entries / mean_sq
    square = zeros
    for _, column in shares:
        value = grad[:, column] - along * old[:, column]
        square += value * value
    spread = jnp.sum(square, axis=1, keepdims=True) / entries + tiny_eps
    step = move_rate / jnp.sqrt(spread)
    norm = 1.0 / jnp.sqrt(mean_sq + 0.25)
    for index, (_, column) in enumerate(shares):
        before = old[:, column]
        across = grad[:, column] - along * before
        atoms_ref[:, column] = (before + step * across) * norm
        if last:
            stores.append(
                pltpu.make_async_copy(
                    atoms_ref.at[:, column], out_hbm.at[rows_of(plan_step), column], sems.at[index]
                )
            )
            stores[-1].start()
    for store in stores:
        store.wait()


def renew(plan, step, held, came, old, mean_sq, renewed, dictionary):
    last = step + 1 == OUTER
    atoms = (BLOCK_ATOMS, old.shape[1])
    earlier = len(renewed) if last else 0
    scratch = [pltpu.VMEM(atoms, jnp.float32)]
    if last:
        scratch = scratch * 2 + [pltpu.SemaphoreType.DMA((2 * held.shape[0] + earlier,))]
    return pl.pallas_call(
        functools.partial(renew_kernel, step, earlier),
        in_specs=[scalars()] + [vmem()] * (4 + earlier) + [hbm()] * last,
        out_specs=hbm() if last else vmem(),
        out_shape=pltpu.HBM(dictionary.shape, jnp.float32) if last else pltpu.VMEM(atoms, jnp.float32),
        scratch_shapes=scratch,
        input_output_aliases={5 + earlier: 0} if last else {},
        compiler_params=pltpu.CompilerParams(vmem_limit_bytes=VMEM_BYTES),
        name="renew",
    )(
        plan,
        held,
        came,
        resident(old),
        mean_sq,
        *([resident(value) for value in renewed] + [far(dictionary)] if last else []),
    )


def whole_channels(signal, codes_init, dictionary_init, threshold, plan):
    channels, segment = signal.shape
    peers = lax.axis_size("tm")
    limit = threshold[None, :]
    def swaps(edges):
        ends = [range(first, peers - 1, 2) for first in (0, 1)]
        pairs = [[p for i in end for p in ((i, i + 1), (i + 1, i))] for end in ends]
        return [lax.ppermute(edge, "tm", pair) for edge, pair in zip(edges, pairs)]

    state, signal, *edges = begin(codes_init, signal)
    following = swaps(edges)
    swapped = following
    taps = layout(dictionary_init, channels)
    dictionary = None
    renewed = []
    for step in range(OUTER):
        for inner in range(INNER + 1):
            turn_index = step * (INNER + 1) + inner
            ferry = None
            if COPIED[turn_index]:
                first = sum(COPIED[:turn_index])
                ferry = (dictionary_init, dictionary, first, COPIED[turn_index])
            if inner == INNER:
                payload, *finals = finish(plan, step, state, swapped, signal, taps, ferry, peers)
                if ferry:
                    *finals, dictionary = finals
                break
            fresh = renewed[-1] if inner == 0 and step else None
            state, *results = iterate(
                plan, step, limit, state, swapped, signal, following, taps, fresh, ferry, peers
            )
            swapped = swaps(results[:2])
            if fresh is not None:
                taps = results[2]
            if ferry:
                dictionary = results[-1]
        blocks = lax.all_to_all(payload, "tm", 0, 0, tiled=True)
        piece = share_gradient(plan, step, blocks, dictionary_init, channels // peers)
        recalled = []

        def recall_beside(held):
            recalled.extend(recall(plan, step, dictionary_init, held))
            return recalled[0]

        held, came = gather_pieces(piece, recall_beside)
        last = step + 1 == OUTER
        result = renew(plan, step, held, came, *recalled, renewed if last else None, dictionary)
        if last:
            dictionary = result
        else:
            renewed.append(result)
    residual, codes = finals
    return codes, dictionary, residual


def renew_atoms(old_atoms, across, mean_sq, spread):
    return (old_atoms + move_rate * across / jnp.sqrt(spread)[:, None]) / jnp.sqrt(mean_sq + 0.25)[
        :, None
    ]


def split_channels(signal, codes_init, dictionary_init, threshold, plan):
    segment = signal.shape[1]
    local_chan = signal.shape[0]
    unit_scale = (C * L) ** (-0.5)
    entries = C * L
    limit = threshold[:, None]

    def convolve(atom_cube, code_low):
        code_edge = shifted(code_low[:, segment - (L - 1) :], "tm", 1)
        extended = jnp.concatenate([code_edge, code_low], axis=1)
        lagged = jnp.stack(
            [extended[:, L - 1 - offset : L - 1 - offset + segment] for offset in range(L)], axis=1
        )
        return unit_scale * jnp.einsum(
            "kcl,klt->ct", atom_cube, lagged, preferred_element_type=jnp.float32
        )

    def resid_columns(resid_low):
        resid_edge = shifted(resid_low[:, : L - 1], "tm", -1)
        extended = jnp.concatenate([resid_low, resid_edge], axis=1)
        lagged = jnp.stack([extended[:, offset : offset + segment] for offset in range(L)], axis=1)
        return lagged.reshape(local_chan * L, segment)

    code_state = codes_init
    dictionary = dictionary_init
    residual = signal.astype(jnp.float32)
    for outer_step in range(OUTER):
        dict_low = dictionary.astype(jnp.bfloat16)
        atom_cube = dict_low.reshape(K, local_chan, L)
        for inner_step in range(INNER):
            code_low = code_state.astype(jnp.bfloat16)
            residual = signal.astype(jnp.float32) - convolve(atom_cube, code_low)
            lagged = resid_columns(residual.astype(jnp.bfloat16))
            partial_value = unit_scale * jnp.dot(
                dict_low, lagged, preferred_element_type=jnp.float32
            )
            scores = lax.psum(partial_value.astype(jnp.bfloat16), "chan").astype(jnp.float32)
            stepped = code_state + code_rate * scores
            code_state = stepped - jnp.clip(stepped, -limit, limit)
        code_low = code_state.astype(jnp.bfloat16)
        residual = signal.astype(jnp.float32) - convolve(atom_cube, code_low)
        lagged = resid_columns(residual.astype(jnp.bfloat16))
        first_row = plan[outer_step] * BLOCK_ATOMS
        code_block = lax.dynamic_slice_in_dim(code_low, first_row, BLOCK_ATOMS, 0)
        local_grad = lax.dot_general(
            code_block, lagged, (((1,), (1,)), ((), ())), preferred_element_type=jnp.float32
        )
        old_atoms = lax.dynamic_slice_in_dim(dictionary, first_row, BLOCK_ATOMS, 0)
        gradient = lax.psum(local_grad, "tm")
        dot_sum, square_sum = lax.psum(
            (jnp.sum(gradient * old_atoms, axis=1), jnp.sum(old_atoms * old_atoms, axis=1)), "chan"
        )
        mean_sq = square_sum / entries + tiny_eps
        along_coef = dot_sum / entries / mean_sq
        across = gradient - along_coef[:, None] * old_atoms
        spread = lax.psum(jnp.sum(across * across, axis=1), "chan") / entries + tiny_eps
        renewed = renew_atoms(old_atoms, across, mean_sq, spread)
        dictionary = lax.dynamic_update_slice_in_dim(dictionary, renewed, first_row, 0)
    return (code_state, dictionary, residual)


def shards(signal, codes_init, dictionary_init, threshold, plan):
    channels, segment = signal.shape
    peers = lax.axis_size("tm")
    fits = (
        lax.axis_size("chan") == 1
        and segment % LANES == 0
        and channels % (GROUPS * ROWS) == 0
        and channels % LANES == 0
        and channels % peers == 0
        and (channels // peers * L) % LANES == 0
        and peers > 2
        and peers & (peers - 1) == 0
    )
    body = whole_channels if fits else split_channels
    return body(signal, codes_init, dictionary_init, threshold, plan)


def solution(mesh):
    placed = (P("chan", "tm"), P(None, "tm"), P(None, "chan"), P(), P())
    return jax.shard_map(
        shards,
        mesh=mesh,
        in_specs=placed,
        out_specs=(P(None, "tm"), P(None, "chan"), P("chan", "tm")),
        check_vma=False,
    )
```

```python
import functools

import jax
import jax.numpy as jnp
from jax import lax
from jax.experimental import pallas as pl
from jax.experimental.pallas import tpu as pltpu
from jax.sharding import PartitionSpec as P

C = 384
K = 128
L = 96
BLOCK_ATOMS = 16
INNER = 2
OUTER = 2

code_rate = 0.3
move_rate = 0.5
tiny_eps = 1e-06

ROWS = 16
COARSE = L // ROWS
STRIDE = L + 1
GROUPS = 4
SUBLANES = 8
COPIED = (32, 40, 32, 24)
FINE = 4
LANES = 128
VMEM_BYTES = 24 * 1024 * 1024

NN = (((1,), (0,)), ((), ()))
NT = (((1,), (1,)), ((), ()))


def shifted(shard, axis, by):
    peers = lax.axis_size(axis)
    pairs = [(i, i + by) for i in range(peers) if 0 <= i + by < peers]
    return lax.ppermute(shard, axis, pairs)


def resident(value):
    return pltpu.with_memory_space_constraint(value, pltpu.VMEM)


def far(value):
    return pltpu.with_memory_space_constraint(value, pltpu.HBM)


def hbm():
    return pl.BlockSpec(memory_space=pltpu.HBM)


def scalars():
    return pl.BlockSpec(memory_space=pltpu.SMEM)


def first_row_of(plan_ref, step):
    return pl.multiple_of(plan_ref[step] * BLOCK_ATOMS, BLOCK_ATOMS)


def vmem():
    return pl.BlockSpec(memory_space=pltpu.VMEM)


def turn(columns, turned_ref):
    side = 2 * LANES
    row = lax.broadcasted_iota(jnp.int32, (side, side), 0)
    column = lax.broadcasted_iota(jnp.int32, (side, side), 1)
    identity = (row == column).astype(jnp.float32).astype(jnp.bfloat16)

    def put(entry, rows):
        end = entry + rows.shape[0]
        begin = entry
        while begin < end:
            channel, tap = begin // L, begin % L
            count = min(end - begin, L - tap)
            target = channel * STRIDE + tap
            turned_ref[target : target + count, :] = rows[begin - entry : begin - entry + count]
            begin += count

    low = columns.astype(jnp.bfloat16)
    through_matrix = ROWS * L // (6 * side) * 4 * side
    for first in range(0, through_matrix, 2 * side):
        pair = jnp.concatenate(
            [low[:, first + half * side : first + (half + 1) * side] for half in range(2)], axis=0
        )
        turned = lax.dot_general(identity, pair, NT, preferred_element_type=jnp.float32)
        for half in range(2):
            put(first + half * side, turned[:, half * K : (half + 1) * K])
    for first in range(through_matrix, ROWS * L, LANES):
        put(first, columns[:, first : first + LANES].astype(jnp.float32).T)


def tap_of(turned_ref, tap):
    return turned_ref[pl.ds(tap, ROWS, stride=STRIDE), :].astype(jnp.bfloat16)


def layout_kernel(dict_ref, taps_ref, *turned):
    def part(group):
        return dict_ref[:, group * ROWS * L : (group + 1) * ROWS * L]

    turn(part(0), turned[0])
    for group in range(GROUPS):
        if group + 1 < GROUPS:
            turn(part(group + 1), turned[group + 1])
        own = pl.ds(pl.multiple_of((pl.program_id(0) * GROUPS + group) * ROWS, ROWS), ROWS)
        for tap in range(L):
            taps_ref[tap // ROWS, tap % ROWS, own, :] = tap_of(turned[group], tap)


def layout(dictionary, channels):
    block = GROUPS * ROWS
    return pl.pallas_call(
        layout_kernel,
        grid=(channels // block,),
        in_specs=[pl.BlockSpec((K, block * L), lambda i: (0, i))],
        out_specs=vmem(),
        out_shape=pltpu.VMEM((COARSE, ROWS, channels, K), jnp.bfloat16),
        scratch_shapes=[pltpu.VMEM((ROWS * STRIDE, K), jnp.float32)] * GROUPS,
        compiler_params=pltpu.CompilerParams(vmem_limit_bytes=VMEM_BYTES),
        name="layout",
    )(far(dictionary))


class Ferry:
    def __init__(self, source, target, first, buffer, sems):
        self.steps = []
        for step in range(buffer.shape[0] // SUBLANES):
            held = buffer.at[pl.ds(step * SUBLANES, SUBLANES)]
            rows = pl.ds(first + step * SUBLANES, SUBLANES)
            fetch = pltpu.make_async_copy(source.at[rows], held, sems.at[0, step])
            store = pltpu.make_async_copy(held, target.at[rows], sems.at[1, step])
            fetch.start()
            self.steps.append((fetch, store))

    def turn_round(self):
        for fetch, store in self.steps:
            fetch.wait()
            store.start()

    def close(self):
        for _, store in self.steps:
            store.wait()


def ferry_scratch(count, entries):
    return [
        pltpu.VMEM((count, entries), jnp.float32),
        pltpu.SemaphoreType.DMA((2, count // SUBLANES)),
    ]


def convolve(zb, begin, count, taps, zz, fine, acc):
    channels = taps.shape[2]
    tiles = channels // LANES
    rows = count + ROWS
    for coarse in range(COARSE):
        first = begin - ROWS - ROWS * coarse
        zz[:rows, coarse * K : (coarse + 1) * K] = zb[first : first + rows, :]
    for lag in range(0, ROWS, FINE):
        slot = lag // FINE % 2 * FINE
        for pair in range(0, FINE, 2):
            weights = jnp.concatenate(
                [
                    jnp.concatenate([taps[m, lag + pair + j] for m in range(COARSE)], axis=1)
                    for j in range(2)
                ],
                axis=0,
            )
            product = lax.dot_general(zz[:rows, :], weights, NT, preferred_element_type=jnp.float32)
            for j in range(2):
                for tile in range(tiles):
                    column = j * channels + tile * LANES
                    fine[slot + pair + j, tile, :rows, :] = product[:, column : column + LANES]
        for tile in range(tiles):
            total = None if lag == 0 else acc[tile, :count, :]
            for j in range(FINE):
                first = ROWS - lag - j
                part = fine[slot + j, tile, first : first + count, :]
                total = part if total is None else total + part
            acc[tile, :count, :] = total


def correlate(rb, count, taps, rr, fine, acc):
    channels = taps.shape[2]
    rows = count + ROWS
    for coarse in range(COARSE):
        first = ROWS * coarse
        rr[:rows, coarse * channels : (coarse + 1) * channels] = rb[first : first + rows, :]
    for lag in range(0, ROWS, FINE):
        slot = lag // FINE % 2 * FINE
        for pair in range(0, FINE, 2):
            weights = jnp.concatenate(
                [
                    jnp.concatenate([taps[m, lag + pair + j] for m in range(COARSE)], axis=0)
                    for j in range(2)
                ],
                axis=1,
            )
            product = lax.dot_general(rr[:rows, :], weights, NN, preferred_element_type=jnp.float32)
            for j in range(2):
                fine[slot + pair + j, 0, :rows, :] = product[:, j * K : (j + 1) * K]
        total = None if lag == 0 else acc[0, :count, :]
        for j in range(FINE):
            part = fine[slot + j, 0, lag + j : lag + j + count, :]
            total = part if total is None else total + part
        acc[0, :count, :] = total


def patch_taps(row, atoms_ref, taps, columns, turned):
    channels = taps.shape[2]
    lane = lax.broadcasted_iota(jnp.int32, (ROWS, K), 1)
    kept = (lane < row) | (lane >= row + BLOCK_ATOMS)
    keep = kept.astype(jnp.float32).astype(jnp.bfloat16)
    columns[...] = jnp.zeros_like(columns)
    width = ROWS * L

    def patch(step, carry):
        part = pl.ds(pl.multiple_of(step * (GROUPS * width), LANES), GROUPS * width)
        columns[pl.ds(row, BLOCK_ATOMS), :] = atoms_ref[:, part].astype(jnp.bfloat16)
        turn(columns[:, :width], turned[0])
        for group in range(GROUPS):
            if group + 1 < GROUPS:
                turn(columns[:, (group + 1) * width : (group + 2) * width], turned[group + 1])
            own = pl.ds(pl.multiple_of((step * GROUPS + group) * ROWS, ROWS), ROWS)
            for tap in range(L):
                before = taps[tap // ROWS, tap % ROWS, own, :]
                taps[tap // ROWS, tap % ROWS, own, :] = before * keep + tap_of(turned[group], tap)
        return carry

    lax.fori_loop(0, channels // (GROUPS * ROWS), patch, 0)


def put_edges(edge_refs, rightward, leftward):
    even = lax.axis_index("tm") % 2 == 0

    def put(first, second):
        first[: rightward.shape[0]] = rightward
        second[: leftward.shape[0]] = leftward
        unused = second.shape[0] - leftward.shape[0]
        if unused:
            second[leftward.shape[0] :] = jnp.zeros((unused, second.shape[1]), second.dtype)

    pl.when(even)(lambda: put(*edge_refs))
    pl.when(jnp.logical_not(even))(lambda: put(*edge_refs[::-1]))


def by_side(put, first_ref, second_ref):
    even = lax.axis_index("tm") % 2 == 0
    pl.when(even)(lambda: put(second_ref, first_ref))
    pl.when(jnp.logical_not(even))(lambda: put(first_ref, second_ref))


def begin_kernel(code_hbm, signal_hbm, state_out, signal_out, first_out, second_out, code_ref, signal_ref, sems):
    fetches = [
        pltpu.make_async_copy(code_hbm, code_ref, sems.at[0]),
        pltpu.make_async_copy(signal_hbm, signal_ref, sems.at[1]),
    ]
    for fetch in fetches:
        fetch.start()
    for fetch in fetches:
        fetch.wait()
    state = code_ref[...].T
    signal = signal_ref[...].astype(jnp.float32).T.astype(jnp.bfloat16)
    state_out[...] = state
    signal_out[...] = signal
    both = jnp.concatenate([state.astype(jnp.bfloat16), signal], axis=1)
    put_edges((first_out, second_out), both[-L:], both[:L])


def begin(code, signal):
    channels, segment = signal.shape
    return pl.pallas_call(
        begin_kernel,
        in_specs=[hbm()] * 2,
        out_specs=[vmem()] * 4,
        out_shape=[
            pltpu.VMEM((segment, K), jnp.float32),
            pltpu.VMEM((segment, channels), jnp.bfloat16),
        ]
        + [jax.ShapeDtypeStruct((L, K + channels), jnp.bfloat16)] * 2,
        scratch_shapes=[
            pltpu.VMEM(code.shape, code.dtype),
            pltpu.VMEM(signal.shape, signal.dtype),
            pltpu.SemaphoreType.DMA((2,)),
        ],
        compiler_params=pltpu.CompilerParams(vmem_limit_bytes=VMEM_BYTES),
        name="begin",
    )(far(code), far(signal))


def taker(refs):
    refs = list(refs)

    def take(count):
        taken = refs[:count]
        del refs[:count]
        return taken

    return take


def reaches(segment):
    near = min(2 * L, segment)
    return near, 2 * L - near


def residual_rows(rb, pieces, start, acc, total_time):
    rows = rb.shape[0]
    moment = start + lax.broadcasted_iota(jnp.int32, (rows, LANES), 0)
    scale = (C * L) ** (-0.5)
    for tile in range(acc.shape[0]):
        column = slice(tile * LANES, (tile + 1) * LANES)
        signal = jnp.concatenate([piece[:, column] for piece in pieces], axis=0)
        value = signal.astype(jnp.float32) - scale * acc[tile, :rows, :]
        rb[:, column] = jnp.where(moment < total_time, value, 0.0).astype(jnp.bfloat16)


def stepped_codes(state, acc, limit):
    scale = (C * L) ** (-0.5)
    stepped = state + code_rate * (scale * acc[0, : state.shape[0], :])
    return stepped - jnp.clip(stepped, -limit, limit)


def iterate_kernel(total_time, patching, copied, plan_ref, limit_ref, *refs):
    take = taker(refs)
    state_ref, first_ref, second_ref, signal_ref, next_first, next_second = take(6)
    atoms = take(1 if patching else 0)
    (taps,) = take(1)
    source = take(1 if copied else 0)
    take(1 if copied and copied[0] else 0)
    state_out, first_out, second_out, far_out = take(4)
    taps = (take(1) if patching else [taps])[0]
    target = take(1 if copied else 0)
    zb, rb, zz, rr, fine, acc, beyond = take(7)
    ferry = Ferry(source[0], target[0], copied[0], *take(2)) if copied else None
    segment, channels = signal_ref.shape
    zb[L : L + segment, :] = state_ref[...].astype(jnp.bfloat16)

    def put(left, right):
        zb[:L, :] = left[:, :K]
        zb[L + segment :, :] = right[:, :K]

    def put_signal(left, right):
        beyond[...] = right[:, K:]

    by_side(put, first_ref, second_ref)
    by_side(put_signal, next_first, next_second)
    if patching:
        columns, *turned = take(1 + GROUPS)
        patch_taps(first_row_of(plan_ref, patching - 1), atoms[0], taps, columns, turned)
    convolve(zb, L, segment + L, taps, zz, fine, acc)
    if ferry:
        ferry.turn_round()
    start = lax.axis_index("tm") * segment
    residual_rows(rb, (signal_ref, beyond), start, acc, total_time)
    correlate(rb, segment, taps, rr, fine, acc)
    state = stepped_codes(state_ref[...], acc, limit_ref[...])
    state_out[...] = state
    low = state.astype(jnp.bfloat16)
    rest = (state - low.astype(jnp.float32)).astype(jnp.bfloat16)
    near, beyond_near = reaches(segment)
    put_edges((first_out, second_out), jnp.concatenate([low[-near:], rest[-L:]], axis=0), low[:L])
    if beyond_near:
        far_out[...] = low[-beyond_near:]
    else:
        far_out[...] = jnp.zeros_like(far_out)
    if ferry:
        ferry.close()


def iterate(plan, step, limit, state, swapped, signal, following, taps, atoms, ferry, peers):
    segment, channels = signal.shape
    patching = atoms is not None
    reach = segment + L
    near, beyond_near = reaches(segment)
    carried = [far(value) for value in ferry[:2] if value is not None]
    aliases = {9: 4} if patching else {}
    if len(carried) == 2:
        aliases[10 + patching] = 4 + patching
    return pl.pallas_call(
        functools.partial(iterate_kernel, peers * segment, step if patching else 0, ferry[2:]),
        in_specs=[scalars()] + [vmem()] * (8 + patching) + [hbm()] * len(carried),
        out_specs=[vmem()] * (4 + patching) + [hbm()],
        out_shape=[pltpu.VMEM((segment, K), jnp.float32)]
        + [jax.ShapeDtypeStruct((near + L, K), jnp.bfloat16)] * 2
        + [jax.ShapeDtypeStruct((max(beyond_near, ROWS), K), jnp.bfloat16)]
        + [pltpu.VMEM(taps.shape, jnp.bfloat16)] * patching
        + [pltpu.HBM(ferry[0].shape, jnp.float32)],
        scratch_shapes=[
            pltpu.VMEM((L + reach, K), jnp.bfloat16),
            pltpu.VMEM((reach, channels), jnp.bfloat16),
            pltpu.VMEM((reach + ROWS, COARSE * K), jnp.bfloat16),
            pltpu.VMEM((segment + ROWS, COARSE * channels), jnp.bfloat16),
            pltpu.VMEM((2 * FINE, channels // LANES, reach + ROWS, LANES), jnp.float32),
            pltpu.VMEM((channels // LANES, reach, LANES), jnp.float32),
            pltpu.VMEM((L, channels), jnp.bfloat16),
        ]
        + ferry_scratch(ferry[3], ferry[0].shape[1])
        + (
            [pltpu.VMEM((K, GROUPS * ROWS * L), jnp.bfloat16)]
            + [pltpu.VMEM((ROWS * STRIDE, K), jnp.float32)] * GROUPS
        )
        * patching,
        input_output_aliases=aliases,
        compiler_params=pltpu.CompilerParams(vmem_limit_bytes=VMEM_BYTES),
        name="iterate",
    )(
        plan,
        limit,
        resident(state),
        *swapped,
        resident(signal),
        *following,
        *([resident(atoms)] if patching else []),
        resident(taps),
        *carried,
    )


def conclude_kernel(peers, step, copied, plan_ref, limit_ref, *refs):
    last = step + 1 == OUTER
    take = taker(refs)
    state_ref, first_ref, second_ref, far_ref, signal_ref, next_first, next_second, taps = take(8)
    source, _, payload_out = take(3)
    outs = take(2 if last else 3)
    (target,) = take(1)
    zb, rb, zz, rr, fine, acc, before, beyond, earlier, tall = take(10)
    ferry = Ferry(source, target, copied[0], *take(2))
    segment, channels = signal_ref.shape
    near, beyond_near = reaches(segment)
    zb[2 * L : 2 * L + segment, :] = state_ref[...].astype(jnp.bfloat16)
    if beyond_near:
        zb[:beyond_near, :] = far_ref[...]

    def put(left, right):
        zb[beyond_near : 2 * L, :] = left[:near]
        earlier[...] = left[near - L : near].astype(jnp.float32) + left[near:].astype(jnp.float32)
        zb[2 * L + segment :, :] = right[:L]

    def put_signal(left, right):
        before[...] = left[:, K:]
        beyond[...] = right[:, K:]

    by_side(put, first_ref, second_ref)
    by_side(put_signal, next_first, next_second)
    convolve(zb, L, 2 * L + segment, taps, zz, fine, acc)
    ferry.turn_round()
    start = lax.axis_index("tm") * segment - L
    residual_rows(rb, (before, signal_ref, beyond), start, acc, peers * segment)
    correlate(rb, L + segment, taps, rr, fine, acc)
    state = jnp.concatenate([earlier[...], state_ref[...]], axis=0)
    state = stepped_codes(state, acc, limit_ref[...])
    moment = start + lax.broadcasted_iota(jnp.int32, state.shape, 0)
    state = jnp.where(moment >= 0, state, 0.0)
    low = state.astype(jnp.bfloat16)
    zb[: L + segment, :] = low
    own = state[L:]
    if last:
        resid_out, codes_out = outs
    else:
        state_out, *edges = outs
        (codes_out,) = take(1)
        state_out[...] = own
        put_edges(edges, low[-L:], low[L : 2 * L])
    codes_out[...] = own.T
    convolve(zb, L, segment, taps, zz, fine, acc)
    scale = (C * L) ** (-0.5)
    for tile in range(channels // LANES):
        column = slice(tile * LANES, (tile + 1) * LANES)
        value = signal_ref[:, column].astype(jnp.float32) - scale * acc[tile, :segment, :]
        value = value.T
        tall[column, :] = value
        if last:
            resid_out[column, :] = value
    block = codes_out[pl.ds(first_row_of(plan_ref, step), BLOCK_ATOMS), :].astype(jnp.bfloat16)
    share = channels // peers
    share_rows = payload_out.shape[1] - BLOCK_ATOMS
    tall[channels:, :] = jnp.zeros((tall.shape[0] - channels, segment), jnp.float32)
    for peer in range(peers):
        part = tall[peer * share : peer * share + share_rows, :]
        payload_out[peer, :share_rows, :] = part.astype(jnp.bfloat16)
        payload_out[peer, share_rows:, :] = block
    ferry.close()


def conclude(plan, step, limit, state, swapped, far_edge, signal, following, taps, ferry, peers):
    segment, channels = signal.shape
    share = channels // peers
    share_rows = -(-share // ROWS) * ROWS
    last = step + 1 == OUTER
    carried = [far(value) for value in ferry[:2]]
    rows = 2 * L + segment
    outs = [
        pltpu.VMEM((channels, segment), jnp.float32),
        pltpu.VMEM((K, segment), jnp.float32),
    ]
    if not last:
        outs = [pltpu.VMEM((segment, K), jnp.float32)]
        outs += [jax.ShapeDtypeStruct((L, K), jnp.bfloat16)] * 2
    return pl.pallas_call(
        functools.partial(conclude_kernel, peers, step, ferry[2:]),
        in_specs=[scalars()] + [vmem()] * 9 + [hbm()] * 2,
        out_specs=[vmem()] * (1 + len(outs)) + [hbm()],
        out_shape=[jax.ShapeDtypeStruct((peers, share_rows + BLOCK_ATOMS, segment), jnp.bfloat16)]
        + outs
        + [pltpu.HBM(ferry[0].shape, jnp.float32)],
        scratch_shapes=[
            pltpu.VMEM((rows + L, K), jnp.bfloat16),
            pltpu.VMEM((rows, channels), jnp.bfloat16),
            pltpu.VMEM((rows + ROWS, COARSE * K), jnp.bfloat16),
            pltpu.VMEM((L + segment + ROWS, COARSE * channels), jnp.bfloat16),
            pltpu.VMEM((2 * FINE, channels // LANES, rows + ROWS, LANES), jnp.float32),
            pltpu.VMEM((channels // LANES, rows, LANES), jnp.float32),
            pltpu.VMEM((L, channels), jnp.bfloat16),
            pltpu.VMEM((L, channels), jnp.bfloat16),
            pltpu.VMEM((L, K), jnp.float32),
            pltpu.VMEM((channels + ROWS, segment), jnp.float32),
        ]
        + ferry_scratch(ferry[3], ferry[0].shape[1])
        + ([] if last else [pltpu.VMEM((K, segment), jnp.float32)]),
        input_output_aliases={11: 1 + len(outs)},
        compiler_params=pltpu.CompilerParams(vmem_limit_bytes=VMEM_BYTES),
        name="conclude",
    )(
        plan,
        limit,
        resident(state),
        *swapped,
        far_edge,
        resident(signal),
        *following,
        resident(taps),
        *carried,
    )


def gradient_kernel(share, step, plan_ref, blocks_ref, dict_hbm, out_ref, rf, zf, rr, zz, old, sem):
    peers, rows, segment = blocks_ref.shape
    share_rows = rows - BLOCK_ATOMS
    span = peers * segment
    entries = share * L
    rows_of = pl.ds(first_row_of(plan_ref, step), BLOCK_ATOMS)
    columns_of = pl.ds(pl.multiple_of(lax.axis_index("tm") * entries, LANES), entries)
    fetch = pltpu.make_async_copy(dict_hbm.at[rows_of, columns_of], old, sem)
    fetch.start()
    rf[:, span:] = jnp.zeros((share_rows, LANES), jnp.float32)
    zf[:, :LANES] = jnp.zeros((BLOCK_ATOMS, LANES), jnp.float32)
    for peer in range(peers):
        column = peer * segment
        rf[:, column : column + segment] = blocks_ref[peer, :share_rows, :].astype(jnp.float32)
        zf[:, LANES + column : LANES + column + segment] = blocks_ref[peer, share_rows:, :].astype(
            jnp.float32
        )
    for lag in range(ROWS):
        rr[lag * share_rows : (lag + 1) * share_rows, :] = rf[:, lag : lag + span].astype(jnp.bfloat16)
    for coarse in range(COARSE):
        begin = LANES - ROWS * coarse
        zz[coarse * BLOCK_ATOMS : (coarse + 1) * BLOCK_ATOMS, :] = zf[:, begin : begin + span].astype(
            jnp.bfloat16
        )
    lagged = lax.dot_general(zz[...], rr[...], NT, preferred_element_type=jnp.float32)
    wide = ROWS * share_rows
    parts = []
    left = lagged
    for _ in range(3):
        parts.append(left.astype(jnp.bfloat16))
        left = left - parts[-1].astype(jnp.float32)
    row = lax.broadcasted_iota(jnp.int32, (wide, wide), 0)
    column = lax.broadcasted_iota(jnp.int32, (wide, wide), 1)
    chosen = (row // share_rows == column % ROWS) & (row % share_rows == column // ROWS)
    chosen = chosen.astype(jnp.float32).astype(jnp.bfloat16)
    by_channel = lax.dot_general(
        jnp.concatenate(parts, axis=0), chosen, NN, preferred_element_type=jnp.float32
    )
    count = COARSE * BLOCK_ATOMS
    by_channel = by_channel[:count] + by_channel[count : 2 * count] + by_channel[2 * count :]
    lane = lax.broadcasted_iota(jnp.int32, (BLOCK_ATOMS, LANES), 1)
    tiles = []
    for tile in range(entries // LANES):
        total = jnp.zeros((BLOCK_ATOMS, LANES), jnp.float32)
        for place in range(LANES // ROWS):
            channel, coarse = divmod(tile * (LANES // ROWS) + place, COARSE)
            first = channel * ROWS // LANES * LANES
            source = by_channel[coarse * BLOCK_ATOMS : (coarse + 1) * BLOCK_ATOMS, first : first + LANES]
            by = (place * ROWS - channel * ROWS) % LANES
            moved = pltpu.roll(source, by, 1) if by else source
            total = jnp.where(lane // ROWS == place, moved, total)
        tiles.append(total)
    gradient = jnp.concatenate(tiles, axis=1)
    fetch.wait()
    before = old[...]
    square = jnp.sum(before * before, axis=1, keepdims=True)
    along = jnp.sum(gradient * before, axis=1, keepdims=True) / (square + tiny_eps)
    out_ref[:, :entries] = (gradient - along * before).astype(jnp.bfloat16)
    terms = jnp.zeros((BLOCK_ATOMS, LANES), jnp.float32)
    for i in range(3):
        term = along.astype(jnp.bfloat16).astype(jnp.float32)
        along = along - term
        terms = jnp.where(lane == i, term, terms)
    out_ref[:, entries:] = terms.astype(jnp.bfloat16)


def share_gradient(plan, step, blocks, dictionary, share):
    peers, rows, segment = blocks.shape
    share_rows = rows - BLOCK_ATOMS
    span = peers * segment
    return pl.pallas_call(
        functools.partial(gradient_kernel, share, step),
        in_specs=[scalars(), vmem(), hbm()],
        out_shape=jax.ShapeDtypeStruct((BLOCK_ATOMS, share * L + LANES), jnp.bfloat16),
        scratch_shapes=[
            pltpu.VMEM((share_rows, span + LANES), jnp.float32),
            pltpu.VMEM((BLOCK_ATOMS, LANES + span), jnp.float32),
            pltpu.VMEM((ROWS * share_rows, span), jnp.bfloat16),
            pltpu.VMEM((COARSE * BLOCK_ATOMS, span), jnp.bfloat16),
            pltpu.VMEM((BLOCK_ATOMS, share * L), jnp.float32),
            pltpu.SemaphoreType.DMA,
        ],
        compiler_params=pltpu.CompilerParams(vmem_limit_bytes=VMEM_BYTES),
        name="gradient",
    )(plan, blocks, far(dictionary))


def gather_steps(peers):
    bits = [1 << i for i in range(peers.bit_length() - 2, 0, -1)]
    steps = []
    for first in range(0, len(bits), 2):
        pair = bits[first : first + 2]
        steps.append(pair + [sum(pair)] if len(pair) == 2 else pair)
    return steps


def gather_slots(peers):
    flips = [0]
    for masks in gather_steps(peers):
        flips = [f ^ m for m in [0] + masks for f in flips]
    return flips


def gather_pieces(piece, meanwhile):
    peers = lax.axis_size("tm")

    def exchanged(shard, mask):
        return lax.ppermute(shard, "tm", [(i, i ^ mask) for i in range(peers)])

    held = piece[None]
    for index, masks in enumerate(gather_steps(peers)):
        held = jnp.concatenate([held] + [exchanged(held, mask) for mask in masks], axis=0)
        if index == 0:
            needed, extra = meanwhile(held)
    ready, _ = lax.optimization_barrier((held, needed))
    return held, exchanged(ready, 1), extra


def recall_kernel(step, plan_ref, dict_hbm, piece_ref, old_ref, mean_ref, sem):
    del piece_ref
    first_row = first_row_of(plan_ref, step)
    fetch = pltpu.make_async_copy(dict_hbm.at[pl.ds(first_row, BLOCK_ATOMS)], old_ref, sem)
    fetch.start()
    fetch.wait()
    width = 9 * LANES if old_ref.shape[1] % (9 * LANES) == 0 else LANES

    def add(step, square):
        before = old_ref[:, pl.ds(pl.multiple_of(step * width, LANES), width)]
        return square + before * before

    square = lax.fori_loop(
        0, old_ref.shape[1] // width, add, jnp.zeros((BLOCK_ATOMS, width), jnp.float32)
    )
    mean_sq = jnp.sum(square, axis=1, keepdims=True) / (C * L) + tiny_eps
    mean_ref[...] = jnp.broadcast_to(mean_sq, mean_ref.shape)


def recall(plan, step, dictionary, piece):
    return pl.pallas_call(
        functools.partial(recall_kernel, step),
        in_specs=[scalars(), hbm(), pl.BlockSpec(memory_space=pl.ANY)],
        out_specs=[vmem(), vmem()],
        out_shape=[
            pltpu.VMEM((BLOCK_ATOMS, dictionary.shape[1]), jnp.float32),
            jax.ShapeDtypeStruct((BLOCK_ATOMS, LANES), jnp.float32),
        ],
        scratch_shapes=[pltpu.SemaphoreType.DMA],
        compiler_params=pltpu.CompilerParams(vmem_limit_bytes=VMEM_BYTES),
        name="recall",
    )(plan, far(dictionary), piece)


def renew_kernel(plan_step, earlier, plan_ref, held_ref, came_ref, old, mean_ref, *refs):
    me = lax.axis_index("tm")
    half, _, wide = held_ref.shape
    width = wide - LANES
    entries = C * L
    before_refs, refs = refs[:earlier], refs[earlier:]
    last = plan_step + 1 == OUTER
    if last:
        _, out_hbm, atoms_ref, grad, sems = refs
    else:
        atoms_ref, grad = refs

    def rows_of(step):
        return pl.ds(first_row_of(plan_ref, step), BLOCK_ATOMS)

    stores = []
    for step in range(earlier):
        stores.append(
            pltpu.make_async_copy(before_refs[step], out_hbm.at[rows_of(step)], sems.at[2 * half + step])
        )
        stores[-1].start()
    shares = []
    for slot, flips in enumerate(gather_slots(2 * half)):
        for source, extra in ((held_ref, 0), (came_ref, 1)):
            owner = me ^ (flips + extra)
            shares.append((source.at[slot], pl.ds(pl.multiple_of(owner * width, LANES), width)))
    zeros = jnp.zeros((BLOCK_ATOMS, width), jnp.float32)
    dot = zeros
    for source, column in shares:
        before = old[:, column]
        along = jnp.sum(source[:, width:].astype(jnp.float32), axis=1, keepdims=True)
        value = source[:, :width].astype(jnp.float32) + along * before
        grad[:, column] = value
        dot += value * before
    mean_sq = mean_ref[:, :1]
    along = jnp.sum(dot, axis=1, keepdims=True) / entries / mean_sq
    square = zeros
    for _, column in shares:
        value = grad[:, column] - along * old[:, column]
        square += value * value
    spread = jnp.sum(square, axis=1, keepdims=True) / entries + tiny_eps
    step = move_rate / jnp.sqrt(spread)
    norm = 1.0 / jnp.sqrt(mean_sq + 0.25)
    for index, (_, column) in enumerate(shares):
        before = old[:, column]
        across = grad[:, column] - along * before
        atoms_ref[:, column] = (before + step * across) * norm
        if last:
            stores.append(
                pltpu.make_async_copy(
                    atoms_ref.at[:, column], out_hbm.at[rows_of(plan_step), column], sems.at[index]
                )
            )
            stores[-1].start()
    for store in stores:
        store.wait()


def renew(plan, step, held, came, old, mean_sq, renewed, dictionary):
    last = step + 1 == OUTER
    atoms = (BLOCK_ATOMS, old.shape[1])
    earlier = len(renewed) if last else 0
    scratch = [pltpu.VMEM(atoms, jnp.float32)]
    if last:
        scratch = scratch * 2 + [pltpu.SemaphoreType.DMA((2 * held.shape[0] + earlier,))]
    return pl.pallas_call(
        functools.partial(renew_kernel, step, earlier),
        in_specs=[scalars()] + [vmem()] * (4 + earlier) + [hbm()] * last,
        out_specs=hbm() if last else vmem(),
        out_shape=pltpu.HBM(dictionary.shape, jnp.float32) if last else pltpu.VMEM(atoms, jnp.float32),
        scratch_shapes=scratch,
        input_output_aliases={5 + earlier: 0} if last else {},
        compiler_params=pltpu.CompilerParams(vmem_limit_bytes=VMEM_BYTES),
        name="renew",
    )(
        plan,
        held,
        came,
        resident(old),
        mean_sq,
        *([resident(value) for value in renewed] + [far(dictionary)] if last else []),
    )


def whole_channels(signal, codes_init, dictionary_init, threshold, plan):
    channels, segment = signal.shape
    peers = lax.axis_size("tm")
    limit = threshold[None, :]
    def swaps(edges):
        ends = [range(first, peers - 1, 2) for first in (0, 1)]
        pairs = [[p for i in end for p in ((i, i + 1), (i + 1, i))] for end in ends]
        return [lax.ppermute(edge, "tm", pair) for edge, pair in zip(edges, pairs)]

    state, signal, *edges = begin(codes_init, signal)
    following = swaps(edges)
    swapped = following
    taps = layout(dictionary_init, channels)
    dictionary = None
    renewed = []
    for step in range(OUTER):
        last = step + 1 == OUTER
        rows = COPIED[2 * step : 2 * step + 2]
        first = sum(COPIED[: 2 * step])
        ferry = (dictionary_init, dictionary, first, rows[0])
        atoms = renewed[-1] if renewed else None
        state, *results = iterate(
            plan, step, limit, state, swapped, signal, following, taps, atoms, ferry, peers
        )
        if renewed:
            taps = results[3]
        edges, far_edge, dictionary = results[:2], results[2], results[-1]
        ferry = (dictionary_init, dictionary, first + rows[0], rows[1])
        payload, *results, dictionary = conclude(
            plan,
            step,
            limit,
            state,
            swaps(edges),
            shifted(far_edge, "tm", 2),
            signal,
            following,
            taps,
            ferry,
            peers,
        )
        blocks = lax.all_to_all(payload, "tm", 0, 0, tiled=True)
        piece = share_gradient(plan, step, blocks, dictionary_init, channels // peers)
        recalled = [] if last else list(recall(plan, step, dictionary_init, piece))

        def beside(held):
            if last:
                recalled.extend(recall(plan, step, dictionary_init, held))
                return recalled[0], None
            state, *edges = results
            edges, _ = lax.optimization_barrier((edges, held))
            return recalled[0], swaps(edges)

        held, came, extra = gather_pieces(piece, beside)
        result = renew(plan, step, held, came, *recalled, renewed if last else None, dictionary)
        if last:
            dictionary = result
        else:
            renewed.append(result)
            state, swapped = results[0], extra
    residual, codes = results
    return codes, dictionary, residual


def renew_atoms(old_atoms, across, mean_sq, spread):
    return (old_atoms + move_rate * across / jnp.sqrt(spread)[:, None]) / jnp.sqrt(mean_sq + 0.25)[
        :, None
    ]


def split_channels(signal, codes_init, dictionary_init, threshold, plan):
    segment = signal.shape[1]
    local_chan = signal.shape[0]
    unit_scale = (C * L) ** (-0.5)
    entries = C * L
    limit = threshold[:, None]

    def convolve(atom_cube, code_low):
        code_edge = shifted(code_low[:, segment - (L - 1) :], "tm", 1)
        extended = jnp.concatenate([code_edge, code_low], axis=1)
        lagged = jnp.stack(
            [extended[:, L - 1 - offset : L - 1 - offset + segment] for offset in range(L)], axis=1
        )
        return unit_scale * jnp.einsum(
            "kcl,klt->ct", atom_cube, lagged, preferred_element_type=jnp.float32
        )

    def resid_columns(resid_low):
        resid_edge = shifted(resid_low[:, : L - 1], "tm", -1)
        extended = jnp.concatenate([resid_low, resid_edge], axis=1)
        lagged = jnp.stack([extended[:, offset : offset + segment] for offset in range(L)], axis=1)
        return lagged.reshape(local_chan * L, segment)

    code_state = codes_init
    dictionary = dictionary_init
    residual = signal.astype(jnp.float32)
    for outer_step in range(OUTER):
        dict_low = dictionary.astype(jnp.bfloat16)
        atom_cube = dict_low.reshape(K, local_chan, L)
        for inner_step in range(INNER):
            code_low = code_state.astype(jnp.bfloat16)
            residual = signal.astype(jnp.float32) - convolve(atom_cube, code_low)
            lagged = resid_columns(residual.astype(jnp.bfloat16))
            partial_value = unit_scale * jnp.dot(
                dict_low, lagged, preferred_element_type=jnp.float32
            )
            scores = lax.psum(partial_value.astype(jnp.bfloat16), "chan").astype(jnp.float32)
            stepped = code_state + code_rate * scores
            code_state = stepped - jnp.clip(stepped, -limit, limit)
        code_low = code_state.astype(jnp.bfloat16)
        residual = signal.astype(jnp.float32) - convolve(atom_cube, code_low)
        lagged = resid_columns(residual.astype(jnp.bfloat16))
        first_row = plan[outer_step] * BLOCK_ATOMS
        code_block = lax.dynamic_slice_in_dim(code_low, first_row, BLOCK_ATOMS, 0)
        local_grad = lax.dot_general(
            code_block, lagged, (((1,), (1,)), ((), ())), preferred_element_type=jnp.float32
        )
        old_atoms = lax.dynamic_slice_in_dim(dictionary, first_row, BLOCK_ATOMS, 0)
        gradient = lax.psum(local_grad, "tm")
        dot_sum, square_sum = lax.psum(
            (jnp.sum(gradient * old_atoms, axis=1), jnp.sum(old_atoms * old_atoms, axis=1)), "chan"
        )
        mean_sq = square_sum / entries + tiny_eps
        along_coef = dot_sum / entries / mean_sq
        across = gradient - along_coef[:, None] * old_atoms
        spread = lax.psum(jnp.sum(across * across, axis=1), "chan") / entries + tiny_eps
        renewed = renew_atoms(old_atoms, across, mean_sq, spread)
        dictionary = lax.dynamic_update_slice_in_dim(dictionary, renewed, first_row, 0)
    return (code_state, dictionary, residual)


def shards(signal, codes_init, dictionary_init, threshold, plan):
    channels, segment = signal.shape
    peers = lax.axis_size("tm")
    fits = (
        lax.axis_size("chan") == 1
        and segment % LANES == 0
        and INNER == 2
        and channels % (GROUPS * ROWS) == 0
        and channels % LANES == 0
        and channels % peers == 0
        and (channels // peers * L) % LANES == 0
        and peers > 2
        and peers & (peers - 1) == 0
    )
    body = whole_channels if fits else split_channels
    return body(signal, codes_init, dictionary_init, threshold, plan)


def solution(mesh):
    placed = (P("chan", "tm"), P(None, "tm"), P(None, "chan"), P(), P())
    return jax.shard_map(
        shards,
        mesh=mesh,
        in_specs=placed,
        out_specs=(P(None, "tm"), P(None, "chan"), P("chan", "tm")),
        check_vma=False,
    )
```

```python
import functools

import jax
import jax.numpy as jnp
from jax import lax
from jax.experimental import pallas as pl
from jax.experimental.pallas import tpu as pltpu
from jax.sharding import PartitionSpec as P

C = 384
K = 128
L = 96
BLOCK_ATOMS = 16
INNER = 2
OUTER = 2

code_rate = 0.3
move_rate = 0.5
tiny_eps = 1e-06

ROWS = 16
COARSE = L // ROWS
STRIDE = L + 1
GROUPS = 4
SUBLANES = 8
COPIED = (32, 72, 24)
FINE = 4
LANES = 128
VMEM_BYTES = 24 * 1024 * 1024

NN = (((1,), (0,)), ((), ()))
NT = (((1,), (1,)), ((), ()))


def shifted(shard, axis, by):
    peers = lax.axis_size(axis)
    pairs = [(i, i + by) for i in range(peers) if 0 <= i + by < peers]
    return lax.ppermute(shard, axis, pairs)


def resident(value):
    return pltpu.with_memory_space_constraint(value, pltpu.VMEM)


def far(value):
    return pltpu.with_memory_space_constraint(value, pltpu.HBM)


def hbm():
    return pl.BlockSpec(memory_space=pltpu.HBM)


def scalars():
    return pl.BlockSpec(memory_space=pltpu.SMEM)


def first_row_of(plan_ref, step):
    return pl.multiple_of(plan_ref[step] * BLOCK_ATOMS, BLOCK_ATOMS)


def vmem():
    return pl.BlockSpec(memory_space=pltpu.VMEM)


def turn(columns, turned_ref):
    side = 2 * LANES
    row = lax.broadcasted_iota(jnp.int32, (side, side), 0)
    column = lax.broadcasted_iota(jnp.int32, (side, side), 1)
    identity = (row == column).astype(jnp.float32).astype(jnp.bfloat16)

    def put(entry, rows):
        end = entry + rows.shape[0]
        begin = entry
        while begin < end:
            channel, tap = begin // L, begin % L
            count = min(end - begin, L - tap)
            target = channel * STRIDE + tap
            turned_ref[target : target + count, :] = rows[begin - entry : begin - entry + count]
            begin += count

    low = columns.astype(jnp.bfloat16)
    through_matrix = ROWS * L // (6 * side) * 4 * side
    for first in range(0, through_matrix, 2 * side):
        pair = jnp.concatenate(
            [low[:, first + half * side : first + (half + 1) * side] for half in range(2)], axis=0
        )
        turned = lax.dot_general(identity, pair, NT, preferred_element_type=jnp.float32)
        for half in range(2):
            put(first + half * side, turned[:, half * K : (half + 1) * K])
    for first in range(through_matrix, ROWS * L, LANES):
        put(first, columns[:, first : first + LANES].astype(jnp.float32).T)


def tap_of(turned_ref, tap):
    return turned_ref[pl.ds(tap, ROWS, stride=STRIDE), :].astype(jnp.bfloat16)


def layout_kernel(dict_ref, taps_ref, copy_hbm, sem, *turned):
    width = dict_ref.shape[1]
    column = pl.ds(pl.multiple_of(pl.program_id(0) * width, LANES), width)
    rows = pl.ds(0, COPIED[0])
    copy = pltpu.make_async_copy(dict_ref.at[rows], copy_hbm.at[rows, column], sem)
    copy.start()

    def part(group):
        return dict_ref[:, group * ROWS * L : (group + 1) * ROWS * L]

    turn(part(0), turned[0])
    for group in range(GROUPS):
        if group + 1 < GROUPS:
            turn(part(group + 1), turned[group + 1])
        own = pl.ds(pl.multiple_of((pl.program_id(0) * GROUPS + group) * ROWS, ROWS), ROWS)
        for tap in range(L):
            taps_ref[tap // ROWS, tap % ROWS, own, :] = tap_of(turned[group], tap)
    copy.wait()


def layout(dictionary, channels):
    block = GROUPS * ROWS
    return pl.pallas_call(
        layout_kernel,
        grid=(channels // block,),
        in_specs=[pl.BlockSpec((K, block * L), lambda i: (0, i))],
        out_specs=[vmem(), hbm()],
        out_shape=[
            pltpu.VMEM((COARSE, ROWS, channels, K), jnp.bfloat16),
            pltpu.HBM(dictionary.shape, jnp.float32),
        ],
        scratch_shapes=[pltpu.SemaphoreType.DMA]
        + [pltpu.VMEM((ROWS * STRIDE, K), jnp.float32)] * GROUPS,
        compiler_params=pltpu.CompilerParams(vmem_limit_bytes=VMEM_BYTES),
        name="layout",
    )(far(dictionary))


class Ferry:
    def __init__(self, source, target, first, buffer, sems):
        self.steps = []
        for step in range(buffer.shape[0] // SUBLANES):
            held = buffer.at[pl.ds(step * SUBLANES, SUBLANES)]
            rows = pl.ds(first + step * SUBLANES, SUBLANES)
            fetch = pltpu.make_async_copy(source.at[rows], held, sems.at[0, step])
            store = pltpu.make_async_copy(held, target.at[rows], sems.at[1, step])
            fetch.start()
            self.steps.append((fetch, store))

    def turn_round(self):
        for fetch, store in self.steps:
            fetch.wait()
            store.start()

    def close(self):
        for _, store in self.steps:
            store.wait()


def ferry_scratch(count, entries):
    return [
        pltpu.VMEM((count, entries), jnp.float32),
        pltpu.SemaphoreType.DMA((2, count // SUBLANES)),
    ]


def convolve(zb, begin, count, taps, zz, fine, acc):
    channels = taps.shape[2]
    tiles = channels // LANES
    rows = count + ROWS
    for coarse in range(COARSE):
        first = begin - ROWS - ROWS * coarse
        zz[:rows, coarse * K : (coarse + 1) * K] = zb[first : first + rows, :]
    for lag in range(0, ROWS, FINE):
        slot = lag // FINE % 2 * FINE
        for pair in range(0, FINE, 2):
            weights = jnp.concatenate(
                [
                    jnp.concatenate([taps[m, lag + pair + j] for m in range(COARSE)], axis=1)
                    for j in range(2)
                ],
                axis=0,
            )
            product = lax.dot_general(zz[:rows, :], weights, NT, preferred_element_type=jnp.float32)
            for j in range(2):
                for tile in range(tiles):
                    column = j * channels + tile * LANES
                    fine[slot + pair + j, tile, :rows, :] = product[:, column : column + LANES]
        for tile in range(tiles):
            total = None if lag == 0 else acc[tile, :count, :]
            for j in range(FINE):
                first = ROWS - lag - j
                part = fine[slot + j, tile, first : first + count, :]
                total = part if total is None else total + part
            acc[tile, :count, :] = total


def correlate(rb, count, taps, rr, fine, acc):
    channels = taps.shape[2]
    rows = count + ROWS
    for coarse in range(COARSE):
        first = ROWS * coarse
        rr[:rows, coarse * channels : (coarse + 1) * channels] = rb[first : first + rows, :]
    for lag in range(0, ROWS, FINE):
        slot = lag // FINE % 2 * FINE
        for pair in range(0, FINE, 2):
            weights = jnp.concatenate(
                [
                    jnp.concatenate([taps[m, lag + pair + j] for m in range(COARSE)], axis=0)
                    for j in range(2)
                ],
                axis=1,
            )
            product = lax.dot_general(rr[:rows, :], weights, NN, preferred_element_type=jnp.float32)
            for j in range(2):
                fine[slot + pair + j, 0, :rows, :] = product[:, j * K : (j + 1) * K]
        total = None if lag == 0 else acc[0, :count, :]
        for j in range(FINE):
            part = fine[slot + j, 0, lag + j : lag + j + count, :]
            total = part if total is None else total + part
        acc[0, :count, :] = total


def patch_taps(row, atoms_ref, taps, columns, turned):
    channels = taps.shape[2]
    lane = lax.broadcasted_iota(jnp.int32, (ROWS, K), 1)
    kept = (lane < row) | (lane >= row + BLOCK_ATOMS)
    keep = kept.astype(jnp.float32).astype(jnp.bfloat16)
    columns[...] = jnp.zeros_like(columns)
    width = ROWS * L

    def patch(step, carry):
        part = pl.ds(pl.multiple_of(step * (GROUPS * width), LANES), GROUPS * width)
        columns[pl.ds(row, BLOCK_ATOMS), :] = atoms_ref[:, part].astype(jnp.bfloat16)
        turn(columns[:, :width], turned[0])
        for group in range(GROUPS):
            if group + 1 < GROUPS:
                turn(columns[:, (group + 1) * width : (group + 2) * width], turned[group + 1])
            own = pl.ds(pl.multiple_of((step * GROUPS + group) * ROWS, ROWS), ROWS)
            for tap in range(L):
                before = taps[tap // ROWS, tap % ROWS, own, :]
                taps[tap // ROWS, tap % ROWS, own, :] = before * keep + tap_of(turned[group], tap)
        return carry

    lax.fori_loop(0, channels // (GROUPS * ROWS), patch, 0)


def put_edges(edge_refs, rightward, leftward):
    even = lax.axis_index("tm") % 2 == 0

    def put(first, second):
        first[: rightward.shape[0]] = rightward
        second[: leftward.shape[0]] = leftward
        unused = second.shape[0] - leftward.shape[0]
        if unused:
            second[leftward.shape[0] :] = jnp.zeros((unused, second.shape[1]), second.dtype)

    pl.when(even)(lambda: put(*edge_refs))
    pl.when(jnp.logical_not(even))(lambda: put(*edge_refs[::-1]))


def by_side(put, first_ref, second_ref):
    even = lax.axis_index("tm") % 2 == 0
    pl.when(even)(lambda: put(second_ref, first_ref))
    pl.when(jnp.logical_not(even))(lambda: put(first_ref, second_ref))


def begin_kernel(code_hbm, signal_hbm, state_out, signal_out, first_out, second_out, code_ref, signal_ref, sems):
    fetches = [
        pltpu.make_async_copy(code_hbm, code_ref, sems.at[0]),
        pltpu.make_async_copy(signal_hbm, signal_ref, sems.at[1]),
    ]
    for fetch in fetches:
        fetch.start()
    for fetch in fetches:
        fetch.wait()
    state = code_ref[...].T
    signal = signal_ref[...].astype(jnp.float32).T.astype(jnp.bfloat16)
    state_out[...] = state
    signal_out[...] = signal
    both = jnp.concatenate([state.astype(jnp.bfloat16), signal], axis=1)
    put_edges((first_out, second_out), both[-L:], both[:L])


def begin(code, signal):
    channels, segment = signal.shape
    return pl.pallas_call(
        begin_kernel,
        in_specs=[hbm()] * 2,
        out_specs=[vmem()] * 4,
        out_shape=[
            pltpu.VMEM((segment, K), jnp.float32),
            pltpu.VMEM((segment, channels), jnp.bfloat16),
        ]
        + [jax.ShapeDtypeStruct((L, K + channels), jnp.bfloat16)] * 2,
        scratch_shapes=[
            pltpu.VMEM(code.shape, code.dtype),
            pltpu.VMEM(signal.shape, signal.dtype),
            pltpu.SemaphoreType.DMA((2,)),
        ],
        compiler_params=pltpu.CompilerParams(vmem_limit_bytes=VMEM_BYTES),
        name="begin",
    )(far(code), far(signal))


def taker(refs):
    refs = list(refs)

    def take(count):
        taken = refs[:count]
        del refs[:count]
        return taken

    return take


def reaches(segment):
    near = min(2 * L, segment)
    return near, 2 * L - near


def residual_rows(rb, pieces, start, acc, total_time):
    rows = rb.shape[0]
    moment = start + lax.broadcasted_iota(jnp.int32, (rows, LANES), 0)
    scale = (C * L) ** (-0.5)
    for tile in range(acc.shape[0]):
        column = slice(tile * LANES, (tile + 1) * LANES)
        signal = jnp.concatenate([piece[:, column] for piece in pieces], axis=0)
        value = signal.astype(jnp.float32) - scale * acc[tile, :rows, :]
        rb[:, column] = jnp.where(moment < total_time, value, 0.0).astype(jnp.bfloat16)


def stepped_codes(state, acc, limit):
    scale = (C * L) ** (-0.5)
    stepped = state + code_rate * (scale * acc[0, : state.shape[0], :])
    return stepped - jnp.clip(stepped, -limit, limit)


def iterate_kernel(total_time, patching, first_copied, plan_ref, limit_ref, *refs):
    take = taker(refs)
    state_ref, first_ref, second_ref, signal_ref, next_first, next_second = take(6)
    atoms = take(1 if patching else 0)
    (taps,) = take(1)
    source = take(2 if patching else 0)
    state_out, first_out, second_out, far_out = take(4)
    taps = (take(1) if patching else [taps])[0]
    target = take(1 if patching else 0)
    zb, rb, zz, rr, fine, acc, beyond = take(7)
    ferry = Ferry(source[0], target[0], first_copied, *take(2)) if patching else None
    segment, channels = signal_ref.shape
    zb[L : L + segment, :] = state_ref[...].astype(jnp.bfloat16)

    def put(left, right):
        zb[:L, :] = left[:, :K]
        zb[L + segment :, :] = right[:, :K]

    def put_signal(left, right):
        beyond[...] = right[:, K:]

    by_side(put, first_ref, second_ref)
    by_side(put_signal, next_first, next_second)
    if patching:
        columns, *turned = take(1 + GROUPS)
        patch_taps(first_row_of(plan_ref, patching - 1), atoms[0], taps, columns, turned)
        ferry.turn_round()
    convolve(zb, L, segment + L, taps, zz, fine, acc)
    start = lax.axis_index("tm") * segment
    residual_rows(rb, (signal_ref, beyond), start, acc, total_time)
    correlate(rb, segment, taps, rr, fine, acc)
    state = stepped_codes(state_ref[...], acc, limit_ref[...])
    state_out[...] = state
    low = state.astype(jnp.bfloat16)
    rest = (state - low.astype(jnp.float32)).astype(jnp.bfloat16)
    near, beyond_near = reaches(segment)
    put_edges((first_out, second_out), jnp.concatenate([low[-near:], rest[-L:]], axis=0), low[:L])
    if beyond_near:
        far_out[...] = low[-beyond_near:]
    else:
        far_out[...] = jnp.zeros_like(far_out)
    if ferry:
        ferry.close()


def iterate(plan, step, limit, state, swapped, signal, following, taps, atoms, ferry, peers):
    segment, channels = signal.shape
    patching = atoms is not None
    reach = segment + L
    near, beyond_near = reaches(segment)
    carried = [far(value) for value in ferry[:2]] if patching else []
    return pl.pallas_call(
        functools.partial(iterate_kernel, peers * segment, step if patching else 0, ferry[2]),
        in_specs=[scalars()] + [vmem()] * (8 + patching) + [hbm()] * len(carried),
        out_specs=[vmem()] * (4 + patching) + [hbm()] * patching,
        out_shape=[pltpu.VMEM((segment, K), jnp.float32)]
        + [jax.ShapeDtypeStruct((near + L, K), jnp.bfloat16)] * 2
        + [jax.ShapeDtypeStruct((max(beyond_near, ROWS), K), jnp.bfloat16)]
        + [pltpu.VMEM(taps.shape, jnp.bfloat16)] * patching
        + [pltpu.HBM(ferry[0].shape, jnp.float32)] * patching,
        scratch_shapes=[
            pltpu.VMEM((L + reach, K), jnp.bfloat16),
            pltpu.VMEM((reach, channels), jnp.bfloat16),
            pltpu.VMEM((reach + ROWS, COARSE * K), jnp.bfloat16),
            pltpu.VMEM((segment + ROWS, COARSE * channels), jnp.bfloat16),
            pltpu.VMEM((2 * FINE, channels // LANES, reach + ROWS, LANES), jnp.float32),
            pltpu.VMEM((channels // LANES, reach, LANES), jnp.float32),
            pltpu.VMEM((L, channels), jnp.bfloat16),
        ]
        + (
            ferry_scratch(ferry[3], ferry[0].shape[1])
            + [pltpu.VMEM((K, GROUPS * ROWS * L), jnp.bfloat16)]
            + [pltpu.VMEM((ROWS * STRIDE, K), jnp.float32)] * GROUPS
        )
        * patching,
        input_output_aliases={9: 4, 11: 5} if patching else {},
        compiler_params=pltpu.CompilerParams(vmem_limit_bytes=VMEM_BYTES),
        name="iterate",
    )(
        plan,
        limit,
        resident(state),
        *swapped,
        resident(signal),
        *following,
        *([resident(atoms)] if patching else []),
        resident(taps),
        *carried,
    )


def conclude_kernel(peers, step, plan_ref, limit_ref, *refs):
    last = step + 1 == OUTER
    take = taker(refs)
    state_ref, first_ref, second_ref, far_ref, signal_ref, next_first, next_second, taps = take(8)
    (payload_out,) = take(1)
    outs = take(2 if last else 3)
    zb, rb, zz, rr, fine, acc, before, beyond, earlier, tall = take(10)
    segment, channels = signal_ref.shape
    near, beyond_near = reaches(segment)
    zb[2 * L : 2 * L + segment, :] = state_ref[...].astype(jnp.bfloat16)
    if beyond_near:
        zb[:beyond_near, :] = far_ref[...]

    def put(left, right):
        zb[beyond_near : 2 * L, :] = left[:near]
        earlier[...] = left[near - L : near].astype(jnp.float32) + left[near:].astype(jnp.float32)
        zb[2 * L + segment :, :] = right[:L]

    def put_signal(left, right):
        before[...] = left[:, K:]
        beyond[...] = right[:, K:]

    by_side(put, first_ref, second_ref)
    by_side(put_signal, next_first, next_second)
    convolve(zb, L, 2 * L + segment, taps, zz, fine, acc)
    start = lax.axis_index("tm") * segment - L
    residual_rows(rb, (before, signal_ref, beyond), start, acc, peers * segment)
    correlate(rb, L + segment, taps, rr, fine, acc)
    state = jnp.concatenate([earlier[...], state_ref[...]], axis=0)
    state = stepped_codes(state, acc, limit_ref[...])
    moment = start + lax.broadcasted_iota(jnp.int32, state.shape, 0)
    state = jnp.where(moment >= 0, state, 0.0)
    low = state.astype(jnp.bfloat16)
    zb[: L + segment, :] = low
    own = state[L:]
    if last:
        resid_out, codes_out = outs
    else:
        state_out, *edges = outs
        (codes_out,) = take(1)
        state_out[...] = own
        put_edges(edges, low[-L:], low[L : 2 * L])
    codes_out[...] = own.T
    convolve(zb, L, segment, taps, zz, fine, acc)
    scale = (C * L) ** (-0.5)
    for tile in range(channels // LANES):
        column = slice(tile * LANES, (tile + 1) * LANES)
        value = signal_ref[:, column].astype(jnp.float32) - scale * acc[tile, :segment, :]
        value = value.T
        tall[column, :] = value
        if last:
            resid_out[column, :] = value
    block = codes_out[pl.ds(first_row_of(plan_ref, step), BLOCK_ATOMS), :].astype(jnp.bfloat16)
    share = channels // peers
    share_rows = payload_out.shape[1] - BLOCK_ATOMS
    tall[channels:, :] = jnp.zeros((tall.shape[0] - channels, segment), jnp.float32)
    for peer in range(peers):
        part = tall[peer * share : peer * share + share_rows, :]
        payload_out[peer, :share_rows, :] = part.astype(jnp.bfloat16)
        payload_out[peer, share_rows:, :] = block


def conclude(plan, step, limit, state, swapped, far_edge, signal, following, taps, peers):
    segment, channels = signal.shape
    share = channels // peers
    share_rows = -(-share // ROWS) * ROWS
    last = step + 1 == OUTER
    rows = 2 * L + segment
    outs = [
        pltpu.VMEM((channels, segment), jnp.float32),
        pltpu.VMEM((K, segment), jnp.float32),
    ]
    if not last:
        outs = [pltpu.VMEM((segment, K), jnp.float32)]
        outs += [jax.ShapeDtypeStruct((L, K), jnp.bfloat16)] * 2
    return pl.pallas_call(
        functools.partial(conclude_kernel, peers, step),
        in_specs=[scalars()] + [vmem()] * 9,
        out_specs=[vmem()] * (1 + len(outs)),
        out_shape=[jax.ShapeDtypeStruct((peers, share_rows + BLOCK_ATOMS, segment), jnp.bfloat16)]
        + outs,
        scratch_shapes=[
            pltpu.VMEM((rows + L, K), jnp.bfloat16),
            pltpu.VMEM((rows, channels), jnp.bfloat16),
            pltpu.VMEM((rows + ROWS, COARSE * K), jnp.bfloat16),
            pltpu.VMEM((L + segment + ROWS, COARSE * channels), jnp.bfloat16),
            pltpu.VMEM((2 * FINE, channels // LANES, rows + ROWS, LANES), jnp.float32),
            pltpu.VMEM((channels // LANES, rows, LANES), jnp.float32),
            pltpu.VMEM((L, channels), jnp.bfloat16),
            pltpu.VMEM((L, channels), jnp.bfloat16),
            pltpu.VMEM((L, K), jnp.float32),
            pltpu.VMEM((channels + ROWS, segment), jnp.float32),
        ]
        + ([] if last else [pltpu.VMEM((K, segment), jnp.float32)]),
        compiler_params=pltpu.CompilerParams(vmem_limit_bytes=VMEM_BYTES),
        name="conclude",
    )(
        plan,
        limit,
        resident(state),
        *swapped,
        far_edge,
        resident(signal),
        *following,
        resident(taps),
    )


def gradient_kernel(share, step, plan_ref, blocks_ref, dict_hbm, out_ref, rf, zf, rr, zz, old, sem):
    peers, rows, segment = blocks_ref.shape
    share_rows = rows - BLOCK_ATOMS
    span = peers * segment
    entries = share * L
    rows_of = pl.ds(first_row_of(plan_ref, step), BLOCK_ATOMS)
    columns_of = pl.ds(pl.multiple_of(lax.axis_index("tm") * entries, LANES), entries)
    fetch = pltpu.make_async_copy(dict_hbm.at[rows_of, columns_of], old, sem)
    fetch.start()
    rf[:, span:] = jnp.zeros((share_rows, LANES), jnp.bfloat16)
    zf[:, :LANES] = jnp.zeros((BLOCK_ATOMS, LANES), jnp.bfloat16)
    for peer in range(peers):
        column = peer * segment
        rf[:, column : column + segment] = blocks_ref[peer, :share_rows, :]
        zf[:, LANES + column : LANES + column + segment] = blocks_ref[peer, share_rows:, :]
    for lag in range(ROWS):
        rr[lag * share_rows : (lag + 1) * share_rows, :] = rf[:, lag : lag + span]
    for coarse in range(COARSE):
        begin = LANES - ROWS * coarse
        zz[coarse * BLOCK_ATOMS : (coarse + 1) * BLOCK_ATOMS, :] = zf[:, begin : begin + span]
    lagged = lax.dot_general(zz[...], rr[...], NT, preferred_element_type=jnp.float32)
    wide = ROWS * share_rows
    parts = []
    left = lagged
    for _ in range(3):
        parts.append(left.astype(jnp.bfloat16))
        left = left - parts[-1].astype(jnp.float32)
    row = lax.broadcasted_iota(jnp.int32, (wide, wide), 0)
    column = lax.broadcasted_iota(jnp.int32, (wide, wide), 1)
    chosen = (row // share_rows == column % ROWS) & (row % share_rows == column // ROWS)
    chosen = chosen.astype(jnp.float32).astype(jnp.bfloat16)
    by_channel = lax.dot_general(
        jnp.concatenate(parts, axis=0), chosen, NN, preferred_element_type=jnp.float32
    )
    count = COARSE * BLOCK_ATOMS
    by_channel = by_channel[:count] + by_channel[count : 2 * count] + by_channel[2 * count :]
    lane = lax.broadcasted_iota(jnp.int32, (BLOCK_ATOMS, LANES), 1)
    tiles = []
    for tile in range(entries // LANES):
        total = jnp.zeros((BLOCK_ATOMS, LANES), jnp.float32)
        for place in range(LANES // ROWS):
            channel, coarse = divmod(tile * (LANES // ROWS) + place, COARSE)
            first = channel * ROWS // LANES * LANES
            source = by_channel[coarse * BLOCK_ATOMS : (coarse + 1) * BLOCK_ATOMS, first : first + LANES]
            by = (place * ROWS - channel * ROWS) % LANES
            moved = pltpu.roll(source, by, 1) if by else source
            total = jnp.where(lane // ROWS == place, moved, total)
        tiles.append(total)
    gradient = jnp.concatenate(tiles, axis=1)
    fetch.wait()
    before = old[...]
    square = jnp.sum(before * before, axis=1, keepdims=True)
    along = jnp.sum(gradient * before, axis=1, keepdims=True) / (square + tiny_eps)
    out_ref[:, :entries] = (gradient - along * before).astype(jnp.bfloat16)
    terms = jnp.zeros((BLOCK_ATOMS, LANES), jnp.float32)
    for i in range(3):
        term = along.astype(jnp.bfloat16).astype(jnp.float32)
        along = along - term
        terms = jnp.where(lane == i, term, terms)
    out_ref[:, entries:] = terms.astype(jnp.bfloat16)


def share_gradient(plan, step, blocks, dictionary, share):
    peers, rows, segment = blocks.shape
    share_rows = rows - BLOCK_ATOMS
    span = peers * segment
    return pl.pallas_call(
        functools.partial(gradient_kernel, share, step),
        in_specs=[scalars(), vmem(), hbm()],
        out_shape=jax.ShapeDtypeStruct((BLOCK_ATOMS, share * L + LANES), jnp.bfloat16),
        scratch_shapes=[
            pltpu.VMEM((share_rows, span + LANES), jnp.bfloat16),
            pltpu.VMEM((BLOCK_ATOMS, LANES + span), jnp.bfloat16),
            pltpu.VMEM((ROWS * share_rows, span), jnp.bfloat16),
            pltpu.VMEM((COARSE * BLOCK_ATOMS, span), jnp.bfloat16),
            pltpu.VMEM((BLOCK_ATOMS, share * L), jnp.float32),
            pltpu.SemaphoreType.DMA,
        ],
        compiler_params=pltpu.CompilerParams(vmem_limit_bytes=VMEM_BYTES),
        name="gradient",
    )(plan, blocks, far(dictionary))


def gather_steps(peers):
    bits = [1 << i for i in range(peers.bit_length() - 2, 0, -1)]
    steps = []
    for first in range(0, len(bits), 2):
        pair = bits[first : first + 2]
        steps.append(pair + [sum(pair)] if len(pair) == 2 else pair)
    return steps


def gather_slots(peers):
    flips = [0]
    for masks in gather_steps(peers):
        flips = [f ^ m for m in [0] + masks for f in flips]
    return flips


def gather_pieces(piece, meanwhile):
    peers = lax.axis_size("tm")

    def exchanged(shard, mask):
        return lax.ppermute(shard, "tm", [(i, i ^ mask) for i in range(peers)])

    held = piece[None]
    for index, masks in enumerate(gather_steps(peers)):
        held = jnp.concatenate([held] + [exchanged(held, mask) for mask in masks], axis=0)
        if index == 0:
            needed, extra = meanwhile(held)
    ready, _ = lax.optimization_barrier((held, needed))
    return held, exchanged(ready, 1), extra


def recall_kernel(step, earlier, plan_ref, dict_hbm, when_ref, *refs):
    del when_ref
    take = taker(refs)
    earlier_refs = take(earlier)
    take(1 if earlier else 0)
    old_ref, mean_ref = take(2)
    target = take(1 if earlier else 0)
    (sem,) = take(1)
    fetch = pltpu.make_async_copy(
        dict_hbm.at[pl.ds(first_row_of(plan_ref, step), BLOCK_ATOMS)], old_ref, sem
    )
    fetch.start()
    if earlier:
        ferry = Ferry(dict_hbm, target[0], sum(COPIED[:-1]), *take(2))
    fetch.wait()
    if earlier:
        ferry.turn_round()
    width = 9 * LANES if old_ref.shape[1] % (9 * LANES) == 0 else LANES

    def add(step, square):
        before = old_ref[:, pl.ds(pl.multiple_of(step * width, LANES), width)]
        return square + before * before

    square = lax.fori_loop(
        0, old_ref.shape[1] // width, add, jnp.zeros((BLOCK_ATOMS, width), jnp.float32)
    )
    mean_sq = jnp.sum(square, axis=1, keepdims=True) / (C * L) + tiny_eps
    mean_ref[...] = jnp.broadcast_to(mean_sq, mean_ref.shape)
    if earlier:
        ferry.close()
        stores = [
            pltpu.make_async_copy(
                earlier_refs[index],
                target[0].at[pl.ds(first_row_of(plan_ref, index), BLOCK_ATOMS)],
                sem,
            )
            for index in range(earlier)
        ]
        for store in stores:
            store.start()
            store.wait()


def recall(plan, step, dictionary, when, renewed, copied):
    entries = dictionary.shape[1]
    earlier = len(renewed)
    return pl.pallas_call(
        functools.partial(recall_kernel, step, earlier),
        in_specs=[scalars(), hbm(), pl.BlockSpec(memory_space=pl.ANY)]
        + [vmem()] * earlier
        + [hbm()] * (earlier > 0),
        out_specs=[vmem(), vmem()] + [hbm()] * (earlier > 0),
        out_shape=[
            pltpu.VMEM((BLOCK_ATOMS, entries), jnp.float32),
            jax.ShapeDtypeStruct((BLOCK_ATOMS, LANES), jnp.float32),
        ]
        + [pltpu.HBM(dictionary.shape, jnp.float32)] * (earlier > 0),
        scratch_shapes=[pltpu.SemaphoreType.DMA]
        + (ferry_scratch(COPIED[-1], entries) if earlier else []),
        input_output_aliases={3 + earlier: 2} if earlier else {},
        compiler_params=pltpu.CompilerParams(vmem_limit_bytes=VMEM_BYTES),
        name="recall",
    )(
        plan,
        far(dictionary),
        when,
        *[resident(value) for value in renewed],
        *([far(copied)] if earlier else []),
    )


def renew_kernel(plan_step, plan_ref, held_ref, came_ref, old, mean_ref, *refs):
    me = lax.axis_index("tm")
    half, _, wide = held_ref.shape
    width = wide - LANES
    entries = C * L
    last = plan_step + 1 == OUTER
    if last:
        _, out_hbm, atoms_ref, grad, sems = refs
    else:
        atoms_ref, grad = refs

    stores = []
    shares = []
    for slot, flips in enumerate(gather_slots(2 * half)):
        for source, extra in ((held_ref, 0), (came_ref, 1)):
            owner = me ^ (flips + extra)
            shares.append((source.at[slot], pl.ds(pl.multiple_of(owner * width, LANES), width)))
    zeros = jnp.zeros((BLOCK_ATOMS, width), jnp.float32)
    dot = zeros
    for source, column in shares:
        before = old[:, column]
        along = jnp.sum(source[:, width:].astype(jnp.float32), axis=1, keepdims=True)
        value = source[:, :width].astype(jnp.float32) + along * before
        grad[:, column] = value
        dot += value * before
    mean_sq = mean_ref[:, :1]
    along = jnp.sum(dot, axis=1, keepdims=True) / entries / mean_sq
    square = zeros
    for _, column in shares:
        value = grad[:, column] - along * old[:, column]
        square += value * value
    spread = jnp.sum(square, axis=1, keepdims=True) / entries + tiny_eps
    step = move_rate / jnp.sqrt(spread)
    norm = 1.0 / jnp.sqrt(mean_sq + 0.25)
    rows = pl.ds(first_row_of(plan_ref, plan_step), BLOCK_ATOMS)
    for index, (_, column) in enumerate(shares):
        before = old[:, column]
        across = grad[:, column] - along * before
        atoms_ref[:, column] = (before + step * across) * norm
        if last:
            stores.append(
                pltpu.make_async_copy(
                    atoms_ref.at[:, column], out_hbm.at[rows, column], sems.at[index]
                )
            )
            stores[-1].start()
    for store in stores:
        store.wait()


def renew(plan, step, held, came, old, mean_sq, dictionary):
    last = dictionary is not None
    atoms = (BLOCK_ATOMS, old.shape[1])
    scratch = [pltpu.VMEM(atoms, jnp.float32)]
    if last:
        scratch = scratch * 2 + [pltpu.SemaphoreType.DMA((2 * held.shape[0],))]
    return pl.pallas_call(
        functools.partial(renew_kernel, step),
        in_specs=[scalars()] + [vmem()] * 4 + [hbm()] * last,
        out_specs=hbm() if last else vmem(),
        out_shape=pltpu.HBM(dictionary.shape, jnp.float32) if last else pltpu.VMEM(atoms, jnp.float32),
        scratch_shapes=scratch,
        input_output_aliases={5: 0} if last else {},
        compiler_params=pltpu.CompilerParams(vmem_limit_bytes=VMEM_BYTES),
        name="renew",
    )(plan, held, came, resident(old), mean_sq, *([far(dictionary)] if last else []))


def whole_channels(signal, codes_init, dictionary_init, threshold, plan):
    channels, segment = signal.shape
    peers = lax.axis_size("tm")
    limit = threshold[None, :]
    def swaps(edges):
        ends = [range(first, peers - 1, 2) for first in (0, 1)]
        pairs = [[p for i in end for p in ((i, i + 1), (i + 1, i))] for end in ends]
        far_first = [lax.ppermute(edge, "tm", pair) for edge, pair in zip(edges[::-1], pairs[::-1])]
        return far_first[::-1]

    state, signal, *edges = begin(codes_init, signal)
    following = swaps(edges)
    swapped = following
    taps, dictionary = layout(dictionary_init, channels)
    renewed = []
    for step in range(OUTER):
        last = step + 1 == OUTER
        ferry = (dictionary_init, dictionary, COPIED[0], COPIED[1])
        atoms = renewed[-1] if renewed else None
        state, *results = iterate(
            plan, step, limit, state, swapped, signal, following, taps, atoms, ferry, peers
        )
        edges, far_edge = results[:2], results[2]
        if renewed:
            taps, dictionary = results[3:]
        beyond = shifted(far_edge, "tm", 2)
        payload, *results = conclude(
            plan, step, limit, state, swaps(edges), beyond, signal, following, taps, peers
        )
        blocks = lax.all_to_all(payload, "tm", 0, 0, tiled=True)
        piece = share_gradient(plan, step, blocks, dictionary_init, channels // peers)
        recalled = []
        if not last:
            recalled.extend(recall(plan, step, dictionary_init, piece, [], None))

        def beside(held):
            if last:
                recalled.extend(recall(plan, step, dictionary_init, held, renewed, dictionary))
                return recalled[0], None
            state, *edges = results
            edges, _ = lax.optimization_barrier((edges, held))
            return recalled[0], swaps(edges)

        held, came, extra = gather_pieces(piece, beside)
        old, mean_sq, *copied = recalled
        result = renew(plan, step, held, came, old, mean_sq, copied[0] if last else None)
        if last:
            dictionary = result
        else:
            renewed.append(result)
            state, swapped = results[0], extra
    residual, codes = results
    return codes, dictionary, residual


def renew_atoms(old_atoms, across, mean_sq, spread):
    return (old_atoms + move_rate * across / jnp.sqrt(spread)[:, None]) / jnp.sqrt(mean_sq + 0.25)[
        :, None
    ]


def split_channels(signal, codes_init, dictionary_init, threshold, plan):
    segment = signal.shape[1]
    local_chan = signal.shape[0]
    unit_scale = (C * L) ** (-0.5)
    entries = C * L
    limit = threshold[:, None]

    def convolve(atom_cube, code_low):
        code_edge = shifted(code_low[:, segment - (L - 1) :], "tm", 1)
        extended = jnp.concatenate([code_edge, code_low], axis=1)
        lagged = jnp.stack(
            [extended[:, L - 1 - offset : L - 1 - offset + segment] for offset in range(L)], axis=1
        )
        return unit_scale * jnp.einsum(
            "kcl,klt->ct", atom_cube, lagged, preferred_element_type=jnp.float32
        )

    def resid_columns(resid_low):
        resid_edge = shifted(resid_low[:, : L - 1], "tm", -1)
        extended = jnp.concatenate([resid_low, resid_edge], axis=1)
        lagged = jnp.stack([extended[:, offset : offset + segment] for offset in range(L)], axis=1)
        return lagged.reshape(local_chan * L, segment)

    code_state = codes_init
    dictionary = dictionary_init
    residual = signal.astype(jnp.float32)
    for outer_step in range(OUTER):
        dict_low = dictionary.astype(jnp.bfloat16)
        atom_cube = dict_low.reshape(K, local_chan, L)
        for inner_step in range(INNER):
            code_low = code_state.astype(jnp.bfloat16)
            residual = signal.astype(jnp.float32) - convolve(atom_cube, code_low)
            lagged = resid_columns(residual.astype(jnp.bfloat16))
            partial_value = unit_scale * jnp.dot(
                dict_low, lagged, preferred_element_type=jnp.float32
            )
            scores = lax.psum(partial_value.astype(jnp.bfloat16), "chan").astype(jnp.float32)
            stepped = code_state + code_rate * scores
            code_state = stepped - jnp.clip(stepped, -limit, limit)
        code_low = code_state.astype(jnp.bfloat16)
        residual = signal.astype(jnp.float32) - convolve(atom_cube, code_low)
        lagged = resid_columns(residual.astype(jnp.bfloat16))
        first_row = plan[outer_step] * BLOCK_ATOMS
        code_block = lax.dynamic_slice_in_dim(code_low, first_row, BLOCK_ATOMS, 0)
        local_grad = lax.dot_general(
            code_block, lagged, (((1,), (1,)), ((), ())), preferred_element_type=jnp.float32
        )
        old_atoms = lax.dynamic_slice_in_dim(dictionary, first_row, BLOCK_ATOMS, 0)
        gradient = lax.psum(local_grad, "tm")
        dot_sum, square_sum = lax.psum(
            (jnp.sum(gradient * old_atoms, axis=1), jnp.sum(old_atoms * old_atoms, axis=1)), "chan"
        )
        mean_sq = square_sum / entries + tiny_eps
        along_coef = dot_sum / entries / mean_sq
        across = gradient - along_coef[:, None] * old_atoms
        spread = lax.psum(jnp.sum(across * across, axis=1), "chan") / entries + tiny_eps
        renewed = renew_atoms(old_atoms, across, mean_sq, spread)
        dictionary = lax.dynamic_update_slice_in_dim(dictionary, renewed, first_row, 0)
    return (code_state, dictionary, residual)


def shards(signal, codes_init, dictionary_init, threshold, plan):
    channels, segment = signal.shape
    peers = lax.axis_size("tm")
    fits = (
        lax.axis_size("chan") == 1
        and segment % LANES == 0
        and INNER == 2
        and OUTER == 2
        and channels % (GROUPS * ROWS) == 0
        and channels % LANES == 0
        and channels % peers == 0
        and (channels // peers * L) % LANES == 0
        and peers > 2
        and peers & (peers - 1) == 0
    )
    body = whole_channels if fits else split_channels
    return body(signal, codes_init, dictionary_init, threshold, plan)


def solution(mesh):
    placed = (P("chan", "tm"), P(None, "tm"), P(None, "chan"), P(), P())
    return jax.shard_map(
        shards,
        mesh=mesh,
        in_specs=placed,
        out_specs=(P(None, "tm"), P(None, "chan"), P("chan", "tm")),
        check_vma=False,
    )
```

```python
import functools

import jax
import jax.numpy as jnp
from jax import lax
from jax.experimental import pallas as pl
from jax.experimental.pallas import tpu as pltpu
from jax.sharding import PartitionSpec as P

C = 384
K = 128
L = 96
BLOCK_ATOMS = 16
INNER = 2
OUTER = 2

code_rate = 0.3
move_rate = 0.5
tiny_eps = 1e-06

ROWS = 16
COARSE = L // ROWS
STRIDE = L + 1
GROUPS = 4
SUBLANES = 8
COPIED = (48, 40, 40)
FINE = 4
LANES = 128
VMEM_BYTES = 24 * 1024 * 1024

NN = (((1,), (0,)), ((), ()))
NT = (((1,), (1,)), ((), ()))


def shifted(shard, axis, by):
    peers = lax.axis_size(axis)
    pairs = [(i, i + by) for i in range(peers) if 0 <= i + by < peers]
    return lax.ppermute(shard, axis, pairs)


def resident(value):
    return pltpu.with_memory_space_constraint(value, pltpu.VMEM)


def far(value):
    return pltpu.with_memory_space_constraint(value, pltpu.HBM)


def hbm():
    return pl.BlockSpec(memory_space=pltpu.HBM)


def scalars():
    return pl.BlockSpec(memory_space=pltpu.SMEM)


def first_row_of(plan_ref, step):
    return pl.multiple_of(plan_ref[step] * BLOCK_ATOMS, BLOCK_ATOMS)


def vmem():
    return pl.BlockSpec(memory_space=pltpu.VMEM)


def turn(columns, turned_ref):
    side = 2 * LANES
    row = lax.broadcasted_iota(jnp.int32, (side, side), 0)
    column = lax.broadcasted_iota(jnp.int32, (side, side), 1)
    identity = (row == column).astype(jnp.float32).astype(jnp.bfloat16)

    def put(entry, rows):
        end = entry + rows.shape[0]
        begin = entry
        while begin < end:
            channel, tap = begin // L, begin % L
            count = min(end - begin, L - tap)
            target = channel * STRIDE + tap
            turned_ref[target : target + count, :] = rows[begin - entry : begin - entry + count]
            begin += count

    low = columns.astype(jnp.bfloat16)
    through_matrix = ROWS * L // (6 * side) * 4 * side
    for first in range(0, through_matrix, 2 * side):
        pair = jnp.concatenate(
            [low[:, first + half * side : first + (half + 1) * side] for half in range(2)], axis=0
        )
        turned = lax.dot_general(identity, pair, NT, preferred_element_type=jnp.float32)
        for half in range(2):
            put(first + half * side, turned[:, half * K : (half + 1) * K])
    for first in range(through_matrix, ROWS * L, LANES):
        put(first, columns[:, first : first + LANES].astype(jnp.float32).T)


def tap_of(turned_ref, tap):
    return turned_ref[pl.ds(tap, ROWS, stride=STRIDE), :].astype(jnp.bfloat16)


def layout_kernel(dict_ref, taps_ref, *turned):
    def part(group):
        return dict_ref[:, group * ROWS * L : (group + 1) * ROWS * L]

    turn(part(0), turned[0])
    for group in range(GROUPS):
        if group + 1 < GROUPS:
            turn(part(group + 1), turned[group + 1])
        own = pl.ds(pl.multiple_of((pl.program_id(0) * GROUPS + group) * ROWS, ROWS), ROWS)
        for tap in range(L):
            taps_ref[tap // ROWS, tap % ROWS, own, :] = tap_of(turned[group], tap)


def layout(dictionary, channels):
    block = GROUPS * ROWS
    return pl.pallas_call(
        layout_kernel,
        grid=(channels // block,),
        in_specs=[pl.BlockSpec((K, block * L), lambda i: (0, i))],
        out_specs=vmem(),
        out_shape=pltpu.VMEM((COARSE, ROWS, channels, K), jnp.bfloat16),
        scratch_shapes=[pltpu.VMEM((ROWS * STRIDE, K), jnp.float32)] * GROUPS,
        compiler_params=pltpu.CompilerParams(vmem_limit_bytes=VMEM_BYTES),
        name="layout",
    )(far(dictionary))


class Ferry:
    def __init__(self, source, target, first, buffer, sems):
        self.steps = []
        for step in range(buffer.shape[0] // SUBLANES):
            held = buffer.at[pl.ds(step * SUBLANES, SUBLANES)]
            rows = pl.ds(first + step * SUBLANES, SUBLANES)
            fetch = pltpu.make_async_copy(source.at[rows], held, sems.at[0, step])
            store = pltpu.make_async_copy(held, target.at[rows], sems.at[1, step])
            fetch.start()
            self.steps.append((fetch, store))

    def turn_round(self):
        for fetch, store in self.steps:
            fetch.wait()
            store.start()

    def close(self):
        for _, store in self.steps:
            store.wait()


def ferry_scratch(count, entries):
    return [
        pltpu.VMEM((count, entries), jnp.float32),
        pltpu.SemaphoreType.DMA((2, count // SUBLANES)),
    ]


def convolve(zb, begin, count, taps, zz, fine, acc):
    channels = taps.shape[2]
    tiles = channels // LANES
    rows = count + ROWS
    for coarse in range(COARSE):
        first = begin - ROWS - ROWS * coarse
        zz[:rows, coarse * K : (coarse + 1) * K] = zb[first : first + rows, :]
    for lag in range(0, ROWS, FINE):
        slot = lag // FINE % 2 * FINE
        for pair in range(0, FINE, 2):
            weights = jnp.concatenate(
                [
                    jnp.concatenate([taps[m, lag + pair + j] for m in range(COARSE)], axis=1)
                    for j in range(2)
                ],
                axis=0,
            )
            product = lax.dot_general(zz[:rows, :], weights, NT, preferred_element_type=jnp.float32)
            for j in range(2):
                for tile in range(tiles):
                    column = j * channels + tile * LANES
                    fine[slot + pair + j, tile, :rows, :] = product[:, column : column + LANES]
        for tile in range(tiles):
            total = None if lag == 0 else acc[tile, :count, :]
            for j in range(FINE):
                first = ROWS - lag - j
                part = fine[slot + j, tile, first : first + count, :]
                total = part if total is None else total + part
            acc[tile, :count, :] = total


def correlate(rb, count, taps, rr, fine, acc):
    channels = taps.shape[2]
    rows = count + ROWS
    for coarse in range(COARSE):
        first = ROWS * coarse
        rr[:rows, coarse * channels : (coarse + 1) * channels] = rb[first : first + rows, :]
    for lag in range(0, ROWS, FINE):
        slot = lag // FINE % 2 * FINE
        for pair in range(0, FINE, 2):
            weights = jnp.concatenate(
                [
                    jnp.concatenate([taps[m, lag + pair + j] for m in range(COARSE)], axis=0)
                    for j in range(2)
                ],
                axis=1,
            )
            product = lax.dot_general(rr[:rows, :], weights, NN, preferred_element_type=jnp.float32)
            for j in range(2):
                fine[slot + pair + j, 0, :rows, :] = product[:, j * K : (j + 1) * K]
        total = None if lag == 0 else acc[0, :count, :]
        for j in range(FINE):
            part = fine[slot + j, 0, lag + j : lag + j + count, :]
            total = part if total is None else total + part
        acc[0, :count, :] = total


def patch_taps(row, atoms_ref, taps, columns, turned):
    channels = taps.shape[2]
    lane = lax.broadcasted_iota(jnp.int32, (ROWS, K), 1)
    kept = (lane < row) | (lane >= row + BLOCK_ATOMS)
    keep = kept.astype(jnp.float32).astype(jnp.bfloat16)
    columns[...] = jnp.zeros_like(columns)
    width = ROWS * L

    def patch(step, carry):
        part = pl.ds(pl.multiple_of(step * (GROUPS * width), LANES), GROUPS * width)
        columns[pl.ds(row, BLOCK_ATOMS), :] = atoms_ref[:, part].astype(jnp.bfloat16)
        turn(columns[:, :width], turned[0])
        for group in range(GROUPS):
            if group + 1 < GROUPS:
                turn(columns[:, (group + 1) * width : (group + 2) * width], turned[group + 1])
            own = pl.ds(pl.multiple_of((step * GROUPS + group) * ROWS, ROWS), ROWS)
            for tap in range(L):
                before = taps[tap // ROWS, tap % ROWS, own, :]
                taps[tap // ROWS, tap % ROWS, own, :] = before * keep + tap_of(turned[group], tap)
        return carry

    lax.fori_loop(0, channels // (GROUPS * ROWS), patch, 0)


def put_edges(edge_refs, rightward, leftward):
    even = lax.axis_index("tm") % 2 == 0

    def put(first, second):
        first[...] = rightward
        second[...] = leftward

    pl.when(even)(lambda: put(*edge_refs))
    pl.when(jnp.logical_not(even))(lambda: put(*edge_refs[::-1]))


def by_side(put, first_ref, second_ref):
    even = lax.axis_index("tm") % 2 == 0
    pl.when(even)(lambda: put(second_ref, first_ref))
    pl.when(jnp.logical_not(even))(lambda: put(first_ref, second_ref))


def begin_kernel(code_hbm, signal_hbm, state_out, signal_out, first_out, second_out, code_ref, signal_ref, sems):
    fetches = [
        pltpu.make_async_copy(code_hbm, code_ref, sems.at[0]),
        pltpu.make_async_copy(signal_hbm, signal_ref, sems.at[1]),
    ]
    for fetch in fetches:
        fetch.start()
    for fetch in fetches:
        fetch.wait()
    state = code_ref[...].T
    signal = signal_ref[...].astype(jnp.float32).T.astype(jnp.bfloat16)
    state_out[...] = state
    signal_out[...] = signal
    both = jnp.concatenate([state.astype(jnp.bfloat16), signal], axis=1)
    put_edges((first_out, second_out), both[-L:], both[:L])


def begin(code, signal):
    channels, segment = signal.shape
    return pl.pallas_call(
        begin_kernel,
        in_specs=[hbm()] * 2,
        out_specs=[vmem()] * 4,
        out_shape=[
            pltpu.VMEM((segment, K), jnp.float32),
            pltpu.VMEM((segment, channels), jnp.bfloat16),
        ]
        + [jax.ShapeDtypeStruct((L, K + channels), jnp.bfloat16)] * 2,
        scratch_shapes=[
            pltpu.VMEM(code.shape, code.dtype),
            pltpu.VMEM(signal.shape, signal.dtype),
            pltpu.SemaphoreType.DMA((2,)),
        ],
        compiler_params=pltpu.CompilerParams(vmem_limit_bytes=VMEM_BYTES),
        name="begin",
    )(far(code), far(signal))


def taker(refs):
    refs = list(refs)

    def take(count):
        taken = refs[:count]
        del refs[:count]
        return taken

    return take


def residual_rows(rb, pieces, start, acc, total_time):
    rows = rb.shape[0]
    moment = start + lax.broadcasted_iota(jnp.int32, (rows, LANES), 0)
    scale = (C * L) ** (-0.5)
    for tile in range(acc.shape[0]):
        column = slice(tile * LANES, (tile + 1) * LANES)
        signal = jnp.concatenate([piece[:, column] for piece in pieces], axis=0)
        value = signal.astype(jnp.float32) - scale * acc[tile, :rows, :]
        rb[:, column] = jnp.where(moment < total_time, value, 0.0).astype(jnp.bfloat16)


def stepped_codes(state, acc, limit):
    scale = (C * L) ** (-0.5)
    stepped = state + code_rate * (scale * acc[0, : state.shape[0], :])
    return stepped - jnp.clip(stepped, -limit, limit)


def iterate_kernel(total_time, patching, first_copied, plan_ref, limit_ref, *refs):
    take = taker(refs)
    state_ref, first_ref, second_ref, signal_ref, next_first, next_second = take(6)
    atoms = take(1 if patching else 0)
    (taps,) = take(1)
    source = take(2 if patching else 0)
    state_out, *edges = take(3)
    taps = (take(1) if patching else [taps])[0]
    target = take(1 if patching else 0)
    zb, rb, zz, rr, fine, acc, beyond = take(7)
    ferry = Ferry(source[0], target[0], first_copied, *take(2)) if patching else None
    segment, channels = signal_ref.shape
    zb[L : L + segment, :] = state_ref[...].astype(jnp.bfloat16)

    def put(left, right):
        zb[:L, :] = left[:, :K]
        zb[L + segment :, :] = right[:, :K]

    def put_signal(left, right):
        beyond[...] = right[:, K:]

    by_side(put, first_ref, second_ref)
    by_side(put_signal, next_first, next_second)
    if patching:
        columns, *turned = take(1 + GROUPS)
        patch_taps(first_row_of(plan_ref, patching - 1), atoms[0], taps, columns, turned)
        ferry.turn_round()
    convolve(zb, L, segment + L, taps, zz, fine, acc)
    start = lax.axis_index("tm") * segment
    residual_rows(rb, (signal_ref, beyond), start, acc, total_time)
    correlate(rb, segment, taps, rr, fine, acc)
    state = stepped_codes(state_ref[...], acc, limit_ref[...])
    state_out[...] = state
    low = state.astype(jnp.bfloat16)
    put_edges(edges, low[-L:], low[:L])
    if ferry:
        ferry.close()


def iterate(plan, step, limit, state, swapped, signal, following, taps, atoms, ferry, peers):
    segment, channels = signal.shape
    patching = atoms is not None
    reach = segment + L
    carried = [far(value) for value in ferry[:2]] if patching else []
    return pl.pallas_call(
        functools.partial(iterate_kernel, peers * segment, step if patching else 0, ferry[2]),
        in_specs=[scalars()] + [vmem()] * (8 + patching) + [hbm()] * len(carried),
        out_specs=[vmem()] * (3 + patching) + [hbm()] * patching,
        out_shape=[pltpu.VMEM((segment, K), jnp.float32)]
        + [jax.ShapeDtypeStruct((L, K), jnp.bfloat16)] * 2
        + [pltpu.VMEM(taps.shape, jnp.bfloat16)] * patching
        + [pltpu.HBM(ferry[0].shape, jnp.float32)] * patching,
        scratch_shapes=[
            pltpu.VMEM((L + reach, K), jnp.bfloat16),
            pltpu.VMEM((reach, channels), jnp.bfloat16),
            pltpu.VMEM((reach + ROWS, COARSE * K), jnp.bfloat16),
            pltpu.VMEM((segment + ROWS, COARSE * channels), jnp.bfloat16),
            pltpu.VMEM((2 * FINE, channels // LANES, reach + ROWS, LANES), jnp.float32),
            pltpu.VMEM((channels // LANES, reach, LANES), jnp.float32),
            pltpu.VMEM((L, channels), jnp.bfloat16),
        ]
        + (
            ferry_scratch(ferry[3], ferry[0].shape[1])
            + [pltpu.VMEM((K, GROUPS * ROWS * L), jnp.bfloat16)]
            + [pltpu.VMEM((ROWS * STRIDE, K), jnp.float32)] * GROUPS
        )
        * patching,
        input_output_aliases={9: 3, 11: 4} if patching else {},
        compiler_params=pltpu.CompilerParams(vmem_limit_bytes=VMEM_BYTES),
        name="iterate",
    )(
        plan,
        limit,
        resident(state),
        *swapped,
        resident(signal),
        *following,
        *([resident(atoms)] if patching else []),
        resident(taps),
        *carried,
    )


def conclude_kernel(peers, step, copied, plan_ref, limit_ref, *refs):
    last = step + 1 == OUTER
    take = taker(refs)
    state_ref, first_ref, second_ref, signal_ref, next_first, next_second, taps = take(7)
    source = take(2 if copied else 1)[0]
    (payload_out,) = take(1)
    state_out, partial_out, codes_out = (None, *take(2)) if last else (*take(1), None, None)
    *edges, target = take(3)
    zb, rb, zz, rr, fine, acc, beyond, tall = take(8)
    ferry = Ferry(source, target, copied, *take(2))
    if not last:
        (codes_out,) = take(1)
    segment, channels = signal_ref.shape
    reach = segment + L
    zb[L:reach, :] = state_ref[...].astype(jnp.bfloat16)

    def put(left, right):
        zb[:L, :] = left[...]
        zb[reach:, :] = right[...]

    def put_signal(left, right):
        beyond[...] = right[:, K:]

    by_side(put, first_ref, second_ref)
    by_side(put_signal, next_first, next_second)
    convolve(zb, L, reach, taps, zz, fine, acc)
    ferry.turn_round()
    start = lax.axis_index("tm") * segment
    residual_rows(rb, (signal_ref, beyond), start, acc, peers * segment)
    correlate(rb, segment, taps, rr, fine, acc)
    state = stepped_codes(state_ref[...], acc, limit_ref[...])
    low = state.astype(jnp.bfloat16)
    if not last:
        state_out[...] = state
    put_edges(edges, low[-L:], low[:L])
    codes_out[...] = state.T
    zb[:L, :] = jnp.zeros((L, K), jnp.bfloat16)
    zb[L:reach, :] = low
    zb[reach:, :] = jnp.zeros((L, K), jnp.bfloat16)
    convolve(zb, L, reach, taps, zz, fine, acc)
    scale = (C * L) ** (-0.5)
    block = codes_out[pl.ds(first_row_of(plan_ref, step), BLOCK_ATOMS), :].astype(jnp.bfloat16)
    share = channels // peers
    share_rows = (payload_out.shape[1] - BLOCK_ATOMS) // 2
    unused = jnp.zeros((tall.shape[1] - channels, segment), jnp.float32)
    for tile in range(channels // LANES):
        column = slice(tile * LANES, (tile + 1) * LANES)
        value = signal_ref[:, column].astype(jnp.float32) - scale * acc[tile, :segment, :]
        if last:
            partial_out[:, column] = value
        tall[0, column, :] = value.T
        spill = jnp.concatenate(
            [-scale * acc[tile, segment:reach, :], jnp.zeros((segment - L, LANES), jnp.float32)], axis=0
        )
        tall[1, column, :] = spill.T
    for part in range(2):
        tall[part, channels:, :] = unused
    for peer in range(peers):
        for part in range(2):
            rows = tall[part, peer * share : peer * share + share_rows, :]
            payload_out[peer, part * share_rows : (part + 1) * share_rows, :] = rows.astype(jnp.bfloat16)
        payload_out[peer, 2 * share_rows :, :] = block
    ferry.close()


def conclude(plan, step, limit, state, swapped, signal, following, taps, ferry, peers):
    segment, channels = signal.shape
    share = channels // peers
    share_rows = -(-share // ROWS) * ROWS
    last = step + 1 == OUTER
    carried = [far(value) for value in ferry[:2] if value is not None]
    reach = segment + L
    outs = [pltpu.VMEM((segment, K), jnp.float32)]
    if last:
        outs = [pltpu.VMEM((segment, channels), jnp.float32), pltpu.VMEM((K, segment), jnp.float32)]
    outs += [jax.ShapeDtypeStruct((L, K), jnp.bfloat16)] * 2
    return pl.pallas_call(
        functools.partial(conclude_kernel, peers, step, ferry[2]),
        in_specs=[scalars()] + [vmem()] * 8 + [hbm()] * len(carried),
        out_specs=[vmem()] * (1 + len(outs)) + [hbm()],
        out_shape=[jax.ShapeDtypeStruct((peers, 2 * share_rows + BLOCK_ATOMS, segment), jnp.bfloat16)]
        + outs
        + [pltpu.HBM(ferry[0].shape, jnp.float32)],
        scratch_shapes=[
            pltpu.VMEM((L + reach, K), jnp.bfloat16),
            pltpu.VMEM((reach, channels), jnp.bfloat16),
            pltpu.VMEM((reach + ROWS, COARSE * K), jnp.bfloat16),
            pltpu.VMEM((segment + ROWS, COARSE * channels), jnp.bfloat16),
            pltpu.VMEM((2 * FINE, channels // LANES, reach + ROWS, LANES), jnp.float32),
            pltpu.VMEM((channels // LANES, reach, LANES), jnp.float32),
            pltpu.VMEM((L, channels), jnp.bfloat16),
            pltpu.VMEM((2, channels + ROWS, segment), jnp.float32),
        ]
        + ferry_scratch(ferry[3], ferry[0].shape[1])
        + ([] if last else [pltpu.VMEM((K, segment), jnp.float32)]),
        input_output_aliases={10: 1 + len(outs)} if len(carried) == 2 else {},
        compiler_params=pltpu.CompilerParams(vmem_limit_bytes=VMEM_BYTES),
        name="conclude",
    )(
        plan,
        limit,
        resident(state),
        *swapped,
        resident(signal),
        *following,
        resident(taps),
        *carried,
    )


def settle_kernel(partial_ref, first_ref, second_ref, taps, resid_out, zb, zz, fine, acc):
    segment, channels = partial_ref.shape

    def put(left, right):
        zb[:L, :] = left[...]

    zb[L:, :] = jnp.zeros((L, K), jnp.bfloat16)
    by_side(put, first_ref, second_ref)
    convolve(zb, L, L, taps, zz, fine, acc)
    scale = (C * L) ** (-0.5)
    for tile in range(channels // LANES):
        column = slice(tile * LANES, (tile + 1) * LANES)
        value = jnp.concatenate(
            [partial_ref[:L, column] - scale * acc[tile], partial_ref[L:, column]], axis=0
        )
        resid_out[column, :] = value.T


def settle(partial, swapped, taps):
    segment, channels = partial.shape
    return pl.pallas_call(
        settle_kernel,
        in_specs=[vmem()] * 4,
        out_specs=vmem(),
        out_shape=pltpu.VMEM((channels, segment), jnp.float32),
        scratch_shapes=[
            pltpu.VMEM((2 * L, K), jnp.bfloat16),
            pltpu.VMEM((L + ROWS, COARSE * K), jnp.bfloat16),
            pltpu.VMEM((2 * FINE, channels // LANES, L + ROWS, LANES), jnp.float32),
            pltpu.VMEM((channels // LANES, L, LANES), jnp.float32),
        ],
        compiler_params=pltpu.CompilerParams(vmem_limit_bytes=VMEM_BYTES),
        name="settle",
    )(resident(partial), *swapped, resident(taps))


def gradient_kernel(share, step, plan_ref, blocks_ref, dict_hbm, out_ref, rf, zf, rr, zz, old, sem):
    peers, rows, segment = blocks_ref.shape
    share_rows = (rows - BLOCK_ATOMS) // 2
    span = peers * segment
    entries = share * L
    rows_of = pl.ds(first_row_of(plan_ref, step), BLOCK_ATOMS)
    columns_of = pl.ds(pl.multiple_of(lax.axis_index("tm") * entries, LANES), entries)
    fetch = pltpu.make_async_copy(dict_hbm.at[rows_of, columns_of], old, sem)
    fetch.start()
    rf[:, span:] = jnp.zeros((share_rows, LANES), jnp.bfloat16)
    zf[:, :LANES] = jnp.zeros((BLOCK_ATOMS, LANES), jnp.bfloat16)
    for peer in range(peers):
        column = peer * segment
        own = blocks_ref[peer, :share_rows, :]
        if peer:
            spill = blocks_ref[peer - 1, share_rows : 2 * share_rows, :]
            own = (own.astype(jnp.float32) + spill.astype(jnp.float32)).astype(jnp.bfloat16)
        rf[:, column : column + segment] = own
        zf[:, LANES + column : LANES + column + segment] = blocks_ref[peer, 2 * share_rows :, :]
    for lag in range(ROWS):
        rr[lag * share_rows : (lag + 1) * share_rows, :] = rf[:, lag : lag + span]
    for coarse in range(COARSE):
        begin = LANES - ROWS * coarse
        zz[coarse * BLOCK_ATOMS : (coarse + 1) * BLOCK_ATOMS, :] = zf[:, begin : begin + span]
    lagged = lax.dot_general(zz[...], rr[...], NT, preferred_element_type=jnp.float32)
    wide = ROWS * share_rows
    parts = []
    left = lagged
    for _ in range(3):
        parts.append(left.astype(jnp.bfloat16))
        left = left - parts[-1].astype(jnp.float32)
    row = lax.broadcasted_iota(jnp.int32, (wide, wide), 0)
    column = lax.broadcasted_iota(jnp.int32, (wide, wide), 1)
    chosen = (row // share_rows == column % ROWS) & (row % share_rows == column // ROWS)
    chosen = chosen.astype(jnp.float32).astype(jnp.bfloat16)
    by_channel = lax.dot_general(
        jnp.concatenate(parts, axis=0), chosen, NN, preferred_element_type=jnp.float32
    )
    count = COARSE * BLOCK_ATOMS
    by_channel = by_channel[:count] + by_channel[count : 2 * count] + by_channel[2 * count :]
    lane = lax.broadcasted_iota(jnp.int32, (BLOCK_ATOMS, LANES), 1)
    tiles = []
    for tile in range(entries // LANES):
        total = jnp.zeros((BLOCK_ATOMS, LANES), jnp.float32)
        for place in range(LANES // ROWS):
            channel, coarse = divmod(tile * (LANES // ROWS) + place, COARSE)
            first = channel * ROWS // LANES * LANES
            source = by_channel[coarse * BLOCK_ATOMS : (coarse + 1) * BLOCK_ATOMS, first : first + LANES]
            by = (place * ROWS - channel * ROWS) % LANES
            moved = pltpu.roll(source, by, 1) if by else source
            total = jnp.where(lane // ROWS == place, moved, total)
        tiles.append(total)
    gradient = jnp.concatenate(tiles, axis=1)
    fetch.wait()
    before = old[...]
    square = jnp.sum(before * before, axis=1, keepdims=True)
    along = jnp.sum(gradient * before, axis=1, keepdims=True) / (square + tiny_eps)
    out_ref[:, :entries] = (gradient - along * before).astype(jnp.bfloat16)
    terms = jnp.zeros((BLOCK_ATOMS, LANES), jnp.float32)
    for i in range(3):
        term = along.astype(jnp.bfloat16).astype(jnp.float32)
        along = along - term
        terms = jnp.where(lane == i, term, terms)
    out_ref[:, entries:] = terms.astype(jnp.bfloat16)


def share_gradient(plan, step, blocks, dictionary, share):
    peers, rows, segment = blocks.shape
    share_rows = (rows - BLOCK_ATOMS) // 2
    span = peers * segment
    return pl.pallas_call(
        functools.partial(gradient_kernel, share, step),
        in_specs=[scalars(), vmem(), hbm()],
        out_shape=jax.ShapeDtypeStruct((BLOCK_ATOMS, share * L + LANES), jnp.bfloat16),
        scratch_shapes=[
            pltpu.VMEM((share_rows, span + LANES), jnp.bfloat16),
            pltpu.VMEM((BLOCK_ATOMS, LANES + span), jnp.bfloat16),
            pltpu.VMEM((ROWS * share_rows, span), jnp.bfloat16),
            pltpu.VMEM((COARSE * BLOCK_ATOMS, span), jnp.bfloat16),
            pltpu.VMEM((BLOCK_ATOMS, share * L), jnp.float32),
            pltpu.SemaphoreType.DMA,
        ],
        compiler_params=pltpu.CompilerParams(vmem_limit_bytes=VMEM_BYTES),
        name="gradient",
    )(plan, blocks, far(dictionary))


def gather_steps(peers):
    bits = [1 << i for i in range(peers.bit_length() - 2, 0, -1)]
    steps = []
    for first in range(0, len(bits), 2):
        pair = bits[first : first + 2]
        steps.append(pair + [sum(pair)] if len(pair) == 2 else pair)
    return steps


def gather_slots(peers):
    flips = [0]
    for masks in gather_steps(peers):
        flips = [f ^ m for m in [0] + masks for f in flips]
    return flips


def gather_pieces(piece, meanwhile):
    peers = lax.axis_size("tm")

    def exchanged(shard, mask):
        return lax.ppermute(shard, "tm", [(i, i ^ mask) for i in range(peers)])

    held = piece[None]
    for index, masks in enumerate(gather_steps(peers)):
        held = jnp.concatenate([held] + [exchanged(held, mask) for mask in masks], axis=0)
        if index == 0:
            needed, extra = meanwhile(held)
    ready, _ = lax.optimization_barrier((held, needed))
    return held, exchanged(ready, 1), extra


def recall_kernel(step, earlier, plan_ref, dict_hbm, when_ref, *refs):
    del when_ref
    take = taker(refs)
    earlier_refs = take(earlier)
    take(1 if earlier else 0)
    old_ref, mean_ref = take(2)
    target = take(1 if earlier else 0)
    (sems,) = take(1)
    fetch = pltpu.make_async_copy(
        dict_hbm.at[pl.ds(first_row_of(plan_ref, step), BLOCK_ATOMS)], old_ref, sems.at[0]
    )
    fetch.start()
    fetch.wait()
    stores = [
        pltpu.make_async_copy(
            earlier_refs[index],
            target[0].at[pl.ds(first_row_of(plan_ref, index), BLOCK_ATOMS)],
            sems.at[1 + index],
        )
        for index in range(earlier)
    ]
    for store in stores:
        store.start()
    width = 9 * LANES if old_ref.shape[1] % (9 * LANES) == 0 else LANES

    def add(step, square):
        before = old_ref[:, pl.ds(pl.multiple_of(step * width, LANES), width)]
        return square + before * before

    square = lax.fori_loop(
        0, old_ref.shape[1] // width, add, jnp.zeros((BLOCK_ATOMS, width), jnp.float32)
    )
    mean_sq = jnp.sum(square, axis=1, keepdims=True) / (C * L) + tiny_eps
    mean_ref[...] = jnp.broadcast_to(mean_sq, mean_ref.shape)
    for store in stores:
        store.wait()


def recall(plan, step, dictionary, when, renewed, copied):
    entries = dictionary.shape[1]
    earlier = len(renewed)
    return pl.pallas_call(
        functools.partial(recall_kernel, step, earlier),
        in_specs=[scalars(), hbm(), pl.BlockSpec(memory_space=pl.ANY)]
        + [vmem()] * earlier
        + [hbm()] * (earlier > 0),
        out_specs=[vmem(), vmem()] + [hbm()] * (earlier > 0),
        out_shape=[
            pltpu.VMEM((BLOCK_ATOMS, entries), jnp.float32),
            jax.ShapeDtypeStruct((BLOCK_ATOMS, LANES), jnp.float32),
        ]
        + [pltpu.HBM(dictionary.shape, jnp.float32)] * (earlier > 0),
        scratch_shapes=[pltpu.SemaphoreType.DMA((1 + earlier,))],
        input_output_aliases={3 + earlier: 2} if earlier else {},
        compiler_params=pltpu.CompilerParams(vmem_limit_bytes=VMEM_BYTES),
        name="recall",
    )(
        plan,
        far(dictionary),
        when,
        *[resident(value) for value in renewed],
        *([far(copied)] if earlier else []),
    )


def renew_kernel(plan_step, plan_ref, held_ref, came_ref, old, mean_ref, *refs):
    me = lax.axis_index("tm")
    half, _, wide = held_ref.shape
    width = wide - LANES
    entries = C * L
    last = plan_step + 1 == OUTER
    if last:
        _, out_hbm, atoms_ref, grad, sems = refs
    else:
        atoms_ref, grad = refs

    stores = []
    shares = []
    for slot, flips in enumerate(gather_slots(2 * half)):
        for source, extra in ((held_ref, 0), (came_ref, 1)):
            owner = me ^ (flips + extra)
            shares.append((source.at[slot], pl.ds(pl.multiple_of(owner * width, LANES), width)))
    zeros = jnp.zeros((BLOCK_ATOMS, width), jnp.float32)
    dot = zeros
    for source, column in shares:
        before = old[:, column]
        along = jnp.sum(source[:, width:].astype(jnp.float32), axis=1, keepdims=True)
        value = source[:, :width].astype(jnp.float32) + along * before
        grad[:, column] = value
        dot += value * before
    mean_sq = mean_ref[:, :1]
    along = jnp.sum(dot, axis=1, keepdims=True) / entries / mean_sq
    square = zeros
    for _, column in shares:
        value = grad[:, column] - along * old[:, column]
        square += value * value
    spread = jnp.sum(square, axis=1, keepdims=True) / entries + tiny_eps
    step = move_rate / jnp.sqrt(spread)
    norm = 1.0 / jnp.sqrt(mean_sq + 0.25)
    rows = pl.ds(first_row_of(plan_ref, plan_step), BLOCK_ATOMS)
    for index, (_, column) in enumerate(shares):
        before = old[:, column]
        across = grad[:, column] - along * before
        atoms_ref[:, column] = (before + step * across) * norm
        if last:
            stores.append(
                pltpu.make_async_copy(
                    atoms_ref.at[:, column], out_hbm.at[rows, column], sems.at[index]
                )
            )
            stores[-1].start()
    for store in stores:
        store.wait()


def renew(plan, step, held, came, old, mean_sq, dictionary):
    last = dictionary is not None
    atoms = (BLOCK_ATOMS, old.shape[1])
    scratch = [pltpu.VMEM(atoms, jnp.float32)]
    if last:
        scratch = scratch * 2 + [pltpu.SemaphoreType.DMA((2 * held.shape[0],))]
    return pl.pallas_call(
        functools.partial(renew_kernel, step),
        in_specs=[scalars()] + [vmem()] * 4 + [hbm()] * last,
        out_specs=hbm() if last else vmem(),
        out_shape=pltpu.HBM(dictionary.shape, jnp.float32) if last else pltpu.VMEM(atoms, jnp.float32),
        scratch_shapes=scratch,
        input_output_aliases={5: 0} if last else {},
        compiler_params=pltpu.CompilerParams(vmem_limit_bytes=VMEM_BYTES),
        name="renew",
    )(plan, held, came, resident(old), mean_sq, *([far(dictionary)] if last else []))


def whole_channels(signal, codes_init, dictionary_init, threshold, plan):
    channels, segment = signal.shape
    peers = lax.axis_size("tm")
    limit = threshold[None, :]
    def swaps(edges):
        ends = [range(first, peers - 1, 2) for first in (0, 1)]
        pairs = [[p for i in end for p in ((i, i + 1), (i + 1, i))] for end in ends]
        far_first = [lax.ppermute(edge, "tm", pair) for edge, pair in zip(edges[::-1], pairs[::-1])]
        return far_first[::-1]

    state, signal, *edges = begin(codes_init, signal)
    following = swaps(edges)
    swapped = following
    taps = layout(dictionary_init, channels)
    dictionary = None
    renewed = []
    for step in range(OUTER):
        last = step + 1 == OUTER
        ferry = (dictionary_init, dictionary, COPIED[0], COPIED[1])
        atoms = renewed[-1] if renewed else None
        state, *results = iterate(
            plan, step, limit, state, swapped, signal, following, taps, atoms, ferry, peers
        )
        edges = results[:2]
        if renewed:
            taps, dictionary = results[2:]
        ferry = (dictionary_init, dictionary, sum(COPIED[: 2 * step]), COPIED[2 * step])
        payload, *results, first_edge, second_edge, dictionary = conclude(
            plan, step, limit, state, swaps(edges), signal, following, taps, ferry, peers
        )
        edges = [first_edge, second_edge]
        blocks = lax.all_to_all(payload, "tm", 0, 0, tiled=True)
        piece = share_gradient(plan, step, blocks, dictionary_init, channels // peers)
        recalled = []
        if last:
            edges, _ = lax.optimization_barrier((edges, piece))
            swapped = swaps(edges)
        else:
            recalled.extend(recall(plan, step, dictionary_init, piece, [], None))

        def beside(held):
            if last:
                recalled.extend(recall(plan, step, dictionary_init, held, renewed, dictionary))
                partial, _ = lax.optimization_barrier((results[0], held))
                residual = settle(partial, swapped, taps)
                return (recalled[0], residual), residual
            later, _ = lax.optimization_barrier((edges, held))
            return recalled[0], swaps(later)

        held, came, extra = gather_pieces(piece, beside)
        old, mean_sq, *copied = recalled
        result = renew(plan, step, held, came, old, mean_sq, copied[0] if last else None)
        if last:
            dictionary = result
        else:
            renewed.append(result)
            state, swapped = results[0], extra
    return results[1], dictionary, extra


def renew_atoms(old_atoms, across, mean_sq, spread):
    return (old_atoms + move_rate * across / jnp.sqrt(spread)[:, None]) / jnp.sqrt(mean_sq + 0.25)[
        :, None
    ]


def split_channels(signal, codes_init, dictionary_init, threshold, plan):
    segment = signal.shape[1]
    local_chan = signal.shape[0]
    unit_scale = (C * L) ** (-0.5)
    entries = C * L
    limit = threshold[:, None]

    def convolve(atom_cube, code_low):
        code_edge = shifted(code_low[:, segment - (L - 1) :], "tm", 1)
        extended = jnp.concatenate([code_edge, code_low], axis=1)
        lagged = jnp.stack(
            [extended[:, L - 1 - offset : L - 1 - offset + segment] for offset in range(L)], axis=1
        )
        return unit_scale * jnp.einsum(
            "kcl,klt->ct", atom_cube, lagged, preferred_element_type=jnp.float32
        )

    def resid_columns(resid_low):
        resid_edge = shifted(resid_low[:, : L - 1], "tm", -1)
        extended = jnp.concatenate([resid_low, resid_edge], axis=1)
        lagged = jnp.stack([extended[:, offset : offset + segment] for offset in range(L)], axis=1)
        return lagged.reshape(local_chan * L, segment)

    code_state = codes_init
    dictionary = dictionary_init
    residual = signal.astype(jnp.float32)
    for outer_step in range(OUTER):
        dict_low = dictionary.astype(jnp.bfloat16)
        atom_cube = dict_low.reshape(K, local_chan, L)
        for inner_step in range(INNER):
            code_low = code_state.astype(jnp.bfloat16)
            residual = signal.astype(jnp.float32) - convolve(atom_cube, code_low)
            lagged = resid_columns(residual.astype(jnp.bfloat16))
            partial_value = unit_scale * jnp.dot(
                dict_low, lagged, preferred_element_type=jnp.float32
            )
            scores = lax.psum(partial_value.astype(jnp.bfloat16), "chan").astype(jnp.float32)
            stepped = code_state + code_rate * scores
            code_state = stepped - jnp.clip(stepped, -limit, limit)
        code_low = code_state.astype(jnp.bfloat16)
        residual = signal.astype(jnp.float32) - convolve(atom_cube, code_low)
        lagged = resid_columns(residual.astype(jnp.bfloat16))
        first_row = plan[outer_step] * BLOCK_ATOMS
        code_block = lax.dynamic_slice_in_dim(code_low, first_row, BLOCK_ATOMS, 0)
        local_grad = lax.dot_general(
            code_block, lagged, (((1,), (1,)), ((), ())), preferred_element_type=jnp.float32
        )
        old_atoms = lax.dynamic_slice_in_dim(dictionary, first_row, BLOCK_ATOMS, 0)
        gradient = lax.psum(local_grad, "tm")
        dot_sum, square_sum = lax.psum(
            (jnp.sum(gradient * old_atoms, axis=1), jnp.sum(old_atoms * old_atoms, axis=1)), "chan"
        )
        mean_sq = square_sum / entries + tiny_eps
        along_coef = dot_sum / entries / mean_sq
        across = gradient - along_coef[:, None] * old_atoms
        spread = lax.psum(jnp.sum(across * across, axis=1), "chan") / entries + tiny_eps
        renewed = renew_atoms(old_atoms, across, mean_sq, spread)
        dictionary = lax.dynamic_update_slice_in_dim(dictionary, renewed, first_row, 0)
    return (code_state, dictionary, residual)


def shards(signal, codes_init, dictionary_init, threshold, plan):
    channels, segment = signal.shape
    peers = lax.axis_size("tm")
    fits = (
        lax.axis_size("chan") == 1
        and segment % LANES == 0
        and INNER == 2
        and OUTER == 2
        and channels % (GROUPS * ROWS) == 0
        and channels % LANES == 0
        and channels % peers == 0
        and (channels // peers * L) % LANES == 0
        and peers > 2
        and peers & (peers - 1) == 0
    )
    body = whole_channels if fits else split_channels
    return body(signal, codes_init, dictionary_init, threshold, plan)


def solution(mesh):
    placed = (P("chan", "tm"), P(None, "tm"), P(None, "chan"), P(), P())
    return jax.shard_map(
        shards,
        mesh=mesh,
        in_specs=placed,
        out_specs=(P(None, "tm"), P(None, "chan"), P("chan", "tm")),
        check_vma=False,
    )
```

```python
import functools

import jax
import jax.numpy as jnp
from jax import lax
from jax.experimental import pallas as pl
from jax.experimental.pallas import tpu as pltpu
from jax.sharding import PartitionSpec as P

C = 384
K = 128
L = 96
BLOCK_ATOMS = 16
INNER = 2
OUTER = 2

code_rate = 0.3
move_rate = 0.5
tiny_eps = 1e-06

ROWS = 16
COARSE = L // ROWS
STRIDE = L + 1
GROUPS = 4
SUBLANES = 8
COPIED = (48, 40, 40)
FINE = 4
LANES = 128
VMEM_BYTES = 24 * 1024 * 1024

NN = (((1,), (0,)), ((), ()))
NT = (((1,), (1,)), ((), ()))


def shifted(shard, axis, by):
    peers = lax.axis_size(axis)
    pairs = [(i, i + by) for i in range(peers) if 0 <= i + by < peers]
    return lax.ppermute(shard, axis, pairs)


def resident(value):
    return pltpu.with_memory_space_constraint(value, pltpu.VMEM)


def far(value):
    return pltpu.with_memory_space_constraint(value, pltpu.HBM)


def hbm():
    return pl.BlockSpec(memory_space=pltpu.HBM)


def scalars():
    return pl.BlockSpec(memory_space=pltpu.SMEM)


def first_row_of(plan_ref, step):
    return pl.multiple_of(plan_ref[step] * BLOCK_ATOMS, BLOCK_ATOMS)


def vmem():
    return pl.BlockSpec(memory_space=pltpu.VMEM)


def turn(columns, turned_ref):
    side = 2 * LANES
    row = lax.broadcasted_iota(jnp.int32, (side, side), 0)
    column = lax.broadcasted_iota(jnp.int32, (side, side), 1)
    identity = (row == column).astype(jnp.float32).astype(jnp.bfloat16)

    def put(entry, rows):
        end = entry + rows.shape[0]
        begin = entry
        while begin < end:
            channel, tap = begin // L, begin % L
            count = min(end - begin, L - tap)
            target = channel * STRIDE + tap
            turned_ref[target : target + count, :] = rows[begin - entry : begin - entry + count]
            begin += count

    low = columns.astype(jnp.bfloat16)
    through_matrix = ROWS * L // (6 * side) * 4 * side
    for first in range(0, through_matrix, 2 * side):
        pair = jnp.concatenate(
            [low[:, first + half * side : first + (half + 1) * side] for half in range(2)], axis=0
        )
        turned = lax.dot_general(identity, pair, NT, preferred_element_type=jnp.float32)
        for half in range(2):
            put(first + half * side, turned[:, half * K : (half + 1) * K])
    for first in range(through_matrix, ROWS * L, LANES):
        put(first, columns[:, first : first + LANES].astype(jnp.float32).T)


def tap_of(turned_ref, tap):
    return turned_ref[pl.ds(tap, ROWS, stride=STRIDE), :].astype(jnp.bfloat16)


def layout_kernel(dict_ref, taps_ref, *turned):
    def part(group):
        return dict_ref[:, group * ROWS * L : (group + 1) * ROWS * L]

    turn(part(0), turned[0])
    for group in range(GROUPS):
        if group + 1 < GROUPS:
            turn(part(group + 1), turned[group + 1])
        own = pl.ds(pl.multiple_of((pl.program_id(0) * GROUPS + group) * ROWS, ROWS), ROWS)
        for tap in range(L):
            taps_ref[tap // ROWS, tap % ROWS, own, :] = tap_of(turned[group], tap)


def layout(dictionary, channels):
    block = GROUPS * ROWS
    return pl.pallas_call(
        layout_kernel,
        grid=(channels // block,),
        in_specs=[pl.BlockSpec((K, block * L), lambda i: (0, i))],
        out_specs=vmem(),
        out_shape=pltpu.VMEM((COARSE, ROWS, channels, K), jnp.bfloat16),
        scratch_shapes=[pltpu.VMEM((ROWS * STRIDE, K), jnp.float32)] * GROUPS,
        compiler_params=pltpu.CompilerParams(vmem_limit_bytes=VMEM_BYTES),
        name="layout",
    )(far(dictionary))


class Ferry:
    def __init__(self, source, target, first, buffer, sems):
        self.steps = []
        for step in range(buffer.shape[0] // SUBLANES):
            held = buffer.at[pl.ds(step * SUBLANES, SUBLANES)]
            rows = pl.ds(first + step * SUBLANES, SUBLANES)
            fetch = pltpu.make_async_copy(source.at[rows], held, sems.at[0, step])
            store = pltpu.make_async_copy(held, target.at[rows], sems.at[1, step])
            fetch.start()
            self.steps.append((fetch, store))

    def turn_round(self):
        for fetch, store in self.steps:
            fetch.wait()
            store.start()

    def close(self):
        for _, store in self.steps:
            store.wait()


def ferry_scratch(count, entries):
    return [
        pltpu.VMEM((count, entries), jnp.float32),
        pltpu.SemaphoreType.DMA((2, count // SUBLANES)),
    ]


def convolve(zb, begin, count, taps, zz, fine, acc):
    channels = taps.shape[2]
    tiles = channels // LANES
    rows = count + ROWS
    for coarse in range(COARSE):
        first = begin - ROWS - ROWS * coarse
        zz[:rows, coarse * K : (coarse + 1) * K] = zb[first : first + rows, :]
    for lag in range(0, ROWS, FINE):
        slot = lag // FINE % 2 * FINE
        for pair in range(0, FINE, 2):
            weights = jnp.concatenate(
                [
                    jnp.concatenate([taps[m, lag + pair + j] for m in range(COARSE)], axis=1)
                    for j in range(2)
                ],
                axis=0,
            )
            product = lax.dot_general(zz[:rows, :], weights, NT, preferred_element_type=jnp.float32)
            for j in range(2):
                for tile in range(tiles):
                    column = j * channels + tile * LANES
                    fine[slot + pair + j, tile, :rows, :] = product[:, column : column + LANES]
        for tile in range(tiles):
            total = None if lag == 0 else acc[tile, :count, :]
            for j in range(FINE):
                first = ROWS - lag - j
                part = fine[slot + j, tile, first : first + count, :]
                total = part if total is None else total + part
            acc[tile, :count, :] = total


def correlate(rb, count, taps, rr, fine, acc):
    channels = taps.shape[2]
    rows = count + ROWS
    for coarse in range(COARSE):
        first = ROWS * coarse
        rr[:rows, coarse * channels : (coarse + 1) * channels] = rb[first : first + rows, :]
    for lag in range(0, ROWS, FINE):
        slot = lag // FINE % 2 * FINE
        for pair in range(0, FINE, 2):
            weights = jnp.concatenate(
                [
                    jnp.concatenate([taps[m, lag + pair + j] for m in range(COARSE)], axis=0)
                    for j in range(2)
                ],
                axis=1,
            )
            product = lax.dot_general(rr[:rows, :], weights, NN, preferred_element_type=jnp.float32)
            for j in range(2):
                fine[slot + pair + j, 0, :rows, :] = product[:, j * K : (j + 1) * K]
        total = None if lag == 0 else acc[0, :count, :]
        for j in range(FINE):
            part = fine[slot + j, 0, lag + j : lag + j + count, :]
            total = part if total is None else total + part
        acc[0, :count, :] = total


def patch_taps(row, atoms_ref, taps, columns, turned):
    channels = taps.shape[2]
    lane = lax.broadcasted_iota(jnp.int32, (ROWS, K), 1)
    kept = (lane < row) | (lane >= row + BLOCK_ATOMS)
    keep = kept.astype(jnp.float32).astype(jnp.bfloat16)
    columns[...] = jnp.zeros_like(columns)
    width = ROWS * L

    def patch(step, carry):
        part = pl.ds(pl.multiple_of(step * (GROUPS * width), LANES), GROUPS * width)
        columns[pl.ds(row, BLOCK_ATOMS), :] = atoms_ref[:, part].astype(jnp.bfloat16)
        turn(columns[:, :width], turned[0])
        for group in range(GROUPS):
            if group + 1 < GROUPS:
                turn(columns[:, (group + 1) * width : (group + 2) * width], turned[group + 1])
            own = pl.ds(pl.multiple_of((step * GROUPS + group) * ROWS, ROWS), ROWS)
            for tap in range(L):
                before = taps[tap // ROWS, tap % ROWS, own, :]
                taps[tap // ROWS, tap % ROWS, own, :] = before * keep + tap_of(turned[group], tap)
        return carry

    lax.fori_loop(0, channels // (GROUPS * ROWS), patch, 0)


def put_edges(edge_refs, rightward, leftward):
    even = lax.axis_index("tm") % 2 == 0

    def put(first, second):
        first[...] = rightward
        second[...] = leftward

    pl.when(even)(lambda: put(*edge_refs))
    pl.when(jnp.logical_not(even))(lambda: put(*edge_refs[::-1]))


def by_side(put, first_ref, second_ref):
    even = lax.axis_index("tm") % 2 == 0
    pl.when(even)(lambda: put(second_ref, first_ref))
    pl.when(jnp.logical_not(even))(lambda: put(first_ref, second_ref))


def begin_kernel(code_hbm, signal_hbm, state_out, signal_out, first_out, second_out, code_ref, signal_ref, sems):
    fetches = [
        pltpu.make_async_copy(code_hbm, code_ref, sems.at[0]),
        pltpu.make_async_copy(signal_hbm, signal_ref, sems.at[1]),
    ]
    for fetch in fetches:
        fetch.start()
    for fetch in fetches:
        fetch.wait()
    state = code_ref[...].T
    signal = signal_ref[...].astype(jnp.float32).T.astype(jnp.bfloat16)
    state_out[...] = state
    signal_out[...] = signal
    both = jnp.concatenate([state.astype(jnp.bfloat16), signal], axis=1)
    put_edges((first_out, second_out), both[-L:], both[:L])


def begin(code, signal):
    channels, segment = signal.shape
    return pl.pallas_call(
        begin_kernel,
        in_specs=[hbm()] * 2,
        out_specs=[vmem()] * 4,
        out_shape=[
            pltpu.VMEM((segment, K), jnp.float32),
            pltpu.VMEM((segment, channels), jnp.bfloat16),
        ]
        + [jax.ShapeDtypeStruct((L, K + channels), jnp.bfloat16)] * 2,
        scratch_shapes=[
            pltpu.VMEM(code.shape, code.dtype),
            pltpu.VMEM(signal.shape, signal.dtype),
            pltpu.SemaphoreType.DMA((2,)),
        ],
        compiler_params=pltpu.CompilerParams(vmem_limit_bytes=VMEM_BYTES),
        name="begin",
    )(far(code), far(signal))


def taker(refs):
    refs = list(refs)

    def take(count):
        taken = refs[:count]
        del refs[:count]
        return taken

    return take


def residual_rows(rb, pieces, start, acc, total_time):
    rows = rb.shape[0]
    moment = start + lax.broadcasted_iota(jnp.int32, (rows, LANES), 0)
    scale = (C * L) ** (-0.5)
    for tile in range(acc.shape[0]):
        column = slice(tile * LANES, (tile + 1) * LANES)
        signal = jnp.concatenate([piece[:, column] for piece in pieces], axis=0)
        value = signal.astype(jnp.float32) - scale * acc[tile, :rows, :]
        rb[:, column] = jnp.where(moment < total_time, value, 0.0).astype(jnp.bfloat16)


def stepped_codes(state, acc, limit):
    scale = (C * L) ** (-0.5)
    stepped = state + code_rate * (scale * acc[0, : state.shape[0], :])
    return stepped - jnp.clip(stepped, -limit, limit)


def iterate_kernel(total_time, patching, first_copied, plan_ref, limit_ref, *refs):
    take = taker(refs)
    state_ref, first_ref, second_ref, signal_ref, next_first, next_second = take(6)
    atoms = take(1 if patching else 0)
    (taps,) = take(1)
    source = take(2 if patching else 0)
    state_out, *edges = take(3)
    taps = (take(1) if patching else [taps])[0]
    target = take(1 if patching else 0)
    zb, rb, zz, rr, fine, acc, beyond = take(7)
    ferry = Ferry(source[0], target[0], first_copied, *take(2)) if patching else None
    segment, channels = signal_ref.shape
    zb[L : L + segment, :] = state_ref[...].astype(jnp.bfloat16)

    def put(left, right):
        zb[:L, :] = left[:, :K]
        zb[L + segment :, :] = right[:, :K]

    def put_signal(left, right):
        beyond[...] = right[:, K:]

    by_side(put, first_ref, second_ref)
    by_side(put_signal, next_first, next_second)
    if patching:
        columns, *turned = take(1 + GROUPS)
        patch_taps(first_row_of(plan_ref, patching - 1), atoms[0], taps, columns, turned)
        ferry.turn_round()
    convolve(zb, L, segment + L, taps, zz, fine, acc)
    start = lax.axis_index("tm") * segment
    residual_rows(rb, (signal_ref, beyond), start, acc, total_time)
    correlate(rb, segment, taps, rr, fine, acc)
    state = stepped_codes(state_ref[...], acc, limit_ref[...])
    state_out[...] = state
    low = state.astype(jnp.bfloat16)
    put_edges(edges, low[-L:], low[:L])
    if ferry:
        ferry.close()


def iterate(plan, step, limit, state, swapped, signal, following, taps, atoms, ferry, peers):
    segment, channels = signal.shape
    patching = atoms is not None
    reach = segment + L
    carried = [far(value) for value in ferry[:2]] if patching else []
    return pl.pallas_call(
        functools.partial(iterate_kernel, peers * segment, step if patching else 0, ferry[2]),
        in_specs=[scalars()] + [vmem()] * (8 + patching) + [hbm()] * len(carried),
        out_specs=[vmem()] * (3 + patching) + [hbm()] * patching,
        out_shape=[pltpu.VMEM((segment, K), jnp.float32)]
        + [jax.ShapeDtypeStruct((L, K), jnp.bfloat16)] * 2
        + [pltpu.VMEM(taps.shape, jnp.bfloat16)] * patching
        + [pltpu.HBM(ferry[0].shape, jnp.float32)] * patching,
        scratch_shapes=[
            pltpu.VMEM((L + reach, K), jnp.bfloat16),
            pltpu.VMEM((reach, channels), jnp.bfloat16),
            pltpu.VMEM((reach + ROWS, COARSE * K), jnp.bfloat16),
            pltpu.VMEM((segment + ROWS, COARSE * channels), jnp.bfloat16),
            pltpu.VMEM((2 * FINE, channels // LANES, reach + ROWS, LANES), jnp.float32),
            pltpu.VMEM((channels // LANES, reach, LANES), jnp.float32),
            pltpu.VMEM((L, channels), jnp.bfloat16),
        ]
        + (
            ferry_scratch(ferry[3], ferry[0].shape[1])
            + [pltpu.VMEM((K, GROUPS * ROWS * L), jnp.bfloat16)]
            + [pltpu.VMEM((ROWS * STRIDE, K), jnp.float32)] * GROUPS
        )
        * patching,
        input_output_aliases={9: 3, 11: 4} if patching else {},
        compiler_params=pltpu.CompilerParams(vmem_limit_bytes=VMEM_BYTES),
        name="iterate",
    )(
        plan,
        limit,
        resident(state),
        *swapped,
        resident(signal),
        *following,
        *([resident(atoms)] if patching else []),
        resident(taps),
        *carried,
    )


def conclude_kernel(peers, step, copied, plan_ref, limit_ref, *refs):
    last = step + 1 == OUTER
    take = taker(refs)
    state_ref, first_ref, second_ref, signal_ref, next_first, next_second, taps = take(7)
    source = take(2 if copied else 1)[0]
    (payload_out,) = take(1)
    state_out, partial_out, codes_out = (None, *take(2)) if last else (*take(1), None, None)
    *edges, target = take(3)
    zb, rb, zz, rr, fine, acc, beyond, tall, packed = take(9)
    ferry = Ferry(source, target, copied, *take(2))
    if not last:
        (codes_out,) = take(1)
    segment, channels = signal_ref.shape
    reach = segment + L
    zb[L:reach, :] = state_ref[...].astype(jnp.bfloat16)

    def put(left, right):
        zb[:L, :] = left[...]
        zb[reach:, :] = right[...]

    def put_signal(left, right):
        beyond[...] = right[:, K:]

    by_side(put, first_ref, second_ref)
    by_side(put_signal, next_first, next_second)
    convolve(zb, L, reach, taps, zz, fine, acc)
    ferry.turn_round()
    start = lax.axis_index("tm") * segment
    residual_rows(rb, (signal_ref, beyond), start, acc, peers * segment)
    correlate(rb, segment, taps, rr, fine, acc)
    state = stepped_codes(state_ref[...], acc, limit_ref[...])
    low = state.astype(jnp.bfloat16)
    if not last:
        state_out[...] = state
    put_edges(edges, low[-L:], low[:L])
    codes_out[...] = state.T
    zb[:L, :] = jnp.zeros((L, K), jnp.bfloat16)
    zb[L:reach, :] = low
    zb[reach:, :] = jnp.zeros((L, K), jnp.bfloat16)
    convolve(zb, L, reach, taps, zz, fine, acc)
    scale = (C * L) ** (-0.5)
    block = codes_out[pl.ds(first_row_of(plan_ref, step), BLOCK_ATOMS), :]
    share = channels // peers
    for tile in range(channels // LANES):
        column = slice(tile * LANES, (tile + 1) * LANES)
        value = signal_ref[:, column].astype(jnp.float32) - scale * acc[tile, :segment, :]
        if last:
            partial_out[:, column] = value
        tall[0, column, :] = value.T
        spill = jnp.concatenate(
            [-scale * acc[tile, segment:reach, :], jnp.zeros((segment - L, LANES), jnp.float32)], axis=0
        )
        tall[1, column, :] = spill.T
    for peer in range(peers):
        for part in range(2):
            packed[peer, part * share : (part + 1) * share, :] = tall[
                part, peer * share : (peer + 1) * share, :
            ]
        packed[peer, 2 * share :, :] = block
    payload_out[...] = packed[...].astype(jnp.bfloat16)
    ferry.close()


def conclude(plan, step, limit, state, swapped, signal, following, taps, ferry, peers):
    segment, channels = signal.shape
    share = channels // peers
    last = step + 1 == OUTER
    carried = [far(value) for value in ferry[:2] if value is not None]
    reach = segment + L
    outs = [pltpu.VMEM((segment, K), jnp.float32)]
    if last:
        outs = [pltpu.VMEM((segment, channels), jnp.float32), pltpu.VMEM((K, segment), jnp.float32)]
    outs += [jax.ShapeDtypeStruct((L, K), jnp.bfloat16)] * 2
    return pl.pallas_call(
        functools.partial(conclude_kernel, peers, step, ferry[2]),
        in_specs=[scalars()] + [vmem()] * 8 + [hbm()] * len(carried),
        out_specs=[vmem()] * (1 + len(outs)) + [hbm()],
        out_shape=[jax.ShapeDtypeStruct((peers, 2 * share + BLOCK_ATOMS, segment), jnp.bfloat16)]
        + outs
        + [pltpu.HBM(ferry[0].shape, jnp.float32)],
        scratch_shapes=[
            pltpu.VMEM((L + reach, K), jnp.bfloat16),
            pltpu.VMEM((reach, channels), jnp.bfloat16),
            pltpu.VMEM((reach + ROWS, COARSE * K), jnp.bfloat16),
            pltpu.VMEM((segment + ROWS, COARSE * channels), jnp.bfloat16),
            pltpu.VMEM((2 * FINE, channels // LANES, reach + ROWS, LANES), jnp.float32),
            pltpu.VMEM((channels // LANES, reach, LANES), jnp.float32),
            pltpu.VMEM((L, channels), jnp.bfloat16),
            pltpu.VMEM((2, channels, segment), jnp.float32),
            pltpu.VMEM((peers, 2 * share + BLOCK_ATOMS, segment), jnp.float32),
        ]
        + ferry_scratch(ferry[3], ferry[0].shape[1])
        + ([] if last else [pltpu.VMEM((K, segment), jnp.float32)]),
        input_output_aliases={10: 1 + len(outs)} if len(carried) == 2 else {},
        compiler_params=pltpu.CompilerParams(vmem_limit_bytes=VMEM_BYTES),
        name="conclude",
    )(
        plan,
        limit,
        resident(state),
        *swapped,
        resident(signal),
        *following,
        resident(taps),
        *carried,
    )


def settle_kernel(earlier, plan_ref, partial_ref, first_ref, second_ref, taps, *refs):
    take = taker(refs)
    atoms = take(earlier)
    _, resid_out, dict_out, zb, zz, fine, acc, sems = refs[earlier:]
    segment, channels = partial_ref.shape
    stores = [
        pltpu.make_async_copy(
            atoms[step], dict_out.at[pl.ds(first_row_of(plan_ref, step), BLOCK_ATOMS)], sems.at[step]
        )
        for step in range(earlier)
    ]
    for store in stores:
        store.start()

    def put(left, right):
        zb[:L, :] = left[...]

    zb[L:, :] = jnp.zeros((L, K), jnp.bfloat16)
    by_side(put, first_ref, second_ref)
    convolve(zb, L, L, taps, zz, fine, acc)
    scale = (C * L) ** (-0.5)
    for tile in range(channels // LANES):
        column = slice(tile * LANES, (tile + 1) * LANES)
        value = jnp.concatenate(
            [partial_ref[:L, column] - scale * acc[tile], partial_ref[L:, column]], axis=0
        )
        resid_out[column, :] = value.T
    for store in stores:
        store.wait()


def settle(plan, partial, swapped, taps, renewed, dictionary):
    segment, channels = partial.shape
    earlier = len(renewed)
    return pl.pallas_call(
        functools.partial(settle_kernel, earlier),
        in_specs=[scalars()] + [vmem()] * (4 + earlier) + [hbm()],
        out_specs=[vmem(), hbm()],
        out_shape=[
            pltpu.VMEM((channels, segment), jnp.float32),
            pltpu.HBM(dictionary.shape, jnp.float32),
        ],
        scratch_shapes=[
            pltpu.VMEM((2 * L, K), jnp.bfloat16),
            pltpu.VMEM((L + ROWS, COARSE * K), jnp.bfloat16),
            pltpu.VMEM((2 * FINE, channels // LANES, L + ROWS, LANES), jnp.float32),
            pltpu.VMEM((channels // LANES, L, LANES), jnp.float32),
            pltpu.SemaphoreType.DMA((earlier,)),
        ],
        input_output_aliases={5 + earlier: 1},
        compiler_params=pltpu.CompilerParams(vmem_limit_bytes=VMEM_BYTES),
        name="settle",
    )(
        plan,
        resident(partial),
        *swapped,
        resident(taps),
        *[resident(value) for value in renewed],
        far(dictionary),
    )


def gradient_kernel(share, step, plan_ref, blocks_ref, dict_hbm, out_ref, packed, rf, zf, rr, zz, old, sem):
    peers, rows, segment = blocks_ref.shape
    share_rows = rf.shape[0]
    span = peers * segment
    entries = share * L
    rows_of = pl.ds(first_row_of(plan_ref, step), BLOCK_ATOMS)
    columns_of = pl.ds(pl.multiple_of(lax.axis_index("tm") * entries, LANES), entries)
    fetch = pltpu.make_async_copy(dict_hbm.at[rows_of, columns_of], old, sem)
    fetch.start()
    rf[:, span:] = jnp.zeros((share_rows, LANES), jnp.bfloat16)
    zf[:, :LANES] = jnp.zeros((BLOCK_ATOMS, LANES), jnp.bfloat16)
    packed[...] = blocks_ref[...].astype(jnp.float32)
    for peer in range(peers):
        column = peer * segment
        own = packed[peer, :share_rows, :]
        if peer:
            own += packed[peer - 1, share : share + share_rows, :]
        rf[:, column : column + segment] = own.astype(jnp.bfloat16)
        zf[:, LANES + column : LANES + column + segment] = packed[peer, 2 * share :, :].astype(
            jnp.bfloat16
        )
    for lag in range(ROWS):
        rr[lag * share_rows : (lag + 1) * share_rows, :] = rf[:, lag : lag + span]
    for coarse in range(COARSE):
        begin = LANES - ROWS * coarse
        zz[coarse * BLOCK_ATOMS : (coarse + 1) * BLOCK_ATOMS, :] = zf[:, begin : begin + span]
    lagged = lax.dot_general(zz[...], rr[...], NT, preferred_element_type=jnp.float32)
    wide = ROWS * share_rows
    parts = []
    left = lagged
    for _ in range(3):
        parts.append(left.astype(jnp.bfloat16))
        left = left - parts[-1].astype(jnp.float32)
    row = lax.broadcasted_iota(jnp.int32, (wide, wide), 0)
    column = lax.broadcasted_iota(jnp.int32, (wide, wide), 1)
    chosen = (row // share_rows == column % ROWS) & (row % share_rows == column // ROWS)
    chosen = chosen.astype(jnp.float32).astype(jnp.bfloat16)
    by_channel = lax.dot_general(
        jnp.concatenate(parts, axis=0), chosen, NN, preferred_element_type=jnp.float32
    )
    count = COARSE * BLOCK_ATOMS
    by_channel = by_channel[:count] + by_channel[count : 2 * count] + by_channel[2 * count :]
    lane = lax.broadcasted_iota(jnp.int32, (BLOCK_ATOMS, LANES), 1)
    tiles = []
    for tile in range(entries // LANES):
        total = jnp.zeros((BLOCK_ATOMS, LANES), jnp.float32)
        for place in range(LANES // ROWS):
            channel, coarse = divmod(tile * (LANES // ROWS) + place, COARSE)
            first = channel * ROWS // LANES * LANES
            source = by_channel[coarse * BLOCK_ATOMS : (coarse + 1) * BLOCK_ATOMS, first : first + LANES]
            by = (place * ROWS - channel * ROWS) % LANES
            moved = pltpu.roll(source, by, 1) if by else source
            total = jnp.where(lane // ROWS == place, moved, total)
        tiles.append(total)
    gradient = jnp.concatenate(tiles, axis=1)
    fetch.wait()
    before = old[...]
    square = jnp.sum(before * before, axis=1, keepdims=True)
    along = jnp.sum(gradient * before, axis=1, keepdims=True) / (square + tiny_eps)
    out_ref[:, :entries] = (gradient - along * before).astype(jnp.bfloat16)
    terms = jnp.zeros((BLOCK_ATOMS, LANES), jnp.float32)
    for i in range(3):
        term = along.astype(jnp.bfloat16).astype(jnp.float32)
        along = along - term
        terms = jnp.where(lane == i, term, terms)
    out_ref[:, entries:] = terms.astype(jnp.bfloat16)


def share_gradient(plan, step, blocks, dictionary, share):
    peers, rows, segment = blocks.shape
    share_rows = -(-share // ROWS) * ROWS
    span = peers * segment
    return pl.pallas_call(
        functools.partial(gradient_kernel, share, step),
        in_specs=[scalars(), vmem(), hbm()],
        out_shape=jax.ShapeDtypeStruct((BLOCK_ATOMS, share * L + LANES), jnp.bfloat16),
        scratch_shapes=[
            pltpu.VMEM(blocks.shape, jnp.float32),
            pltpu.VMEM((share_rows, span + LANES), jnp.bfloat16),
            pltpu.VMEM((BLOCK_ATOMS, LANES + span), jnp.bfloat16),
            pltpu.VMEM((ROWS * share_rows, span), jnp.bfloat16),
            pltpu.VMEM((COARSE * BLOCK_ATOMS, span), jnp.bfloat16),
            pltpu.VMEM((BLOCK_ATOMS, share * L), jnp.float32),
            pltpu.SemaphoreType.DMA,
        ],
        compiler_params=pltpu.CompilerParams(vmem_limit_bytes=VMEM_BYTES),
        name="gradient",
    )(plan, blocks, far(dictionary))


def gather_steps(peers):
    bits = [1 << i for i in range(peers.bit_length() - 2, 0, -1)]
    steps = []
    for first in range(0, len(bits), 2):
        pair = bits[first : first + 2]
        steps.append(pair + [sum(pair)] if len(pair) == 2 else pair)
    return steps


def gather_slots(peers):
    flips = [0]
    for masks in gather_steps(peers):
        flips = [f ^ m for m in [0] + masks for f in flips]
    return flips


def gather_pieces(piece, meanwhile):
    peers = lax.axis_size("tm")

    def exchanged(shard, mask):
        return lax.ppermute(shard, "tm", [(i, i ^ mask) for i in range(peers)])

    held = piece[None]
    for index, masks in enumerate(gather_steps(peers)):
        held = jnp.concatenate([held] + [exchanged(held, mask) for mask in masks], axis=0)
        if index == 0:
            needed, extra = meanwhile(held)
    ready, _ = lax.optimization_barrier((held, needed))
    return held, exchanged(ready, 1), extra


def recall_kernel(plan_ref, dict_hbm, when_ref, *refs):
    del when_ref
    take = taker(refs)
    olds, means = take(OUTER), take(OUTER)
    (sems,) = take(1)
    entries = olds[0].shape[1]
    fetches = [
        pltpu.make_async_copy(
            dict_hbm.at[pl.ds(first_row_of(plan_ref, step), BLOCK_ATOMS)], olds[step], sems.at[step]
        )
        for step in range(OUTER)
    ]
    for fetch in fetches:
        fetch.start()
    width = 9 * LANES if entries % (9 * LANES) == 0 else LANES
    for fetch, old_ref, mean_ref in zip(fetches, olds, means):
        fetch.wait()

        def add(step, square):
            before = old_ref[:, pl.ds(pl.multiple_of(step * width, LANES), width)]
            return square + before * before

        zeros = jnp.zeros((BLOCK_ATOMS, width), jnp.float32)
        square = lax.fori_loop(0, entries // width, add, zeros)
        mean_sq = jnp.sum(square, axis=1, keepdims=True) / (C * L) + tiny_eps
        mean_ref[...] = jnp.broadcast_to(mean_sq, mean_ref.shape)


def recall(plan, dictionary, when):
    entries = dictionary.shape[1]
    results = pl.pallas_call(
        recall_kernel,
        in_specs=[scalars(), hbm(), pl.BlockSpec(memory_space=pl.ANY)],
        out_specs=[vmem()] * (2 * OUTER),
        out_shape=[pltpu.VMEM((BLOCK_ATOMS, entries), jnp.float32)] * OUTER
        + [pltpu.VMEM((BLOCK_ATOMS, LANES), jnp.float32)] * OUTER,
        scratch_shapes=[pltpu.SemaphoreType.DMA((OUTER,))],
        compiler_params=pltpu.CompilerParams(vmem_limit_bytes=VMEM_BYTES),
        name="recall",
    )(plan, far(dictionary), when)
    return list(zip(results[:OUTER], results[OUTER:]))


def renew_kernel(plan_step, plan_ref, held_ref, came_ref, old, mean_ref, *refs):
    me = lax.axis_index("tm")
    half, _, wide = held_ref.shape
    width = wide - LANES
    entries = C * L
    last = plan_step + 1 == OUTER
    if last:
        _, out_hbm, atoms_ref, grad, sems = refs
    else:
        atoms_ref, grad = refs

    stores = []
    shares = []
    for slot, flips in enumerate(gather_slots(2 * half)):
        for source, extra in ((held_ref, 0), (came_ref, 1)):
            owner = me ^ (flips + extra)
            shares.append((source.at[slot], pl.ds(pl.multiple_of(owner * width, LANES), width)))
    zeros = jnp.zeros((BLOCK_ATOMS, width), jnp.float32)
    dot = zeros
    for source, column in shares:
        before = old[:, column]
        along = jnp.sum(source[:, width:].astype(jnp.float32), axis=1, keepdims=True)
        value = source[:, :width].astype(jnp.float32) + along * before
        grad[:, column] = value
        dot += value * before
    mean_sq = mean_ref[:, :1]
    along = jnp.sum(dot, axis=1, keepdims=True) / entries / mean_sq
    square = zeros
    for _, column in shares:
        value = grad[:, column] - along * old[:, column]
        square += value * value
    spread = jnp.sum(square, axis=1, keepdims=True) / entries + tiny_eps
    step = move_rate / jnp.sqrt(spread)
    norm = 1.0 / jnp.sqrt(mean_sq + 0.25)
    rows = pl.ds(first_row_of(plan_ref, plan_step), BLOCK_ATOMS)
    for index, (_, column) in enumerate(shares):
        before = old[:, column]
        across = grad[:, column] - along * before
        atoms_ref[:, column] = (before + step * across) * norm
        if last:
            stores.append(
                pltpu.make_async_copy(
                    atoms_ref.at[:, column], out_hbm.at[rows, column], sems.at[index]
                )
            )
            stores[-1].start()
    for store in stores:
        store.wait()


def renew(plan, step, held, came, old, mean_sq, dictionary):
    last = dictionary is not None
    atoms = (BLOCK_ATOMS, old.shape[1])
    scratch = [pltpu.VMEM(atoms, jnp.float32)]
    if last:
        scratch = scratch * 2 + [pltpu.SemaphoreType.DMA((2 * held.shape[0],))]
    return pl.pallas_call(
        functools.partial(renew_kernel, step),
        in_specs=[scalars()] + [vmem()] * 4 + [hbm()] * last,
        out_specs=hbm() if last else vmem(),
        out_shape=pltpu.HBM(dictionary.shape, jnp.float32) if last else pltpu.VMEM(atoms, jnp.float32),
        scratch_shapes=scratch,
        input_output_aliases={5: 0} if last else {},
        compiler_params=pltpu.CompilerParams(vmem_limit_bytes=VMEM_BYTES),
        name="renew",
    )(plan, held, came, resident(old), resident(mean_sq), *([far(dictionary)] if last else []))


def whole_channels(signal, codes_init, dictionary_init, threshold, plan):
    channels, segment = signal.shape
    peers = lax.axis_size("tm")
    limit = threshold[None, :]
    def swaps(edges):
        ends = [range(first, peers - 1, 2) for first in (0, 1)]
        pairs = [[p for i in end for p in ((i, i + 1), (i + 1, i))] for end in ends]
        far_first = [lax.ppermute(edge, "tm", pair) for edge, pair in zip(edges[::-1], pairs[::-1])]
        return far_first[::-1]

    state, signal, *edges = begin(codes_init, signal)
    following = swaps(edges)
    swapped = following
    taps = layout(dictionary_init, channels)
    dictionary = None
    renewed = []
    for step in range(OUTER):
        last = step + 1 == OUTER
        ferry = (dictionary_init, dictionary, COPIED[0], COPIED[1])
        atoms = renewed[-1] if renewed else None
        state, *results = iterate(
            plan, step, limit, state, swapped, signal, following, taps, atoms, ferry, peers
        )
        edges = results[:2]
        if renewed:
            taps, dictionary = results[2:]
        ferry = (dictionary_init, dictionary, sum(COPIED[: 2 * step]), COPIED[2 * step])
        payload, *results, first_edge, second_edge, dictionary = conclude(
            plan, step, limit, state, swaps(edges), signal, following, taps, ferry, peers
        )
        edges = [first_edge, second_edge]
        blocks = lax.all_to_all(payload, "tm", 0, 0, tiled=True)
        piece = share_gradient(plan, step, blocks, dictionary_init, channels // peers)
        edges, _ = lax.optimization_barrier((edges, piece))
        swapped = swaps(edges)

        def beside(held):
            if not last:
                recalled = recall(plan, dictionary_init, held)
                return (recalled[0][0], swapped), recalled
            partial, _ = lax.optimization_barrier((results[0], held))
            settled = settle(plan, partial, swapped, taps, renewed, dictionary)
            return settled[0], settled

        held, came, extra = gather_pieces(piece, beside)
        if last:
            residual, dictionary = extra
            dictionary = renew(plan, step, held, came, *recalled[step], dictionary)
        else:
            recalled, state = extra, results[0]
            renewed.append(renew(plan, step, held, came, *recalled[step], None))
    return results[1], dictionary, residual


def renew_atoms(old_atoms, across, mean_sq, spread):
    return (old_atoms + move_rate * across / jnp.sqrt(spread)[:, None]) / jnp.sqrt(mean_sq + 0.25)[
        :, None
    ]


def split_channels(signal, codes_init, dictionary_init, threshold, plan):
    segment = signal.shape[1]
    local_chan = signal.shape[0]
    unit_scale = (C * L) ** (-0.5)
    entries = C * L
    limit = threshold[:, None]

    def convolve(atom_cube, code_low):
        code_edge = shifted(code_low[:, segment - (L - 1) :], "tm", 1)
        extended = jnp.concatenate([code_edge, code_low], axis=1)
        lagged = jnp.stack(
            [extended[:, L - 1 - offset : L - 1 - offset + segment] for offset in range(L)], axis=1
        )
        return unit_scale * jnp.einsum(
            "kcl,klt->ct", atom_cube, lagged, preferred_element_type=jnp.float32
        )

    def resid_columns(resid_low):
        resid_edge = shifted(resid_low[:, : L - 1], "tm", -1)
        extended = jnp.concatenate([resid_low, resid_edge], axis=1)
        lagged = jnp.stack([extended[:, offset : offset + segment] for offset in range(L)], axis=1)
        return lagged.reshape(local_chan * L, segment)

    code_state = codes_init
    dictionary = dictionary_init
    residual = signal.astype(jnp.float32)
    for outer_step in range(OUTER):
        dict_low = dictionary.astype(jnp.bfloat16)
        atom_cube = dict_low.reshape(K, local_chan, L)
        for inner_step in range(INNER):
            code_low = code_state.astype(jnp.bfloat16)
            residual = signal.astype(jnp.float32) - convolve(atom_cube, code_low)
            lagged = resid_columns(residual.astype(jnp.bfloat16))
            partial_value = unit_scale * jnp.dot(
                dict_low, lagged, preferred_element_type=jnp.float32
            )
            scores = lax.psum(partial_value.astype(jnp.bfloat16), "chan").astype(jnp.float32)
            stepped = code_state + code_rate * scores
            code_state = stepped - jnp.clip(stepped, -limit, limit)
        code_low = code_state.astype(jnp.bfloat16)
        residual = signal.astype(jnp.float32) - convolve(atom_cube, code_low)
        lagged = resid_columns(residual.astype(jnp.bfloat16))
        first_row = plan[outer_step] * BLOCK_ATOMS
        code_block = lax.dynamic_slice_in_dim(code_low, first_row, BLOCK_ATOMS, 0)
        local_grad = lax.dot_general(
            code_block, lagged, (((1,), (1,)), ((), ())), preferred_element_type=jnp.float32
        )
        old_atoms = lax.dynamic_slice_in_dim(dictionary, first_row, BLOCK_ATOMS, 0)
        gradient = lax.psum(local_grad, "tm")
        dot_sum, square_sum = lax.psum(
            (jnp.sum(gradient * old_atoms, axis=1), jnp.sum(old_atoms * old_atoms, axis=1)), "chan"
        )
        mean_sq = square_sum / entries + tiny_eps
        along_coef = dot_sum / entries / mean_sq
        across = gradient - along_coef[:, None] * old_atoms
        spread = lax.psum(jnp.sum(across * across, axis=1), "chan") / entries + tiny_eps
        renewed = renew_atoms(old_atoms, across, mean_sq, spread)
        dictionary = lax.dynamic_update_slice_in_dim(dictionary, renewed, first_row, 0)
    return (code_state, dictionary, residual)


def shards(signal, codes_init, dictionary_init, threshold, plan):
    channels, segment = signal.shape
    peers = lax.axis_size("tm")
    fits = (
        lax.axis_size("chan") == 1
        and segment % LANES == 0
        and INNER == 2
        and OUTER == 2
        and channels % (GROUPS * ROWS) == 0
        and channels % LANES == 0
        and channels % peers == 0
        and (channels // peers * L) % LANES == 0
        and peers > 2
        and peers & (peers - 1) == 0
    )
    body = whole_channels if fits else split_channels
    return body(signal, codes_init, dictionary_init, threshold, plan)


def solution(mesh):
    placed = (P("chan", "tm"), P(None, "tm"), P(None, "chan"), P(), P())
    return jax.shard_map(
        shards,
        mesh=mesh,
        in_specs=placed,
        out_specs=(P(None, "tm"), P(None, "chan"), P("chan", "tm")),
        check_vma=False,
    )
```

```python
import functools

import jax
import jax.numpy as jnp
from jax import lax
from jax.experimental import pallas as pl
from jax.experimental.pallas import tpu as pltpu
from jax.sharding import PartitionSpec as P

C = 384
K = 128
L = 96
BLOCK_ATOMS = 16
INNER = 2
OUTER = 2

code_rate = 0.3
move_rate = 0.5
tiny_eps = 1e-06

ROWS = 16
COARSE = L // ROWS
STRIDE = L + 1
GROUPS = 4
SUBLANES = 8
COPIED = (48, 40, 40)
FINE = 4
LANES = 128
VMEM_BYTES = 24 * 1024 * 1024

NN = (((1,), (0,)), ((), ()))
NT = (((1,), (1,)), ((), ()))


def shifted(shard, axis, by):
    peers = lax.axis_size(axis)
    pairs = [(i, i + by) for i in range(peers) if 0 <= i + by < peers]
    return lax.ppermute(shard, axis, pairs)


def resident(value):
    return pltpu.with_memory_space_constraint(value, pltpu.VMEM)


def far(value):
    return pltpu.with_memory_space_constraint(value, pltpu.HBM)


def hbm():
    return pl.BlockSpec(memory_space=pltpu.HBM)


def scalars():
    return pl.BlockSpec(memory_space=pltpu.SMEM)


def first_row_of(plan_ref, step):
    return pl.multiple_of(plan_ref[step] * BLOCK_ATOMS, BLOCK_ATOMS)


def vmem():
    return pl.BlockSpec(memory_space=pltpu.VMEM)


def turn(columns, turned_ref):
    side = 2 * LANES
    row = lax.broadcasted_iota(jnp.int32, (side, side), 0)
    column = lax.broadcasted_iota(jnp.int32, (side, side), 1)
    identity = (row == column).astype(jnp.float32).astype(jnp.bfloat16)

    def put(entry, rows):
        end = entry + rows.shape[0]
        begin = entry
        while begin < end:
            channel, tap = begin // L, begin % L
            count = min(end - begin, L - tap)
            target = channel * STRIDE + tap
            turned_ref[target : target + count, :] = rows[begin - entry : begin - entry + count]
            begin += count

    low = columns.astype(jnp.bfloat16)
    through_matrix = ROWS * L // (6 * side) * 4 * side
    for first in range(0, through_matrix, 2 * side):
        pair = jnp.concatenate(
            [low[:, first + half * side : first + (half + 1) * side] for half in range(2)], axis=0
        )
        turned = lax.dot_general(identity, pair, NT, preferred_element_type=jnp.float32)
        for half in range(2):
            put(first + half * side, turned[:, half * K : (half + 1) * K])
    for first in range(through_matrix, ROWS * L, LANES):
        put(first, columns[:, first : first + LANES].astype(jnp.float32).T)


def tap_of(turned_ref, tap):
    return turned_ref[pl.ds(tap, ROWS, stride=STRIDE), :].astype(jnp.bfloat16)


def layout_kernel(dict_ref, taps_ref, *turned):
    def part(group):
        return dict_ref[:, group * ROWS * L : (group + 1) * ROWS * L]

    turn(part(0), turned[0])
    for group in range(GROUPS):
        if group + 1 < GROUPS:
            turn(part(group + 1), turned[group + 1])
        own = pl.ds(pl.multiple_of((pl.program_id(0) * GROUPS + group) * ROWS, ROWS), ROWS)
        for tap in range(L):
            taps_ref[tap // ROWS, tap % ROWS, own, :] = tap_of(turned[group], tap)


def layout(dictionary, channels):
    block = GROUPS * ROWS
    return pl.pallas_call(
        layout_kernel,
        grid=(channels // block,),
        in_specs=[pl.BlockSpec((K, block * L), lambda i: (0, i))],
        out_specs=vmem(),
        out_shape=pltpu.VMEM((COARSE, ROWS, channels, K), jnp.bfloat16),
        scratch_shapes=[pltpu.VMEM((ROWS * STRIDE, K), jnp.float32)] * GROUPS,
        compiler_params=pltpu.CompilerParams(vmem_limit_bytes=VMEM_BYTES),
        name="layout",
    )(far(dictionary))


class Ferry:
    def __init__(self, source, target, first, buffer, sems):
        self.steps = []
        for step in range(buffer.shape[0] // SUBLANES):
            held = buffer.at[pl.ds(step * SUBLANES, SUBLANES)]
            rows = pl.ds(first + step * SUBLANES, SUBLANES)
            fetch = pltpu.make_async_copy(source.at[rows], held, sems.at[0, step])
            store = pltpu.make_async_copy(held, target.at[rows], sems.at[1, step])
            fetch.start()
            self.steps.append((fetch, store))

    def turn_round(self):
        for fetch, store in self.steps:
            fetch.wait()
            store.start()

    def close(self):
        for _, store in self.steps:
            store.wait()


def ferry_scratch(count, entries):
    return [
        pltpu.VMEM((count, entries), jnp.float32),
        pltpu.SemaphoreType.DMA((2, count // SUBLANES)),
    ]


def lag_rows(zb, begin, count, zz):
    rows = count + ROWS
    for coarse in range(COARSE):
        first = begin - ROWS - ROWS * coarse
        zz[:rows, coarse * K : (coarse + 1) * K] = zb[first : first + rows, :]


def convolve_lags(lag, columns, count, taps, zz, fine, acc):
    channels = len(columns) * LANES
    own = slice(columns[0] * LANES, columns[0] * LANES + channels)
    rows = count + ROWS
    slot = lag // FINE % 2 * FINE
    for pair in range(0, FINE, 2):
        weights = jnp.concatenate(
            [
                jnp.concatenate([taps[m, lag + pair + j, own, :] for m in range(COARSE)], axis=1)
                for j in range(2)
            ],
            axis=0,
        )
        product = lax.dot_general(zz[:rows, :], weights, NT, preferred_element_type=jnp.float32)
        for j in range(2):
            for index, tile in enumerate(columns):
                column = j * channels + index * LANES
                fine[slot + pair + j, tile, :rows, :] = product[:, column : column + LANES]
    for tile in columns:
        total = None if lag == 0 else acc[tile, :count, :]
        for j in range(FINE):
            first = ROWS - lag - j
            part = fine[slot + j, tile, first : first + count, :]
            total = part if total is None else total + part
        acc[tile, :count, :] = total


def convolve(zb, begin, count, taps, zz, fine, acc):
    lag_rows(zb, begin, count, zz)
    columns = list(range(taps.shape[2] // LANES))
    for lag in range(0, ROWS, FINE):
        convolve_lags(lag, columns, count, taps, zz, fine, acc)


def correlate(rb, count, taps, rr, fine, acc):
    channels = taps.shape[2]
    rows = count + ROWS
    for coarse in range(COARSE):
        first = ROWS * coarse
        rr[:rows, coarse * channels : (coarse + 1) * channels] = rb[first : first + rows, :]
    for lag in range(0, ROWS, FINE):
        slot = lag // FINE % 2 * FINE
        for pair in range(0, FINE, 2):
            weights = jnp.concatenate(
                [
                    jnp.concatenate([taps[m, lag + pair + j] for m in range(COARSE)], axis=0)
                    for j in range(2)
                ],
                axis=1,
            )
            product = lax.dot_general(rr[:rows, :], weights, NN, preferred_element_type=jnp.float32)
            for j in range(2):
                fine[slot + pair + j, 0, :rows, :] = product[:, j * K : (j + 1) * K]
        total = None if lag == 0 else acc[0, :count, :]
        for j in range(FINE):
            part = fine[slot + j, 0, lag + j : lag + j + count, :]
            total = part if total is None else total + part
        acc[0, :count, :] = total


def patch_taps(row, atoms_ref, taps, columns, turned, convolve_after):
    lane = lax.broadcasted_iota(jnp.int32, (ROWS, K), 1)
    kept = (lane < row) | (lane >= row + BLOCK_ATOMS)
    keep = kept.astype(jnp.float32).astype(jnp.bfloat16)
    columns[...] = jnp.zeros_like(columns)
    width = ROWS * L
    steps = LANES // (GROUPS * ROWS)

    def patch(step, after):
        part = pl.ds(pl.multiple_of(step * (GROUPS * width), LANES), GROUPS * width)
        columns[pl.ds(row, BLOCK_ATOMS), :] = atoms_ref[:, part].astype(jnp.bfloat16)
        turn(columns[:, :width], turned[0])
        for group in range(GROUPS):
            if group + 1 < GROUPS:
                turn(columns[:, (group + 1) * width : (group + 2) * width], turned[group + 1])
            own = pl.ds(pl.multiple_of((step * GROUPS + group) * ROWS, ROWS), ROWS)
            for tap in range(L):
                before = taps[tap // ROWS, tap % ROWS, own, :]
                taps[tap // ROWS, tap % ROWS, own, :] = before * keep + tap_of(turned[group], tap)
            after(group)

    def alone(step, carry):
        patch(step, lambda group: None)
        return carry

    lax.fori_loop(0, steps, alone, 0)
    tiles = taps.shape[2] // LANES
    lags = list(range(0, ROWS, FINE))
    for tile in range(1, tiles):
        for step in range(steps):

            def after(group):
                done = (step * GROUPS + group + 1) * len(lags) // (steps * GROUPS)
                past = (step * GROUPS + group) * len(lags) // (steps * GROUPS)
                for index in range(past, done):
                    convolve_after(lags[index], tile - 1)

            patch(tile * steps + step, after)
    for lag in lags:
        convolve_after(lag, tiles - 1)


def put_edges(edge_refs, rightward, leftward):
    even = lax.axis_index("tm") % 2 == 0

    def put(first, second):
        first[...] = rightward
        second[...] = leftward

    pl.when(even)(lambda: put(*edge_refs))
    pl.when(jnp.logical_not(even))(lambda: put(*edge_refs[::-1]))


def by_side(put, first_ref, second_ref):
    even = lax.axis_index("tm") % 2 == 0
    pl.when(even)(lambda: put(second_ref, first_ref))
    pl.when(jnp.logical_not(even))(lambda: put(first_ref, second_ref))


def begin_kernel(code_hbm, signal_hbm, state_out, signal_out, first_out, second_out, code_ref, signal_ref, sems):
    fetches = [
        pltpu.make_async_copy(code_hbm, code_ref, sems.at[0]),
        pltpu.make_async_copy(signal_hbm, signal_ref, sems.at[1]),
    ]
    for fetch in fetches:
        fetch.start()
    for fetch in fetches:
        fetch.wait()
    state = code_ref[...].T
    signal = signal_ref[...].astype(jnp.float32).T.astype(jnp.bfloat16)
    state_out[...] = state
    signal_out[...] = signal
    both = jnp.concatenate([state.astype(jnp.bfloat16), signal], axis=1)
    put_edges((first_out, second_out), both[-L:], both[:L])


def begin(code, signal):
    channels, segment = signal.shape
    return pl.pallas_call(
        begin_kernel,
        in_specs=[hbm()] * 2,
        out_specs=[vmem()] * 4,
        out_shape=[
            pltpu.VMEM((segment, K), jnp.float32),
            pltpu.VMEM((segment, channels), jnp.bfloat16),
        ]
        + [jax.ShapeDtypeStruct((L, K + channels), jnp.bfloat16)] * 2,
        scratch_shapes=[
            pltpu.VMEM(code.shape, code.dtype),
            pltpu.VMEM(signal.shape, signal.dtype),
            pltpu.SemaphoreType.DMA((2,)),
        ],
        compiler_params=pltpu.CompilerParams(vmem_limit_bytes=VMEM_BYTES),
        name="begin",
    )(far(code), far(signal))


def taker(refs):
    refs = list(refs)

    def take(count):
        taken = refs[:count]
        del refs[:count]
        return taken

    return take


def residual_rows(rb, pieces, start, acc, total_time):
    rows = rb.shape[0]
    moment = start + lax.broadcasted_iota(jnp.int32, (rows, LANES), 0)
    scale = (C * L) ** (-0.5)
    for tile in range(acc.shape[0]):
        column = slice(tile * LANES, (tile + 1) * LANES)
        signal = jnp.concatenate([piece[:, column] for piece in pieces], axis=0)
        value = signal.astype(jnp.float32) - scale * acc[tile, :rows, :]
        rb[:, column] = jnp.where(moment < total_time, value, 0.0).astype(jnp.bfloat16)


def stepped_codes(state, acc, limit):
    scale = (C * L) ** (-0.5)
    stepped = state + code_rate * (scale * acc[0, : state.shape[0], :])
    return stepped - jnp.clip(stepped, -limit, limit)


def iterate_kernel(total_time, patching, first_copied, plan_ref, limit_ref, *refs):
    take = taker(refs)
    state_ref, first_ref, second_ref, signal_ref, next_first, next_second = take(6)
    atoms = take(1 if patching else 0)
    (taps,) = take(1)
    source = take(2 if patching else 0)
    state_out, *edges = take(3)
    taps = (take(1) if patching else [taps])[0]
    target = take(1 if patching else 0)
    zb, rb, zz, rr, fine, acc, beyond = take(7)
    ferry = Ferry(source[0], target[0], first_copied, *take(2)) if patching else None
    segment, channels = signal_ref.shape
    zb[L : L + segment, :] = state_ref[...].astype(jnp.bfloat16)

    def put(left, right):
        zb[:L, :] = left[:, :K]
        zb[L + segment :, :] = right[:, :K]

    def put_signal(left, right):
        beyond[...] = right[:, K:]

    by_side(put, first_ref, second_ref)
    by_side(put_signal, next_first, next_second)
    if patching:
        columns, *turned = take(1 + GROUPS)
        lag_rows(zb, L, segment + L, zz)

        def convolve_after(lag, tile):
            convolve_lags(lag, [tile], segment + L, taps, zz, fine, acc)

        patch_taps(
            first_row_of(plan_ref, patching - 1), atoms[0], taps, columns, turned, convolve_after
        )
        ferry.turn_round()
    else:
        convolve(zb, L, segment + L, taps, zz, fine, acc)
    start = lax.axis_index("tm") * segment
    residual_rows(rb, (signal_ref, beyond), start, acc, total_time)
    correlate(rb, segment, taps, rr, fine, acc)
    state = stepped_codes(state_ref[...], acc, limit_ref[...])
    state_out[...] = state
    low = state.astype(jnp.bfloat16)
    put_edges(edges, low[-L:], low[:L])
    if ferry:
        ferry.close()


def iterate(plan, step, limit, state, swapped, signal, following, taps, atoms, ferry, peers):
    segment, channels = signal.shape
    patching = atoms is not None
    reach = segment + L
    carried = [far(value) for value in ferry[:2]] if patching else []
    return pl.pallas_call(
        functools.partial(iterate_kernel, peers * segment, step if patching else 0, ferry[2]),
        in_specs=[scalars()] + [vmem()] * (8 + patching) + [hbm()] * len(carried),
        out_specs=[vmem()] * (3 + patching) + [hbm()] * patching,
        out_shape=[pltpu.VMEM((segment, K), jnp.float32)]
        + [jax.ShapeDtypeStruct((L, K), jnp.bfloat16)] * 2
        + [pltpu.VMEM(taps.shape, jnp.bfloat16)] * patching
        + [pltpu.HBM(ferry[0].shape, jnp.float32)] * patching,
        scratch_shapes=[
            pltpu.VMEM((L + reach, K), jnp.bfloat16),
            pltpu.VMEM((reach, channels), jnp.bfloat16),
            pltpu.VMEM((reach + ROWS, COARSE * K), jnp.bfloat16),
            pltpu.VMEM((segment + ROWS, COARSE * channels), jnp.bfloat16),
            pltpu.VMEM((2 * FINE, channels // LANES, reach + ROWS, LANES), jnp.float32),
            pltpu.VMEM((channels // LANES, reach, LANES), jnp.float32),
            pltpu.VMEM((L, channels), jnp.bfloat16),
        ]
        + (
            ferry_scratch(ferry[3], ferry[0].shape[1])
            + [pltpu.VMEM((K, GROUPS * ROWS * L), jnp.bfloat16)]
            + [pltpu.VMEM((ROWS * STRIDE, K), jnp.float32)] * GROUPS
        )
        * patching,
        input_output_aliases={9: 3, 11: 4} if patching else {},
        compiler_params=pltpu.CompilerParams(vmem_limit_bytes=VMEM_BYTES),
        name="iterate",
    )(
        plan,
        limit,
        resident(state),
        *swapped,
        resident(signal),
        *following,
        *([resident(atoms)] if patching else []),
        resident(taps),
        *carried,
    )


def conclude_kernel(peers, step, copied, plan_ref, limit_ref, *refs):
    last = step + 1 == OUTER
    take = taker(refs)
    state_ref, first_ref, second_ref, signal_ref, next_first, next_second, taps = take(7)
    source = take(2 if copied else 1)[0]
    (payload_out,) = take(1)
    state_out, partial_out, codes_out = (None, *take(2)) if last else (*take(1), None, None)
    *edges, target = take(3)
    zb, rb, zz, rr, fine, acc, beyond, tall, packed = take(9)
    ferry = Ferry(source, target, copied, *take(2))
    if not last:
        (codes_out,) = take(1)
    segment, channels = signal_ref.shape
    reach = segment + L
    zb[L:reach, :] = state_ref[...].astype(jnp.bfloat16)

    def put(left, right):
        zb[:L, :] = left[...]
        zb[reach:, :] = right[...]

    def put_signal(left, right):
        beyond[...] = right[:, K:]

    by_side(put, first_ref, second_ref)
    by_side(put_signal, next_first, next_second)
    convolve(zb, L, reach, taps, zz, fine, acc)
    ferry.turn_round()
    start = lax.axis_index("tm") * segment
    residual_rows(rb, (signal_ref, beyond), start, acc, peers * segment)
    correlate(rb, segment, taps, rr, fine, acc)
    state = stepped_codes(state_ref[...], acc, limit_ref[...])
    low = state.astype(jnp.bfloat16)
    if not last:
        state_out[...] = state
    put_edges(edges, low[-L:], low[:L])
    codes_out[...] = state.T
    zb[:L, :] = jnp.zeros((L, K), jnp.bfloat16)
    zb[L:reach, :] = low
    zb[reach:, :] = jnp.zeros((L, K), jnp.bfloat16)
    convolve(zb, L, reach, taps, zz, fine, acc)
    scale = (C * L) ** (-0.5)
    block = codes_out[pl.ds(first_row_of(plan_ref, step), BLOCK_ATOMS), :]
    share = channels // peers
    for tile in range(channels // LANES):
        column = slice(tile * LANES, (tile + 1) * LANES)
        value = signal_ref[:, column].astype(jnp.float32) - scale * acc[tile, :segment, :]
        if last:
            partial_out[:, column] = value
        tall[0, column, :] = value.T
        spill = jnp.concatenate(
            [-scale * acc[tile, segment:reach, :], jnp.zeros((segment - L, LANES), jnp.float32)], axis=0
        )
        tall[1, column, :] = spill.T
    for peer in range(peers):
        for part in range(2):
            packed[peer, part * share : (part + 1) * share, :] = tall[
                part, peer * share : (peer + 1) * share, :
            ]
        packed[peer, 2 * share :, :] = block
    payload_out[...] = packed[...].astype(jnp.bfloat16)
    ferry.close()


def conclude(plan, step, limit, state, swapped, signal, following, taps, ferry, peers):
    segment, channels = signal.shape
    share = channels // peers
    last = step + 1 == OUTER
    carried = [far(value) for value in ferry[:2] if value is not None]
    reach = segment + L
    outs = [pltpu.VMEM((segment, K), jnp.float32)]
    if last:
        outs = [pltpu.VMEM((segment, channels), jnp.float32), pltpu.VMEM((K, segment), jnp.float32)]
    outs += [jax.ShapeDtypeStruct((L, K), jnp.bfloat16)] * 2
    return pl.pallas_call(
        functools.partial(conclude_kernel, peers, step, ferry[2]),
        in_specs=[scalars()] + [vmem()] * 8 + [hbm()] * len(carried),
        out_specs=[vmem()] * (1 + len(outs)) + [hbm()],
        out_shape=[jax.ShapeDtypeStruct((peers, 2 * share + BLOCK_ATOMS, segment), jnp.bfloat16)]
        + outs
        + [pltpu.HBM(ferry[0].shape, jnp.float32)],
        scratch_shapes=[
            pltpu.VMEM((L + reach, K), jnp.bfloat16),
            pltpu.VMEM((reach, channels), jnp.bfloat16),
            pltpu.VMEM((reach + ROWS, COARSE * K), jnp.bfloat16),
            pltpu.VMEM((segment + ROWS, COARSE * channels), jnp.bfloat16),
            pltpu.VMEM((2 * FINE, channels // LANES, reach + ROWS, LANES), jnp.float32),
            pltpu.VMEM((channels // LANES, reach, LANES), jnp.float32),
            pltpu.VMEM((L, channels), jnp.bfloat16),
            pltpu.VMEM((2, channels, segment), jnp.float32),
            pltpu.VMEM((peers, 2 * share + BLOCK_ATOMS, segment), jnp.float32),
        ]
        + ferry_scratch(ferry[3], ferry[0].shape[1])
        + ([] if last else [pltpu.VMEM((K, segment), jnp.float32)]),
        input_output_aliases={10: 1 + len(outs)} if len(carried) == 2 else {},
        compiler_params=pltpu.CompilerParams(vmem_limit_bytes=VMEM_BYTES),
        name="conclude",
    )(
        plan,
        limit,
        resident(state),
        *swapped,
        resident(signal),
        *following,
        resident(taps),
        *carried,
    )


def settle_kernel(earlier, plan_ref, partial_ref, first_ref, second_ref, taps, *refs):
    take = taker(refs)
    atoms = take(earlier)
    _, resid_out, dict_out, zb, zz, fine, acc, sems = refs[earlier:]
    segment, channels = partial_ref.shape
    stores = [
        pltpu.make_async_copy(
            atoms[step], dict_out.at[pl.ds(first_row_of(plan_ref, step), BLOCK_ATOMS)], sems.at[step]
        )
        for step in range(earlier)
    ]
    for store in stores:
        store.start()

    def put(left, right):
        zb[:L, :] = left[...]

    zb[L:, :] = jnp.zeros((L, K), jnp.bfloat16)
    by_side(put, first_ref, second_ref)
    convolve(zb, L, L, taps, zz, fine, acc)
    scale = (C * L) ** (-0.5)
    for tile in range(channels // LANES):
        column = slice(tile * LANES, (tile + 1) * LANES)
        value = jnp.concatenate(
            [partial_ref[:L, column] - scale * acc[tile], partial_ref[L:, column]], axis=0
        )
        resid_out[column, :] = value.T
    for store in stores:
        store.wait()


def settle(plan, partial, swapped, taps, renewed, dictionary):
    segment, channels = partial.shape
    earlier = len(renewed)
    return pl.pallas_call(
        functools.partial(settle_kernel, earlier),
        in_specs=[scalars()] + [vmem()] * (4 + earlier) + [hbm()],
        out_specs=[vmem(), hbm()],
        out_shape=[
            pltpu.VMEM((channels, segment), jnp.float32),
            pltpu.HBM(dictionary.shape, jnp.float32),
        ],
        scratch_shapes=[
            pltpu.VMEM((2 * L, K), jnp.bfloat16),
            pltpu.VMEM((L + ROWS, COARSE * K), jnp.bfloat16),
            pltpu.VMEM((2 * FINE, channels // LANES, L + ROWS, LANES), jnp.float32),
            pltpu.VMEM((channels // LANES, L, LANES), jnp.float32),
            pltpu.SemaphoreType.DMA((earlier,)),
        ],
        input_output_aliases={5 + earlier: 1},
        compiler_params=pltpu.CompilerParams(vmem_limit_bytes=VMEM_BYTES),
        name="settle",
    )(
        plan,
        resident(partial),
        *swapped,
        resident(taps),
        *[resident(value) for value in renewed],
        far(dictionary),
    )


def gradient_kernel(share, step, plan_ref, blocks_ref, dict_hbm, out_ref, packed, rf, zf, rr, zz, old, sem):
    peers, rows, segment = blocks_ref.shape
    share_rows = rf.shape[0]
    span = peers * segment
    entries = share * L
    rows_of = pl.ds(first_row_of(plan_ref, step), BLOCK_ATOMS)
    columns_of = pl.ds(pl.multiple_of(lax.axis_index("tm") * entries, LANES), entries)
    fetch = pltpu.make_async_copy(dict_hbm.at[rows_of, columns_of], old, sem)
    fetch.start()
    rf[:, span:] = jnp.zeros((share_rows, LANES), jnp.bfloat16)
    zf[:, :LANES] = jnp.zeros((BLOCK_ATOMS, LANES), jnp.bfloat16)
    packed[...] = blocks_ref[...].astype(jnp.float32)
    for peer in range(peers):
        column = peer * segment
        own = packed[peer, :share_rows, :]
        if peer:
            own += packed[peer - 1, share : share + share_rows, :]
        rf[:, column : column + segment] = own.astype(jnp.bfloat16)
        zf[:, LANES + column : LANES + column + segment] = packed[peer, 2 * share :, :].astype(
            jnp.bfloat16
        )
    for lag in range(ROWS):
        rr[lag * share_rows : (lag + 1) * share_rows, :] = rf[:, lag : lag + span]
    for coarse in range(COARSE):
        begin = LANES - ROWS * coarse
        zz[coarse * BLOCK_ATOMS : (coarse + 1) * BLOCK_ATOMS, :] = zf[:, begin : begin + span]
    lagged = lax.dot_general(zz[...], rr[...], NT, preferred_element_type=jnp.float32)
    wide = ROWS * share_rows
    parts = []
    left = lagged
    for _ in range(3):
        parts.append(left.astype(jnp.bfloat16))
        left = left - parts[-1].astype(jnp.float32)
    row = lax.broadcasted_iota(jnp.int32, (wide, wide), 0)
    column = lax.broadcasted_iota(jnp.int32, (wide, wide), 1)
    chosen = (row // share_rows == column % ROWS) & (row % share_rows == column // ROWS)
    chosen = chosen.astype(jnp.float32).astype(jnp.bfloat16)
    by_channel = lax.dot_general(
        jnp.concatenate(parts, axis=0), chosen, NN, preferred_element_type=jnp.float32
    )
    count = COARSE * BLOCK_ATOMS
    by_channel = by_channel[:count] + by_channel[count : 2 * count] + by_channel[2 * count :]
    lane = lax.broadcasted_iota(jnp.int32, (BLOCK_ATOMS, LANES), 1)
    tiles = []
    for tile in range(entries // LANES):
        total = jnp.zeros((BLOCK_ATOMS, LANES), jnp.float32)
        for place in range(LANES // ROWS):
            channel, coarse = divmod(tile * (LANES // ROWS) + place, COARSE)
            first = channel * ROWS // LANES * LANES
            source = by_channel[coarse * BLOCK_ATOMS : (coarse + 1) * BLOCK_ATOMS, first : first + LANES]
            by = (place * ROWS - channel * ROWS) % LANES
            moved = pltpu.roll(source, by, 1) if by else source
            total = jnp.where(lane // ROWS == place, moved, total)
        tiles.append(total)
    gradient = jnp.concatenate(tiles, axis=1)
    fetch.wait()
    before = old[...]
    square = jnp.sum(before * before, axis=1, keepdims=True)
    along = jnp.sum(gradient * before, axis=1, keepdims=True) / (square + tiny_eps)
    out_ref[:, :entries] = (gradient - along * before).astype(jnp.bfloat16)
    terms = jnp.zeros((BLOCK_ATOMS, LANES), jnp.float32)
    for i in range(3):
        term = along.astype(jnp.bfloat16).astype(jnp.float32)
        along = along - term
        terms = jnp.where(lane == i, term, terms)
    out_ref[:, entries:] = terms.astype(jnp.bfloat16)


def share_gradient(plan, step, blocks, dictionary, share):
    peers, rows, segment = blocks.shape
    share_rows = -(-share // ROWS) * ROWS
    span = peers * segment
    return pl.pallas_call(
        functools.partial(gradient_kernel, share, step),
        in_specs=[scalars(), vmem(), hbm()],
        out_shape=jax.ShapeDtypeStruct((BLOCK_ATOMS, share * L + LANES), jnp.bfloat16),
        scratch_shapes=[
            pltpu.VMEM(blocks.shape, jnp.float32),
            pltpu.VMEM((share_rows, span + LANES), jnp.bfloat16),
            pltpu.VMEM((BLOCK_ATOMS, LANES + span), jnp.bfloat16),
            pltpu.VMEM((ROWS * share_rows, span), jnp.bfloat16),
            pltpu.VMEM((COARSE * BLOCK_ATOMS, span), jnp.bfloat16),
            pltpu.VMEM((BLOCK_ATOMS, share * L), jnp.float32),
            pltpu.SemaphoreType.DMA,
        ],
        compiler_params=pltpu.CompilerParams(vmem_limit_bytes=VMEM_BYTES),
        name="gradient",
    )(plan, blocks, far(dictionary))


def gather_steps(peers):
    bits = [1 << i for i in range(peers.bit_length() - 2, 0, -1)]
    steps = []
    for first in range(0, len(bits), 2):
        pair = bits[first : first + 2]
        steps.append(pair + [sum(pair)] if len(pair) == 2 else pair)
    return steps


def gather_slots(peers):
    flips = [0]
    for masks in gather_steps(peers):
        flips = [f ^ m for m in [0] + masks for f in flips]
    return flips


def gather_pieces(piece, meanwhile):
    peers = lax.axis_size("tm")

    def exchanged(shard, mask):
        return lax.ppermute(shard, "tm", [(i, i ^ mask) for i in range(peers)])

    held = piece[None]
    for index, masks in enumerate(gather_steps(peers)):
        held = jnp.concatenate([held] + [exchanged(held, mask) for mask in masks], axis=0)
        if index == 0:
            needed, extra = meanwhile(held)
    ready, _ = lax.optimization_barrier((held, needed))
    return held, exchanged(ready, 1), extra


def recall_kernel(plan_ref, dict_hbm, when_ref, *refs):
    del when_ref
    take = taker(refs)
    olds, means = take(OUTER), take(OUTER)
    (sems,) = take(1)
    entries = olds[0].shape[1]
    fetches = [
        pltpu.make_async_copy(
            dict_hbm.at[pl.ds(first_row_of(plan_ref, step), BLOCK_ATOMS)], olds[step], sems.at[step]
        )
        for step in range(OUTER)
    ]
    for fetch in fetches:
        fetch.start()
    width = 9 * LANES if entries % (9 * LANES) == 0 else LANES
    for fetch, old_ref, mean_ref in zip(fetches, olds, means):
        fetch.wait()

        def add(step, square):
            before = old_ref[:, pl.ds(pl.multiple_of(step * width, LANES), width)]
            return square + before * before

        zeros = jnp.zeros((BLOCK_ATOMS, width), jnp.float32)
        square = lax.fori_loop(0, entries // width, add, zeros)
        mean_sq = jnp.sum(square, axis=1, keepdims=True) / (C * L) + tiny_eps
        mean_ref[...] = jnp.broadcast_to(mean_sq, mean_ref.shape)


def recall(plan, dictionary, when):
    entries = dictionary.shape[1]
    results = pl.pallas_call(
        recall_kernel,
        in_specs=[scalars(), hbm(), pl.BlockSpec(memory_space=pl.ANY)],
        out_specs=[vmem()] * (2 * OUTER),
        out_shape=[pltpu.VMEM((BLOCK_ATOMS, entries), jnp.float32)] * OUTER
        + [pltpu.VMEM((BLOCK_ATOMS, LANES), jnp.float32)] * OUTER,
        scratch_shapes=[pltpu.SemaphoreType.DMA((OUTER,))],
        compiler_params=pltpu.CompilerParams(vmem_limit_bytes=VMEM_BYTES),
        name="recall",
    )(plan, far(dictionary), when)
    return list(zip(results[:OUTER], results[OUTER:]))


def renew_kernel(plan_step, plan_ref, held_ref, came_ref, old, mean_ref, *refs):
    me = lax.axis_index("tm")
    half, _, wide = held_ref.shape
    width = wide - LANES
    entries = C * L
    last = plan_step + 1 == OUTER
    if last:
        _, out_hbm, atoms_ref, grad, sems = refs
    else:
        atoms_ref, grad = refs

    stores = []
    shares = []
    for slot, flips in enumerate(gather_slots(2 * half)):
        for source, extra in ((held_ref, 0), (came_ref, 1)):
            owner = me ^ (flips + extra)
            shares.append((source.at[slot], pl.ds(pl.multiple_of(owner * width, LANES), width)))
    zeros = jnp.zeros((BLOCK_ATOMS, width), jnp.float32)
    dot = zeros
    for source, column in shares:
        before = old[:, column]
        along = jnp.sum(source[:, width:].astype(jnp.float32), axis=1, keepdims=True)
        value = source[:, :width].astype(jnp.float32) + along * before
        grad[:, column] = value
        dot += value * before
    mean_sq = mean_ref[:, :1]
    along = jnp.sum(dot, axis=1, keepdims=True) / entries / mean_sq
    square = zeros
    for _, column in shares:
        value = grad[:, column] - along * old[:, column]
        square += value * value
    spread = jnp.sum(square, axis=1, keepdims=True) / entries + tiny_eps
    step = move_rate / jnp.sqrt(spread)
    norm = 1.0 / jnp.sqrt(mean_sq + 0.25)
    rows = pl.ds(first_row_of(plan_ref, plan_step), BLOCK_ATOMS)
    for index, (_, column) in enumerate(shares):
        before = old[:, column]
        across = grad[:, column] - along * before
        atoms_ref[:, column] = (before + step * across) * norm
        if last:
            stores.append(
                pltpu.make_async_copy(
                    atoms_ref.at[:, column], out_hbm.at[rows, column], sems.at[index]
                )
            )
            stores[-1].start()
    for store in stores:
        store.wait()


def renew(plan, step, held, came, old, mean_sq, dictionary):
    last = dictionary is not None
    atoms = (BLOCK_ATOMS, old.shape[1])
    scratch = [pltpu.VMEM(atoms, jnp.float32)]
    if last:
        scratch = scratch * 2 + [pltpu.SemaphoreType.DMA((2 * held.shape[0],))]
    return pl.pallas_call(
        functools.partial(renew_kernel, step),
        in_specs=[scalars()] + [vmem()] * 4 + [hbm()] * last,
        out_specs=hbm() if last else vmem(),
        out_shape=pltpu.HBM(dictionary.shape, jnp.float32) if last else pltpu.VMEM(atoms, jnp.float32),
        scratch_shapes=scratch,
        input_output_aliases={5: 0} if last else {},
        compiler_params=pltpu.CompilerParams(vmem_limit_bytes=VMEM_BYTES),
        name="renew",
    )(plan, held, came, resident(old), resident(mean_sq), *([far(dictionary)] if last else []))


def whole_channels(signal, codes_init, dictionary_init, threshold, plan):
    channels, segment = signal.shape
    peers = lax.axis_size("tm")
    limit = threshold[None, :]
    def swaps(edges):
        ends = [range(first, peers - 1, 2) for first in (0, 1)]
        pairs = [[p for i in end for p in ((i, i + 1), (i + 1, i))] for end in ends]
        far_first = [lax.ppermute(edge, "tm", pair) for edge, pair in zip(edges[::-1], pairs[::-1])]
        return far_first[::-1]

    state, signal, *edges = begin(codes_init, signal)
    following = swaps(edges)
    swapped = following
    taps = layout(dictionary_init, channels)
    dictionary = None
    renewed = []
    for step in range(OUTER):
        last = step + 1 == OUTER
        ferry = (dictionary_init, dictionary, COPIED[0], COPIED[1])
        atoms = renewed[-1] if renewed else None
        state, *results = iterate(
            plan, step, limit, state, swapped, signal, following, taps, atoms, ferry, peers
        )
        edges = results[:2]
        if renewed:
            taps, dictionary = results[2:]
        ferry = (dictionary_init, dictionary, sum(COPIED[: 2 * step]), COPIED[2 * step])
        payload, *results, first_edge, second_edge, dictionary = conclude(
            plan, step, limit, state, swaps(edges), signal, following, taps, ferry, peers
        )
        edges = [first_edge, second_edge]
        blocks = lax.all_to_all(payload, "tm", 0, 0, tiled=True)
        piece = share_gradient(plan, step, blocks, dictionary_init, channels // peers)
        edges, _ = lax.optimization_barrier((edges, piece))
        swapped = swaps(edges)

        def beside(held):
            if not last:
                recalled = recall(plan, dictionary_init, held)
                return (recalled[0][0], swapped), recalled
            partial, _ = lax.optimization_barrier((results[0], held))
            settled = settle(plan, partial, swapped, taps, renewed, dictionary)
            return settled[0], settled

        held, came, extra = gather_pieces(piece, beside)
        if last:
            residual, dictionary = extra
            dictionary = renew(plan, step, held, came, *recalled[step], dictionary)
        else:
            recalled, state = extra, results[0]
            renewed.append(renew(plan, step, held, came, *recalled[step], None))
    return results[1], dictionary, residual


def renew_atoms(old_atoms, across, mean_sq, spread):
    return (old_atoms + move_rate * across / jnp.sqrt(spread)[:, None]) / jnp.sqrt(mean_sq + 0.25)[
        :, None
    ]


def split_channels(signal, codes_init, dictionary_init, threshold, plan):
    segment = signal.shape[1]
    local_chan = signal.shape[0]
    unit_scale = (C * L) ** (-0.5)
    entries = C * L
    limit = threshold[:, None]

    def convolve(atom_cube, code_low):
        code_edge = shifted(code_low[:, segment - (L - 1) :], "tm", 1)
        extended = jnp.concatenate([code_edge, code_low], axis=1)
        lagged = jnp.stack(
            [extended[:, L - 1 - offset : L - 1 - offset + segment] for offset in range(L)], axis=1
        )
        return unit_scale * jnp.einsum(
            "kcl,klt->ct", atom_cube, lagged, preferred_element_type=jnp.float32
        )

    def resid_columns(resid_low):
        resid_edge = shifted(resid_low[:, : L - 1], "tm", -1)
        extended = jnp.concatenate([resid_low, resid_edge], axis=1)
        lagged = jnp.stack([extended[:, offset : offset + segment] for offset in range(L)], axis=1)
        return lagged.reshape(local_chan * L, segment)

    code_state = codes_init
    dictionary = dictionary_init
    residual = signal.astype(jnp.float32)
    for outer_step in range(OUTER):
        dict_low = dictionary.astype(jnp.bfloat16)
        atom_cube = dict_low.reshape(K, local_chan, L)
        for inner_step in range(INNER):
            code_low = code_state.astype(jnp.bfloat16)
            residual = signal.astype(jnp.float32) - convolve(atom_cube, code_low)
            lagged = resid_columns(residual.astype(jnp.bfloat16))
            partial_value = unit_scale * jnp.dot(
                dict_low, lagged, preferred_element_type=jnp.float32
            )
            scores = lax.psum(partial_value.astype(jnp.bfloat16), "chan").astype(jnp.float32)
            stepped = code_state + code_rate * scores
            code_state = stepped - jnp.clip(stepped, -limit, limit)
        code_low = code_state.astype(jnp.bfloat16)
        residual = signal.astype(jnp.float32) - convolve(atom_cube, code_low)
        lagged = resid_columns(residual.astype(jnp.bfloat16))
        first_row = plan[outer_step] * BLOCK_ATOMS
        code_block = lax.dynamic_slice_in_dim(code_low, first_row, BLOCK_ATOMS, 0)
        local_grad = lax.dot_general(
            code_block, lagged, (((1,), (1,)), ((), ())), preferred_element_type=jnp.float32
        )
        old_atoms = lax.dynamic_slice_in_dim(dictionary, first_row, BLOCK_ATOMS, 0)
        gradient = lax.psum(local_grad, "tm")
        dot_sum, square_sum = lax.psum(
            (jnp.sum(gradient * old_atoms, axis=1), jnp.sum(old_atoms * old_atoms, axis=1)), "chan"
        )
        mean_sq = square_sum / entries + tiny_eps
        along_coef = dot_sum / entries / mean_sq
        across = gradient - along_coef[:, None] * old_atoms
        spread = lax.psum(jnp.sum(across * across, axis=1), "chan") / entries + tiny_eps
        renewed = renew_atoms(old_atoms, across, mean_sq, spread)
        dictionary = lax.dynamic_update_slice_in_dim(dictionary, renewed, first_row, 0)
    return (code_state, dictionary, residual)


def shards(signal, codes_init, dictionary_init, threshold, plan):
    channels, segment = signal.shape
    peers = lax.axis_size("tm")
    fits = (
        lax.axis_size("chan") == 1
        and segment % LANES == 0
        and INNER == 2
        and OUTER == 2
        and channels % LANES == 0
        and channels % peers == 0
        and (channels // peers * L) % LANES == 0
        and peers > 2
        and peers & (peers - 1) == 0
    )
    body = whole_channels if fits else split_channels
    return body(signal, codes_init, dictionary_init, threshold, plan)


def solution(mesh):
    placed = (P("chan", "tm"), P(None, "tm"), P(None, "chan"), P(), P())
    return jax.shard_map(
        shards,
        mesh=mesh,
        in_specs=placed,
        out_specs=(P(None, "tm"), P(None, "chan"), P("chan", "tm")),
        check_vma=False,
    )
```

```python
import functools

import jax
import jax.numpy as jnp
from jax import lax
from jax.experimental import pallas as pl
from jax.experimental.pallas import tpu as pltpu
from jax.sharding import PartitionSpec as P

C = 384
K = 128
L = 96
BLOCK_ATOMS = 16
INNER = 2
OUTER = 2

code_rate = 0.3
move_rate = 0.5
tiny_eps = 1e-06

ROWS = 16
COARSE = L // ROWS
STRIDE = L + 1
GROUPS = 4
SUBLANES = 8
COPIED = (48, 40, 40)
FINE = 4
LANES = 128
VMEM_BYTES = 24 * 1024 * 1024

NN = (((1,), (0,)), ((), ()))
NT = (((1,), (1,)), ((), ()))


def shifted(shard, axis, by):
    peers = lax.axis_size(axis)
    pairs = [(i, i + by) for i in range(peers) if 0 <= i + by < peers]
    return lax.ppermute(shard, axis, pairs)


def resident(value):
    return pltpu.with_memory_space_constraint(value, pltpu.VMEM)


def far(value):
    return pltpu.with_memory_space_constraint(value, pltpu.HBM)


def hbm():
    return pl.BlockSpec(memory_space=pltpu.HBM)


def scalars():
    return pl.BlockSpec(memory_space=pltpu.SMEM)


def first_row_of(plan_ref, step):
    return pl.multiple_of(plan_ref[step] * BLOCK_ATOMS, BLOCK_ATOMS)


def vmem():
    return pl.BlockSpec(memory_space=pltpu.VMEM)


def turn(columns, turned_ref):
    side = 2 * LANES
    row = lax.broadcasted_iota(jnp.int32, (side, side), 0)
    column = lax.broadcasted_iota(jnp.int32, (side, side), 1)
    identity = (row == column).astype(jnp.float32).astype(jnp.bfloat16)

    def put(entry, rows):
        end = entry + rows.shape[0]
        begin = entry
        while begin < end:
            channel, tap = begin // L, begin % L
            count = min(end - begin, L - tap)
            target = channel * STRIDE + tap
            turned_ref[target : target + count, :] = rows[begin - entry : begin - entry + count]
            begin += count

    low = columns.astype(jnp.bfloat16)
    through_matrix = ROWS * L // (6 * side) * 4 * side
    for first in range(0, through_matrix, 2 * side):
        pair = jnp.concatenate(
            [low[:, first + half * side : first + (half + 1) * side] for half in range(2)], axis=0
        )
        turned = lax.dot_general(identity, pair, NT, preferred_element_type=jnp.float32)
        for half in range(2):
            put(first + half * side, turned[:, half * K : (half + 1) * K])
    for first in range(through_matrix, ROWS * L, LANES):
        put(first, columns[:, first : first + LANES].astype(jnp.float32).T)


def tap_of(turned_ref, tap):
    return turned_ref[pl.ds(tap, ROWS, stride=STRIDE), :].astype(jnp.bfloat16)


def layout_kernel(dict_ref, taps_ref, *turned):
    def part(group):
        return dict_ref[:, group * ROWS * L : (group + 1) * ROWS * L]

    turn(part(0), turned[0])
    for group in range(GROUPS):
        if group + 1 < GROUPS:
            turn(part(group + 1), turned[group + 1])
        own = pl.ds(pl.multiple_of((pl.program_id(0) * GROUPS + group) * ROWS, ROWS), ROWS)
        for tap in range(L):
            taps_ref[tap // ROWS, tap % ROWS, own, :] = tap_of(turned[group], tap)


def layout(dictionary, channels):
    block = GROUPS * ROWS
    return pl.pallas_call(
        layout_kernel,
        grid=(channels // block,),
        in_specs=[pl.BlockSpec((K, block * L), lambda i: (0, i))],
        out_specs=vmem(),
        out_shape=pltpu.VMEM((COARSE, ROWS, channels, K), jnp.bfloat16),
        scratch_shapes=[pltpu.VMEM((ROWS * STRIDE, K), jnp.float32)] * GROUPS,
        compiler_params=pltpu.CompilerParams(vmem_limit_bytes=VMEM_BYTES),
        name="layout",
    )(far(dictionary))


class Ferry:
    def __init__(self, source, target, first, buffer, sems):
        self.steps = []
        for step in range(buffer.shape[0] // SUBLANES):
            held = buffer.at[pl.ds(step * SUBLANES, SUBLANES)]
            rows = pl.ds(first + step * SUBLANES, SUBLANES)
            fetch = pltpu.make_async_copy(source.at[rows], held, sems.at[0, step])
            store = pltpu.make_async_copy(held, target.at[rows], sems.at[1, step])
            fetch.start()
            self.steps.append((fetch, store))

    def turn_round(self):
        for fetch, store in self.steps:
            fetch.wait()
            store.start()

    def close(self):
        for _, store in self.steps:
            store.wait()


def ferry_scratch(count, entries):
    return [
        pltpu.VMEM((count, entries), jnp.float32),
        pltpu.SemaphoreType.DMA((2, count // SUBLANES)),
    ]


def lag_rows(zb, begin, count, zz):
    rows = count + ROWS
    for coarse in range(COARSE):
        first = begin - ROWS - ROWS * coarse
        zz[:rows, coarse * K : (coarse + 1) * K] = zb[first : first + rows, :]


def convolve_lags(lag, tile, count, taps, zz, fine, acc):
    own = slice(tile * LANES, (tile + 1) * LANES)
    rows = count + ROWS
    slot = lag // FINE % 2 * FINE
    for pair in range(0, FINE, 2):
        weights = jnp.concatenate(
            [
                jnp.concatenate([taps[m, lag + pair + j, own, :] for m in range(COARSE)], axis=1)
                for j in range(2)
            ],
            axis=0,
        )
        product = lax.dot_general(zz[:rows, :], weights, NT, preferred_element_type=jnp.float32)
        for j in range(2):
            fine[slot + pair + j, tile, :rows, :] = product[:, j * LANES : (j + 1) * LANES]
    total = None if lag == 0 else acc[tile, :count, :]
    for j in range(FINE):
        first = ROWS - lag - j
        part = fine[slot + j, tile, first : first + count, :]
        total = part if total is None else total + part
    acc[tile, :count, :] = total


def convolve(zb, begin, count, taps, zz, fine, acc, after):
    lag_rows(zb, begin, count, zz)
    for tile in range(taps.shape[2] // LANES):
        for lag in range(0, ROWS, FINE):
            convolve_lags(lag, tile, count, taps, zz, fine, acc)
        after(tile)


def correlate(count, taps, rr, fine, acc):
    rows = count + ROWS
    for lag in range(0, ROWS, FINE):
        slot = lag // FINE % 2 * FINE
        for pair in range(0, FINE, 2):
            weights = jnp.concatenate(
                [
                    jnp.concatenate([taps[m, lag + pair + j] for m in range(COARSE)], axis=0)
                    for j in range(2)
                ],
                axis=1,
            )
            product = lax.dot_general(rr[:rows, :], weights, NN, preferred_element_type=jnp.float32)
            for j in range(2):
                fine[slot + pair + j, 0, :rows, :] = product[:, j * K : (j + 1) * K]
        total = None if lag == 0 else acc[0, :count, :]
        for j in range(FINE):
            part = fine[slot + j, 0, lag + j : lag + j + count, :]
            total = part if total is None else total + part
        acc[0, :count, :] = total


def patch_taps(row, atoms_ref, taps, columns, turned, convolve_after):
    lane = lax.broadcasted_iota(jnp.int32, (ROWS, K), 1)
    kept = (lane < row) | (lane >= row + BLOCK_ATOMS)
    keep = kept.astype(jnp.float32).astype(jnp.bfloat16)
    columns[...] = jnp.zeros_like(columns)
    width = ROWS * L
    steps = LANES // (GROUPS * ROWS)

    def patch(step, after):
        part = pl.ds(pl.multiple_of(step * (GROUPS * width), LANES), GROUPS * width)
        columns[pl.ds(row, BLOCK_ATOMS), :] = atoms_ref[:, part].astype(jnp.bfloat16)
        turn(columns[:, :width], turned[0])
        for group in range(GROUPS):
            if group + 1 < GROUPS:
                turn(columns[:, (group + 1) * width : (group + 2) * width], turned[group + 1])
            own = pl.ds(pl.multiple_of((step * GROUPS + group) * ROWS, ROWS), ROWS)
            for tap in range(L):
                before = taps[tap // ROWS, tap % ROWS, own, :]
                taps[tap // ROWS, tap % ROWS, own, :] = before * keep + tap_of(turned[group], tap)
            after(group)

    def alone(step, carry):
        patch(step, lambda group: None)
        return carry

    lax.fori_loop(0, steps, alone, 0)
    tiles = taps.shape[2] // LANES
    lags = list(range(0, ROWS, FINE))
    for tile in range(1, tiles):
        for step in range(steps):

            def after(group):
                done = (step * GROUPS + group + 1) * len(lags) // (steps * GROUPS)
                past = (step * GROUPS + group) * len(lags) // (steps * GROUPS)
                for index in range(past, done):
                    convolve_after(lags[index], tile - 1)

            patch(tile * steps + step, after)
    for lag in lags:
        convolve_after(lag, tiles - 1)


def put_edges(edge_refs, rightward, leftward):
    even = lax.axis_index("tm") % 2 == 0

    def put(first, second):
        first[...] = rightward
        second[...] = leftward

    pl.when(even)(lambda: put(*edge_refs))
    pl.when(jnp.logical_not(even))(lambda: put(*edge_refs[::-1]))


def by_side(put, first_ref, second_ref):
    even = lax.axis_index("tm") % 2 == 0
    pl.when(even)(lambda: put(second_ref, first_ref))
    pl.when(jnp.logical_not(even))(lambda: put(first_ref, second_ref))


def begin_kernel(code_hbm, signal_hbm, state_out, signal_out, first_out, second_out, code_ref, signal_ref, sems):
    fetches = [
        pltpu.make_async_copy(code_hbm, code_ref, sems.at[0]),
        pltpu.make_async_copy(signal_hbm, signal_ref, sems.at[1]),
    ]
    for fetch in fetches:
        fetch.start()
    for fetch in fetches:
        fetch.wait()
    state = code_ref[...].T
    signal = signal_ref[...].astype(jnp.float32).T.astype(jnp.bfloat16)
    state_out[...] = state
    signal_out[...] = signal
    both = jnp.concatenate([state.astype(jnp.bfloat16), signal], axis=1)
    put_edges((first_out, second_out), both[-L:], both[:L])


def begin(code, signal):
    channels, segment = signal.shape
    return pl.pallas_call(
        begin_kernel,
        in_specs=[hbm()] * 2,
        out_specs=[vmem()] * 4,
        out_shape=[
            pltpu.VMEM((segment, K), jnp.float32),
            pltpu.VMEM((segment, channels), jnp.bfloat16),
        ]
        + [jax.ShapeDtypeStruct((L, K + channels), jnp.bfloat16)] * 2,
        scratch_shapes=[
            pltpu.VMEM(code.shape, code.dtype),
            pltpu.VMEM(signal.shape, signal.dtype),
            pltpu.SemaphoreType.DMA((2,)),
        ],
        compiler_params=pltpu.CompilerParams(vmem_limit_bytes=VMEM_BYTES),
        name="begin",
    )(far(code), far(signal))


def taker(refs):
    refs = list(refs)

    def take(count):
        taken = refs[:count]
        del refs[:count]
        return taken

    return take


def residual_tile(tile, rb, rr, pieces, start, acc, total_time):
    rows, channels = rb.shape
    column = slice(tile * LANES, (tile + 1) * LANES)
    moment = start + lax.broadcasted_iota(jnp.int32, (rows, LANES), 0)
    scale = (C * L) ** (-0.5)
    signal = jnp.concatenate([piece[:, column] for piece in pieces], axis=0)
    value = signal.astype(jnp.float32) - scale * acc[tile, :rows, :]
    rb[:, column] = jnp.where(moment < total_time, value, 0.0).astype(jnp.bfloat16)
    for coarse in range(COARSE):
        first = coarse * channels + tile * LANES
        part = rb[ROWS * coarse : ROWS * coarse + rr.shape[0], column]
        rr[:, first : first + LANES] = part


def stepped_codes(state, acc, limit):
    scale = (C * L) ** (-0.5)
    stepped = state + code_rate * (scale * acc[0, : state.shape[0], :])
    return stepped - jnp.clip(stepped, -limit, limit)


def iterate_kernel(total_time, patching, first_copied, plan_ref, limit_ref, *refs):
    take = taker(refs)
    state_ref, first_ref, second_ref, signal_ref, next_first, next_second = take(6)
    atoms = take(1 if patching else 0)
    (taps,) = take(1)
    source = take(2 if patching else 0)
    state_out, *edges = take(3)
    taps = (take(1) if patching else [taps])[0]
    target = take(1 if patching else 0)
    zb, rb, zz, rr, fine, acc, beyond = take(7)
    ferry = Ferry(source[0], target[0], first_copied, *take(2)) if patching else None
    segment, channels = signal_ref.shape
    zb[L : L + segment, :] = state_ref[...].astype(jnp.bfloat16)

    def put(left, right):
        zb[:L, :] = left[:, :K]
        zb[L + segment :, :] = right[:, :K]

    def put_signal(left, right):
        beyond[...] = right[:, K:]

    by_side(put, first_ref, second_ref)
    by_side(put_signal, next_first, next_second)
    start = lax.axis_index("tm") * segment

    def settle_tile(tile):
        residual_tile(tile, rb, rr, (signal_ref, beyond), start, acc, total_time)

    if patching:
        columns, *turned = take(1 + GROUPS)
        lag_rows(zb, L, segment + L, zz)

        def convolve_after(lag, tile):
            convolve_lags(lag, tile, segment + L, taps, zz, fine, acc)
            if lag + FINE == ROWS:
                settle_tile(tile)

        patch_taps(
            first_row_of(plan_ref, patching - 1), atoms[0], taps, columns, turned, convolve_after
        )
        ferry.turn_round()
    else:
        convolve(zb, L, segment + L, taps, zz, fine, acc, settle_tile)
    correlate(segment, taps, rr, fine, acc)
    state = stepped_codes(state_ref[...], acc, limit_ref[...])
    state_out[...] = state
    low = state.astype(jnp.bfloat16)
    put_edges(edges, low[-L:], low[:L])
    if ferry:
        ferry.close()


def iterate(plan, step, limit, state, swapped, signal, following, taps, atoms, ferry, peers):
    segment, channels = signal.shape
    patching = atoms is not None
    reach = segment + L
    carried = [far(value) for value in ferry[:2]] if patching else []
    return pl.pallas_call(
        functools.partial(iterate_kernel, peers * segment, step if patching else 0, ferry[2]),
        in_specs=[scalars()] + [vmem()] * (8 + patching) + [hbm()] * len(carried),
        out_specs=[vmem()] * (3 + patching) + [hbm()] * patching,
        out_shape=[pltpu.VMEM((segment, K), jnp.float32)]
        + [jax.ShapeDtypeStruct((L, K), jnp.bfloat16)] * 2
        + [pltpu.VMEM(taps.shape, jnp.bfloat16)] * patching
        + [pltpu.HBM(ferry[0].shape, jnp.float32)] * patching,
        scratch_shapes=[
            pltpu.VMEM((L + reach, K), jnp.bfloat16),
            pltpu.VMEM((reach, channels), jnp.bfloat16),
            pltpu.VMEM((reach + ROWS, COARSE * K), jnp.bfloat16),
            pltpu.VMEM((segment + ROWS, COARSE * channels), jnp.bfloat16),
            pltpu.VMEM((2 * FINE, channels // LANES, reach + ROWS, LANES), jnp.float32),
            pltpu.VMEM((channels // LANES, reach, LANES), jnp.float32),
            pltpu.VMEM((L, channels), jnp.bfloat16),
        ]
        + (
            ferry_scratch(ferry[3], ferry[0].shape[1])
            + [pltpu.VMEM((K, GROUPS * ROWS * L), jnp.bfloat16)]
            + [pltpu.VMEM((ROWS * STRIDE, K), jnp.float32)] * GROUPS
        )
        * patching,
        input_output_aliases={9: 3, 11: 4} if patching else {},
        compiler_params=pltpu.CompilerParams(vmem_limit_bytes=VMEM_BYTES),
        name="iterate",
    )(
        plan,
        limit,
        resident(state),
        *swapped,
        resident(signal),
        *following,
        *([resident(atoms)] if patching else []),
        resident(taps),
        *carried,
    )


def conclude_kernel(peers, step, copied, plan_ref, limit_ref, *refs):
    last = step + 1 == OUTER
    take = taker(refs)
    state_ref, first_ref, second_ref, signal_ref, next_first, next_second, taps = take(7)
    source = take(2 if copied else 1)[0]
    (payload_out,) = take(1)
    state_out, partial_out, codes_out = (None, *take(2)) if last else (*take(1), None, None)
    *edges, target = take(3)
    zb, rb, zz, rr, fine, acc, beyond, tall, packed = take(9)
    ferry = Ferry(source, target, copied, *take(2))
    if not last:
        (codes_out,) = take(1)
    segment, channels = signal_ref.shape
    reach = segment + L
    zb[L:reach, :] = state_ref[...].astype(jnp.bfloat16)

    def put(left, right):
        zb[:L, :] = left[...]
        zb[reach:, :] = right[...]

    def put_signal(left, right):
        beyond[...] = right[:, K:]

    by_side(put, first_ref, second_ref)
    by_side(put_signal, next_first, next_second)
    start = lax.axis_index("tm") * segment

    def settle_tile(tile):
        residual_tile(tile, rb, rr, (signal_ref, beyond), start, acc, peers * segment)

    convolve(zb, L, reach, taps, zz, fine, acc, settle_tile)
    ferry.turn_round()
    correlate(segment, taps, rr, fine, acc)
    state = stepped_codes(state_ref[...], acc, limit_ref[...])
    low = state.astype(jnp.bfloat16)
    if not last:
        state_out[...] = state
    put_edges(edges, low[-L:], low[:L])
    codes_out[...] = state.T
    zb[:L, :] = jnp.zeros((L, K), jnp.bfloat16)
    zb[L:reach, :] = low
    zb[reach:, :] = jnp.zeros((L, K), jnp.bfloat16)
    scale = (C * L) ** (-0.5)
    block = codes_out[pl.ds(first_row_of(plan_ref, step), BLOCK_ATOMS), :]
    share = channels // peers

    def pack_tile(tile):
        column = slice(tile * LANES, (tile + 1) * LANES)
        value = signal_ref[:, column].astype(jnp.float32) - scale * acc[tile, :segment, :]
        if last:
            partial_out[:, column] = value
        tall[0, column, :] = value.T
        spill = jnp.concatenate(
            [-scale * acc[tile, segment:reach, :], jnp.zeros((segment - L, LANES), jnp.float32)], axis=0
        )
        tall[1, column, :] = spill.T
        for peer in range(tile * LANES // share, (tile + 1) * LANES // share):
            for part in range(2):
                packed[peer, part * share : (part + 1) * share, :] = tall[
                    part, peer * share : (peer + 1) * share, :
                ]
            packed[peer, 2 * share :, :] = block

    convolve(zb, L, reach, taps, zz, fine, acc, pack_tile)
    payload_out[...] = packed[...].astype(jnp.bfloat16)
    ferry.close()


def conclude(plan, step, limit, state, swapped, signal, following, taps, ferry, peers):
    segment, channels = signal.shape
    share = channels // peers
    last = step + 1 == OUTER
    carried = [far(value) for value in ferry[:2] if value is not None]
    reach = segment + L
    outs = [pltpu.VMEM((segment, K), jnp.float32)]
    if last:
        outs = [pltpu.VMEM((segment, channels), jnp.float32), pltpu.VMEM((K, segment), jnp.float32)]
    outs += [jax.ShapeDtypeStruct((L, K), jnp.bfloat16)] * 2
    return pl.pallas_call(
        functools.partial(conclude_kernel, peers, step, ferry[2]),
        in_specs=[scalars()] + [vmem()] * 8 + [hbm()] * len(carried),
        out_specs=[vmem()] * (1 + len(outs)) + [hbm()],
        out_shape=[jax.ShapeDtypeStruct((peers, 2 * share + BLOCK_ATOMS, segment), jnp.bfloat16)]
        + outs
        + [pltpu.HBM(ferry[0].shape, jnp.float32)],
        scratch_shapes=[
            pltpu.VMEM((L + reach, K), jnp.bfloat16),
            pltpu.VMEM((reach, channels), jnp.bfloat16),
            pltpu.VMEM((reach + ROWS, COARSE * K), jnp.bfloat16),
            pltpu.VMEM((segment + ROWS, COARSE * channels), jnp.bfloat16),
            pltpu.VMEM((2 * FINE, channels // LANES, reach + ROWS, LANES), jnp.float32),
            pltpu.VMEM((channels // LANES, reach, LANES), jnp.float32),
            pltpu.VMEM((L, channels), jnp.bfloat16),
            pltpu.VMEM((2, channels, segment), jnp.float32),
            pltpu.VMEM((peers, 2 * share + BLOCK_ATOMS, segment), jnp.float32),
        ]
        + ferry_scratch(ferry[3], ferry[0].shape[1])
        + ([] if last else [pltpu.VMEM((K, segment), jnp.float32)]),
        input_output_aliases={10: 1 + len(outs)} if len(carried) == 2 else {},
        compiler_params=pltpu.CompilerParams(vmem_limit_bytes=VMEM_BYTES),
        name="conclude",
    )(
        plan,
        limit,
        resident(state),
        *swapped,
        resident(signal),
        *following,
        resident(taps),
        *carried,
    )


def settle_kernel(earlier, plan_ref, partial_ref, first_ref, second_ref, taps, *refs):
    take = taker(refs)
    atoms = take(earlier)
    _, resid_out, dict_out, zb, zz, fine, acc, sems = refs[earlier:]
    segment, channels = partial_ref.shape
    stores = [
        pltpu.make_async_copy(
            atoms[step], dict_out.at[pl.ds(first_row_of(plan_ref, step), BLOCK_ATOMS)], sems.at[step]
        )
        for step in range(earlier)
    ]
    for store in stores:
        store.start()

    def put(left, right):
        zb[:L, :] = left[...]

    zb[L:, :] = jnp.zeros((L, K), jnp.bfloat16)
    by_side(put, first_ref, second_ref)
    scale = (C * L) ** (-0.5)

    def settle_tile(tile):
        column = slice(tile * LANES, (tile + 1) * LANES)
        value = jnp.concatenate(
            [partial_ref[:L, column] - scale * acc[tile], partial_ref[L:, column]], axis=0
        )
        resid_out[column, :] = value.T

    convolve(zb, L, L, taps, zz, fine, acc, settle_tile)
    for store in stores:
        store.wait()


def settle(plan, partial, swapped, taps, renewed, dictionary):
    segment, channels = partial.shape
    earlier = len(renewed)
    return pl.pallas_call(
        functools.partial(settle_kernel, earlier),
        in_specs=[scalars()] + [vmem()] * (4 + earlier) + [hbm()],
        out_specs=[vmem(), hbm()],
        out_shape=[
            pltpu.VMEM((channels, segment), jnp.float32),
            pltpu.HBM(dictionary.shape, jnp.float32),
        ],
        scratch_shapes=[
            pltpu.VMEM((2 * L, K), jnp.bfloat16),
            pltpu.VMEM((L + ROWS, COARSE * K), jnp.bfloat16),
            pltpu.VMEM((2 * FINE, channels // LANES, L + ROWS, LANES), jnp.float32),
            pltpu.VMEM((channels // LANES, L, LANES), jnp.float32),
            pltpu.SemaphoreType.DMA((earlier,)),
        ],
        input_output_aliases={5 + earlier: 1},
        compiler_params=pltpu.CompilerParams(vmem_limit_bytes=VMEM_BYTES),
        name="settle",
    )(
        plan,
        resident(partial),
        *swapped,
        resident(taps),
        *[resident(value) for value in renewed],
        far(dictionary),
    )


def gradient_kernel(share, step, plan_ref, blocks_ref, dict_hbm, out_ref, packed, rf, zf, rr, zz, old, sem):
    peers, rows, segment = blocks_ref.shape
    share_rows = rf.shape[0]
    span = peers * segment
    entries = share * L
    rows_of = pl.ds(first_row_of(plan_ref, step), BLOCK_ATOMS)
    columns_of = pl.ds(pl.multiple_of(lax.axis_index("tm") * entries, LANES), entries)
    fetch = pltpu.make_async_copy(dict_hbm.at[rows_of, columns_of], old, sem)
    fetch.start()
    rf[:, span:] = jnp.zeros((share_rows, LANES), jnp.bfloat16)
    zf[:, :LANES] = jnp.zeros((BLOCK_ATOMS, LANES), jnp.bfloat16)
    packed[...] = blocks_ref[...].astype(jnp.float32)
    for peer in range(peers):
        column = peer * segment
        own = packed[peer, :share_rows, :]
        if peer:
            own += packed[peer - 1, share : share + share_rows, :]
        rf[:, column : column + segment] = own.astype(jnp.bfloat16)
        zf[:, LANES + column : LANES + column + segment] = packed[peer, 2 * share :, :].astype(
            jnp.bfloat16
        )
    for lag in range(ROWS):
        rr[lag * share_rows : (lag + 1) * share_rows, :] = rf[:, lag : lag + span]
    for coarse in range(COARSE):
        begin = LANES - ROWS * coarse
        zz[coarse * BLOCK_ATOMS : (coarse + 1) * BLOCK_ATOMS, :] = zf[:, begin : begin + span]
    lagged = lax.dot_general(zz[...], rr[...], NT, preferred_element_type=jnp.float32)
    wide = ROWS * share_rows
    parts = []
    left = lagged
    for _ in range(3):
        parts.append(left.astype(jnp.bfloat16))
        left = left - parts[-1].astype(jnp.float32)
    row = lax.broadcasted_iota(jnp.int32, (wide, wide), 0)
    column = lax.broadcasted_iota(jnp.int32, (wide, wide), 1)
    chosen = (row // share_rows == column % ROWS) & (row % share_rows == column // ROWS)
    chosen = chosen.astype(jnp.float32).astype(jnp.bfloat16)
    by_channel = lax.dot_general(
        jnp.concatenate(parts, axis=0), chosen, NN, preferred_element_type=jnp.float32
    )
    count = COARSE * BLOCK_ATOMS
    by_channel = by_channel[:count] + by_channel[count : 2 * count] + by_channel[2 * count :]
    lane = lax.broadcasted_iota(jnp.int32, (BLOCK_ATOMS, LANES), 1)
    tiles = []
    for tile in range(entries // LANES):
        total = jnp.zeros((BLOCK_ATOMS, LANES), jnp.float32)
        for place in range(LANES // ROWS):
            channel, coarse = divmod(tile * (LANES // ROWS) + place, COARSE)
            first = channel * ROWS // LANES * LANES
            source = by_channel[coarse * BLOCK_ATOMS : (coarse + 1) * BLOCK_ATOMS, first : first + LANES]
            by = (place * ROWS - channel * ROWS) % LANES
            moved = pltpu.roll(source, by, 1) if by else source
            total = jnp.where(lane // ROWS == place, moved, total)
        tiles.append(total)
    gradient = jnp.concatenate(tiles, axis=1)
    fetch.wait()
    before = old[...]
    square = jnp.sum(before * before, axis=1, keepdims=True)
    along = jnp.sum(gradient * before, axis=1, keepdims=True) / (square + tiny_eps)
    out_ref[:, :entries] = (gradient - along * before).astype(jnp.bfloat16)
    terms = jnp.zeros((BLOCK_ATOMS, LANES), jnp.float32)
    for i in range(3):
        term = along.astype(jnp.bfloat16).astype(jnp.float32)
        along = along - term
        terms = jnp.where(lane == i, term, terms)
    out_ref[:, entries:] = terms.astype(jnp.bfloat16)


def share_gradient(plan, step, blocks, dictionary, share):
    peers, rows, segment = blocks.shape
    share_rows = -(-share // ROWS) * ROWS
    span = peers * segment
    return pl.pallas_call(
        functools.partial(gradient_kernel, share, step),
        in_specs=[scalars(), vmem(), hbm()],
        out_shape=jax.ShapeDtypeStruct((BLOCK_ATOMS, share * L + LANES), jnp.bfloat16),
        scratch_shapes=[
            pltpu.VMEM(blocks.shape, jnp.float32),
            pltpu.VMEM((share_rows, span + LANES), jnp.bfloat16),
            pltpu.VMEM((BLOCK_ATOMS, LANES + span), jnp.bfloat16),
            pltpu.VMEM((ROWS * share_rows, span), jnp.bfloat16),
            pltpu.VMEM((COARSE * BLOCK_ATOMS, span), jnp.bfloat16),
            pltpu.VMEM((BLOCK_ATOMS, share * L), jnp.float32),
            pltpu.SemaphoreType.DMA,
        ],
        compiler_params=pltpu.CompilerParams(vmem_limit_bytes=VMEM_BYTES),
        name="gradient",
    )(plan, blocks, far(dictionary))


def gather_steps(peers):
    bits = [1 << i for i in range(peers.bit_length() - 2, 0, -1)]
    steps = []
    for first in range(0, len(bits), 2):
        pair = bits[first : first + 2]
        steps.append(pair + [sum(pair)] if len(pair) == 2 else pair)
    return steps


def gather_slots(peers):
    flips = [0]
    for masks in gather_steps(peers):
        flips = [f ^ m for m in [0] + masks for f in flips]
    return flips


def gather_pieces(piece, meanwhile):
    peers = lax.axis_size("tm")

    def exchanged(shard, mask):
        return lax.ppermute(shard, "tm", [(i, i ^ mask) for i in range(peers)])

    held = piece[None]
    for index, masks in enumerate(gather_steps(peers)):
        held = jnp.concatenate([held] + [exchanged(held, mask) for mask in masks], axis=0)
        if index == 0:
            needed, extra = meanwhile(held)
    ready, _ = lax.optimization_barrier((held, needed))
    return held, exchanged(ready, 1), extra


def recall_kernel(plan_ref, dict_hbm, when_ref, *refs):
    del when_ref
    take = taker(refs)
    olds, means = take(OUTER), take(OUTER)
    (sems,) = take(1)
    entries = olds[0].shape[1]
    fetches = [
        pltpu.make_async_copy(
            dict_hbm.at[pl.ds(first_row_of(plan_ref, step), BLOCK_ATOMS)], olds[step], sems.at[step]
        )
        for step in range(OUTER)
    ]
    for fetch in fetches:
        fetch.start()
    width = 9 * LANES if entries % (9 * LANES) == 0 else LANES
    for fetch, old_ref, mean_ref in zip(fetches, olds, means):
        fetch.wait()

        def add(step, square):
            before = old_ref[:, pl.ds(pl.multiple_of(step * width, LANES), width)]
            return square + before * before

        zeros = jnp.zeros((BLOCK_ATOMS, width), jnp.float32)
        square = lax.fori_loop(0, entries // width, add, zeros)
        mean_sq = jnp.sum(square, axis=1, keepdims=True) / (C * L) + tiny_eps
        mean_ref[...] = jnp.broadcast_to(mean_sq, mean_ref.shape)


def recall(plan, dictionary, when):
    entries = dictionary.shape[1]
    results = pl.pallas_call(
        recall_kernel,
        in_specs=[scalars(), hbm(), pl.BlockSpec(memory_space=pl.ANY)],
        out_specs=[vmem()] * (2 * OUTER),
        out_shape=[pltpu.VMEM((BLOCK_ATOMS, entries), jnp.float32)] * OUTER
        + [pltpu.VMEM((BLOCK_ATOMS, LANES), jnp.float32)] * OUTER,
        scratch_shapes=[pltpu.SemaphoreType.DMA((OUTER,))],
        compiler_params=pltpu.CompilerParams(vmem_limit_bytes=VMEM_BYTES),
        name="recall",
    )(plan, far(dictionary), when)
    return list(zip(results[:OUTER], results[OUTER:]))


def renew_kernel(plan_step, plan_ref, held_ref, came_ref, old, mean_ref, *refs):
    me = lax.axis_index("tm")
    half, _, wide = held_ref.shape
    width = wide - LANES
    entries = C * L
    last = plan_step + 1 == OUTER
    if last:
        _, out_hbm, atoms_ref, grad, sems = refs
    else:
        atoms_ref, grad = refs

    stores = []
    shares = []
    for slot, flips in enumerate(gather_slots(2 * half)):
        for source, extra in ((held_ref, 0), (came_ref, 1)):
            owner = me ^ (flips + extra)
            shares.append((source.at[slot], pl.ds(pl.multiple_of(owner * width, LANES), width)))
    zeros = jnp.zeros((BLOCK_ATOMS, width), jnp.float32)
    dot = zeros
    for source, column in shares:
        before = old[:, column]
        along = jnp.sum(source[:, width:].astype(jnp.float32), axis=1, keepdims=True)
        value = source[:, :width].astype(jnp.float32) + along * before
        grad[:, column] = value
        dot += value * before
    mean_sq = mean_ref[:, :1]
    along = jnp.sum(dot, axis=1, keepdims=True) / entries / mean_sq
    square = zeros
    for _, column in shares:
        value = grad[:, column] - along * old[:, column]
        square += value * value
    spread = jnp.sum(square, axis=1, keepdims=True) / entries + tiny_eps
    step = move_rate / jnp.sqrt(spread)
    norm = 1.0 / jnp.sqrt(mean_sq + 0.25)
    rows = pl.ds(first_row_of(plan_ref, plan_step), BLOCK_ATOMS)
    for index, (_, column) in enumerate(shares):
        before = old[:, column]
        across = grad[:, column] - along * before
        atoms_ref[:, column] = (before + step * across) * norm
        if last:
            stores.append(
                pltpu.make_async_copy(
                    atoms_ref.at[:, column], out_hbm.at[rows, column], sems.at[index]
                )
            )
            stores[-1].start()
    for store in stores:
        store.wait()


def renew(plan, step, held, came, old, mean_sq, dictionary):
    last = dictionary is not None
    atoms = (BLOCK_ATOMS, old.shape[1])
    scratch = [pltpu.VMEM(atoms, jnp.float32)]
    if last:
        scratch = scratch * 2 + [pltpu.SemaphoreType.DMA((2 * held.shape[0],))]
    return pl.pallas_call(
        functools.partial(renew_kernel, step),
        in_specs=[scalars()] + [vmem()] * 4 + [hbm()] * last,
        out_specs=hbm() if last else vmem(),
        out_shape=pltpu.HBM(dictionary.shape, jnp.float32) if last else pltpu.VMEM(atoms, jnp.float32),
        scratch_shapes=scratch,
        input_output_aliases={5: 0} if last else {},
        compiler_params=pltpu.CompilerParams(vmem_limit_bytes=VMEM_BYTES),
        name="renew",
    )(plan, held, came, resident(old), resident(mean_sq), *([far(dictionary)] if last else []))


def whole_channels(signal, codes_init, dictionary_init, threshold, plan):
    channels, segment = signal.shape
    peers = lax.axis_size("tm")
    limit = threshold[None, :]
    def swaps(edges):
        ends = [range(first, peers - 1, 2) for first in (0, 1)]
        pairs = [[p for i in end for p in ((i, i + 1), (i + 1, i))] for end in ends]
        far_first = [lax.ppermute(edge, "tm", pair) for edge, pair in zip(edges[::-1], pairs[::-1])]
        return far_first[::-1]

    state, signal, *edges = begin(codes_init, signal)
    following = swaps(edges)
    swapped = following
    taps = layout(dictionary_init, channels)
    dictionary = None
    renewed = []
    for step in range(OUTER):
        last = step + 1 == OUTER
        ferry = (dictionary_init, dictionary, COPIED[0], COPIED[1])
        atoms = renewed[-1] if renewed else None
        state, *results = iterate(
            plan, step, limit, state, swapped, signal, following, taps, atoms, ferry, peers
        )
        edges = results[:2]
        if renewed:
            taps, dictionary = results[2:]
        ferry = (dictionary_init, dictionary, sum(COPIED[: 2 * step]), COPIED[2 * step])
        payload, *results, first_edge, second_edge, dictionary = conclude(
            plan, step, limit, state, swaps(edges), signal, following, taps, ferry, peers
        )
        edges = [first_edge, second_edge]
        blocks = lax.all_to_all(payload, "tm", 0, 0, tiled=True)
        piece = share_gradient(plan, step, blocks, dictionary_init, channels // peers)
        edges, _ = lax.optimization_barrier((edges, piece))
        swapped = swaps(edges)

        def beside(held):
            if not last:
                recalled = recall(plan, dictionary_init, held)
                return (recalled[0][0], swapped), recalled
            partial, _ = lax.optimization_barrier((results[0], held))
            settled = settle(plan, partial, swapped, taps, renewed, dictionary)
            return settled[0], settled

        held, came, extra = gather_pieces(piece, beside)
        if last:
            residual, dictionary = extra
            dictionary = renew(plan, step, held, came, *recalled[step], dictionary)
        else:
            recalled, state = extra, results[0]
            renewed.append(renew(plan, step, held, came, *recalled[step], None))
    return results[1], dictionary, residual


def renew_atoms(old_atoms, across, mean_sq, spread):
    return (old_atoms + move_rate * across / jnp.sqrt(spread)[:, None]) / jnp.sqrt(mean_sq + 0.25)[
        :, None
    ]


def split_channels(signal, codes_init, dictionary_init, threshold, plan):
    segment = signal.shape[1]
    local_chan = signal.shape[0]
    unit_scale = (C * L) ** (-0.5)
    entries = C * L
    limit = threshold[:, None]

    def convolve(atom_cube, code_low):
        code_edge = shifted(code_low[:, segment - (L - 1) :], "tm", 1)
        extended = jnp.concatenate([code_edge, code_low], axis=1)
        lagged = jnp.stack(
            [extended[:, L - 1 - offset : L - 1 - offset + segment] for offset in range(L)], axis=1
        )
        return unit_scale * jnp.einsum(
            "kcl,klt->ct", atom_cube, lagged, preferred_element_type=jnp.float32
        )

    def resid_columns(resid_low):
        resid_edge = shifted(resid_low[:, : L - 1], "tm", -1)
        extended = jnp.concatenate([resid_low, resid_edge], axis=1)
        lagged = jnp.stack([extended[:, offset : offset + segment] for offset in range(L)], axis=1)
        return lagged.reshape(local_chan * L, segment)

    code_state = codes_init
    dictionary = dictionary_init
    residual = signal.astype(jnp.float32)
    for outer_step in range(OUTER):
        dict_low = dictionary.astype(jnp.bfloat16)
        atom_cube = dict_low.reshape(K, local_chan, L)
        for inner_step in range(INNER):
            code_low = code_state.astype(jnp.bfloat16)
            residual = signal.astype(jnp.float32) - convolve(atom_cube, code_low)
            lagged = resid_columns(residual.astype(jnp.bfloat16))
            partial_value = unit_scale * jnp.dot(
                dict_low, lagged, preferred_element_type=jnp.float32
            )
            scores = lax.psum(partial_value.astype(jnp.bfloat16), "chan").astype(jnp.float32)
            stepped = code_state + code_rate * scores
            code_state = stepped - jnp.clip(stepped, -limit, limit)
        code_low = code_state.astype(jnp.bfloat16)
        residual = signal.astype(jnp.float32) - convolve(atom_cube, code_low)
        lagged = resid_columns(residual.astype(jnp.bfloat16))
        first_row = plan[outer_step] * BLOCK_ATOMS
        code_block = lax.dynamic_slice_in_dim(code_low, first_row, BLOCK_ATOMS, 0)
        local_grad = lax.dot_general(
            code_block, lagged, (((1,), (1,)), ((), ())), preferred_element_type=jnp.float32
        )
        old_atoms = lax.dynamic_slice_in_dim(dictionary, first_row, BLOCK_ATOMS, 0)
        gradient = lax.psum(local_grad, "tm")
        dot_sum, square_sum = lax.psum(
            (jnp.sum(gradient * old_atoms, axis=1), jnp.sum(old_atoms * old_atoms, axis=1)), "chan"
        )
        mean_sq = square_sum / entries + tiny_eps
        along_coef = dot_sum / entries / mean_sq
        across = gradient - along_coef[:, None] * old_atoms
        spread = lax.psum(jnp.sum(across * across, axis=1), "chan") / entries + tiny_eps
        renewed = renew_atoms(old_atoms, across, mean_sq, spread)
        dictionary = lax.dynamic_update_slice_in_dim(dictionary, renewed, first_row, 0)
    return (code_state, dictionary, residual)


def shards(signal, codes_init, dictionary_init, threshold, plan):
    channels, segment = signal.shape
    peers = lax.axis_size("tm")
    fits = (
        lax.axis_size("chan") == 1
        and segment % LANES == 0
        and INNER == 2
        and OUTER == 2
        and channels % LANES == 0
        and channels % peers == 0
        and (channels // peers * L) % LANES == 0
        and peers > 2
        and peers & (peers - 1) == 0
    )
    body = whole_channels if fits else split_channels
    return body(signal, codes_init, dictionary_init, threshold, plan)


def solution(mesh):
    placed = (P("chan", "tm"), P(None, "tm"), P(None, "chan"), P(), P())
    return jax.shard_map(
        shards,
        mesh=mesh,
        in_specs=placed,
        out_specs=(P(None, "tm"), P(None, "chan"), P("chan", "tm")),
        check_vma=False,
    )
```

```python
import functools

import jax
import jax.numpy as jnp
from jax import lax
from jax.experimental import pallas as pl
from jax.experimental.pallas import tpu as pltpu
from jax.sharding import PartitionSpec as P

C = 384
K = 128
L = 96
BLOCK_ATOMS = 16
INNER = 2
OUTER = 2

code_rate = 0.3
move_rate = 0.5
tiny_eps = 1e-06

ROWS = 16
COARSE = L // ROWS
STRIDE = L + 1
TURNED_ROWS = -(-(ROWS + 1) * STRIDE // 8) * 8
GROUPS = 4
SUBLANES = 8
COPIED = (48, 40, 40)
FINE = 4
LANES = 128
VMEM_BYTES = 24 * 1024 * 1024

NN = (((1,), (0,)), ((), ()))
NT = (((1,), (1,)), ((), ()))


def shifted(shard, axis, by):
    peers = lax.axis_size(axis)
    pairs = [(i, i + by) for i in range(peers) if 0 <= i + by < peers]
    return lax.ppermute(shard, axis, pairs)


def resident(value):
    return pltpu.with_memory_space_constraint(value, pltpu.VMEM)


def far(value):
    return pltpu.with_memory_space_constraint(value, pltpu.HBM)


def hbm():
    return pl.BlockSpec(memory_space=pltpu.HBM)


def scalars():
    return pl.BlockSpec(memory_space=pltpu.SMEM)


def first_row_of(plan_ref, step):
    return pl.multiple_of(plan_ref[step] * BLOCK_ATOMS, BLOCK_ATOMS)


def vmem():
    return pl.BlockSpec(memory_space=pltpu.VMEM)


def turn(columns, turned_ref):
    side = 2 * LANES
    row = lax.broadcasted_iota(jnp.int32, (side, side), 0)
    column = lax.broadcasted_iota(jnp.int32, (side, side), 1)
    identity = (row == column).astype(jnp.float32).astype(jnp.bfloat16)

    def put(entry, rows):
        end = entry + rows.shape[0]
        begin = entry
        while begin < end:
            channel, tap = begin // L, begin % L
            count = min(end - begin, L - tap)
            target = channel * STRIDE + tap
            turned_ref[target : target + count, :] = rows[begin - entry : begin - entry + count]
            begin += count

    low = columns.astype(jnp.bfloat16)
    through_matrix = ROWS * L // (6 * side) * 4 * side
    for first in range(0, through_matrix, 2 * side):
        pair = jnp.concatenate(
            [low[:, first + half * side : first + (half + 1) * side] for half in range(2)], axis=0
        )
        turned = lax.dot_general(identity, pair, NT, preferred_element_type=jnp.float32)
        for half in range(2):
            put(first + half * side, turned[:, half * K : (half + 1) * K])
    for first in range(through_matrix, ROWS * L, LANES):
        put(first, columns[:, first : first + LANES].astype(jnp.float32).T)


def tap_of(turned_ref, tap):
    return turned_ref[pl.ds(tap, ROWS, stride=STRIDE), :].astype(jnp.bfloat16)


def layout_kernel(dict_ref, taps_ref, *turned):
    def part(group):
        return dict_ref[:, group * ROWS * L : (group + 1) * ROWS * L]

    turn(part(0), turned[0])
    for group in range(GROUPS):
        if group + 1 < GROUPS:
            turn(part(group + 1), turned[group + 1])
        own = pl.ds(pl.multiple_of((pl.program_id(0) * GROUPS + group) * ROWS, ROWS), ROWS)
        for tap in range(L):
            taps_ref[tap // ROWS, tap % ROWS, own, :] = tap_of(turned[group], tap)


def layout(dictionary, channels):
    block = GROUPS * ROWS
    return pl.pallas_call(
        layout_kernel,
        grid=(channels // block,),
        in_specs=[pl.BlockSpec((K, block * L), lambda i: (0, i))],
        out_specs=vmem(),
        out_shape=pltpu.VMEM((COARSE, ROWS, channels, K), jnp.bfloat16),
        scratch_shapes=[pltpu.VMEM((TURNED_ROWS, K), jnp.float32)] * GROUPS,
        compiler_params=pltpu.CompilerParams(vmem_limit_bytes=VMEM_BYTES),
        name="layout",
    )(far(dictionary))


class Ferry:
    def __init__(self, source, target, first, buffer, sems):
        self.steps = []
        for step in range(buffer.shape[0] // SUBLANES):
            held = buffer.at[pl.ds(step * SUBLANES, SUBLANES)]
            rows = pl.ds(first + step * SUBLANES, SUBLANES)
            fetch = pltpu.make_async_copy(source.at[rows], held, sems.at[0, step])
            store = pltpu.make_async_copy(held, target.at[rows], sems.at[1, step])
            fetch.start()
            self.steps.append((fetch, store))

    def turn_round(self):
        for fetch, store in self.steps:
            fetch.wait()
            store.start()

    def close(self):
        for _, store in self.steps:
            store.wait()


def ferry_scratch(count, entries):
    return [
        pltpu.VMEM((count, entries), jnp.float32),
        pltpu.SemaphoreType.DMA((2, count // SUBLANES)),
    ]


def lag_rows(zb, begin, count, zz):
    rows = count + ROWS
    for coarse in range(COARSE):
        first = begin - ROWS - ROWS * coarse
        zz[:rows, coarse * K : (coarse + 1) * K] = zb[first : first + rows, :]


def convolve_lags(lag, tile, count, taps, zz, fine, acc):
    own = slice(tile * LANES, (tile + 1) * LANES)
    rows = count + ROWS
    slot = lag // FINE % 2 * FINE
    for pair in range(0, FINE, 2):
        weights = jnp.concatenate(
            [
                jnp.concatenate([taps[m, lag + pair + j, own, :] for m in range(COARSE)], axis=1)
                for j in range(2)
            ],
            axis=0,
        )
        product = lax.dot_general(zz[:rows, :], weights, NT, preferred_element_type=jnp.float32)
        for j in range(2):
            fine[slot + pair + j, tile, :rows, :] = product[:, j * LANES : (j + 1) * LANES]
    total = None if lag == 0 else acc[tile, :count, :]
    for j in range(FINE):
        first = ROWS - lag - j
        part = fine[slot + j, tile, first : first + count, :]
        total = part if total is None else total + part
    acc[tile, :count, :] = total


def convolve(zb, begin, count, taps, zz, fine, acc, after):
    lag_rows(zb, begin, count, zz)
    for tile in range(taps.shape[2] // LANES):
        for lag in range(0, ROWS, FINE):
            convolve_lags(lag, tile, count, taps, zz, fine, acc)
        after(tile)


def correlate(count, taps, rr, fine, acc):
    rows = count + ROWS
    for lag in range(0, ROWS, FINE):
        slot = lag // FINE % 2 * FINE
        for pair in range(0, FINE, 2):
            weights = jnp.concatenate(
                [
                    jnp.concatenate([taps[m, lag + pair + j] for m in range(COARSE)], axis=0)
                    for j in range(2)
                ],
                axis=1,
            )
            product = lax.dot_general(rr[:rows, :], weights, NN, preferred_element_type=jnp.float32)
            for j in range(2):
                fine[slot + pair + j, 0, :rows, :] = product[:, j * K : (j + 1) * K]
        total = None if lag == 0 else acc[0, :count, :]
        for j in range(FINE):
            part = fine[slot + j, 0, lag + j : lag + j + count, :]
            total = part if total is None else total + part
        acc[0, :count, :] = total


def patch_taps(row, atoms_ref, taps, columns, turned, convolve_after):
    lane = lax.broadcasted_iota(jnp.int32, (ROWS, K), 1)
    kept = (lane < row) | (lane >= row + BLOCK_ATOMS)
    keep = kept.astype(jnp.float32).astype(jnp.bfloat16)
    columns[...] = jnp.zeros_like(columns)
    width = ROWS * L
    steps = LANES // (GROUPS * ROWS)

    def patch(step, after):
        part = pl.ds(pl.multiple_of(step * (GROUPS * width), LANES), GROUPS * width)
        columns[pl.ds(row, BLOCK_ATOMS), :] = atoms_ref[:, part].astype(jnp.bfloat16)
        turn(columns[:, :width], turned[0])
        for group in range(GROUPS):
            if group + 1 < GROUPS:
                turn(columns[:, (group + 1) * width : (group + 2) * width], turned[group + 1])
            own = pl.ds(pl.multiple_of((step * GROUPS + group) * ROWS, ROWS), ROWS)
            for tap in range(L):
                before = taps[tap // ROWS, tap % ROWS, own, :]
                taps[tap // ROWS, tap % ROWS, own, :] = before * keep + tap_of(turned[group], tap)
            after(group)

    def alone(step, carry):
        patch(step, lambda group: None)
        return carry

    lax.fori_loop(0, steps, alone, 0)
    tiles = taps.shape[2] // LANES
    lags = list(range(0, ROWS, FINE))
    for tile in range(1, tiles):
        for step in range(steps):

            def after(group):
                done = (step * GROUPS + group + 1) * len(lags) // (steps * GROUPS)
                past = (step * GROUPS + group) * len(lags) // (steps * GROUPS)
                for index in range(past, done):
                    convolve_after(lags[index], tile - 1)

            patch(tile * steps + step, after)
    for lag in lags:
        convolve_after(lag, tiles - 1)


def put_edges(edge_refs, rightward, leftward):
    even = lax.axis_index("tm") % 2 == 0

    def put(first, second):
        first[...] = rightward
        second[...] = leftward

    pl.when(even)(lambda: put(*edge_refs))
    pl.when(jnp.logical_not(even))(lambda: put(*edge_refs[::-1]))


def by_side(put, first_ref, second_ref):
    even = lax.axis_index("tm") % 2 == 0
    pl.when(even)(lambda: put(second_ref, first_ref))
    pl.when(jnp.logical_not(even))(lambda: put(first_ref, second_ref))


def begin_kernel(code_hbm, signal_hbm, state_out, signal_out, first_out, second_out, code_ref, signal_ref, sems):
    fetches = [
        pltpu.make_async_copy(code_hbm, code_ref, sems.at[0]),
        pltpu.make_async_copy(signal_hbm, signal_ref, sems.at[1]),
    ]
    for fetch in fetches:
        fetch.start()
    for fetch in fetches:
        fetch.wait()
    state = code_ref[...].T
    signal = signal_ref[...].astype(jnp.float32).T.astype(jnp.bfloat16)
    state_out[...] = state
    signal_out[...] = signal
    both = jnp.concatenate([state.astype(jnp.bfloat16), signal], axis=1)
    put_edges((first_out, second_out), both[-L:], both[:L])


def begin(code, signal):
    channels, segment = signal.shape
    return pl.pallas_call(
        begin_kernel,
        in_specs=[hbm()] * 2,
        out_specs=[vmem()] * 4,
        out_shape=[
            pltpu.VMEM((segment, K), jnp.float32),
            pltpu.VMEM((segment, channels), jnp.bfloat16),
        ]
        + [jax.ShapeDtypeStruct((L, K + channels), jnp.bfloat16)] * 2,
        scratch_shapes=[
            pltpu.VMEM(code.shape, code.dtype),
            pltpu.VMEM(signal.shape, signal.dtype),
            pltpu.SemaphoreType.DMA((2,)),
        ],
        compiler_params=pltpu.CompilerParams(vmem_limit_bytes=VMEM_BYTES),
        name="begin",
    )(far(code), far(signal))


def taker(refs):
    refs = list(refs)

    def take(count):
        taken = refs[:count]
        del refs[:count]
        return taken

    return take


def residual_tile(tile, rb, rr, pieces, start, acc, total_time):
    rows, channels = rb.shape
    column = slice(tile * LANES, (tile + 1) * LANES)
    moment = start + lax.broadcasted_iota(jnp.int32, (rows, LANES), 0)
    scale = (C * L) ** (-0.5)
    signal = jnp.concatenate([piece[:, column] for piece in pieces], axis=0)
    value = signal.astype(jnp.float32) - scale * acc[tile, :rows, :]
    rb[:, column] = jnp.where(moment < total_time, value, 0.0).astype(jnp.bfloat16)
    for coarse in range(COARSE):
        first = coarse * channels + tile * LANES
        part = rb[ROWS * coarse : ROWS * coarse + rr.shape[0], column]
        rr[:, first : first + LANES] = part


def stepped_codes(state, acc, limit):
    scale = (C * L) ** (-0.5)
    stepped = state + code_rate * (scale * acc[0, : state.shape[0], :])
    return stepped - jnp.clip(stepped, -limit, limit)


def iterate_kernel(total_time, patching, first_copied, plan_ref, limit_ref, *refs):
    take = taker(refs)
    state_ref, first_ref, second_ref, signal_ref, next_first, next_second = take(6)
    atoms = take(1 if patching else 0)
    (taps,) = take(1)
    source = take(2 if patching else 0)
    state_out, *edges = take(3)
    taps = (take(1) if patching else [taps])[0]
    target = take(1 if patching else 0)
    zb, rb, zz, rr, fine, acc, beyond = take(7)
    ferry = Ferry(source[0], target[0], first_copied, *take(2)) if patching else None
    segment, channels = signal_ref.shape
    zb[L : L + segment, :] = state_ref[...].astype(jnp.bfloat16)

    def put(left, right):
        zb[:L, :] = left[:, :K]
        zb[L + segment :, :] = right[:, :K]

    def put_signal(left, right):
        beyond[...] = right[:, K:]

    by_side(put, first_ref, second_ref)
    by_side(put_signal, next_first, next_second)
    start = lax.axis_index("tm") * segment

    def settle_tile(tile):
        residual_tile(tile, rb, rr, (signal_ref, beyond), start, acc, total_time)

    if patching:
        columns, *turned = take(1 + GROUPS)
        lag_rows(zb, L, segment + L, zz)

        def convolve_after(lag, tile):
            convolve_lags(lag, tile, segment + L, taps, zz, fine, acc)
            if lag + FINE == ROWS:
                settle_tile(tile)

        patch_taps(
            first_row_of(plan_ref, patching - 1), atoms[0], taps, columns, turned, convolve_after
        )
        ferry.turn_round()
    else:
        convolve(zb, L, segment + L, taps, zz, fine, acc, settle_tile)
    correlate(segment, taps, rr, fine, acc)
    state = stepped_codes(state_ref[...], acc, limit_ref[...])
    state_out[...] = state
    low = state.astype(jnp.bfloat16)
    put_edges(edges, low[-L:], low[:L])
    if ferry:
        ferry.close()


def iterate(plan, step, limit, state, swapped, signal, following, taps, atoms, ferry, peers):
    segment, channels = signal.shape
    patching = atoms is not None
    reach = segment + L
    carried = [far(value) for value in ferry[:2]] if patching else []
    return pl.pallas_call(
        functools.partial(iterate_kernel, peers * segment, step if patching else 0, ferry[2]),
        in_specs=[scalars()] + [vmem()] * (8 + patching) + [hbm()] * len(carried),
        out_specs=[vmem()] * (3 + patching) + [hbm()] * patching,
        out_shape=[pltpu.VMEM((segment, K), jnp.float32)]
        + [jax.ShapeDtypeStruct((L, K), jnp.bfloat16)] * 2
        + [pltpu.VMEM(taps.shape, jnp.bfloat16)] * patching
        + [pltpu.HBM(ferry[0].shape, jnp.float32)] * patching,
        scratch_shapes=[
            pltpu.VMEM((L + reach, K), jnp.bfloat16),
            pltpu.VMEM((reach, channels), jnp.bfloat16),
            pltpu.VMEM((reach + ROWS, COARSE * K), jnp.bfloat16),
            pltpu.VMEM((segment + ROWS, COARSE * channels), jnp.bfloat16),
            pltpu.VMEM((2 * FINE, channels // LANES, reach + ROWS, LANES), jnp.float32),
            pltpu.VMEM((channels // LANES, reach, LANES), jnp.float32),
            pltpu.VMEM((L, channels), jnp.bfloat16),
        ]
        + (
            ferry_scratch(ferry[3], ferry[0].shape[1])
            + [pltpu.VMEM((K, GROUPS * ROWS * L), jnp.bfloat16)]
            + [pltpu.VMEM((TURNED_ROWS, K), jnp.float32)] * GROUPS
        )
        * patching,
        input_output_aliases={9: 3, 11: 4} if patching else {},
        compiler_params=pltpu.CompilerParams(vmem_limit_bytes=VMEM_BYTES),
        name="iterate",
    )(
        plan,
        limit,
        resident(state),
        *swapped,
        resident(signal),
        *following,
        *([resident(atoms)] if patching else []),
        resident(taps),
        *carried,
    )


def conclude_kernel(peers, step, copied, plan_ref, limit_ref, *refs):
    last = step + 1 == OUTER
    take = taker(refs)
    state_ref, first_ref, second_ref, signal_ref, next_first, next_second, taps = take(7)
    source = take(2 if copied else 1)[0]
    (payload_out,) = take(1)
    state_out, partial_out, codes_out = (None, *take(2)) if last else (*take(1), None, None)
    *edges, target = take(3)
    zb, rb, zz, rr, fine, acc, beyond, tall, packed = take(9)
    ferry = Ferry(source, target, copied, *take(2))
    if not last:
        (codes_out,) = take(1)
    segment, channels = signal_ref.shape
    reach = segment + L
    zb[L:reach, :] = state_ref[...].astype(jnp.bfloat16)

    def put(left, right):
        zb[:L, :] = left[...]
        zb[reach:, :] = right[...]

    def put_signal(left, right):
        beyond[...] = right[:, K:]

    by_side(put, first_ref, second_ref)
    by_side(put_signal, next_first, next_second)
    start = lax.axis_index("tm") * segment

    def settle_tile(tile):
        residual_tile(tile, rb, rr, (signal_ref, beyond), start, acc, peers * segment)

    convolve(zb, L, reach, taps, zz, fine, acc, settle_tile)
    ferry.turn_round()
    correlate(segment, taps, rr, fine, acc)
    state = stepped_codes(state_ref[...], acc, limit_ref[...])
    low = state.astype(jnp.bfloat16)
    if not last:
        state_out[...] = state
    put_edges(edges, low[-L:], low[:L])
    codes_out[...] = state.T
    zb[:L, :] = jnp.zeros((L, K), jnp.bfloat16)
    zb[L:reach, :] = low
    zb[reach:, :] = jnp.zeros((L, K), jnp.bfloat16)
    scale = (C * L) ** (-0.5)
    block = codes_out[pl.ds(first_row_of(plan_ref, step), BLOCK_ATOMS), :]
    share = channels // peers

    def pack_tile(tile):
        column = slice(tile * LANES, (tile + 1) * LANES)
        value = signal_ref[:, column].astype(jnp.float32) - scale * acc[tile, :segment, :]
        if last:
            partial_out[:, column] = value
        tall[0, column, :] = value.T
        spill = jnp.concatenate(
            [-scale * acc[tile, segment:reach, :], jnp.zeros((segment - L, LANES), jnp.float32)], axis=0
        )
        tall[1, column, :] = spill.T
        for peer in range(tile * LANES // share, (tile + 1) * LANES // share):
            for part in range(2):
                packed[peer, part * share : (part + 1) * share, :] = tall[
                    part, peer * share : (peer + 1) * share, :
                ]
            packed[peer, 2 * share :, :] = block

    convolve(zb, L, reach, taps, zz, fine, acc, pack_tile)
    payload_out[...] = packed[...].astype(jnp.bfloat16)
    ferry.close()


def conclude(plan, step, limit, state, swapped, signal, following, taps, ferry, peers):
    segment, channels = signal.shape
    share = channels // peers
    last = step + 1 == OUTER
    carried = [far(value) for value in ferry[:2] if value is not None]
    reach = segment + L
    outs = [pltpu.VMEM((segment, K), jnp.float32)]
    if last:
        outs = [pltpu.VMEM((segment, channels), jnp.float32), pltpu.VMEM((K, segment), jnp.float32)]
    outs += [jax.ShapeDtypeStruct((L, K), jnp.bfloat16)] * 2
    return pl.pallas_call(
        functools.partial(conclude_kernel, peers, step, ferry[2]),
        in_specs=[scalars()] + [vmem()] * 8 + [hbm()] * len(carried),
        out_specs=[vmem()] * (1 + len(outs)) + [hbm()],
        out_shape=[jax.ShapeDtypeStruct((peers, 2 * share + BLOCK_ATOMS, segment), jnp.bfloat16)]
        + outs
        + [pltpu.HBM(ferry[0].shape, jnp.float32)],
        scratch_shapes=[
            pltpu.VMEM((L + reach, K), jnp.bfloat16),
            pltpu.VMEM((reach, channels), jnp.bfloat16),
            pltpu.VMEM((reach + ROWS, COARSE * K), jnp.bfloat16),
            pltpu.VMEM((segment + ROWS, COARSE * channels), jnp.bfloat16),
            pltpu.VMEM((2 * FINE, channels // LANES, reach + ROWS, LANES), jnp.float32),
            pltpu.VMEM((channels // LANES, reach, LANES), jnp.float32),
            pltpu.VMEM((L, channels), jnp.bfloat16),
            pltpu.VMEM((2, channels, segment), jnp.float32),
            pltpu.VMEM((peers, 2 * share + BLOCK_ATOMS, segment), jnp.float32),
        ]
        + ferry_scratch(ferry[3], ferry[0].shape[1])
        + ([] if last else [pltpu.VMEM((K, segment), jnp.float32)]),
        input_output_aliases={10: 1 + len(outs)} if len(carried) == 2 else {},
        compiler_params=pltpu.CompilerParams(vmem_limit_bytes=VMEM_BYTES),
        name="conclude",
    )(
        plan,
        limit,
        resident(state),
        *swapped,
        resident(signal),
        *following,
        resident(taps),
        *carried,
    )


def settle_kernel(earlier, plan_ref, partial_ref, first_ref, second_ref, taps, *refs):
    take = taker(refs)
    atoms = take(earlier)
    _, resid_out, dict_out, zb, zz, fine, acc, sems = refs[earlier:]
    segment, channels = partial_ref.shape
    stores = [
        pltpu.make_async_copy(
            atoms[step], dict_out.at[pl.ds(first_row_of(plan_ref, step), BLOCK_ATOMS)], sems.at[step]
        )
        for step in range(earlier)
    ]
    for store in stores:
        store.start()

    def put(left, right):
        zb[:L, :] = left[...]

    zb[L:, :] = jnp.zeros((L, K), jnp.bfloat16)
    by_side(put, first_ref, second_ref)
    scale = (C * L) ** (-0.5)

    def settle_tile(tile):
        column = slice(tile * LANES, (tile + 1) * LANES)
        value = jnp.concatenate(
            [partial_ref[:L, column] - scale * acc[tile], partial_ref[L:, column]], axis=0
        )
        resid_out[column, :] = value.T

    convolve(zb, L, L, taps, zz, fine, acc, settle_tile)
    for store in stores:
        store.wait()


def settle(plan, partial, swapped, taps, renewed, dictionary):
    segment, channels = partial.shape
    earlier = len(renewed)
    return pl.pallas_call(
        functools.partial(settle_kernel, earlier),
        in_specs=[scalars()] + [vmem()] * (4 + earlier) + [hbm()],
        out_specs=[vmem(), hbm()],
        out_shape=[
            pltpu.VMEM((channels, segment), jnp.float32),
            pltpu.HBM(dictionary.shape, jnp.float32),
        ],
        scratch_shapes=[
            pltpu.VMEM((2 * L, K), jnp.bfloat16),
            pltpu.VMEM((L + ROWS, COARSE * K), jnp.bfloat16),
            pltpu.VMEM((2 * FINE, channels // LANES, L + ROWS, LANES), jnp.float32),
            pltpu.VMEM((channels // LANES, L, LANES), jnp.float32),
            pltpu.SemaphoreType.DMA((earlier,)),
        ],
        input_output_aliases={5 + earlier: 1},
        compiler_params=pltpu.CompilerParams(vmem_limit_bytes=VMEM_BYTES),
        name="settle",
    )(
        plan,
        resident(partial),
        *swapped,
        resident(taps),
        *[resident(value) for value in renewed],
        far(dictionary),
    )


def gradient_kernel(share, step, plan_ref, blocks_ref, dict_hbm, out_ref, packed, rf, zf, rr, zz, old, sem):
    peers, rows, segment = blocks_ref.shape
    share_rows = rf.shape[0]
    span = peers * segment
    entries = share * L
    rows_of = pl.ds(first_row_of(plan_ref, step), BLOCK_ATOMS)
    columns_of = pl.ds(pl.multiple_of(lax.axis_index("tm") * entries, LANES), entries)
    fetch = pltpu.make_async_copy(dict_hbm.at[rows_of, columns_of], old, sem)
    fetch.start()
    rf[:, span:] = jnp.zeros((share_rows, LANES), jnp.bfloat16)
    zf[:, :LANES] = jnp.zeros((BLOCK_ATOMS, LANES), jnp.bfloat16)
    packed[...] = blocks_ref[...].astype(jnp.float32)
    for peer in range(peers):
        column = peer * segment
        own = packed[peer, :share_rows, :]
        if peer:
            own += packed[peer - 1, share : share + share_rows, :]
        rf[:, column : column + segment] = own.astype(jnp.bfloat16)
        zf[:, LANES + column : LANES + column + segment] = packed[peer, 2 * share :, :].astype(
            jnp.bfloat16
        )
    for lag in range(ROWS):
        rr[lag * share_rows : (lag + 1) * share_rows, :] = rf[:, lag : lag + span]
    for coarse in range(COARSE):
        begin = LANES - ROWS * coarse
        zz[coarse * BLOCK_ATOMS : (coarse + 1) * BLOCK_ATOMS, :] = zf[:, begin : begin + span]
    lagged = lax.dot_general(zz[...], rr[...], NT, preferred_element_type=jnp.float32)
    wide = ROWS * share_rows
    parts = []
    left = lagged
    for _ in range(3):
        parts.append(left.astype(jnp.bfloat16))
        left = left - parts[-1].astype(jnp.float32)
    row = lax.broadcasted_iota(jnp.int32, (wide, wide), 0)
    column = lax.broadcasted_iota(jnp.int32, (wide, wide), 1)
    chosen = (row // share_rows == column % ROWS) & (row % share_rows == column // ROWS)
    chosen = chosen.astype(jnp.float32).astype(jnp.bfloat16)
    by_channel = lax.dot_general(
        jnp.concatenate(parts, axis=0), chosen, NN, preferred_element_type=jnp.float32
    )
    count = COARSE * BLOCK_ATOMS
    by_channel = by_channel[:count] + by_channel[count : 2 * count] + by_channel[2 * count :]
    lane = lax.broadcasted_iota(jnp.int32, (BLOCK_ATOMS, LANES), 1)
    tiles = []
    for tile in range(entries // LANES):
        total = jnp.zeros((BLOCK_ATOMS, LANES), jnp.float32)
        for place in range(LANES // ROWS):
            channel, coarse = divmod(tile * (LANES // ROWS) + place, COARSE)
            first = channel * ROWS // LANES * LANES
            source = by_channel[coarse * BLOCK_ATOMS : (coarse + 1) * BLOCK_ATOMS, first : first + LANES]
            by = (place * ROWS - channel * ROWS) % LANES
            moved = pltpu.roll(source, by, 1) if by else source
            total = jnp.where(lane // ROWS == place, moved, total)
        tiles.append(total)
    gradient = jnp.concatenate(tiles, axis=1)
    fetch.wait()
    before = old[...]
    square = jnp.sum(before * before, axis=1, keepdims=True)
    along = jnp.sum(gradient * before, axis=1, keepdims=True) / (square + tiny_eps)
    out_ref[:, :entries] = (gradient - along * before).astype(jnp.bfloat16)
    terms = jnp.zeros((BLOCK_ATOMS, LANES), jnp.float32)
    for i in range(3):
        term = along.astype(jnp.bfloat16).astype(jnp.float32)
        along = along - term
        terms = jnp.where(lane == i, term, terms)
    out_ref[:, entries:] = terms.astype(jnp.bfloat16)


def share_gradient(plan, step, blocks, dictionary, share):
    peers, rows, segment = blocks.shape
    share_rows = -(-share // ROWS) * ROWS
    span = peers * segment
    return pl.pallas_call(
        functools.partial(gradient_kernel, share, step),
        in_specs=[scalars(), vmem(), hbm()],
        out_shape=jax.ShapeDtypeStruct((BLOCK_ATOMS, share * L + LANES), jnp.bfloat16),
        scratch_shapes=[
            pltpu.VMEM(blocks.shape, jnp.float32),
            pltpu.VMEM((share_rows, span + LANES), jnp.bfloat16),
            pltpu.VMEM((BLOCK_ATOMS, LANES + span), jnp.bfloat16),
            pltpu.VMEM((ROWS * share_rows, span), jnp.bfloat16),
            pltpu.VMEM((COARSE * BLOCK_ATOMS, span), jnp.bfloat16),
            pltpu.VMEM((BLOCK_ATOMS, share * L), jnp.float32),
            pltpu.SemaphoreType.DMA,
        ],
        compiler_params=pltpu.CompilerParams(vmem_limit_bytes=VMEM_BYTES),
        name="gradient",
    )(plan, blocks, far(dictionary))


def gather_steps(peers):
    bits = [1 << i for i in range(peers.bit_length() - 2, 0, -1)]
    steps = []
    for first in range(0, len(bits), 2):
        pair = bits[first : first + 2]
        steps.append(pair + [sum(pair)] if len(pair) == 2 else pair)
    return steps


def gather_slots(peers):
    flips = [0]
    for masks in gather_steps(peers):
        flips = [f ^ m for m in [0] + masks for f in flips]
    return flips


def gather_pieces(piece, meanwhile):
    peers = lax.axis_size("tm")

    def exchanged(shard, mask):
        return lax.ppermute(shard, "tm", [(i, i ^ mask) for i in range(peers)])

    held = piece[None]
    for index, masks in enumerate(gather_steps(peers)):
        held = jnp.concatenate([held] + [exchanged(held, mask) for mask in masks], axis=0)
        if index == 0:
            needed, extra = meanwhile(held)
    ready, _ = lax.optimization_barrier((held, needed))
    return held, exchanged(ready, 1), extra


def recall_kernel(plan_ref, dict_hbm, when_ref, *refs):
    del when_ref
    take = taker(refs)
    olds, means = take(OUTER), take(OUTER)
    (sems,) = take(1)
    entries = olds[0].shape[1]
    fetches = [
        pltpu.make_async_copy(
            dict_hbm.at[pl.ds(first_row_of(plan_ref, step), BLOCK_ATOMS)], olds[step], sems.at[step]
        )
        for step in range(OUTER)
    ]
    for fetch in fetches:
        fetch.start()
    width = 9 * LANES if entries % (9 * LANES) == 0 else LANES
    for fetch, old_ref, mean_ref in zip(fetches, olds, means):
        fetch.wait()

        def add(step, square):
            before = old_ref[:, pl.ds(pl.multiple_of(step * width, LANES), width)]
            return square + before * before

        zeros = jnp.zeros((BLOCK_ATOMS, width), jnp.float32)
        square = lax.fori_loop(0, entries // width, add, zeros)
        mean_sq = jnp.sum(square, axis=1, keepdims=True) / (C * L) + tiny_eps
        mean_ref[...] = jnp.broadcast_to(mean_sq, mean_ref.shape)


def recall(plan, dictionary, when):
    entries = dictionary.shape[1]
    results = pl.pallas_call(
        recall_kernel,
        in_specs=[scalars(), hbm(), pl.BlockSpec(memory_space=pl.ANY)],
        out_specs=[vmem()] * (2 * OUTER),
        out_shape=[pltpu.VMEM((BLOCK_ATOMS, entries), jnp.float32)] * OUTER
        + [pltpu.VMEM((BLOCK_ATOMS, LANES), jnp.float32)] * OUTER,
        scratch_shapes=[pltpu.SemaphoreType.DMA((OUTER,))],
        compiler_params=pltpu.CompilerParams(vmem_limit_bytes=VMEM_BYTES),
        name="recall",
    )(plan, far(dictionary), when)
    return list(zip(results[:OUTER], results[OUTER:]))


def renew_kernel(plan_step, plan_ref, held_ref, came_ref, old, mean_ref, *refs):
    me = lax.axis_index("tm")
    half, _, wide = held_ref.shape
    width = wide - LANES
    entries = C * L
    last = plan_step + 1 == OUTER
    if last:
        _, out_hbm, atoms_ref, grad, sems = refs
    else:
        atoms_ref, grad = refs

    stores = []
    shares = []
    for slot, flips in enumerate(gather_slots(2 * half)):
        for source, extra in ((held_ref, 0), (came_ref, 1)):
            owner = me ^ (flips + extra)
            shares.append((source.at[slot], pl.ds(pl.multiple_of(owner * width, LANES), width)))
    zeros = jnp.zeros((BLOCK_ATOMS, width), jnp.float32)
    dot = zeros
    for source, column in shares:
        before = old[:, column]
        along = jnp.sum(source[:, width:].astype(jnp.float32), axis=1, keepdims=True)
        value = source[:, :width].astype(jnp.float32) + along * before
        grad[:, column] = value
        dot += value * before
    mean_sq = mean_ref[:, :1]
    along = jnp.sum(dot, axis=1, keepdims=True) / entries / mean_sq
    square = zeros
    for _, column in shares:
        value = grad[:, column] - along * old[:, column]
        square += value * value
    spread = jnp.sum(square, axis=1, keepdims=True) / entries + tiny_eps
    step = move_rate / jnp.sqrt(spread)
    norm = 1.0 / jnp.sqrt(mean_sq + 0.25)
    rows = pl.ds(first_row_of(plan_ref, plan_step), BLOCK_ATOMS)
    for index, (_, column) in enumerate(shares):
        before = old[:, column]
        across = grad[:, column] - along * before
        atoms_ref[:, column] = (before + step * across) * norm
        if last:
            stores.append(
                pltpu.make_async_copy(
                    atoms_ref.at[:, column], out_hbm.at[rows, column], sems.at[index]
                )
            )
            stores[-1].start()
    for store in stores:
        store.wait()


def renew(plan, step, held, came, old, mean_sq, dictionary):
    last = dictionary is not None
    atoms = (BLOCK_ATOMS, old.shape[1])
    scratch = [pltpu.VMEM(atoms, jnp.float32)]
    if last:
        scratch = scratch * 2 + [pltpu.SemaphoreType.DMA((2 * held.shape[0],))]
    return pl.pallas_call(
        functools.partial(renew_kernel, step),
        in_specs=[scalars()] + [vmem()] * 4 + [hbm()] * last,
        out_specs=hbm() if last else vmem(),
        out_shape=pltpu.HBM(dictionary.shape, jnp.float32) if last else pltpu.VMEM(atoms, jnp.float32),
        scratch_shapes=scratch,
        input_output_aliases={5: 0} if last else {},
        compiler_params=pltpu.CompilerParams(vmem_limit_bytes=VMEM_BYTES),
        name="renew",
    )(plan, held, came, resident(old), resident(mean_sq), *([far(dictionary)] if last else []))


def whole_channels(signal, codes_init, dictionary_init, threshold, plan):
    channels, segment = signal.shape
    peers = lax.axis_size("tm")
    limit = threshold[None, :]
    def swaps(edges):
        ends = [range(first, peers - 1, 2) for first in (0, 1)]
        pairs = [[p for i in end for p in ((i, i + 1), (i + 1, i))] for end in ends]
        far_first = [lax.ppermute(edge, "tm", pair) for edge, pair in zip(edges[::-1], pairs[::-1])]
        return far_first[::-1]

    state, signal, *edges = begin(codes_init, signal)
    following = swaps(edges)
    swapped = following
    taps = layout(dictionary_init, channels)
    dictionary = None
    renewed = []
    for step in range(OUTER):
        last = step + 1 == OUTER
        ferry = (dictionary_init, dictionary, COPIED[0], COPIED[1])
        atoms = renewed[-1] if renewed else None
        state, *results = iterate(
            plan, step, limit, state, swapped, signal, following, taps, atoms, ferry, peers
        )
        edges = results[:2]
        if renewed:
            taps, dictionary = results[2:]
        ferry = (dictionary_init, dictionary, sum(COPIED[: 2 * step]), COPIED[2 * step])
        payload, *results, first_edge, second_edge, dictionary = conclude(
            plan, step, limit, state, swaps(edges), signal, following, taps, ferry, peers
        )
        edges = [first_edge, second_edge]
        blocks = lax.all_to_all(payload, "tm", 0, 0, tiled=True)
        piece = share_gradient(plan, step, blocks, dictionary_init, channels // peers)
        edges, _ = lax.optimization_barrier((edges, piece))
        swapped = swaps(edges)

        def beside(held):
            if not last:
                recalled = recall(plan, dictionary_init, held)
                return (recalled[0][0], swapped), recalled
            partial, _ = lax.optimization_barrier((results[0], held))
            settled = settle(plan, partial, swapped, taps, renewed, dictionary)
            return settled[0], settled

        held, came, extra = gather_pieces(piece, beside)
        if last:
            residual, dictionary = extra
            dictionary = renew(plan, step, held, came, *recalled[step], dictionary)
        else:
            recalled, state = extra, results[0]
            renewed.append(renew(plan, step, held, came, *recalled[step], None))
    return results[1], dictionary, residual


def renew_atoms(old_atoms, across, mean_sq, spread):
    return (old_atoms + move_rate * across / jnp.sqrt(spread)[:, None]) / jnp.sqrt(mean_sq + 0.25)[
        :, None
    ]


def split_channels(signal, codes_init, dictionary_init, threshold, plan):
    segment = signal.shape[1]
    local_chan = signal.shape[0]
    unit_scale = (C * L) ** (-0.5)
    entries = C * L
    limit = threshold[:, None]

    def convolve(atom_cube, code_low):
        code_edge = shifted(code_low[:, segment - (L - 1) :], "tm", 1)
        extended = jnp.concatenate([code_edge, code_low], axis=1)
        lagged = jnp.stack(
            [extended[:, L - 1 - offset : L - 1 - offset + segment] for offset in range(L)], axis=1
        )
        return unit_scale * jnp.einsum(
            "kcl,klt->ct", atom_cube, lagged, preferred_element_type=jnp.float32
        )

    def resid_columns(resid_low):
        resid_edge = shifted(resid_low[:, : L - 1], "tm", -1)
        extended = jnp.concatenate([resid_low, resid_edge], axis=1)
        lagged = jnp.stack([extended[:, offset : offset + segment] for offset in range(L)], axis=1)
        return lagged.reshape(local_chan * L, segment)

    code_state = codes_init
    dictionary = dictionary_init
    residual = signal.astype(jnp.float32)
    for outer_step in range(OUTER):
        dict_low = dictionary.astype(jnp.bfloat16)
        atom_cube = dict_low.reshape(K, local_chan, L)
        for inner_step in range(INNER):
            code_low = code_state.astype(jnp.bfloat16)
            residual = signal.astype(jnp.float32) - convolve(atom_cube, code_low)
            lagged = resid_columns(residual.astype(jnp.bfloat16))
            partial_value = unit_scale * jnp.dot(
                dict_low, lagged, preferred_element_type=jnp.float32
            )
            scores = lax.psum(partial_value.astype(jnp.bfloat16), "chan").astype(jnp.float32)
            stepped = code_state + code_rate * scores
            code_state = stepped - jnp.clip(stepped, -limit, limit)
        code_low = code_state.astype(jnp.bfloat16)
        residual = signal.astype(jnp.float32) - convolve(atom_cube, code_low)
        lagged = resid_columns(residual.astype(jnp.bfloat16))
        first_row = plan[outer_step] * BLOCK_ATOMS
        code_block = lax.dynamic_slice_in_dim(code_low, first_row, BLOCK_ATOMS, 0)
        local_grad = lax.dot_general(
            code_block, lagged, (((1,), (1,)), ((), ())), preferred_element_type=jnp.float32
        )
        old_atoms = lax.dynamic_slice_in_dim(dictionary, first_row, BLOCK_ATOMS, 0)
        gradient = lax.psum(local_grad, "tm")
        dot_sum, square_sum = lax.psum(
            (jnp.sum(gradient * old_atoms, axis=1), jnp.sum(old_atoms * old_atoms, axis=1)), "chan"
        )
        mean_sq = square_sum / entries + tiny_eps
        along_coef = dot_sum / entries / mean_sq
        across = gradient - along_coef[:, None] * old_atoms
        spread = lax.psum(jnp.sum(across * across, axis=1), "chan") / entries + tiny_eps
        renewed = renew_atoms(old_atoms, across, mean_sq, spread)
        dictionary = lax.dynamic_update_slice_in_dim(dictionary, renewed, first_row, 0)
    return (code_state, dictionary, residual)


def shards(signal, codes_init, dictionary_init, threshold, plan):
    channels, segment = signal.shape
    peers = lax.axis_size("tm")
    fits = (
        lax.axis_size("chan") == 1
        and segment % LANES == 0
        and INNER == 2
        and OUTER == 2
        and channels % LANES == 0
        and channels % peers == 0
        and (channels // peers * L) % LANES == 0
        and peers > 2
        and peers & (peers - 1) == 0
    )
    body = whole_channels if fits else split_channels
    return body(signal, codes_init, dictionary_init, threshold, plan)


def solution(mesh):
    placed = (P("chan", "tm"), P(None, "tm"), P(None, "chan"), P(), P())
    return jax.shard_map(
        shards,
        mesh=mesh,
        in_specs=placed,
        out_specs=(P(None, "tm"), P(None, "chan"), P("chan", "tm")),
        check_vma=False,
    )
```
